32 devices in a mesh: kx: 4 (over z), ht: 2 (over y), real: 4 (over x, core).
Axes of the slice: x: 2, y: 2, z: 4, core: 2. Of those that a mesh axis runs over, the one named last changes fastest.
Arguments:
- velocity: float32 [3, 4, 16, 512, 128], P(None, 'real', 'kx', 'ht'), may hold values from -6 to 6
- low_index: int32 [8], replicated, may hold values from 0 to 15, as said below
- neighbours: int32 [16, 8], P('kx'), may hold values from 0 to 15, as said below
- owner_map: int32 [64], replicated, may hold values from 0 to 63, each once
- mode_counts: int32 [16], P('kx'), may hold values from 16 to 64
- helmholtz: float32 [64, 512, 512], P(('kx', 'ht')), may hold values from -0.25 to 0.25
Outputs:
- velocity_next: float32 [3, 4, 16, 512, 128], P(None, 'real', 'kx', 'ht')
The draws below stay inside these ranges and needn't reach their ends.
Inputs may be any that keep to these rules, and one draw needn't show every extreme that they name: `low_index`: distinct values. neighbours[m, j] lies within 4 modes of m, counting circularly over the 16 modes; offsets of + 4 and - 4 both occur.
All inputs are finite; a program needn't handle non-finite values.
Results may differ from the reference program's by a relative error of at most 0.0001.
Values sent between devices are 32-bit elements; how exact they have to be, the bound alone decides.
No kernel may reach another device: no remote copies, remote signals or barrier semaphores. Data moves between devices by JAX's collectives and lax.ppermute only.
A program may use at most 128 MiB of HBM per device.

```python
import jax
import jax.numpy as jnp
from jax import lax

COMP = 3
REALS = 4
KX_DEV = 4
KX = 16
NLOW = 8
KZ = 64
NZP = 256
NY = 512
SUBSTEPS = 1


def draw_low_index(key, part):
    return jax.random.permutation(key, KX)[:NLOW].astype(jnp.int32)


def draw_neighbours(key, part):
    offsets = jax.random.randint(jax.random.fold_in(key, 1), (KX * NLOW,), -KX_DEV, KX_DEV + 1)
    first_pick = jax.random.randint(jax.random.fold_in(key, 2), (), 0, KX * NLOW)
    second_pick = (first_pick + 1 + jax.random.randint(jax.random.fold_in(key, 3), (), 0, KX * NLOW - 1)) % (KX * NLOW)
    flat_offsets = offsets.at[first_pick].set(KX_DEV).at[second_pick].set(-KX_DEV)
    return ((jnp.arange(KX)[:, None] + flat_offsets.reshape(KX, NLOW)) % KX).astype(jnp.int32)


def set_ends(drawn, own_key, smallest, largest):
    place = [jax.random.randint(jax.random.fold_in(own_key, axis), (), 0, length) for axis, length in enumerate(drawn.shape)]
    main_axis = drawn.shape.index(max(drawn.shape))
    next_to = place[:main_axis] + [(place[main_axis] + 1) % drawn.shape[main_axis]] + place[main_axis + 1:]
    return drawn.at[tuple(place)].set(smallest).at[tuple(next_to)].set(largest)


def shard_levels(own_key, extent, pieces, low, largest):
    def one(position, shards_of):
        steps = jax.random.uniform(jax.random.fold_in(jax.random.fold_in(own_key, 6), position), (shards_of,), jnp.float32, low / len(pieces), largest / len(pieces))
        return jnp.repeat(jnp.exp(steps), extent[position] // shards_of).reshape((-1,) + (1,) * (len(extent) - position - 1))

    gain = one(*pieces[0])
    for cut in pieces[1:]:
        gain = gain * one(*cut)
    return gain


def noise(rng, shape, spread, most, pieces=(), held_as=jnp.bfloat16):
    gain = shard_levels(rng, shape, pieces, -0.22, 0.18) if pieces else 1.0
    drawn = jax.random.normal(rng, shape, jnp.float32) * spread * gain
    return jnp.minimum(jnp.maximum(drawn, -most), most).astype(held_as)


def setup_inputs(seed: int = 0) -> dict:
    streams_of = jax.random.split(jax.random.key(seed), 7)
    return {
        "velocity": noise(streams_of[0], (COMP, REALS, KX, NY, 2 * KZ), 1.0, 6.0, ((1, 4), (2, 4), (3, 2)), jnp.float32),
        "low_index": draw_low_index(jax.random.fold_in(streams_of[6], 71), 0),
        "neighbours": draw_neighbours(jax.random.fold_in(streams_of[6], 71), 0),
        "owner_map": jax.random.permutation(streams_of[3], KZ).astype(jnp.int32),
        "mode_counts": set_ends(jax.random.randint(streams_of[4], (KX,), KZ // 4, KZ + 1), jax.random.fold_in(streams_of[4], 1), KZ // 4, KZ).astype(jnp.int32),
        "helmholtz": noise(streams_of[5], (KZ, NY, NY), NY ** -0.5, 0.25, ((0, 8),), jnp.float32),
    }


dt_step = 0.1

def spanwise_tables(mode_count, point_count):
    column_ids = jnp.arange(2 * mode_count)
    wavenumber = (column_ids // 2).astype(jnp.float32)
    imag_part = column_ids % 2
    positions = 2.0 * jnp.pi * jnp.arange(point_count).astype(jnp.float32) / point_count
    phases = wavenumber[:, None] * positions[None, :]
    forward = jnp.where(imag_part[:, None] == 0, jnp.cos(phases), -jnp.sin(phases)) / jnp.sqrt(jnp.float32(mode_count))
    backward = forward.T * (2.0 * mode_count / point_count)
    return (forward, backward)

def reference(velocity, low_index, neighbours, owner_map, mode_counts, helmholtz):
    highest = lax.Precision.HIGHEST
    forward, backward = spanwise_tables(KZ, NZP)
    kx_modes = jnp.arange(KX, dtype=jnp.int32)
    low_select = (low_index[:, None] == kx_modes[None, :]).astype(jnp.float32)
    high_mask = 1.0 - lax.optimization_barrier(jnp.sum(low_select, axis=0))
    column_mask = ((jnp.arange(2 * KZ) // 2)[None, :] < mode_counts[:, None]).astype(jnp.float32)
    inverse_map = jnp.zeros((KZ,), jnp.int32).at[owner_map].set(jnp.arange(KZ, dtype=jnp.int32))
    current = velocity

    def one_real(fields):
        physical = jnp.dot(fields, forward, precision=highest)
        low_fields = jnp.einsum('jm,cmyz->cjyz', low_select, physical, precision=highest)
        high_low = jnp.zeros_like(physical)
        stresses = []
        for member in range(NLOW):
            partner = jnp.take(physical, neighbours[:, member], axis=1)
            low_one = low_fields[:, member:member + 1]
            high_low = high_low + low_one * partner[1:2] + partner * low_one[1:2]
            weighted = physical * (partner[1:2] * high_mask[None, :, None, None])
            stresses.append(lax.optimization_barrier(jnp.sum(weighted, axis=1)))
        return (jnp.dot(high_low, backward, precision=highest), jnp.stack(stresses, axis=1))
    for substep in range(SUBSTEPS):
        nonlinear, stress = lax.map(one_real, jnp.moveaxis(current, 1, 0))
        nonlinear = jnp.moveaxis(nonlinear, 0, 1)
        low_forcing = jnp.dot(lax.optimization_barrier(jnp.sum(stress, axis=0)) / REALS, backward, precision=highest)
        forcing = nonlinear * high_mask[None, None, :, None, None]
        forcing = forcing + jnp.einsum('jm,cjyk->cmyk', low_select, low_forcing, precision=highest)[:, None]
        forcing = forcing * column_mask[None, None, :, None, :]
        updated = current + dt_step * forcing
        slotted = jnp.take(updated.reshape(COMP, REALS, KX, NY, KZ, 2), owner_map, axis=4)
        solved = jnp.einsum('syx,crmxsp->crmysp', helmholtz, slotted, precision=highest)
        current = jnp.take(solved, inverse_map, axis=4).reshape(COMP, REALS, KX, NY, 2 * KZ)
    return current
```

```python
import jax
import jax.numpy as jnp
from jax import lax
from jax.sharding import PartitionSpec as P

dt_step = 0.1


def spanwise_tables(mode_count, point_count):
    column_ids = jnp.arange(2 * mode_count)
    wavenumber = (column_ids // 2).astype(jnp.float32)
    imag_part = column_ids % 2
    positions = 2.0 * jnp.pi * jnp.arange(point_count).astype(jnp.float32) / point_count
    phases = wavenumber[:, None] * positions[None, :]
    forward = jnp.where(imag_part[:, None] == 0, jnp.cos(phases), -jnp.sin(phases)) / jnp.sqrt(
        jnp.float32(mode_count)
    )
    backward = forward.T * (2.0 * mode_count / point_count)
    return (forward, backward)


def nonlinear_rows(fields, low_index, neighbours, mode_counts, forward, backward):
    precision = lax.Precision.HIGH
    realizations, modes, columns = (fields.shape[1], fields.shape[2], fields.shape[4])
    low_select = (low_index[:, None] == jnp.arange(modes)[None, :]).astype(jnp.float32)
    high_mask = 1.0 - jnp.sum(low_select, axis=0)
    high_rows = high_mask[None, None, :, None, None]
    column_mask = ((jnp.arange(columns) // 2)[None, :] < mode_counts[:, None]).astype(jnp.float32)
    physical = jnp.dot(fields, forward, precision=precision)
    low_fields = jnp.take(physical, low_index, axis=2)
    high_low = jnp.zeros_like(physical)
    stresses = []
    for member in range(low_index.shape[0]):
        partner = jnp.take(physical, neighbours[:, member], axis=2)
        low_one = low_fields[:, :, member : member + 1]
        high_low = high_low + low_one * partner[1:2] + partner * low_one[1:2]
        stresses.append(jnp.sum(physical * (partner[1:2] * high_rows), axis=(1, 2)))
    stress = jnp.stack(stresses, axis=1) / realizations
    forcing = jnp.dot(high_low, backward, precision=precision) * high_rows
    low_forcing = jnp.dot(stress, backward, precision=precision)
    low_rows = jnp.einsum("jm,cjyk->cmyk", low_select, low_forcing, precision=lax.Precision.HIGHEST)
    forcing = (forcing + low_rows[:, None]) * column_mask[None, None, :, None, :]
    return fields + dt_step * forcing


def local(velocity, low_index, neighbours, owner_map, mode_counts, helmholtz):
    components, reals_dev, band_modes, rows_ht, columns = velocity.shape
    kz_modes = columns // 2
    forward, backward = spanwise_tables(kz_modes, 4 * kz_modes)
    kx_count, ht_count = (lax.axis_size("kx"), lax.axis_size("ht"))
    real_count = lax.axis_size("real")
    modes, realizations = (band_modes * kx_count, reals_dev * real_count)
    slots_dev = kz_modes // (kx_count * ht_count)
    rows_dev = rows_ht // (kx_count * real_count)
    small = jnp.concatenate([neighbours, mode_counts[:, None]], axis=1)
    small = lax.all_gather(small, "kx", axis=0, tiled=True)
    neighbours, mode_counts = (small[:, :-1], small[:, -1])
    inverse_map = (
        jnp.zeros((kz_modes,), jnp.int32).at[owner_map].set(jnp.arange(kz_modes, dtype=jnp.int32))
    )
    split = velocity.reshape(
        components, reals_dev, band_modes, kx_count * real_count, rows_dev, columns
    )
    split = split.transpose(3, 0, 1, 2, 4, 5)
    split = lax.all_to_all(split, ("kx", "real"), split_axis=0, concat_axis=0, tiled=True)
    fields = split.reshape(
        kx_count, real_count, components, reals_dev, band_modes, rows_dev, columns
    )
    fields = fields.transpose(2, 1, 3, 0, 4, 5, 6).reshape(
        components, realizations, modes, rows_dev, columns
    )
    updated = nonlinear_rows(fields, low_index, neighbours, mode_counts, forward, backward)
    slotted = jnp.take(
        updated.reshape(components, realizations, modes, rows_dev, kz_modes, 2), owner_map, axis=4
    )
    slotted = slotted.reshape(
        components, real_count, reals_dev, modes, rows_dev, kx_count * ht_count, slots_dev, 2
    )
    outgoing = slotted.transpose(5, 1, 6, 2, 0, 3, 7, 4).reshape(
        kx_count * ht_count * real_count, slots_dev, reals_dev * components * modes * 2, rows_dev
    )
    incoming = lax.all_to_all(
        outgoing, ("kx", "ht", "real"), split_axis=0, concat_axis=0, tiled=True
    )
    incoming = incoming.reshape(
        kx_count, ht_count, real_count, slots_dev, reals_dev * components * modes * 2, rows_dev
    )
    incoming = incoming.transpose(3, 4, 1, 0, 2, 5).reshape(
        slots_dev, reals_dev * components * modes * 2, ht_count * rows_ht
    )
    solved = jnp.einsum("syx,snx->sny", helmholtz, incoming, precision=lax.Precision.HIGH)
    solved = solved.reshape(
        slots_dev, reals_dev, components, kx_count, band_modes, 2, ht_count, rows_ht
    )
    solved = solved.transpose(3, 6, 0, 5, 1, 2, 4, 7).reshape(
        kx_count * ht_count, slots_dev * 2, reals_dev * components * band_modes, rows_ht
    )
    returned = lax.all_to_all(solved, ("kx", "ht"), split_axis=0, concat_axis=0, tiled=True)
    restored = returned.reshape(
        kz_modes, 2, reals_dev, components, band_modes, rows_ht
    )
    restored = jnp.take(restored, inverse_map, axis=0)
    return restored.transpose(3, 2, 4, 5, 0, 1).reshape(velocity.shape)


def solution(mesh):
    in_specs = (
        P(None, "real", "kx", "ht", None),
        P(),
        P("kx", None),
        P(),
        P("kx"),
        P(("kx", "ht"), None, None),
    )
    out_specs = P(None, "real", "kx", "ht", None)
    return jax.shard_map(local, mesh=mesh, in_specs=in_specs, out_specs=out_specs, check_vma=False)
```

```python
import functools

import jax
import jax.numpy as jnp
from jax import lax
from jax.experimental import pallas as pl
from jax.experimental.pallas import tpu as pltpu
from jax.sharding import PartitionSpec as P

dt_step = 0.1


def spanwise_tables(mode_count, point_count):
    column_ids = jnp.arange(2 * mode_count)
    wavenumber = (column_ids // 2).astype(jnp.float32)
    imag_part = column_ids % 2
    positions = 2.0 * jnp.pi * jnp.arange(point_count).astype(jnp.float32) / point_count
    phases = wavenumber[:, None] * positions[None, :]
    forward = jnp.where(imag_part[:, None] == 0, jnp.cos(phases), -jnp.sin(phases)) / jnp.sqrt(
        jnp.float32(mode_count)
    )
    backward = forward.T * (2.0 * mode_count / point_count)
    return (forward, backward)


def nonlinear_rows(fields, low_index, neighbours, mode_counts, forward, backward):
    precision = lax.Precision.HIGH
    realizations, modes, columns = (fields.shape[1], fields.shape[2], fields.shape[4])
    low_select = (low_index[:, None] == jnp.arange(modes)[None, :]).astype(jnp.float32)
    high_mask = 1.0 - jnp.sum(low_select, axis=0)
    high_rows = high_mask[None, None, :, None, None]
    column_mask = ((jnp.arange(columns) // 2)[None, :] < mode_counts[:, None]).astype(jnp.float32)
    physical = jnp.dot(fields, forward, precision=precision)
    low_fields = jnp.take(physical, low_index, axis=2)
    high_low = jnp.zeros_like(physical)
    stresses = []
    for member in range(low_index.shape[0]):
        partner = jnp.take(physical, neighbours[:, member], axis=2)
        low_one = low_fields[:, :, member : member + 1]
        high_low = high_low + low_one * partner[1:2] + partner * low_one[1:2]
        stresses.append(jnp.sum(physical * (partner[1:2] * high_rows), axis=(1, 2)))
    stress = jnp.stack(stresses, axis=1) / realizations
    forcing = jnp.dot(high_low, backward, precision=precision) * high_rows
    low_forcing = jnp.dot(stress, backward, precision=precision)
    low_rows = jnp.einsum("jm,cjyk->cmyk", low_select, low_forcing, precision=lax.Precision.HIGHEST)
    forcing = (forcing + low_rows[:, None]) * column_mask[None, None, :, None, :]
    return fields + dt_step * forcing


def local_plain(velocity, low_index, neighbours, owner_map, mode_counts, helmholtz):
    components, reals_dev, band_modes, rows_ht, columns = velocity.shape
    kz_modes = columns // 2
    forward, backward = spanwise_tables(kz_modes, 4 * kz_modes)
    kx_count, ht_count = (lax.axis_size("kx"), lax.axis_size("ht"))
    real_count = lax.axis_size("real")
    modes, realizations = (band_modes * kx_count, reals_dev * real_count)
    slots_dev = kz_modes // (kx_count * ht_count)
    rows_dev = rows_ht // (kx_count * real_count)
    small = jnp.concatenate([neighbours, mode_counts[:, None]], axis=1)
    small = lax.all_gather(small, "kx", axis=0, tiled=True)
    neighbours, mode_counts = (small[:, :-1], small[:, -1])
    inverse_map = (
        jnp.zeros((kz_modes,), jnp.int32).at[owner_map].set(jnp.arange(kz_modes, dtype=jnp.int32))
    )
    split = velocity.reshape(
        components, reals_dev, band_modes, kx_count * real_count, rows_dev, columns
    )
    split = split.transpose(3, 0, 1, 2, 4, 5)
    split = lax.all_to_all(split, ("kx", "real"), split_axis=0, concat_axis=0, tiled=True)
    fields = split.reshape(
        kx_count, real_count, components, reals_dev, band_modes, rows_dev, columns
    )
    fields = fields.transpose(2, 1, 3, 0, 4, 5, 6).reshape(
        components, realizations, modes, rows_dev, columns
    )
    updated = nonlinear_rows(fields, low_index, neighbours, mode_counts, forward, backward)
    slotted = jnp.take(
        updated.reshape(components, realizations, modes, rows_dev, kz_modes, 2), owner_map, axis=4
    )
    slotted = slotted.reshape(
        components, real_count, reals_dev, modes, rows_dev, kx_count * ht_count, slots_dev, 2
    )
    outgoing = slotted.transpose(5, 1, 6, 2, 0, 3, 7, 4).reshape(
        kx_count * ht_count * real_count, slots_dev, reals_dev * components * modes * 2, rows_dev
    )
    incoming = lax.all_to_all(
        outgoing, ("kx", "ht", "real"), split_axis=0, concat_axis=0, tiled=True
    )
    incoming = incoming.reshape(
        kx_count, ht_count, real_count, slots_dev, reals_dev * components * modes * 2, rows_dev
    )
    incoming = incoming.transpose(3, 4, 1, 0, 2, 5).reshape(
        slots_dev, reals_dev * components * modes * 2, ht_count * rows_ht
    )
    solved = jnp.einsum("syx,snx->sny", helmholtz, incoming, precision=lax.Precision.HIGH)
    solved = solved.reshape(
        slots_dev, reals_dev, components, kx_count, band_modes, 2, ht_count, rows_ht
    )
    solved = solved.transpose(3, 6, 0, 5, 1, 2, 4, 7).reshape(
        kx_count * ht_count, slots_dev * 2, reals_dev * components * band_modes, rows_ht
    )
    returned = lax.all_to_all(solved, ("kx", "ht"), split_axis=0, concat_axis=0, tiled=True)
    restored = returned.reshape(
        kz_modes, 2, reals_dev, components, band_modes, rows_ht
    )
    restored = jnp.take(restored, inverse_map, axis=0)
    return restored.transpose(3, 2, 4, 5, 0, 1).reshape(velocity.shape)


LANES = 128
PIECES = 1
VMEM = pl.BlockSpec(memory_space=pltpu.VMEM)
SMEM = pl.BlockSpec(memory_space=pltpu.SMEM)


def params():
    return pltpu.CompilerParams(vmem_limit_bytes=48 * 1024 * 1024)


def two_parts(value):
    top = value.astype(jnp.bfloat16)
    rest = (value - top.astype(jnp.float32)).astype(jnp.bfloat16)
    return top, rest


def dot(left, right, dims=((1,), (0,))):
    return lax.dot_general(left, right, (dims, ((), ())), preferred_element_type=jnp.float32)


def nonlinear_kernel(
    low_ref, near_ref, block_ref, first_ref, second_ref, back_ref, mask_ref,
    slotted_ref, stress_ref, physical, products, sums, high_ref,
):
    bands, components, band_modes, rows, columns = block_ref.shape
    modes, points = (bands * band_modes, physical.shape[3])
    members, highs = (stress_ref.shape[1], products.shape[1])
    found = jnp.int32(0)
    for mode in range(modes):
        is_low = jnp.int32(0)
        for member in range(members):
            is_low = is_low | (low_ref[member] == mode).astype(jnp.int32)
        high_ref[found] = mode
        found = found + 1 - is_low

    def transform(step, carry):
        band, component = (step // components, step % components)
        top, rest = two_parts(block_ref[band, component].reshape(band_modes * rows, columns))
        both = dot(jnp.concatenate([top, rest], axis=1), first_ref[...])
        fields = both[:, :points] + dot(top, second_ref[...])
        place = pl.ds(band * band_modes, band_modes)
        physical[component, place] = fields.reshape(band_modes, rows, points)
        slotted_ref[component, place] = both[:, points:].reshape(band_modes, rows, columns)
        return carry

    lax.fori_loop(0, bands * components, transform, 0)

    def pairs(step, carry):
        halves = points // LANES
        place = (
            pl.ds(pl.multiple_of((step // halves) * 8, 8), 8),
            pl.ds(pl.multiple_of((step % halves) * LANES, LANES), LANES),
        )

        def one_high(index, totals):
            mode = high_ref[index]
            own = [physical[(c, mode) + place] for c in range(components)]
            result = [jnp.zeros((8, LANES), jnp.float32) for _ in range(components)]
            totals = list(totals)
            for member in range(members):
                low = low_ref[member]
                near = near_ref[mode, member]
                partner = [physical[(c, near) + place] for c in range(components)]
                low_one = [physical[(c, low) + place] for c in range(components)]
                for c in range(components):
                    if c == 1:
                        result[c] = result[c] + low_one[1] * partner[1]
                    else:
                        result[c] = result[c] + (low_one[c] * partner[1] + partner[c] * low_one[1])
                    slot = member * components + c
                    totals[slot] = totals[slot] + own[c] * partner[1]
            for c in range(components):
                products[(c, index) + place] = result[c] * 2.0 if c == 1 else result[c]
            return tuple(totals)

        empty = tuple(jnp.zeros((8, LANES), jnp.float32) for _ in range(members * components))
        totals = lax.fori_loop(0, highs, one_high, empty)
        for member in range(members):
            for c in range(components):
                sums[(c, member) + place] = totals[member * components + c]
        return carry

    lax.fori_loop(0, (rows // 8) * (points // LANES), pairs, 0)

    def inverse(fields):
        top, rest = two_parts(fields)
        both = dot(top, back_ref[...])
        return both[:, :columns] + both[:, columns:] + dot(rest, back_ref[:, :columns])

    def finish(component, carry):
        forcing = inverse(products[component].reshape(highs * rows, points))
        forcing = forcing.reshape(highs, rows, columns)
        for index in range(highs):
            mode = high_ref[index]
            slotted_ref[component, mode] += forcing[index] * mask_ref[mode]
        stress = inverse(sums[component].reshape(members * rows, points))
        stress_ref[component] = stress.reshape(members, rows, columns)
        return carry

    lax.fori_loop(0, components, finish, 0)


def nonlinear(block, low_index, neighbours, tables, mask):
    bands, components, band_modes, rows, columns = block.shape
    members, modes, points = (low_index.shape[0], bands * band_modes, 2 * columns)
    highs = modes - members
    return pl.pallas_call(
        nonlinear_kernel,
        out_shape=(
            jax.ShapeDtypeStruct((components, modes, rows, columns), jnp.float32),
            jax.ShapeDtypeStruct((components, members, rows, columns), jnp.float32),
        ),
        in_specs=[SMEM, SMEM] + [VMEM] * 5,
        out_specs=(VMEM, VMEM),
        scratch_shapes=[
            pltpu.VMEM((components, modes, rows, points), jnp.float32),
            pltpu.VMEM((components, highs, rows, points), jnp.float32),
            pltpu.VMEM((components, members, rows, points), jnp.float32),
            pltpu.SMEM((modes + 1,), jnp.int32),
        ],
        compiler_params=params(),
        name="nonlinear",
    )(low_index, neighbours, block, *tables, mask)


def outgoing_kernel(low_ref, slotted_ref, stress_ref, mask_ref, out_ref, full, *, groups, owners):
    components, modes, rows, columns = slotted_ref.shape
    members = stress_ref.shape[1]
    per_slot = out_ref.shape[0] // (columns // 2)
    full[...] = slotted_ref[...]
    for member in range(members):
        mode = low_ref[member]
        for c in range(components):
            full[c, mode] += stress_ref[c, member] * mask_ref[mode]
    inner = modes // groups
    for c in range(components):
        for part in range(inner):
            tile = jnp.concatenate([full[c, part + inner * g] for g in range(groups)], axis=0)
            turned = tile.T
            band_low, band_mode = (part // owners["band"], part % owners["band"])
            for p in range(2):
                row = ((band_low * 2 + p) * components + c) * owners["band"] + band_mode
                out_ref[pl.ds(row, columns // 2, stride=per_slot), :] = turned[
                    p * (columns // 2) : (p + 1) * (columns // 2)
                ]


def outgoing(slotted, stress, low_index, mask, groups, band_modes):
    components, modes, rows, columns = slotted.shape
    per_slot = (modes // groups) * 2 * components
    return pl.pallas_call(
        functools.partial(outgoing_kernel, groups=groups, owners={"band": band_modes}),
        out_shape=jax.ShapeDtypeStruct((columns // 2 * per_slot, groups * rows), jnp.float32),
        in_specs=[SMEM, VMEM, VMEM, VMEM],
        out_specs=VMEM,
        scratch_shapes=[pltpu.VMEM(slotted.shape, jnp.float32)],
        compiler_params=params(),
        name="outgoing",
    )(low_index, slotted, stress, mask)


def regroup(blocks, rows):
    count = len(blocks)
    lane = lax.broadcasted_iota(jnp.int32, blocks[0].shape, 1) // rows
    step = 1
    while step < count:
        take = (lane & step) == 0
        for i in range(count):
            if i & step == 0:
                here, there = (blocks[i], blocks[i + step])
                blocks[i] = jnp.where(take, here, pltpu.roll(there, step * rows, 1))
                blocks[i + step] = jnp.where(
                    take, pltpu.roll(here, LANES - step * rows, 1), there
                )
        step *= 2
    return blocks


def solve_kernel(*refs, groups, kx_count, ht_count):
    pieces = len(refs) - 2
    block_refs, matrix_ref, out_ref = (refs[:pieces], refs[pieces], refs[pieces + 1])
    rows = LANES // groups
    tiles = []
    for h in range(ht_count):
        for piece in range(pieces):
            for first in range(0, kx_count, groups):
                blocks = [
                    block_refs[piece][(first + g) * ht_count + h, 0] for g in range(groups)
                ]
                tiles.append(jnp.concatenate(regroup(blocks, rows), axis=0))
    top, rest = two_parts(jnp.concatenate(tiles, axis=1))
    count = top.shape[0]
    matrix_top, matrix_rest = two_parts(matrix_ref[0])
    last = ((1,), (1,))
    both = dot(jnp.concatenate([top, rest], axis=0), matrix_top, last)
    solved = both[:count] + both[count:] + dot(top, matrix_rest, last)
    lane_tiles, per_band = out_ref.shape[2:4]
    for band in range(kx_count):
        for tile in range(ht_count * lane_tiles):
            out_ref[band * ht_count + tile // lane_tiles, 0, tile % lane_tiles] = solved[
                band * per_band : (band + 1) * per_band, tile * LANES : (tile + 1) * LANES
            ]


def solve(blocks, helmholtz, groups, kx_count, ht_count):
    owners, slots, per_slot, lanes = blocks[0].shape
    heights = helmholtz.shape[1]
    lane_tiles = heights // ht_count // LANES
    out = (owners, slots, lane_tiles, per_slot * groups // kx_count, LANES)
    return pl.pallas_call(
        functools.partial(solve_kernel, groups=groups, kx_count=kx_count, ht_count=ht_count),
        out_shape=jax.ShapeDtypeStruct(out, jnp.float32),
        grid=(slots,),
        in_specs=[pl.BlockSpec((owners, 1, per_slot, lanes), lambda s: (0, s, 0, 0))] * len(blocks)
        + [pl.BlockSpec((1, heights, heights), lambda s: (s, 0, 0))],
        out_specs=pl.BlockSpec((owners, 1) + out[2:], lambda s: (0, s, 0, 0, 0)),
        compiler_params=params(),
        name="solve",
    )(*blocks, helmholtz)


def restore_kernel(block_ref, order_ref, out_ref):
    components, band_modes, rows, columns = out_ref.shape
    slots = columns // 2
    per_slot = block_ref.shape[0] // slots
    for c in range(components):
        for mode in range(band_modes):
            for tile in range(rows // LANES):
                parts = []
                for p in range(2):
                    row = ((tile * 2 + p) * components + c) * band_modes + mode
                    parts.append(block_ref[pl.ds(row, slots, stride=per_slot), :])
                top, rest = two_parts(jnp.concatenate(parts, axis=0))
                both = jnp.concatenate([top, rest], axis=0)
                out_ref[c, mode, pl.ds(tile * LANES, LANES)] = dot(
                    both, order_ref[...], ((0,), (0,))
                )


def restore(block, order, components, band_modes, rows):
    columns = order.shape[1]
    return pl.pallas_call(
        restore_kernel,
        out_shape=jax.ShapeDtypeStruct((components, band_modes, rows, columns), jnp.float32),
        in_specs=[VMEM, VMEM],
        out_specs=VMEM,
        compiler_params=params(),
        name="restore",
    )(block, order)


def table_parts(value):
    top = lax.reduce_precision(value, 8, 7)
    return top.astype(jnp.bfloat16), (value - top).astype(jnp.bfloat16)


def slot_tables(owner_map, mode_counts, columns, realizations):
    forward, backward = spanwise_tables(columns // 2, 2 * columns)
    slot_columns = (2 * owner_map[None, :] + jnp.arange(2)[:, None]).reshape(columns)
    select = slot_columns[None, :] == jnp.arange(columns)[:, None]
    forward_top, forward_rest = table_parts(forward)
    first = jnp.concatenate([forward_top, select.astype(jnp.bfloat16)], axis=1)
    first = jnp.concatenate([first, first], axis=0)
    slotted_back = jnp.dot(
        backward, select.astype(jnp.float32), precision=lax.Precision.HIGHEST
    )
    back = jnp.concatenate(table_parts(slotted_back), axis=1)
    active = (slot_columns // 2)[None, :] < mode_counts[:, None]
    mask = jnp.where(active, jnp.float32(dt_step), 0.0)[:, None, :]
    order = select.T.astype(jnp.bfloat16)
    order = jnp.concatenate([order, order], axis=0)
    return (first, forward_rest, back), mask, mask / realizations, order


def local(velocity, low_index, neighbours, owner_map, mode_counts, helmholtz):
    components, reals_dev, band_modes, rows_ht, columns = velocity.shape
    kx_count, ht_count = (lax.axis_size("kx"), lax.axis_size("ht"))
    owners, pieces = (kx_count * ht_count, PIECES)
    rows = rows_ht // (kx_count * pieces)
    groups = LANES // rows if rows else 0
    slots = columns // 2 // owners
    if (
        columns != LANES or reals_dev != 1 or rows_ht % LANES or rows % 8 or LANES % rows or kx_count % groups
        or (band_modes * 2 * components) % 8 or slots % 8 or low_index.shape[0] >= kx_count * band_modes
    ):
        return local_plain(velocity, low_index, neighbours, owner_map, mode_counts, helmholtz)
    realizations = lax.axis_size("real")
    small = jnp.concatenate([neighbours, mode_counts[:, None]], axis=1)
    small = lax.all_gather(small, "kx", axis=0, tiled=True)
    neighbours, mode_counts = (small[:, :-1], small[:, -1])
    tables, mask, low_mask, order = slot_tables(owner_map, mode_counts, columns, realizations)
    split = velocity.reshape(components, band_modes, pieces, kx_count, rows, columns)
    received = []
    for piece in range(pieces):
        part = split[:, :, piece].transpose(2, 0, 1, 3, 4)
        part = lax.all_to_all(part, "kx", split_axis=0, concat_axis=0, tiled=True)
        slotted, stress = nonlinear(part, low_index, neighbours, tables, mask)
        stress = lax.psum(stress, "real")
        block = outgoing(slotted, stress, low_index, low_mask, groups, band_modes)
        block = block.reshape(owners, slots, -1, LANES)
        received.append(
            lax.all_to_all(block, ("kx", "ht"), split_axis=0, concat_axis=0, tiled=True)
        )
    solved = solve(received, helmholtz, groups, kx_count, ht_count)
    returned = lax.all_to_all(solved, ("kx", "ht"), split_axis=0, concat_axis=0, tiled=True)
    result = restore(returned.reshape(-1, LANES), order, components, band_modes, rows_ht)
    return result.reshape(velocity.shape)


def solution(mesh):
    in_specs = (
        P(None, "real", "kx", "ht", None),
        P(),
        P("kx", None),
        P(),
        P("kx"),
        P(("kx", "ht"), None, None),
    )
    out_specs = P(None, "real", "kx", "ht", None)
    return jax.shard_map(local, mesh=mesh, in_specs=in_specs, out_specs=out_specs, check_vma=False)
```

```python
import functools

import jax
import jax.numpy as jnp
from jax import lax
from jax.experimental import pallas as pl
from jax.experimental.pallas import tpu as pltpu
from jax.sharding import PartitionSpec as P

dt_step = 0.1


def spanwise_tables(mode_count, point_count):
    column_ids = jnp.arange(2 * mode_count)
    wavenumber = (column_ids // 2).astype(jnp.float32)
    imag_part = column_ids % 2
    positions = 2.0 * jnp.pi * jnp.arange(point_count).astype(jnp.float32) / point_count
    phases = wavenumber[:, None] * positions[None, :]
    forward = jnp.where(imag_part[:, None] == 0, jnp.cos(phases), -jnp.sin(phases)) / jnp.sqrt(
        jnp.float32(mode_count)
    )
    backward = forward.T * (2.0 * mode_count / point_count)
    return (forward, backward)


def nonlinear_rows(fields, low_index, neighbours, mode_counts, forward, backward):
    precision = lax.Precision.HIGH
    realizations, modes, columns = (fields.shape[1], fields.shape[2], fields.shape[4])
    low_select = (low_index[:, None] == jnp.arange(modes)[None, :]).astype(jnp.float32)
    high_mask = 1.0 - jnp.sum(low_select, axis=0)
    high_rows = high_mask[None, None, :, None, None]
    column_mask = ((jnp.arange(columns) // 2)[None, :] < mode_counts[:, None]).astype(jnp.float32)
    physical = jnp.dot(fields, forward, precision=precision)
    low_fields = jnp.take(physical, low_index, axis=2)
    high_low = jnp.zeros_like(physical)
    stresses = []
    for member in range(low_index.shape[0]):
        partner = jnp.take(physical, neighbours[:, member], axis=2)
        low_one = low_fields[:, :, member : member + 1]
        high_low = high_low + low_one * partner[1:2] + partner * low_one[1:2]
        stresses.append(jnp.sum(physical * (partner[1:2] * high_rows), axis=(1, 2)))
    stress = jnp.stack(stresses, axis=1) / realizations
    forcing = jnp.dot(high_low, backward, precision=precision) * high_rows
    low_forcing = jnp.dot(stress, backward, precision=precision)
    low_rows = jnp.einsum("jm,cjyk->cmyk", low_select, low_forcing, precision=lax.Precision.HIGHEST)
    forcing = (forcing + low_rows[:, None]) * column_mask[None, None, :, None, :]
    return fields + dt_step * forcing


def local_plain(velocity, low_index, neighbours, owner_map, mode_counts, helmholtz):
    components, reals_dev, band_modes, rows_ht, columns = velocity.shape
    kz_modes = columns // 2
    forward, backward = spanwise_tables(kz_modes, 4 * kz_modes)
    kx_count, ht_count = (lax.axis_size("kx"), lax.axis_size("ht"))
    real_count = lax.axis_size("real")
    modes, realizations = (band_modes * kx_count, reals_dev * real_count)
    slots_dev = kz_modes // (kx_count * ht_count)
    rows_dev = rows_ht // (kx_count * real_count)
    small = jnp.concatenate([neighbours, mode_counts[:, None]], axis=1)
    small = lax.all_gather(small, "kx", axis=0, tiled=True)
    neighbours, mode_counts = (small[:, :-1], small[:, -1])
    inverse_map = (
        jnp.zeros((kz_modes,), jnp.int32).at[owner_map].set(jnp.arange(kz_modes, dtype=jnp.int32))
    )
    split = velocity.reshape(
        components, reals_dev, band_modes, kx_count * real_count, rows_dev, columns
    )
    split = split.transpose(3, 0, 1, 2, 4, 5)
    split = lax.all_to_all(split, ("kx", "real"), split_axis=0, concat_axis=0, tiled=True)
    fields = split.reshape(
        kx_count, real_count, components, reals_dev, band_modes, rows_dev, columns
    )
    fields = fields.transpose(2, 1, 3, 0, 4, 5, 6).reshape(
        components, realizations, modes, rows_dev, columns
    )
    updated = nonlinear_rows(fields, low_index, neighbours, mode_counts, forward, backward)
    slotted = jnp.take(
        updated.reshape(components, realizations, modes, rows_dev, kz_modes, 2), owner_map, axis=4
    )
    slotted = slotted.reshape(
        components, real_count, reals_dev, modes, rows_dev, kx_count * ht_count, slots_dev, 2
    )
    outgoing = slotted.transpose(5, 1, 6, 2, 0, 3, 7, 4).reshape(
        kx_count * ht_count * real_count, slots_dev, reals_dev * components * modes * 2, rows_dev
    )
    incoming = lax.all_to_all(
        outgoing, ("kx", "ht", "real"), split_axis=0, concat_axis=0, tiled=True
    )
    incoming = incoming.reshape(
        kx_count, ht_count, real_count, slots_dev, reals_dev * components * modes * 2, rows_dev
    )
    incoming = incoming.transpose(3, 4, 1, 0, 2, 5).reshape(
        slots_dev, reals_dev * components * modes * 2, ht_count * rows_ht
    )
    solved = jnp.einsum("syx,snx->sny", helmholtz, incoming, precision=lax.Precision.HIGH)
    solved = solved.reshape(
        slots_dev, reals_dev, components, kx_count, band_modes, 2, ht_count, rows_ht
    )
    solved = solved.transpose(3, 6, 0, 5, 1, 2, 4, 7).reshape(
        kx_count * ht_count, slots_dev * 2, reals_dev * components * band_modes, rows_ht
    )
    returned = lax.all_to_all(solved, ("kx", "ht"), split_axis=0, concat_axis=0, tiled=True)
    restored = returned.reshape(
        kz_modes, 2, reals_dev, components, band_modes, rows_ht
    )
    restored = jnp.take(restored, inverse_map, axis=0)
    return restored.transpose(3, 2, 4, 5, 0, 1).reshape(velocity.shape)


LANES = 128
PIECES = 2
VMEM = pl.BlockSpec(memory_space=pltpu.VMEM)
SMEM = pl.BlockSpec(memory_space=pltpu.SMEM)


def params():
    return pltpu.CompilerParams(vmem_limit_bytes=48 * 1024 * 1024)


def two_parts(value):
    top = value.astype(jnp.bfloat16)
    rest = (value - top.astype(jnp.float32)).astype(jnp.bfloat16)
    return top, rest


def dot(left, right, dims=((1,), (0,))):
    return lax.dot_general(left, right, (dims, ((), ())), preferred_element_type=jnp.float32)


def pack_kernel(near_ref, count_ref, velocity_ref, out_ref):
    chunks, rows, columns = (velocity_ref.shape[0], velocity_ref.shape[3], velocity_ref.shape[4])
    out_ref[0, : chunks * rows] = velocity_ref[:, 0, 0].reshape(chunks * rows, columns)
    if out_ref.shape[1] == chunks * rows:
        return
    shape = (out_ref.shape[1] - chunks * rows, columns)
    row = lax.broadcasted_iota(jnp.int32, shape, 0)
    lane = lax.broadcasted_iota(jnp.int32, shape, 1)
    extra = jnp.zeros(shape, jnp.int32)
    modes, members = near_ref.shape
    for mode in range(modes):
        line = jnp.where(lane == members, count_ref[mode], 0)
        for member in range(members):
            line = jnp.where(lane == member, near_ref[mode, member], line)
        extra = jnp.where(row == mode, line, extra)
    out_ref[0, chunks * rows :] = extra.astype(jnp.float32)


def pack(velocity, neighbours, mode_counts, piece, extra_rows):
    chunks, pieces, kx_count, rows, columns = velocity.shape
    total = chunks * rows + extra_rows
    return pl.pallas_call(
        pack_kernel,
        out_shape=jax.ShapeDtypeStruct((kx_count, total, columns), jnp.float32),
        grid=(kx_count,),
        in_specs=[
            SMEM,
            SMEM,
            pl.BlockSpec((chunks, 1, 1, rows, columns), lambda k: (0, piece, k, 0, 0)),
        ],
        out_specs=pl.BlockSpec((1, total, columns), lambda k: (k, 0, 0)),
        compiler_params=params(),
        name="pack",
    )(neighbours, mode_counts, velocity)


def split_matrix_kernel(matrix_ref, top_ref, rest_ref):
    top, rest = two_parts(matrix_ref[0].T)
    top_ref[0] = top
    rest_ref[0] = rest


def split_matrix(helmholtz):
    slots, heights, _ = helmholtz.shape
    spec = pl.BlockSpec((1, heights, heights), lambda s: (s, 0, 0))
    shape = jax.ShapeDtypeStruct(helmholtz.shape, jnp.bfloat16)
    return pl.pallas_call(
        split_matrix_kernel,
        out_shape=(shape, shape),
        grid=(slots,),
        in_specs=[spec],
        out_specs=(spec, spec),
        compiler_params=params(),
        cost_estimate=pl.CostEstimate(
            flops=0, bytes_accessed=2 * helmholtz.size * 4, transcendentals=0
        ),
        name="split_matrix",
    )(helmholtz)


def nonlinear_kernel(
    low_ref, near_ref, block_ref, first_ref, second_ref, back_ref, mask_ref,
    slotted_ref, stress_ref, physical, products, sums, high_ref,
):
    components, modes, rows, columns = slotted_ref.shape
    bands, points = (block_ref.shape[0], physical.shape[3])
    band_modes = modes // bands
    members, highs = (stress_ref.shape[1], products.shape[1])
    found = jnp.int32(0)
    for mode in range(modes):
        is_low = jnp.int32(0)
        for member in range(members):
            is_low = is_low | (low_ref[member] == mode).astype(jnp.int32)
        high_ref[found] = mode
        found = found + 1 - is_low

    def transform(step, carry):
        band, component = (step // components, step % components)
        size = band_modes * rows
        top, rest = two_parts(block_ref[band, pl.ds(pl.multiple_of(component * size, 8), size)])
        both = dot(jnp.concatenate([top, rest], axis=1), first_ref[...])
        fields = both[:, :points] + dot(top, second_ref[...])
        place = pl.ds(band * band_modes, band_modes)
        physical[component, place] = fields.reshape(band_modes, rows, points)
        slotted_ref[component, place] = both[:, points:].reshape(band_modes, rows, columns)
        return carry

    lax.fori_loop(0, bands * components, transform, 0)

    def pairs(step, carry):
        halves = points // LANES
        place = (
            pl.ds(pl.multiple_of((step // halves) * 8, 8), 8),
            pl.ds(pl.multiple_of((step % halves) * LANES, LANES), LANES),
        )

        def one_high(index, totals):
            mode = high_ref[index]
            own = [physical[(c, mode) + place] for c in range(components)]
            result = [jnp.zeros((8, LANES), jnp.float32) for _ in range(components)]
            totals = list(totals)
            for member in range(members):
                low = low_ref[member]
                near = near_ref[mode, member]
                partner = [physical[(c, near) + place] for c in range(components)]
                low_one = [physical[(c, low) + place] for c in range(components)]
                for c in range(components):
                    if c == 1:
                        result[c] = result[c] + low_one[1] * partner[1]
                    else:
                        result[c] = result[c] + (low_one[c] * partner[1] + partner[c] * low_one[1])
                    slot = member * components + c
                    totals[slot] = totals[slot] + own[c] * partner[1]
            for c in range(components):
                products[(c, index) + place] = result[c] * 2.0 if c == 1 else result[c]
            return tuple(totals)

        empty = tuple(jnp.zeros((8, LANES), jnp.float32) for _ in range(members * components))
        totals = lax.fori_loop(0, highs, one_high, empty)
        for member in range(members):
            for c in range(components):
                sums[(c, member) + place] = totals[member * components + c]
        return carry

    lax.fori_loop(0, (rows // 8) * (points // LANES), pairs, 0)

    def inverse(fields):
        top, rest = two_parts(fields)
        both = dot(top, back_ref[...])
        return both[:, :columns] + both[:, columns:] + dot(rest, back_ref[:, :columns])

    def finish(component, carry):
        forcing = inverse(products[component].reshape(highs * rows, points))
        forcing = forcing.reshape(highs, rows, columns)
        for index in range(highs):
            mode = high_ref[index]
            slotted_ref[component, mode] += forcing[index] * mask_ref[mode]
        stress = inverse(sums[component].reshape(members * rows, points))
        stress_ref[component] = stress.reshape(members, rows, columns)
        return carry

    lax.fori_loop(0, components, finish, 0)


def nonlinear(block, shape, low_index, neighbours, tables, mask):
    components, modes, rows, columns = shape
    members, points = (low_index.shape[0], 2 * columns)
    highs = modes - members
    return pl.pallas_call(
        nonlinear_kernel,
        out_shape=(
            jax.ShapeDtypeStruct((components, modes, rows, columns), jnp.float32),
            jax.ShapeDtypeStruct((components, members, rows, columns), jnp.float32),
        ),
        in_specs=[SMEM, SMEM] + [VMEM] * 5,
        out_specs=(VMEM, VMEM),
        scratch_shapes=[
            pltpu.VMEM((components, modes, rows, points), jnp.float32),
            pltpu.VMEM((components, highs, rows, points), jnp.float32),
            pltpu.VMEM((components, members, rows, points), jnp.float32),
            pltpu.SMEM((modes + 1,), jnp.int32),
        ],
        compiler_params=params(),
        name="nonlinear",
    )(low_index, neighbours, block, *tables, mask)


def outgoing_kernel(
    low_ref, slotted_ref, stress_ref, other_ref, mask_ref, out_ref, full, *, groups, band_modes
):
    components, modes, rows, columns = slotted_ref.shape
    members = stress_ref.shape[1]
    per_slot = out_ref.shape[0] // (columns // 2)
    full[...] = slotted_ref[...]
    for member in range(members):
        mode = low_ref[member]
        for c in range(components):
            stress = stress_ref[c, member] + other_ref[c, member]
            full[c, mode] += stress * mask_ref[mode]
    inner = modes // groups
    for c in range(components):
        for part in range(inner):
            tile = jnp.concatenate([full[c, part + inner * g] for g in range(groups)], axis=0)
            turned = tile.T
            band_low, band_mode = (part // band_modes, part % band_modes)
            for p in range(2):
                row = ((band_low * 2 + p) * components + c) * band_modes + band_mode
                out_ref[pl.ds(row, columns // 2, stride=per_slot), :] = turned[
                    p * (columns // 2) : (p + 1) * (columns // 2)
                ]


def outgoing(slotted, stress, other, low_index, mask, groups, band_modes):
    components, modes, rows, columns = slotted.shape
    per_slot = (modes // groups) * 2 * components
    return pl.pallas_call(
        functools.partial(outgoing_kernel, groups=groups, band_modes=band_modes),
        out_shape=jax.ShapeDtypeStruct((columns // 2 * per_slot, groups * rows), jnp.float32),
        in_specs=[SMEM, VMEM, VMEM, VMEM, VMEM],
        out_specs=VMEM,
        scratch_shapes=[pltpu.VMEM(slotted.shape, jnp.float32)],
        compiler_params=params(),
        name="outgoing",
    )(low_index, slotted, stress, other, mask)


def regroup(blocks, rows):
    count = len(blocks)
    lane = lax.broadcasted_iota(jnp.int32, blocks[0].shape, 1) // rows
    step = 1
    while step < count:
        take = (lane & step) == 0
        for i in range(count):
            if i & step == 0:
                here, there = (blocks[i], blocks[i + step])
                blocks[i] = jnp.where(take, here, pltpu.roll(there, step * rows, 1))
                blocks[i + step] = jnp.where(
                    take, pltpu.roll(here, LANES - step * rows, 1), there
                )
        step *= 2
    return blocks


def solve_kernel(*refs, groups, kx_count, ht_count):
    pieces = len(refs) - 3
    block_refs, (top_ref, rest_ref, out_ref) = (refs[:pieces], refs[pieces:])
    rows = LANES // groups
    tiles = []
    for h in range(ht_count):
        for piece in range(pieces):
            for first in range(0, kx_count, groups):
                blocks = [
                    block_refs[piece][(first + g) * ht_count + h, 0] for g in range(groups)
                ]
                tiles.append(jnp.concatenate(regroup(blocks, rows), axis=0))
    top, rest = two_parts(jnp.concatenate(tiles, axis=1))
    count = top.shape[0]
    both = dot(jnp.concatenate([top, rest], axis=0), top_ref[0])
    solved = both[:count] + both[count:] + dot(top, rest_ref[0])
    lane_tiles, per_band = out_ref.shape[2:4]
    for band in range(kx_count):
        for tile in range(ht_count * lane_tiles):
            out_ref[band * ht_count + tile // lane_tiles, 0, tile % lane_tiles] = solved[
                band * per_band : (band + 1) * per_band, tile * LANES : (tile + 1) * LANES
            ]


def solve(blocks, matrices, groups, kx_count, ht_count):
    owners, slots, per_slot, lanes = blocks[0].shape
    heights = matrices[0].shape[1]
    lane_tiles = heights // ht_count // LANES
    out = (owners, slots, lane_tiles, per_slot * groups // kx_count, LANES)
    return pl.pallas_call(
        functools.partial(solve_kernel, groups=groups, kx_count=kx_count, ht_count=ht_count),
        out_shape=jax.ShapeDtypeStruct(out, jnp.float32),
        grid=(slots,),
        in_specs=[pl.BlockSpec((owners, 1, per_slot, lanes), lambda s: (0, s, 0, 0))] * len(blocks)
        + [pl.BlockSpec((1, heights, heights), lambda s: (s, 0, 0))] * 2,
        out_specs=pl.BlockSpec((owners, 1) + out[2:], lambda s: (0, s, 0, 0, 0)),
        compiler_params=params(),
        name="solve",
    )(*blocks, *matrices)


def restore_kernel(block_ref, order_ref, out_ref):
    components, band_modes, rows, columns = out_ref.shape
    slots = columns // 2
    per_slot = block_ref.shape[0] // slots
    for c in range(components):
        for mode in range(band_modes):
            for tile in range(rows // LANES):
                parts = []
                for p in range(2):
                    row = ((tile * 2 + p) * components + c) * band_modes + mode
                    parts.append(block_ref[pl.ds(row, slots, stride=per_slot), :])
                top, rest = two_parts(jnp.concatenate(parts, axis=0))
                both = jnp.concatenate([top, rest], axis=0)
                out_ref[c, mode, pl.ds(tile * LANES, LANES)] = dot(
                    both, order_ref[...], ((0,), (0,))
                )


def restore(block, order, components, band_modes, rows):
    columns = order.shape[1]
    return pl.pallas_call(
        restore_kernel,
        out_shape=jax.ShapeDtypeStruct((components, band_modes, rows, columns), jnp.float32),
        in_specs=[VMEM, VMEM],
        out_specs=VMEM,
        compiler_params=params(),
        name="restore",
    )(block, order)


def table_parts(value):
    top = lax.reduce_precision(value, 8, 7)
    return top.astype(jnp.bfloat16), (value - top).astype(jnp.bfloat16)


def slot_tables(owner_map, columns):
    forward, backward = spanwise_tables(columns // 2, 2 * columns)
    slot_columns = (2 * owner_map[None, :] + jnp.arange(2)[:, None]).reshape(columns)
    select = slot_columns[None, :] == jnp.arange(columns)[:, None]
    forward_top, forward_rest = table_parts(forward)
    first = jnp.concatenate([forward_top, select.astype(jnp.bfloat16)], axis=1)
    first = jnp.concatenate([first, first], axis=0)
    slotted_back = jnp.dot(
        backward, select.astype(jnp.float32), precision=lax.Precision.HIGHEST
    )
    back = jnp.concatenate(table_parts(slotted_back), axis=1)
    order = select.T.astype(jnp.bfloat16)
    order = jnp.concatenate([order, order], axis=0)
    return (first, forward_rest, back), order


def slot_masks(owner_map, mode_counts, realizations):
    active = jnp.tile(owner_map, 2)[None, :] < mode_counts[:, None]
    mask = jnp.where(active, jnp.float32(dt_step), 0.0)[:, None, :]
    return mask, mask / realizations


def local(velocity, low_index, neighbours, owner_map, mode_counts, helmholtz):
    components, reals_dev, band_modes, rows_ht, columns = velocity.shape
    kx_count, ht_count = (lax.axis_size("kx"), lax.axis_size("ht"))
    owners, pieces, real_count = (kx_count * ht_count, PIECES, lax.axis_size("real"))
    rows = rows_ht // (kx_count * pieces)
    groups = LANES // rows if rows else 0
    slots = columns // 2 // owners
    if (
        columns != LANES or reals_dev != 1 or rows_ht % LANES or rows % 8 or LANES % rows or kx_count % groups
        or (band_modes * 2 * components) % 8 or slots % 8 or low_index.shape[0] >= kx_count * band_modes
        or low_index.shape[0] >= columns or real_count < 2 or real_count & (real_count - 1)
    ):
        return local_plain(velocity, low_index, neighbours, owner_map, mode_counts, helmholtz)
    realizations, members = (real_count, low_index.shape[0])
    chunks, modes = (components * band_modes, band_modes * kx_count)
    shape = (components, modes, rows, columns)
    extra_rows = -(-band_modes // 8) * 8
    split = velocity.reshape(chunks, pieces, kx_count, rows, columns)
    parts = []
    for piece in range(pieces):
        part = pack(split, neighbours, mode_counts, piece, 0 if piece else extra_rows)
        parts.append(lax.all_to_all(part, "kx", split_axis=0, concat_axis=0, tiled=True))
    matrices = split_matrix(helmholtz)
    small = parts[0][:, chunks * rows : chunks * rows + band_modes, : members + 1]
    small = small.reshape(modes, members + 1).astype(jnp.int32)
    neighbours, mode_counts = (small[:, :-1], small[:, -1])
    tables, order = slot_tables(owner_map, columns)
    mask, low_mask = slot_masks(owner_map, mode_counts, realizations)
    received = []
    for part in parts:
        slotted, stress = nonlinear(part, shape, low_index, neighbours, tables, mask)
        step, other = (1, None)
        while step < realizations:
            stress = stress if other is None else stress + other
            exchange = [(i, i ^ step) for i in range(realizations)]
            other = lax.ppermute(stress, "real", exchange)
            step *= 2
        block = outgoing(slotted, stress, other, low_index, low_mask, groups, band_modes)
        block = block.reshape(owners, slots, -1, LANES)
        received.append(
            lax.all_to_all(block, ("kx", "ht"), split_axis=0, concat_axis=0, tiled=True)
        )
    solved = solve(received, matrices, groups, kx_count, ht_count)
    returned = lax.all_to_all(solved, ("kx", "ht"), split_axis=0, concat_axis=0, tiled=True)
    result = restore(returned.reshape(-1, LANES), order, components, band_modes, rows_ht)
    return result.reshape(velocity.shape)


def solution(mesh):
    in_specs = (
        P(None, "real", "kx", "ht", None),
        P(),
        P("kx", None),
        P(),
        P("kx"),
        P(("kx", "ht"), None, None),
    )
    out_specs = P(None, "real", "kx", "ht", None)
    return jax.shard_map(local, mesh=mesh, in_specs=in_specs, out_specs=out_specs, check_vma=False)
```

```python
import functools

import jax
import jax.numpy as jnp
from jax import lax
from jax.experimental import pallas as pl
from jax.experimental.pallas import tpu as pltpu
from jax.sharding import PartitionSpec as P

dt_step = 0.1


def spanwise_tables(mode_count, point_count):
    column_ids = jnp.arange(2 * mode_count)
    wavenumber = (column_ids // 2).astype(jnp.float32)
    imag_part = column_ids % 2
    positions = 2.0 * jnp.pi * jnp.arange(point_count).astype(jnp.float32) / point_count
    phases = wavenumber[:, None] * positions[None, :]
    forward = jnp.where(imag_part[:, None] == 0, jnp.cos(phases), -jnp.sin(phases)) / jnp.sqrt(
        jnp.float32(mode_count)
    )
    backward = forward.T * (2.0 * mode_count / point_count)
    return (forward, backward)


def nonlinear_rows(fields, low_index, neighbours, mode_counts, forward, backward):
    precision = lax.Precision.HIGH
    realizations, modes, columns = (fields.shape[1], fields.shape[2], fields.shape[4])
    low_select = (low_index[:, None] == jnp.arange(modes)[None, :]).astype(jnp.float32)
    high_mask = 1.0 - jnp.sum(low_select, axis=0)
    high_rows = high_mask[None, None, :, None, None]
    column_mask = ((jnp.arange(columns) // 2)[None, :] < mode_counts[:, None]).astype(jnp.float32)
    physical = jnp.dot(fields, forward, precision=precision)
    low_fields = jnp.take(physical, low_index, axis=2)
    high_low = jnp.zeros_like(physical)
    stresses = []
    for member in range(low_index.shape[0]):
        partner = jnp.take(physical, neighbours[:, member], axis=2)
        low_one = low_fields[:, :, member : member + 1]
        high_low = high_low + low_one * partner[1:2] + partner * low_one[1:2]
        stresses.append(jnp.sum(physical * (partner[1:2] * high_rows), axis=(1, 2)))
    stress = jnp.stack(stresses, axis=1) / realizations
    forcing = jnp.dot(high_low, backward, precision=precision) * high_rows
    low_forcing = jnp.dot(stress, backward, precision=precision)
    low_rows = jnp.einsum("jm,cjyk->cmyk", low_select, low_forcing, precision=lax.Precision.HIGHEST)
    forcing = (forcing + low_rows[:, None]) * column_mask[None, None, :, None, :]
    return fields + dt_step * forcing


def local_plain(velocity, low_index, neighbours, owner_map, mode_counts, helmholtz):
    components, reals_dev, band_modes, rows_ht, columns = velocity.shape
    kz_modes = columns // 2
    forward, backward = spanwise_tables(kz_modes, 4 * kz_modes)
    kx_count, ht_count = (lax.axis_size("kx"), lax.axis_size("ht"))
    real_count = lax.axis_size("real")
    modes, realizations = (band_modes * kx_count, reals_dev * real_count)
    slots_dev = kz_modes // (kx_count * ht_count)
    rows_dev = rows_ht // (kx_count * real_count)
    small = jnp.concatenate([neighbours, mode_counts[:, None]], axis=1)
    small = lax.all_gather(small, "kx", axis=0, tiled=True)
    neighbours, mode_counts = (small[:, :-1], small[:, -1])
    inverse_map = (
        jnp.zeros((kz_modes,), jnp.int32).at[owner_map].set(jnp.arange(kz_modes, dtype=jnp.int32))
    )
    split = velocity.reshape(
        components, reals_dev, band_modes, kx_count * real_count, rows_dev, columns
    )
    split = split.transpose(3, 0, 1, 2, 4, 5)
    split = lax.all_to_all(split, ("kx", "real"), split_axis=0, concat_axis=0, tiled=True)
    fields = split.reshape(
        kx_count, real_count, components, reals_dev, band_modes, rows_dev, columns
    )
    fields = fields.transpose(2, 1, 3, 0, 4, 5, 6).reshape(
        components, realizations, modes, rows_dev, columns
    )
    updated = nonlinear_rows(fields, low_index, neighbours, mode_counts, forward, backward)
    slotted = jnp.take(
        updated.reshape(components, realizations, modes, rows_dev, kz_modes, 2), owner_map, axis=4
    )
    slotted = slotted.reshape(
        components, real_count, reals_dev, modes, rows_dev, kx_count * ht_count, slots_dev, 2
    )
    outgoing = slotted.transpose(5, 1, 6, 2, 0, 3, 7, 4).reshape(
        kx_count * ht_count * real_count, slots_dev, reals_dev * components * modes * 2, rows_dev
    )
    incoming = lax.all_to_all(
        outgoing, ("kx", "ht", "real"), split_axis=0, concat_axis=0, tiled=True
    )
    incoming = incoming.reshape(
        kx_count, ht_count, real_count, slots_dev, reals_dev * components * modes * 2, rows_dev
    )
    incoming = incoming.transpose(3, 4, 1, 0, 2, 5).reshape(
        slots_dev, reals_dev * components * modes * 2, ht_count * rows_ht
    )
    solved = jnp.einsum("syx,snx->sny", helmholtz, incoming, precision=lax.Precision.HIGH)
    solved = solved.reshape(
        slots_dev, reals_dev, components, kx_count, band_modes, 2, ht_count, rows_ht
    )
    solved = solved.transpose(3, 6, 0, 5, 1, 2, 4, 7).reshape(
        kx_count * ht_count, slots_dev * 2, reals_dev * components * band_modes, rows_ht
    )
    returned = lax.all_to_all(solved, ("kx", "ht"), split_axis=0, concat_axis=0, tiled=True)
    restored = returned.reshape(
        kz_modes, 2, reals_dev, components, band_modes, rows_ht
    )
    restored = jnp.take(restored, inverse_map, axis=0)
    return restored.transpose(3, 2, 4, 5, 0, 1).reshape(velocity.shape)


LANES = 128
PIECES = 2
VMEM = pl.BlockSpec(memory_space=pltpu.VMEM)
SMEM = pl.BlockSpec(memory_space=pltpu.SMEM)


def params():
    return pltpu.CompilerParams(vmem_limit_bytes=48 * 1024 * 1024)


def two_parts(value):
    top = value.astype(jnp.bfloat16)
    rest = (value - top.astype(jnp.float32)).astype(jnp.bfloat16)
    return top, rest


def dot(left, right, dims=((1,), (0,))):
    return lax.dot_general(left, right, (dims, ((), ())), preferred_element_type=jnp.float32)


def pack_kernel(near_ref, count_ref, velocity_ref, out_ref):
    chunks, rows, columns = (velocity_ref.shape[0], velocity_ref.shape[3], velocity_ref.shape[4])
    out_ref[0, : chunks * rows] = velocity_ref[:, 0, 0].reshape(chunks * rows, columns)
    if out_ref.shape[1] == chunks * rows:
        return
    shape = (out_ref.shape[1] - chunks * rows, columns)
    row = lax.broadcasted_iota(jnp.int32, shape, 0)
    lane = lax.broadcasted_iota(jnp.int32, shape, 1)
    extra = jnp.zeros(shape, jnp.int32)
    modes, members = near_ref.shape
    for mode in range(modes):
        line = jnp.where(lane == members, count_ref[mode], 0)
        for member in range(members):
            line = jnp.where(lane == member, near_ref[mode, member], line)
        extra = jnp.where(row == mode, line, extra)
    out_ref[0, chunks * rows :] = extra.astype(jnp.float32)


def pack(velocity, neighbours, mode_counts, piece, extra_rows):
    chunks, pieces, kx_count, rows, columns = velocity.shape
    total = chunks * rows + extra_rows
    return pl.pallas_call(
        pack_kernel,
        out_shape=jax.ShapeDtypeStruct((kx_count, total, columns), jnp.float32),
        grid=(kx_count,),
        in_specs=[
            SMEM,
            SMEM,
            pl.BlockSpec((chunks, 1, 1, rows, columns), lambda k: (0, piece, k, 0, 0)),
        ],
        out_specs=pl.BlockSpec((1, total, columns), lambda k: (k, 0, 0)),
        compiler_params=params(),
        name="pack",
    )(neighbours, mode_counts, velocity)


def split_matrix_kernel(matrix_ref, top_ref, rest_ref, mark_ref):
    top, rest = two_parts(matrix_ref[0].T)
    top_ref[0] = top
    rest_ref[0] = rest
    mark_ref[...] = jnp.zeros_like(mark_ref)


def split_matrix(helmholtz):
    slots, heights, _ = helmholtz.shape
    spec = pl.BlockSpec((1, heights, heights), lambda s: (s, 0, 0))
    shape = jax.ShapeDtypeStruct(helmholtz.shape, jnp.bfloat16)
    return pl.pallas_call(
        split_matrix_kernel,
        out_shape=(shape, shape, jax.ShapeDtypeStruct((8, LANES), jnp.float32)),
        grid=(slots,),
        in_specs=[spec],
        out_specs=(spec, spec, pl.BlockSpec((8, LANES), lambda s: (0, 0))),
        compiler_params=params(),
        cost_estimate=pl.CostEstimate(
            flops=0, bytes_accessed=2 * helmholtz.size * 4, transcendentals=0
        ),
        name="split_matrix",
    )(helmholtz)


def nonlinear_kernel(
    low_ref, near_ref, block_ref, first_ref, second_ref, back_ref, mask_ref, after_ref,
    slotted_ref, stress_ref, physical, products, sums, high_ref,
):
    components, modes, rows, columns = slotted_ref.shape
    bands, points = (block_ref.shape[0], physical.shape[3])
    band_modes = modes // bands
    members, highs = (stress_ref.shape[1], products.shape[1])
    found = jnp.int32(0)
    for mode in range(modes):
        is_low = jnp.int32(0)
        for member in range(members):
            is_low = is_low | (low_ref[member] == mode).astype(jnp.int32)
        high_ref[found] = mode
        found = found + 1 - is_low

    def transform(step, carry):
        band, component = (step // components, step % components)
        size = band_modes * rows
        top, rest = two_parts(block_ref[band, pl.ds(pl.multiple_of(component * size, 8), size)])
        both = dot(jnp.concatenate([top, rest], axis=1), first_ref[...])
        fields = both[:, :points] + dot(top, second_ref[...])
        place = pl.ds(band * band_modes, band_modes)
        physical[component, place] = fields.reshape(band_modes, rows, points)
        slotted_ref[component, place] = both[:, points:].reshape(band_modes, rows, columns)
        return carry

    lax.fori_loop(0, bands * components, transform, 0)

    def pairs(step, carry):
        halves = points // LANES
        place = (
            pl.ds(pl.multiple_of((step // halves) * 8, 8), 8),
            pl.ds(pl.multiple_of((step % halves) * LANES, LANES), LANES),
        )

        def one_high(index, totals):
            mode = high_ref[index]
            own = [physical[(c, mode) + place] for c in range(components)]
            result = [jnp.zeros((8, LANES), jnp.float32) for _ in range(components)]
            totals = list(totals)
            for member in range(members):
                low = low_ref[member]
                near = near_ref[mode, member]
                partner = [physical[(c, near) + place] for c in range(components)]
                low_one = [physical[(c, low) + place] for c in range(components)]
                for c in range(components):
                    if c == 1:
                        result[c] = result[c] + low_one[1] * partner[1]
                    else:
                        result[c] = result[c] + (low_one[c] * partner[1] + partner[c] * low_one[1])
                    slot = member * components + c
                    totals[slot] = totals[slot] + own[c] * partner[1]
            for c in range(components):
                products[(c, index) + place] = result[c] * 2.0 if c == 1 else result[c]
            return tuple(totals)

        empty = tuple(jnp.zeros((8, LANES), jnp.float32) for _ in range(members * components))
        totals = lax.fori_loop(0, highs, one_high, empty)
        for member in range(members):
            for c in range(components):
                sums[(c, member) + place] = totals[member * components + c]
        return carry

    lax.fori_loop(0, (rows // 8) * (points // LANES), pairs, 0)

    def inverse(fields):
        top, rest = two_parts(fields)
        both = dot(top, back_ref[...])
        return both[:, :columns] + both[:, columns:] + dot(rest, back_ref[:, :columns])

    def finish(component, carry):
        forcing = inverse(products[component].reshape(highs * rows, points))
        forcing = forcing.reshape(highs, rows, columns)
        for index in range(highs):
            mode = high_ref[index]
            slotted_ref[component, mode] += forcing[index] * mask_ref[mode]
        stress = inverse(sums[component].reshape(members * rows, points))
        stress_ref[component] = stress.reshape(members, rows, columns)
        return carry

    lax.fori_loop(0, components, finish, 0)


def nonlinear(block, shape, low_index, neighbours, tables, mask, after):
    components, modes, rows, columns = shape
    members, points = (low_index.shape[0], 2 * columns)
    highs = modes - members
    return pl.pallas_call(
        nonlinear_kernel,
        out_shape=(
            jax.ShapeDtypeStruct((components, modes, rows, columns), jnp.float32),
            jax.ShapeDtypeStruct((components, members, rows, columns), jnp.float32),
        ),
        in_specs=[SMEM, SMEM] + [VMEM] * 5 + [pl.BlockSpec(memory_space=pl.ANY)],
        out_specs=(VMEM, VMEM),
        scratch_shapes=[
            pltpu.VMEM((components, modes, rows, points), jnp.float32),
            pltpu.VMEM((components, highs, rows, points), jnp.float32),
            pltpu.VMEM((components, members, rows, points), jnp.float32),
            pltpu.SMEM((modes + 1,), jnp.int32),
        ],
        compiler_params=params(),
        name="nonlinear",
    )(low_index, neighbours, block, *tables, mask, after)


def outgoing_kernel(
    low_ref, slotted_ref, stress_ref, other_ref, mask_ref, out_ref, full, *, groups, band_modes
):
    components, modes, rows, columns = slotted_ref.shape
    members = stress_ref.shape[1]
    per_slot = out_ref.shape[0] // (columns // 2)
    full[...] = slotted_ref[...]
    for member in range(members):
        mode = low_ref[member]
        for c in range(components):
            stress = stress_ref[c, member] + other_ref[c, member]
            full[c, mode] += stress * mask_ref[mode]
    inner = modes // groups
    for c in range(components):
        for part in range(inner):
            tile = jnp.concatenate([full[c, part + inner * g] for g in range(groups)], axis=0)
            turned = tile.T
            band_low, band_mode = (part // band_modes, part % band_modes)
            for p in range(2):
                row = ((band_low * 2 + p) * components + c) * band_modes + band_mode
                out_ref[pl.ds(row, columns // 2, stride=per_slot), :] = turned[
                    p * (columns // 2) : (p + 1) * (columns // 2)
                ]


def outgoing(slotted, stress, other, low_index, mask, groups, band_modes):
    components, modes, rows, columns = slotted.shape
    per_slot = (modes // groups) * 2 * components
    return pl.pallas_call(
        functools.partial(outgoing_kernel, groups=groups, band_modes=band_modes),
        out_shape=jax.ShapeDtypeStruct((columns // 2 * per_slot, groups * rows), jnp.float32),
        in_specs=[SMEM, VMEM, VMEM, VMEM, VMEM],
        out_specs=VMEM,
        scratch_shapes=[pltpu.VMEM(slotted.shape, jnp.float32)],
        compiler_params=params(),
        name="outgoing",
    )(low_index, slotted, stress, other, mask)


def regroup(blocks, rows):
    count = len(blocks)
    lane = lax.broadcasted_iota(jnp.int32, blocks[0].shape, 1) // rows
    step = 1
    while step < count:
        take = (lane & step) == 0
        for i in range(count):
            if i & step == 0:
                here, there = (blocks[i], blocks[i + step])
                blocks[i] = jnp.where(take, here, pltpu.roll(there, step * rows, 1))
                blocks[i + step] = jnp.where(
                    take, pltpu.roll(here, LANES - step * rows, 1), there
                )
        step *= 2
    return blocks


def solve_kernel(*refs, groups, kx_count, ht_count):
    pieces = len(refs) - 3
    block_refs, (top_ref, rest_ref, out_ref) = (refs[:pieces], refs[pieces:])
    rows = LANES // groups
    tiles = []
    for h in range(ht_count):
        for piece in range(pieces):
            for first in range(0, kx_count, groups):
                blocks = [
                    block_refs[piece][(first + g) * ht_count + h, 0] for g in range(groups)
                ]
                tiles.append(jnp.concatenate(regroup(blocks, rows), axis=0))
    top, rest = two_parts(jnp.concatenate(tiles, axis=1))
    count = top.shape[0]
    both = dot(jnp.concatenate([top, rest], axis=0), top_ref[0])
    solved = both[:count] + both[count:] + dot(top, rest_ref[0])
    lane_tiles, per_band = out_ref.shape[2:4]
    for band in range(kx_count):
        for tile in range(ht_count * lane_tiles):
            out_ref[band * ht_count + tile // lane_tiles, 0, tile % lane_tiles] = solved[
                band * per_band : (band + 1) * per_band, tile * LANES : (tile + 1) * LANES
            ]


def solve(blocks, matrices, groups, kx_count, ht_count, first, slots):
    owners, _, per_slot, lanes = blocks[0].shape
    heights = matrices[0].shape[1]
    lane_tiles = heights // ht_count // LANES
    out = (owners, slots, lane_tiles, per_slot * groups // kx_count, LANES)
    return pl.pallas_call(
        functools.partial(solve_kernel, groups=groups, kx_count=kx_count, ht_count=ht_count),
        out_shape=jax.ShapeDtypeStruct(out, jnp.float32),
        grid=(slots,),
        in_specs=[
            pl.BlockSpec((owners, 1, per_slot, lanes), lambda s: (0, first + s, 0, 0))
        ] * len(blocks)
        + [pl.BlockSpec((1, heights, heights), lambda s: (first + s, 0, 0))] * 2,
        out_specs=pl.BlockSpec((owners, 1) + out[2:], lambda s: (0, s, 0, 0, 0)),
        compiler_params=params(),
        name="solve",
    )(*blocks, *matrices)


def restore_kernel(*refs):
    block_refs, (order_ref, out_ref) = (refs[:-2], refs[-2:])
    components, band_modes, rows, columns = out_ref.shape
    slots = columns // 2 // len(block_refs)
    per_slot = block_refs[0].shape[0] // slots
    for c in range(components):
        for mode in range(band_modes):
            for tile in range(rows // LANES):
                parts = []
                for p in range(2):
                    row = ((tile * 2 + p) * components + c) * band_modes + mode
                    for block_ref in block_refs:
                        parts.append(block_ref[pl.ds(row, slots, stride=per_slot), :])
                top, rest = two_parts(jnp.concatenate(parts, axis=0))
                both = jnp.concatenate([top, rest], axis=0)
                out_ref[c, mode, pl.ds(tile * LANES, LANES)] = dot(
                    both, order_ref[...], ((0,), (0,))
                )


def restore(blocks, order, components, band_modes, rows):
    columns = order.shape[1]
    return pl.pallas_call(
        restore_kernel,
        out_shape=jax.ShapeDtypeStruct((components, band_modes, rows, columns), jnp.float32),
        in_specs=[VMEM] * (len(blocks) + 1),
        out_specs=VMEM,
        compiler_params=params(),
        name="restore",
    )(*blocks, order)


def table_parts(value):
    top = lax.reduce_precision(value, 8, 7)
    return top.astype(jnp.bfloat16), (value - top).astype(jnp.bfloat16)


def slot_tables(owner_map, columns, owners, pieces):
    forward, backward = spanwise_tables(columns // 2, 2 * columns)
    slot_columns = (2 * owner_map[None, :] + jnp.arange(2)[:, None]).reshape(columns)
    select = slot_columns[None, :] == jnp.arange(columns)[:, None]
    forward_top, forward_rest = table_parts(forward)
    first = jnp.concatenate([forward_top, select.astype(jnp.bfloat16)], axis=1)
    first = jnp.concatenate([first, first], axis=0)
    slotted_back = jnp.dot(
        backward, select.astype(jnp.float32), precision=lax.Precision.HIGHEST
    )
    back = jnp.concatenate(table_parts(slotted_back), axis=1)
    order = select.T.reshape(2, owners, pieces, -1, columns).transpose(0, 2, 1, 3, 4)
    order = order.reshape(columns, columns).astype(jnp.bfloat16)
    order = jnp.concatenate([order, order], axis=0)
    return (first, forward_rest, back), order


def slot_masks(owner_map, mode_counts, realizations):
    active = jnp.tile(owner_map, 2)[None, :] < mode_counts[:, None]
    mask = jnp.where(active, jnp.float32(dt_step), 0.0)[:, None, :]
    return mask, mask / realizations


def local(velocity, low_index, neighbours, owner_map, mode_counts, helmholtz):
    components, reals_dev, band_modes, rows_ht, columns = velocity.shape
    kx_count, ht_count = (lax.axis_size("kx"), lax.axis_size("ht"))
    owners, pieces, real_count = (kx_count * ht_count, PIECES, lax.axis_size("real"))
    rows = rows_ht // (kx_count * pieces)
    groups = LANES // rows if rows else 0
    slots = columns // 2 // owners
    if (
        columns != LANES or reals_dev != 1 or rows_ht % LANES or rows % 8 or LANES % rows or kx_count % groups
        or (band_modes * 2 * components) % 8 or slots % 8 or slots // pieces * owners % 8 or low_index.shape[0] >= kx_count * band_modes
        or low_index.shape[0] >= columns or real_count < 2 or real_count & (real_count - 1)
    ):
        return local_plain(velocity, low_index, neighbours, owner_map, mode_counts, helmholtz)
    realizations, members = (real_count, low_index.shape[0])
    chunks, modes = (components * band_modes, band_modes * kx_count)
    shape = (components, modes, rows, columns)
    extra_rows = -(-band_modes // 8) * 8
    split = velocity.reshape(chunks, pieces, kx_count, rows, columns)
    parts = []
    for piece in range(pieces):
        part = pack(split, neighbours, mode_counts, piece, 0 if piece else extra_rows)
        parts.append(lax.all_to_all(part, "kx", split_axis=0, concat_axis=0, tiled=True))
    *matrices, after = split_matrix(helmholtz)
    small = parts[0][:, chunks * rows : chunks * rows + band_modes, : members + 1]
    small = small.reshape(modes, members + 1).astype(jnp.int32)
    neighbours, mode_counts = (small[:, :-1], small[:, -1])
    tables, order = slot_tables(owner_map, columns, owners, pieces)
    mask, low_mask = slot_masks(owner_map, mode_counts, realizations)
    received = []
    for part in parts:
        slotted, stress = nonlinear(part, shape, low_index, neighbours, tables, mask, after)
        step, other = (1, None)
        while step < realizations:
            stress = stress if other is None else stress + other
            exchange = [(i, i ^ step) for i in range(realizations)]
            other = lax.ppermute(stress, "real", exchange)
            step *= 2
        after = stress
        block = outgoing(slotted, stress, other, low_index, low_mask, groups, band_modes)
        block = block.reshape(owners, slots, -1, LANES)
        received.append(
            lax.all_to_all(block, ("kx", "ht"), split_axis=0, concat_axis=0, tiled=True)
        )
    returned = []
    for piece in range(pieces):
        count = slots // pieces
        solved = solve(received, matrices, groups, kx_count, ht_count, piece * count, count)
        solved = lax.all_to_all(solved, ("kx", "ht"), split_axis=0, concat_axis=0, tiled=True)
        returned.append(solved.reshape(-1, LANES))
    result = restore(returned, order, components, band_modes, rows_ht)
    return result.reshape(velocity.shape)


def solution(mesh):
    in_specs = (
        P(None, "real", "kx", "ht", None),
        P(),
        P("kx", None),
        P(),
        P("kx"),
        P(("kx", "ht"), None, None),
    )
    out_specs = P(None, "real", "kx", "ht", None)
    return jax.shard_map(local, mesh=mesh, in_specs=in_specs, out_specs=out_specs, check_vma=False)
```

```python
import functools

import jax
import jax.numpy as jnp
from jax import lax
from jax.experimental import pallas as pl
from jax.experimental.pallas import tpu as pltpu
from jax.sharding import PartitionSpec as P

dt_step = 0.1


def spanwise_tables(mode_count, point_count):
    column_ids = jnp.arange(2 * mode_count)
    wavenumber = (column_ids // 2).astype(jnp.float32)
    imag_part = column_ids % 2
    positions = 2.0 * jnp.pi * jnp.arange(point_count).astype(jnp.float32) / point_count
    phases = wavenumber[:, None] * positions[None, :]
    forward = jnp.where(imag_part[:, None] == 0, jnp.cos(phases), -jnp.sin(phases)) / jnp.sqrt(
        jnp.float32(mode_count)
    )
    backward = forward.T * (2.0 * mode_count / point_count)
    return (forward, backward)


def nonlinear_rows(fields, low_index, neighbours, mode_counts, forward, backward):
    precision = lax.Precision.HIGH
    realizations, modes, columns = (fields.shape[1], fields.shape[2], fields.shape[4])
    low_select = (low_index[:, None] == jnp.arange(modes)[None, :]).astype(jnp.float32)
    high_mask = 1.0 - jnp.sum(low_select, axis=0)
    high_rows = high_mask[None, None, :, None, None]
    column_mask = ((jnp.arange(columns) // 2)[None, :] < mode_counts[:, None]).astype(jnp.float32)
    physical = jnp.dot(fields, forward, precision=precision)
    low_fields = jnp.take(physical, low_index, axis=2)
    high_low = jnp.zeros_like(physical)
    stresses = []
    for member in range(low_index.shape[0]):
        partner = jnp.take(physical, neighbours[:, member], axis=2)
        low_one = low_fields[:, :, member : member + 1]
        high_low = high_low + low_one * partner[1:2] + partner * low_one[1:2]
        stresses.append(jnp.sum(physical * (partner[1:2] * high_rows), axis=(1, 2)))
    stress = jnp.stack(stresses, axis=1) / realizations
    forcing = jnp.dot(high_low, backward, precision=precision) * high_rows
    low_forcing = jnp.dot(stress, backward, precision=precision)
    low_rows = jnp.einsum("jm,cjyk->cmyk", low_select, low_forcing, precision=lax.Precision.HIGHEST)
    forcing = (forcing + low_rows[:, None]) * column_mask[None, None, :, None, :]
    return fields + dt_step * forcing


def local_plain(velocity, low_index, neighbours, owner_map, mode_counts, helmholtz):
    components, reals_dev, band_modes, rows_ht, columns = velocity.shape
    kz_modes = columns // 2
    forward, backward = spanwise_tables(kz_modes, 4 * kz_modes)
    kx_count, ht_count = (lax.axis_size("kx"), lax.axis_size("ht"))
    real_count = lax.axis_size("real")
    modes, realizations = (band_modes * kx_count, reals_dev * real_count)
    slots_dev = kz_modes // (kx_count * ht_count)
    rows_dev = rows_ht // (kx_count * real_count)
    small = jnp.concatenate([neighbours, mode_counts[:, None]], axis=1)
    small = lax.all_gather(small, "kx", axis=0, tiled=True)
    neighbours, mode_counts = (small[:, :-1], small[:, -1])
    inverse_map = (
        jnp.zeros((kz_modes,), jnp.int32).at[owner_map].set(jnp.arange(kz_modes, dtype=jnp.int32))
    )
    split = velocity.reshape(
        components, reals_dev, band_modes, kx_count * real_count, rows_dev, columns
    )
    split = split.transpose(3, 0, 1, 2, 4, 5)
    split = lax.all_to_all(split, ("kx", "real"), split_axis=0, concat_axis=0, tiled=True)
    fields = split.reshape(
        kx_count, real_count, components, reals_dev, band_modes, rows_dev, columns
    )
    fields = fields.transpose(2, 1, 3, 0, 4, 5, 6).reshape(
        components, realizations, modes, rows_dev, columns
    )
    updated = nonlinear_rows(fields, low_index, neighbours, mode_counts, forward, backward)
    slotted = jnp.take(
        updated.reshape(components, realizations, modes, rows_dev, kz_modes, 2), owner_map, axis=4
    )
    slotted = slotted.reshape(
        components, real_count, reals_dev, modes, rows_dev, kx_count * ht_count, slots_dev, 2
    )
    outgoing = slotted.transpose(5, 1, 6, 2, 0, 3, 7, 4).reshape(
        kx_count * ht_count * real_count, slots_dev, reals_dev * components * modes * 2, rows_dev
    )
    incoming = lax.all_to_all(
        outgoing, ("kx", "ht", "real"), split_axis=0, concat_axis=0, tiled=True
    )
    incoming = incoming.reshape(
        kx_count, ht_count, real_count, slots_dev, reals_dev * components * modes * 2, rows_dev
    )
    incoming = incoming.transpose(3, 4, 1, 0, 2, 5).reshape(
        slots_dev, reals_dev * components * modes * 2, ht_count * rows_ht
    )
    solved = jnp.einsum("syx,snx->sny", helmholtz, incoming, precision=lax.Precision.HIGH)
    solved = solved.reshape(
        slots_dev, reals_dev, components, kx_count, band_modes, 2, ht_count, rows_ht
    )
    solved = solved.transpose(3, 6, 0, 5, 1, 2, 4, 7).reshape(
        kx_count * ht_count, slots_dev * 2, reals_dev * components * band_modes, rows_ht
    )
    returned = lax.all_to_all(solved, ("kx", "ht"), split_axis=0, concat_axis=0, tiled=True)
    restored = returned.reshape(
        kz_modes, 2, reals_dev, components, band_modes, rows_ht
    )
    restored = jnp.take(restored, inverse_map, axis=0)
    return restored.transpose(3, 2, 4, 5, 0, 1).reshape(velocity.shape)


LANES = 128
PIECES = 2
VMEM = pl.BlockSpec(memory_space=pltpu.VMEM)
SMEM = pl.BlockSpec(memory_space=pltpu.SMEM)


def params():
    return pltpu.CompilerParams(vmem_limit_bytes=48 * 1024 * 1024)


def two_parts(value):
    top = value.astype(jnp.bfloat16)
    rest = (value - top.astype(jnp.float32)).astype(jnp.bfloat16)
    return top, rest


def dot(left, right, dims=((1,), (0,))):
    return lax.dot_general(left, right, (dims, ((), ())), preferred_element_type=jnp.float32)


def pack_kernel(near_ref, count_ref, velocity_ref, *out_refs):
    chunks, pieces, kx_count, rows, columns = velocity_ref.shape
    own = lax.axis_index("kx")
    for index, out_ref in enumerate(out_refs):
        piece, partner = (index // kx_count, own ^ (index % kx_count))
        for chunk in range(chunks):
            out_ref[chunk * rows : (chunk + 1) * rows] = velocity_ref[chunk, piece, partner]
    shape = (out_refs[0].shape[0] - chunks * rows, columns)
    row = lax.broadcasted_iota(jnp.int32, shape, 0)
    lane = lax.broadcasted_iota(jnp.int32, shape, 1)
    extra = jnp.zeros(shape, jnp.int32)
    modes, members = near_ref.shape
    for mode in range(modes):
        line = jnp.where(lane == members, count_ref[mode], 0)
        for member in range(members):
            line = jnp.where(lane == member, near_ref[mode, member], line)
        extra = jnp.where(row == mode, line, extra)
    extra = extra.astype(jnp.float32)
    for out_ref in out_refs[:kx_count]:
        out_ref[chunks * rows :] = extra


def pack(velocity, neighbours, mode_counts, extra_rows):
    chunks, pieces, kx_count, rows, columns = velocity.shape
    shapes = []
    for piece in range(pieces):
        total = chunks * rows + (0 if piece else extra_rows)
        shapes += [jax.ShapeDtypeStruct((total, columns), jnp.float32)] * kx_count
    out = pl.pallas_call(
        pack_kernel,
        out_shape=tuple(shapes),
        in_specs=[SMEM, SMEM, VMEM],
        out_specs=(VMEM,) * len(shapes),
        name="pack",
    )(neighbours, mode_counts, velocity)
    return [out[piece * kx_count : (piece + 1) * kx_count] for piece in range(pieces)]


def split_matrix_kernel(matrix_ref, top_ref, rest_ref, mark_ref, turned, *, pieces, kx_count):
    ht_count, heights, width = turned.shape
    rows = width // (pieces * kx_count)
    own_kx, own_ht = (lax.axis_index("kx"), lax.axis_index("ht"))
    for h in range(ht_count):
        turned[h] = matrix_ref[0, h * width : (h + 1) * width, :].T
    for block in range(heights // rows):
        piece, h, k = (
            block // (ht_count * kx_count), block // kx_count % ht_count, block % kx_count
        )
        source = (((own_ht ^ h) * pieces + piece) * kx_count + (own_kx ^ k)) * rows
        for j in range(ht_count):
            value = turned[own_ht ^ j, pl.ds(pl.multiple_of(source, rows), rows), :]
            place = (0, slice(block * rows, (block + 1) * rows), slice(j * width, (j + 1) * width))
            top_ref[place], rest_ref[place] = two_parts(value)
    mark_ref[...] = jnp.zeros_like(mark_ref)


def split_matrix(helmholtz, pieces, kx_count, ht_count):
    slots, heights, _ = helmholtz.shape
    spec = pl.BlockSpec((1, heights, heights), lambda s: (s, 0, 0))
    shape = jax.ShapeDtypeStruct(helmholtz.shape, jnp.bfloat16)
    return pl.pallas_call(
        functools.partial(split_matrix_kernel, pieces=pieces, kx_count=kx_count),
        out_shape=(shape, shape, jax.ShapeDtypeStruct((8, LANES), jnp.float32)),
        grid=(slots,),
        in_specs=[spec],
        out_specs=(spec, spec, pl.BlockSpec((8, LANES), lambda s: (0, 0))),
        scratch_shapes=[pltpu.VMEM((ht_count, heights, heights // ht_count), jnp.float32)],
        compiler_params=params(),
        cost_estimate=pl.CostEstimate(
            flops=0, bytes_accessed=2 * helmholtz.size * 4, transcendentals=0
        ),
        name="split_matrix",
    )(helmholtz)


def nonlinear_kernel(low_ref, near_ref, *refs):
    block_refs, refs = (refs[:-11], refs[-11:])
    first_ref, second_ref, back_ref, mask_ref, _, slotted_ref, stress_ref, *scratch = refs
    physical, products, sums, high_ref = scratch
    components, modes, rows, columns = slotted_ref.shape
    bands, points = (len(block_refs), physical.shape[3])
    band_modes = modes // bands
    own = lax.axis_index("kx")
    members, highs = (stress_ref.shape[1], products.shape[1])
    found = jnp.int32(0)
    for mode in range(modes):
        is_low = jnp.int32(0)
        for member in range(members):
            is_low = is_low | (low_ref[member] == mode).astype(jnp.int32)
        high_ref[found] = mode
        found = found + 1 - is_low

    def transform(component, carry):
        size = band_modes * rows
        for index, block_ref in enumerate(block_refs):
            top, rest = two_parts(block_ref[pl.ds(pl.multiple_of(component * size, 8), size)])
            both = dot(jnp.concatenate([top, rest], axis=1), first_ref[...])
            fields = both[:, :points] + dot(top, second_ref[...])
            place = pl.ds((own ^ index) * band_modes, band_modes)
            physical[component, place] = fields.reshape(band_modes, rows, points)
            slotted_ref[component, place] = both[:, points:].reshape(band_modes, rows, columns)
        return carry

    lax.fori_loop(0, components, transform, 0)

    def pairs(step, carry):
        halves = points // LANES
        place = (
            pl.ds(pl.multiple_of((step // halves) * 8, 8), 8),
            pl.ds(pl.multiple_of((step % halves) * LANES, LANES), LANES),
        )

        def one_high(index, totals):
            mode = high_ref[index]
            own = [physical[(c, mode) + place] for c in range(components)]
            result = [jnp.zeros((8, LANES), jnp.float32) for _ in range(components)]
            totals = list(totals)
            for member in range(members):
                low = low_ref[member]
                near = near_ref[mode, member]
                partner = [physical[(c, near) + place] for c in range(components)]
                low_one = [physical[(c, low) + place] for c in range(components)]
                for c in range(components):
                    if c == 1:
                        result[c] = result[c] + low_one[1] * partner[1]
                    else:
                        result[c] = result[c] + (low_one[c] * partner[1] + partner[c] * low_one[1])
                    slot = member * components + c
                    totals[slot] = totals[slot] + own[c] * partner[1]
            for c in range(components):
                products[(c, index) + place] = result[c] * 2.0 if c == 1 else result[c]
            return tuple(totals)

        empty = tuple(jnp.zeros((8, LANES), jnp.float32) for _ in range(members * components))
        totals = lax.fori_loop(0, highs, one_high, empty)
        for member in range(members):
            for c in range(components):
                sums[(c, member) + place] = totals[member * components + c]
        return carry

    lax.fori_loop(0, (rows // 8) * (points // LANES), pairs, 0)

    def inverse(fields):
        top, rest = two_parts(fields)
        both = dot(top, back_ref[...])
        return both[:, :columns] + both[:, columns:] + dot(rest, back_ref[:, :columns])

    def finish(component, carry):
        forcing = inverse(products[component].reshape(highs * rows, points))
        forcing = forcing.reshape(highs, rows, columns)
        for index in range(highs):
            mode = high_ref[index]
            slotted_ref[component, mode] += forcing[index] * mask_ref[mode]
        stress = inverse(sums[component].reshape(members * rows, points))
        stress_ref[component] = stress.reshape(members, rows, columns)
        return carry

    lax.fori_loop(0, components, finish, 0)


def nonlinear(blocks, shape, low_index, neighbours, tables, mask, after):
    components, modes, rows, columns = shape
    members, points = (low_index.shape[0], 2 * columns)
    highs = modes - members
    return pl.pallas_call(
        nonlinear_kernel,
        out_shape=(
            jax.ShapeDtypeStruct((components, modes, rows, columns), jnp.float32),
            jax.ShapeDtypeStruct((components, members, rows, columns), jnp.float32),
        ),
        in_specs=[SMEM, SMEM] + [VMEM] * (len(blocks) + 4) + [pl.BlockSpec(memory_space=pl.ANY)],
        out_specs=(VMEM, VMEM),
        scratch_shapes=[
            pltpu.VMEM((components, modes, rows, points), jnp.float32),
            pltpu.VMEM((components, highs, rows, points), jnp.float32),
            pltpu.VMEM((components, members, rows, points), jnp.float32),
            pltpu.SMEM((modes + 1,), jnp.int32),
        ],
        compiler_params=params(),
        name="nonlinear",
    )(low_index, neighbours, *blocks, *tables, mask, after)


def outgoing_kernel(
    low_ref, slotted_ref, stress_ref, other_ref, mask_ref, *refs, groups, band_modes
):
    out_refs, full = (refs[:-1], refs[-1])
    components, modes, rows, columns = slotted_ref.shape
    members, owners = (stress_ref.shape[1], len(out_refs))
    slots = columns // 2 // owners
    per_slot = out_refs[0].shape[0] // slots
    full[...] = slotted_ref[...]
    for member in range(members):
        mode = low_ref[member]
        for c in range(components):
            stress = stress_ref[c, member] + other_ref[c, member]
            full[c, mode] += stress * mask_ref[mode]
    inner = modes // groups
    for c in range(components):
        for part in range(inner):
            tile = jnp.concatenate([full[c, part + inner * g] for g in range(groups)], axis=0)
            turned = tile.T
            band_low, band_mode = (part // band_modes, part % band_modes)
            for p in range(2):
                row = ((band_low * 2 + p) * components + c) * band_modes + band_mode
                for owner in range(owners):
                    start = (p * owners + owner) * slots
                    out_refs[owner][pl.ds(row, slots, stride=per_slot), :] = turned[
                        start : start + slots
                    ]


def outgoing(slotted, stress, other, low_index, mask, groups, band_modes, owners):
    components, modes, rows, columns = slotted.shape
    total = (columns // 2 // owners) * (modes // groups) * 2 * components
    return pl.pallas_call(
        functools.partial(outgoing_kernel, groups=groups, band_modes=band_modes),
        out_shape=(jax.ShapeDtypeStruct((total, groups * rows), jnp.float32),) * owners,
        in_specs=[SMEM, VMEM, VMEM, VMEM, VMEM],
        out_specs=(VMEM,) * owners,
        scratch_shapes=[pltpu.VMEM(slotted.shape, jnp.float32)],
        compiler_params=params(),
        name="outgoing",
    )(low_index, slotted, stress, other, mask)


def regroup(blocks, rows):
    count = len(blocks)
    lane = lax.broadcasted_iota(jnp.int32, blocks[0].shape, 1) // rows
    step = 1
    while step < count:
        take = (lane & step) == 0
        for i in range(count):
            if i & step == 0:
                here, there = (blocks[i], blocks[i + step])
                blocks[i] = jnp.where(take, here, pltpu.roll(there, step * rows, 1))
                blocks[i + step] = jnp.where(
                    take, pltpu.roll(here, LANES - step * rows, 1), there
                )
        step *= 2
    return blocks


def solve_kernel(*refs, groups, kx_count, ht_count, started, last):
    owners = kx_count * ht_count
    block_refs, (top_ref, rest_ref), refs = (
        refs[:owners], refs[owners : owners + 2], refs[owners + 2 :]
    )
    rows = LANES // groups
    tiles = []
    for h in range(ht_count):
        for first in range(0, kx_count, groups):
            blocks = [block_refs[(first + g) * ht_count + h][0] for g in range(groups)]
            tiles.append(jnp.concatenate(regroup(blocks, rows), axis=0))
    top, rest = two_parts(jnp.concatenate(tiles, axis=1))
    count = top.shape[0]
    both = dot(jnp.concatenate([top, rest], axis=0), top_ref[0])
    solved = both[:count] + both[count:] + dot(top, rest_ref[0])
    if started:
        solved, refs = (solved + refs[0][0], refs[1:])
    if not last:
        refs[0][0] = solved
        return
    out_refs, full = (refs[:owners], refs[owners])
    full[...] = solved
    own = lax.axis_index("kx")
    lane_tiles, per_band = out_refs[0].shape[1:3]
    for k in range(kx_count):
        band = pl.ds(pl.multiple_of((own ^ k) * per_band, 8), per_band)
        for tile in range(ht_count * lane_tiles):
            out_refs[k * ht_count + tile // lane_tiles][0, tile % lane_tiles] = full[
                band, tile * LANES : (tile + 1) * LANES
            ]


def solve(blocks, matrices, piece, pieces, partial, groups, kx_count, ht_count):
    slots, per_slot, lanes = blocks[0].shape
    heights, last = (matrices[0].shape[2], piece == pieces - 1)
    count, owners = (per_slot * groups, kx_count * ht_count)
    whole = pl.BlockSpec((1, count, heights), lambda s: (s, 0, 0))
    if last:
        shape = (slots, heights // ht_count // LANES, count // kx_count, LANES)
        out_shape = (jax.ShapeDtypeStruct(shape, jnp.float32),) * owners
        out_specs = (pl.BlockSpec((1,) + shape[1:], lambda s: (s, 0, 0, 0)),) * owners
        scratch = [pltpu.VMEM((count, heights), jnp.float32)]
    else:
        out_shape = jax.ShapeDtypeStruct((slots, count, heights), jnp.float32)
        out_specs, scratch = (whole, [])
    return pl.pallas_call(
        functools.partial(
            solve_kernel, groups=groups, kx_count=kx_count, ht_count=ht_count,
            started=partial is not None, last=last,
        ),
        out_shape=out_shape,
        grid=(slots,),
        in_specs=[pl.BlockSpec((1, per_slot, lanes), lambda s: (s, 0, 0))] * owners
        + [pl.BlockSpec((1, heights // pieces, heights), lambda s: (s, piece, 0))] * 2
        + ([] if partial is None else [whole]),
        out_specs=out_specs,
        scratch_shapes=scratch,
        compiler_params=params(),
        cost_estimate=pl.CostEstimate(
            flops=6 * slots * count * heights * heights // pieces,
            bytes_accessed=slots * heights * heights * 4 // pieces, transcendentals=0,
        ),
        name="solve",
    )(*blocks, *matrices, *([] if partial is None else [partial]))


def restore_kernel(*refs):
    block_refs, (order_ref, out_ref) = (refs[:-2], refs[-2:])
    components, band_modes, rows, columns = out_ref.shape
    slots = columns // 2 // len(block_refs)
    per_slot = block_refs[0].shape[0] // slots
    for c in range(components):
        for mode in range(band_modes):
            for tile in range(rows // LANES):
                parts = []
                for p in range(2):
                    row = ((tile * 2 + p) * components + c) * band_modes + mode
                    for block_ref in block_refs:
                        parts.append(block_ref[pl.ds(row, slots, stride=per_slot), :])
                top, rest = two_parts(jnp.concatenate(parts, axis=0))
                both = jnp.concatenate([top, rest], axis=0)
                out_ref[c, mode, pl.ds(tile * LANES, LANES)] = dot(
                    both, order_ref[...], ((0,), (0,))
                )


def restore(blocks, order, components, band_modes, rows):
    columns = order.shape[1]
    return pl.pallas_call(
        restore_kernel,
        out_shape=jax.ShapeDtypeStruct((components, band_modes, rows, columns), jnp.float32),
        in_specs=[VMEM] * (len(blocks) + 1),
        out_specs=VMEM,
        compiler_params=params(),
        name="restore",
    )(*blocks, order)


def table_parts(value):
    top = lax.reduce_precision(value, 8, 7)
    return top.astype(jnp.bfloat16), (value - top).astype(jnp.bfloat16)


def slot_tables(owner_map, columns):
    forward, backward = spanwise_tables(columns // 2, 2 * columns)
    slot_columns = (2 * owner_map[None, :] + jnp.arange(2)[:, None]).reshape(columns)
    select = slot_columns[None, :] == jnp.arange(columns)[:, None]
    forward_top, forward_rest = table_parts(forward)
    first = jnp.concatenate([forward_top, select.astype(jnp.bfloat16)], axis=1)
    first = jnp.concatenate([first, first], axis=0)
    slotted_back = jnp.dot(
        backward, select.astype(jnp.float32), precision=lax.Precision.HIGHEST
    )
    back = jnp.concatenate(table_parts(slotted_back), axis=1)
    order = select.T.astype(jnp.bfloat16)
    order = jnp.concatenate([order, order], axis=0)
    return (first, forward_rest, back), order


def slot_masks(owner_map, mode_counts, realizations):
    active = jnp.tile(owner_map, 2)[None, :] < mode_counts[:, None]
    mask = jnp.where(active, jnp.float32(dt_step), 0.0)[:, None, :]
    return mask, mask / realizations


def partners(count, step):
    return [(index, index ^ step) for index in range(count)]


def exchange(blocks, axes):
    result = list(blocks)
    for step in range(len(blocks) - 1, 0, -1):
        result[step] = lax.ppermute(blocks[step], axes, partners(len(blocks), step))
    return result


def local(velocity, low_index, neighbours, owner_map, mode_counts, helmholtz):
    components, reals_dev, band_modes, rows_ht, columns = velocity.shape
    kx_count, ht_count = (lax.axis_size("kx"), lax.axis_size("ht"))
    own_kx, own_ht = (lax.axis_index("kx"), lax.axis_index("ht"))
    owners, pieces, real_count = (kx_count * ht_count, PIECES, lax.axis_size("real"))
    rows = rows_ht // (kx_count * pieces)
    groups = LANES // rows if rows else 0
    slots = columns // 2 // owners
    if (
        columns != LANES or reals_dev != 1 or rows_ht % LANES or rows % 8 or LANES % rows or kx_count % groups
        or (band_modes * 2 * components) % 8 or slots % 8 or owners & (owners - 1) or low_index.shape[0] >= kx_count * band_modes
        or low_index.shape[0] >= columns or real_count < 2 or real_count & (real_count - 1)
    ):
        return local_plain(velocity, low_index, neighbours, owner_map, mode_counts, helmholtz)
    realizations, members = (real_count, low_index.shape[0])
    chunks, modes = (components * band_modes, band_modes * kx_count)
    shape = (components, modes, rows, columns)
    extra_rows = -(-band_modes // 8) * 8
    split = velocity.reshape(chunks, pieces, kx_count, rows, columns)
    everyone = (own_kx * ht_count + own_ht) ^ jnp.arange(owners)
    owner_map = owner_map.reshape(owners, slots)[everyone].reshape(-1)
    parts = [
        exchange(blocks, "kx") for blocks in pack(split, neighbours, mode_counts, extra_rows)
    ]
    *matrices, after = split_matrix(helmholtz, pieces, kx_count, ht_count)
    small = 0.0
    for index, block in enumerate(parts[0]):
        lines = block[chunks * rows : chunks * rows + band_modes, : members + 1]
        here = (own_kx ^ index) == jnp.arange(kx_count)
        small = small + jnp.where(here[:, None, None], lines[None], 0.0)
    small = small.reshape(modes, members + 1).astype(jnp.int32)
    neighbours, mode_counts = (small[:, :-1], small[:, -1])
    tables, order = slot_tables(owner_map, columns)
    mask, low_mask = slot_masks(owner_map, mode_counts, realizations)
    received = []
    for part in parts:
        slotted, stress = nonlinear(part, shape, low_index, neighbours, tables, mask, after)
        step, other = (1, None)
        while step < realizations:
            stress = stress if other is None else stress + other
            other = lax.ppermute(stress, "real", partners(realizations, step))
            step *= 2
        after = stress
        blocks = outgoing(
            slotted, stress, other, low_index, low_mask, groups, band_modes, owners
        )
        blocks = [block.reshape(slots, -1, LANES) for block in blocks]
        received.append(exchange(blocks, ("kx", "ht")))
    solved = None
    for piece, blocks in enumerate(received):
        solved = solve(blocks, matrices, piece, pieces, solved, groups, kx_count, ht_count)
    returned = [block.reshape(-1, LANES) for block in exchange(solved, ("kx", "ht"))]
    result = restore(returned, order, components, band_modes, rows_ht)
    return result.reshape(velocity.shape)


def solution(mesh):
    in_specs = (
        P(None, "real", "kx", "ht", None),
        P(),
        P("kx", None),
        P(),
        P("kx"),
        P(("kx", "ht"), None, None),
    )
    out_specs = P(None, "real", "kx", "ht", None)
    return jax.shard_map(local, mesh=mesh, in_specs=in_specs, out_specs=out_specs, check_vma=False)
```

```python
import functools

import jax
import jax.numpy as jnp
from jax import lax
from jax.experimental import pallas as pl
from jax.experimental.pallas import tpu as pltpu
from jax.sharding import PartitionSpec as P

dt_step = 0.1


def spanwise_tables(mode_count, point_count):
    column_ids = jnp.arange(2 * mode_count)
    wavenumber = (column_ids // 2).astype(jnp.float32)
    imag_part = column_ids % 2
    positions = 2.0 * jnp.pi * jnp.arange(point_count).astype(jnp.float32) / point_count
    phases = wavenumber[:, None] * positions[None, :]
    forward = jnp.where(imag_part[:, None] == 0, jnp.cos(phases), -jnp.sin(phases)) / jnp.sqrt(
        jnp.float32(mode_count)
    )
    backward = forward.T * (2.0 * mode_count / point_count)
    return (forward, backward)


def nonlinear_rows(fields, low_index, neighbours, mode_counts, forward, backward):
    precision = lax.Precision.HIGH
    realizations, modes, columns = (fields.shape[1], fields.shape[2], fields.shape[4])
    low_select = (low_index[:, None] == jnp.arange(modes)[None, :]).astype(jnp.float32)
    high_mask = 1.0 - jnp.sum(low_select, axis=0)
    high_rows = high_mask[None, None, :, None, None]
    column_mask = ((jnp.arange(columns) // 2)[None, :] < mode_counts[:, None]).astype(jnp.float32)
    physical = jnp.dot(fields, forward, precision=precision)
    low_fields = jnp.take(physical, low_index, axis=2)
    high_low = jnp.zeros_like(physical)
    stresses = []
    for member in range(low_index.shape[0]):
        partner = jnp.take(physical, neighbours[:, member], axis=2)
        low_one = low_fields[:, :, member : member + 1]
        high_low = high_low + low_one * partner[1:2] + partner * low_one[1:2]
        stresses.append(jnp.sum(physical * (partner[1:2] * high_rows), axis=(1, 2)))
    stress = jnp.stack(stresses, axis=1) / realizations
    forcing = jnp.dot(high_low, backward, precision=precision) * high_rows
    low_forcing = jnp.dot(stress, backward, precision=precision)
    low_rows = jnp.einsum("jm,cjyk->cmyk", low_select, low_forcing, precision=lax.Precision.HIGHEST)
    forcing = (forcing + low_rows[:, None]) * column_mask[None, None, :, None, :]
    return fields + dt_step * forcing


def local_plain(velocity, low_index, neighbours, owner_map, mode_counts, helmholtz):
    components, reals_dev, band_modes, rows_ht, columns = velocity.shape
    kz_modes = columns // 2
    forward, backward = spanwise_tables(kz_modes, 4 * kz_modes)
    kx_count, ht_count = (lax.axis_size("kx"), lax.axis_size("ht"))
    real_count = lax.axis_size("real")
    modes, realizations = (band_modes * kx_count, reals_dev * real_count)
    slots_dev = kz_modes // (kx_count * ht_count)
    rows_dev = rows_ht // (kx_count * real_count)
    small = jnp.concatenate([neighbours, mode_counts[:, None]], axis=1)
    small = lax.all_gather(small, "kx", axis=0, tiled=True)
    neighbours, mode_counts = (small[:, :-1], small[:, -1])
    inverse_map = (
        jnp.zeros((kz_modes,), jnp.int32).at[owner_map].set(jnp.arange(kz_modes, dtype=jnp.int32))
    )
    split = velocity.reshape(
        components, reals_dev, band_modes, kx_count * real_count, rows_dev, columns
    )
    split = split.transpose(3, 0, 1, 2, 4, 5)
    split = lax.all_to_all(split, ("kx", "real"), split_axis=0, concat_axis=0, tiled=True)
    fields = split.reshape(
        kx_count, real_count, components, reals_dev, band_modes, rows_dev, columns
    )
    fields = fields.transpose(2, 1, 3, 0, 4, 5, 6).reshape(
        components, realizations, modes, rows_dev, columns
    )
    updated = nonlinear_rows(fields, low_index, neighbours, mode_counts, forward, backward)
    slotted = jnp.take(
        updated.reshape(components, realizations, modes, rows_dev, kz_modes, 2), owner_map, axis=4
    )
    slotted = slotted.reshape(
        components, real_count, reals_dev, modes, rows_dev, kx_count * ht_count, slots_dev, 2
    )
    outgoing = slotted.transpose(5, 1, 6, 2, 0, 3, 7, 4).reshape(
        kx_count * ht_count * real_count, slots_dev, reals_dev * components * modes * 2, rows_dev
    )
    incoming = lax.all_to_all(
        outgoing, ("kx", "ht", "real"), split_axis=0, concat_axis=0, tiled=True
    )
    incoming = incoming.reshape(
        kx_count, ht_count, real_count, slots_dev, reals_dev * components * modes * 2, rows_dev
    )
    incoming = incoming.transpose(3, 4, 1, 0, 2, 5).reshape(
        slots_dev, reals_dev * components * modes * 2, ht_count * rows_ht
    )
    solved = jnp.einsum("syx,snx->sny", helmholtz, incoming, precision=lax.Precision.HIGH)
    solved = solved.reshape(
        slots_dev, reals_dev, components, kx_count, band_modes, 2, ht_count, rows_ht
    )
    solved = solved.transpose(3, 6, 0, 5, 1, 2, 4, 7).reshape(
        kx_count * ht_count, slots_dev * 2, reals_dev * components * band_modes, rows_ht
    )
    returned = lax.all_to_all(solved, ("kx", "ht"), split_axis=0, concat_axis=0, tiled=True)
    restored = returned.reshape(
        kz_modes, 2, reals_dev, components, band_modes, rows_ht
    )
    restored = jnp.take(restored, inverse_map, axis=0)
    return restored.transpose(3, 2, 4, 5, 0, 1).reshape(velocity.shape)


LANES = 128
PIECES = 2
VMEM = pl.BlockSpec(memory_space=pltpu.VMEM)
SMEM = pl.BlockSpec(memory_space=pltpu.SMEM)


def params():
    return pltpu.CompilerParams(vmem_limit_bytes=48 * 1024 * 1024)


ORDERS = {4: (1, 3, 2), 8: (4, 1, 2, 6, 5, 3, 7)}


def steps_of(count):
    even = ORDERS.get(count, tuple(range(1, count)))
    odd = list(even)
    for first in range(0, count - 2, 2):
        odd[first], odd[first + 1] = (even[first + 1], even[first])
    return (0,) + tuple(even), (0,) + tuple(odd)


def step_at(count, position):
    even, odd = steps_of(count)
    return jnp.where(lax.axis_index("real") % 2 == 0, even[position], odd[position])


def cost(size):
    return pl.CostEstimate(flops=0, bytes_accessed=size, transcendentals=0)


def two_parts(value):
    top = value.astype(jnp.bfloat16)
    rest = (value - top.astype(jnp.float32)).astype(jnp.bfloat16)
    return top, rest


def dot(left, right, dims=((1,), (0,))):
    return lax.dot_general(left, right, (dims, ((), ())), preferred_element_type=jnp.float32)


def pack_kernel(near_ref, count_ref, velocity_ref, *out_refs):
    chunks, pieces, kx_count, rows, columns = velocity_ref.shape
    own = lax.axis_index("kx")
    for index, out_ref in enumerate(out_refs):
        piece, partner = (index // kx_count, own ^ step_at(kx_count, index % kx_count))
        for chunk in range(chunks):
            out_ref[chunk * rows : (chunk + 1) * rows] = velocity_ref[chunk, piece, partner]
    shape = (out_refs[0].shape[0] - chunks * rows, columns)
    row = lax.broadcasted_iota(jnp.int32, shape, 0)
    lane = lax.broadcasted_iota(jnp.int32, shape, 1)
    extra = jnp.zeros(shape, jnp.int32)
    modes, members = near_ref.shape
    for mode in range(modes):
        line = jnp.where(lane == members, count_ref[mode], 0)
        for member in range(members):
            line = jnp.where(lane == member, near_ref[mode, member], line)
        extra = jnp.where(row == mode, line, extra)
    extra = extra.astype(jnp.float32)
    for out_ref in out_refs[:kx_count]:
        out_ref[chunks * rows :] = extra


def pack(velocity, neighbours, mode_counts, extra_rows):
    chunks, pieces, kx_count, rows, columns = velocity.shape
    shapes = []
    for piece in range(pieces):
        total = chunks * rows + (0 if piece else extra_rows)
        shapes += [jax.ShapeDtypeStruct((total, columns), jnp.float32)] * kx_count
    out = pl.pallas_call(
        pack_kernel,
        out_shape=tuple(shapes),
        in_specs=[SMEM, SMEM, VMEM],
        out_specs=(VMEM,) * len(shapes),
        cost_estimate=cost(8 * velocity.size),
        name="pack",
    )(neighbours, mode_counts, velocity)
    return [out[piece * kx_count : (piece + 1) * kx_count] for piece in range(pieces)]


def split_matrix_kernel(matrix_ref, top_ref, rest_ref, mark_ref, turned, *, pieces, kx_count):
    ht_count, heights, width = turned.shape
    rows = width // (pieces * kx_count)
    owners = kx_count * ht_count
    own_kx, own_ht = (lax.axis_index("kx"), lax.axis_index("ht"))
    for h in range(ht_count):
        turned[h] = matrix_ref[0, h * width : (h + 1) * width, :].T
    for position in range(owners):
        step = step_at(owners, position)
        kx, ht = (own_kx ^ (step // ht_count), own_ht ^ (step % ht_count))
        for piece in range(pieces):
            source = pl.multiple_of(((ht * pieces + piece) * kx_count + kx) * rows, rows)
            start = (piece * owners + position) * rows
            for h in range(ht_count):
                place = (0, slice(start, start + rows), slice(h * width, (h + 1) * width))
                value = turned[h, pl.ds(source, rows), :]
                top_ref[place], rest_ref[place] = two_parts(value)
    mark_ref[...] = jnp.zeros_like(mark_ref)


def split_matrix(helmholtz, pieces, kx_count, ht_count):
    slots, heights, _ = helmholtz.shape
    spec = pl.BlockSpec((1, heights, heights), lambda s: (s, 0, 0))
    shape = jax.ShapeDtypeStruct(helmholtz.shape, jnp.bfloat16)
    return pl.pallas_call(
        functools.partial(split_matrix_kernel, pieces=pieces, kx_count=kx_count),
        out_shape=(shape, shape, jax.ShapeDtypeStruct((8, LANES), jnp.float32)),
        grid=(slots,),
        in_specs=[spec],
        out_specs=(spec, spec, pl.BlockSpec((8, LANES), lambda s: (0, 0))),
        scratch_shapes=[pltpu.VMEM((ht_count, heights, heights // ht_count), jnp.float32)],
        compiler_params=params(),
        cost_estimate=cost(8 * helmholtz.size),
        name="split_matrix",
    )(helmholtz)


def nonlinear_kernel(low_ref, near_ref, *refs):
    block_refs, refs = (refs[:-11], refs[-11:])
    first_ref, second_ref, back_ref, mask_ref, _, slotted_ref, stress_ref, *scratch = refs
    physical, products, sums, high_ref = scratch
    components, modes, rows, columns = slotted_ref.shape
    bands, points = (len(block_refs), physical.shape[3])
    band_modes = modes // bands
    own = lax.axis_index("kx")
    members, highs = (stress_ref.shape[1], products.shape[1])
    found = jnp.int32(0)
    for mode in range(modes):
        is_low = jnp.int32(0)
        for member in range(members):
            is_low = is_low | (low_ref[member] == mode).astype(jnp.int32)
        high_ref[found] = mode
        found = found + 1 - is_low

    def transform(component, carry):
        size = band_modes * rows
        for index, block_ref in enumerate(block_refs):
            top, rest = two_parts(block_ref[pl.ds(pl.multiple_of(component * size, 8), size)])
            both = dot(jnp.concatenate([top, rest], axis=1), first_ref[...])
            fields = both[:, :points] + dot(top, second_ref[...])
            place = pl.ds((own ^ step_at(bands, index)) * band_modes, band_modes)
            physical[component, place] = fields.reshape(band_modes, rows, points)
            slotted_ref[component, place] = both[:, points:].reshape(band_modes, rows, columns)
        return carry

    lax.fori_loop(0, components, transform, 0)

    def pairs(step, carry):
        halves = points // LANES
        place = (
            pl.ds(pl.multiple_of((step // halves) * 8, 8), 8),
            pl.ds(pl.multiple_of((step % halves) * LANES, LANES), LANES),
        )

        def one_high(index, totals):
            mode = high_ref[index]
            own = [physical[(c, mode) + place] for c in range(components)]
            result = [jnp.zeros((8, LANES), jnp.float32) for _ in range(components)]
            totals = list(totals)
            for member in range(members):
                low = low_ref[member]
                near = near_ref[mode, member]
                partner = [physical[(c, near) + place] for c in range(components)]
                low_one = [physical[(c, low) + place] for c in range(components)]
                for c in range(components):
                    if c == 1:
                        result[c] = result[c] + low_one[1] * partner[1]
                    else:
                        result[c] = result[c] + (low_one[c] * partner[1] + partner[c] * low_one[1])
                    slot = member * components + c
                    totals[slot] = totals[slot] + own[c] * partner[1]
            for c in range(components):
                products[(c, index) + place] = result[c] * 2.0 if c == 1 else result[c]
            return tuple(totals)

        empty = tuple(jnp.zeros((8, LANES), jnp.float32) for _ in range(members * components))
        totals = lax.fori_loop(0, highs, one_high, empty)
        for member in range(members):
            for c in range(components):
                sums[(c, member) + place] = totals[member * components + c]
        return carry

    lax.fori_loop(0, (rows // 8) * (points // LANES), pairs, 0)

    def inverse(fields, start):
        top, rest = two_parts(fields)
        both = dot(top, back_ref[:, start : start + 2 * columns])
        return (
            both[:, :columns] + both[:, columns:]
            + dot(rest, back_ref[:, start : start + columns])
        )

    def finish(component, carry):
        forcing = inverse(products[component].reshape(highs * rows, points), 0)
        forcing = forcing.reshape(highs, rows, columns)
        for index in range(highs):
            mode = high_ref[index]
            slotted_ref[component, mode] += forcing[index] * mask_ref[mode]
        stress = inverse(sums[component].reshape(members * rows, points), 2 * columns)
        stress_ref[component] = stress.reshape(members, rows, columns)
        return carry

    lax.fori_loop(0, components, finish, 0)


def nonlinear(blocks, shape, low_index, neighbours, tables, mask, after):
    components, modes, rows, columns = shape
    members, points = (low_index.shape[0], 2 * columns)
    highs = modes - members
    return pl.pallas_call(
        nonlinear_kernel,
        out_shape=(
            jax.ShapeDtypeStruct((components, modes, rows, columns), jnp.float32),
            jax.ShapeDtypeStruct((components, members, rows, columns), jnp.float32),
        ),
        in_specs=[SMEM, SMEM] + [VMEM] * (len(blocks) + 4) + [pl.BlockSpec(memory_space=pl.ANY)],
        out_specs=(VMEM, VMEM),
        scratch_shapes=[
            pltpu.VMEM((components, modes, rows, points), jnp.float32),
            pltpu.VMEM((components, highs, rows, points), jnp.float32),
            pltpu.VMEM((components, members, rows, points), jnp.float32),
            pltpu.SMEM((modes + 1,), jnp.int32),
        ],
        compiler_params=params(),
        cost_estimate=cost(8 * components * modes * rows * points * members),
        name="nonlinear",
    )(low_index, neighbours, *blocks, *tables, mask, after)


def outgoing_kernel(
    low_ref, slotted_ref, stress_ref, other_ref, mask_ref, *refs, groups, band_modes
):
    out_refs, full = (refs[:-1], refs[-1])
    components, modes, rows, columns = slotted_ref.shape
    members, owners = (stress_ref.shape[1], len(out_refs))
    slots = columns // 2 // owners
    per_slot = out_refs[0].shape[0] // slots
    full[...] = slotted_ref[...]
    position = lax.broadcasted_iota(jnp.int32, (rows, columns), 1) // slots % owners
    odd = lax.axis_index("real") % 2 == 1
    upper = odd & (position % 2 == 1) & (position < owners - 1)
    lower = odd & (position % 2 == 0) & (position > 0)
    for member in range(members):
        mode = low_ref[member]
        for c in range(components):
            stress = stress_ref[c, member] + other_ref[c, member]
            stress = jnp.where(
                upper, pltpu.roll(stress, columns - slots, 1),
                jnp.where(lower, pltpu.roll(stress, slots, 1), stress),
            )
            full[c, mode] += stress * mask_ref[mode]
    inner = modes // groups
    for c in range(components):
        for part in range(inner):
            tile = jnp.concatenate([full[c, part + inner * g] for g in range(groups)], axis=0)
            turned = tile.T
            band_low, band_mode = (part // band_modes, part % band_modes)
            for p in range(2):
                row = ((band_low * 2 + p) * components + c) * band_modes + band_mode
                for owner in range(owners):
                    start = (p * owners + owner) * slots
                    out_refs[owner][pl.ds(row, slots, stride=per_slot), :] = turned[
                        start : start + slots
                    ]


def outgoing(slotted, stress, other, low_index, mask, groups, band_modes, owners):
    components, modes, rows, columns = slotted.shape
    total = (columns // 2 // owners) * (modes // groups) * 2 * components
    return pl.pallas_call(
        functools.partial(outgoing_kernel, groups=groups, band_modes=band_modes),
        out_shape=(jax.ShapeDtypeStruct((total, groups * rows), jnp.float32),) * owners,
        in_specs=[SMEM, VMEM, VMEM, VMEM, VMEM],
        out_specs=(VMEM,) * owners,
        scratch_shapes=[pltpu.VMEM(slotted.shape, jnp.float32)],
        compiler_params=params(),
        cost_estimate=cost(8 * slotted.size),
        name="outgoing",
    )(low_index, slotted, stress, other, mask)


def regroup(blocks, rows):
    count = len(blocks)
    lane = lax.broadcasted_iota(jnp.int32, blocks[0].shape, 1) // rows
    step = 1
    while step < count:
        take = (lane & step) == 0
        for i in range(count):
            if i & step == 0:
                here, there = (blocks[i], blocks[i + step])
                blocks[i] = jnp.where(take, here, pltpu.roll(there, step * rows, 1))
                blocks[i + step] = jnp.where(
                    take, pltpu.roll(here, LANES - step * rows, 1), there
                )
        step *= 2
    return blocks


def solve_kernel(*refs, groups, kx_count, ht_count, started, last):
    owners = kx_count * ht_count
    block_refs, (top_ref, rest_ref), refs = (
        refs[:owners], refs[owners : owners + 2], refs[owners + 2 :]
    )
    rows = LANES // groups
    tiles = []
    for first in range(0, owners, groups):
        blocks = [block_refs[first + g][0] for g in range(groups)]
        tiles.append(jnp.concatenate(regroup(blocks, rows), axis=0))
    top, rest = two_parts(jnp.concatenate(tiles, axis=1))
    count = top.shape[0]
    both = dot(jnp.concatenate([top, rest], axis=0), top_ref[0])
    solved = both[:count] + both[count:] + dot(top, rest_ref[0])
    if started:
        solved, refs = (solved + refs[0][0], refs[1:])
    if not last:
        refs[0][0] = solved
        return
    out_refs, full = (refs[:owners], refs[owners])
    for tile in range(full.shape[0]):
        full[tile] = solved[:, tile * LANES : (tile + 1) * LANES]
    own_kx, own_ht = (lax.axis_index("kx"), lax.axis_index("ht"))
    lane_tiles, per_band = out_refs[0].shape[1:3]
    for position, out_ref in enumerate(out_refs):
        step = step_at(owners, position)
        kx, ht = (own_kx ^ (step // ht_count), own_ht ^ (step % ht_count))
        band = pl.ds(pl.multiple_of(kx * per_band, 8), per_band)
        for tile in range(lane_tiles):
            out_ref[0, tile] = full[ht * lane_tiles + tile, band]


def solve(blocks, matrices, piece, pieces, partial, groups, kx_count, ht_count):
    slots, per_slot, lanes = blocks[0].shape
    heights, last = (matrices[0].shape[2], piece == pieces - 1)
    count, owners = (per_slot * groups, kx_count * ht_count)
    whole = pl.BlockSpec((1, count, heights), lambda s: (s, 0, 0))
    if last:
        shape = (slots, heights // ht_count // LANES, count // kx_count, LANES)
        out_shape = (jax.ShapeDtypeStruct(shape, jnp.float32),) * owners
        out_specs = (pl.BlockSpec((1,) + shape[1:], lambda s: (s, 0, 0, 0)),) * owners
        scratch = [pltpu.VMEM((heights // LANES, count, LANES), jnp.float32)]
    else:
        out_shape = jax.ShapeDtypeStruct((slots, count, heights), jnp.float32)
        out_specs, scratch = (whole, [])
    return pl.pallas_call(
        functools.partial(
            solve_kernel, groups=groups, kx_count=kx_count, ht_count=ht_count,
            started=partial is not None, last=last,
        ),
        out_shape=out_shape,
        grid=(slots,),
        in_specs=[pl.BlockSpec((1, per_slot, lanes), lambda s: (s, 0, 0))] * owners
        + [pl.BlockSpec((1, heights // pieces, heights), lambda s: (s, piece, 0))] * 2
        + ([] if partial is None else [whole]),
        out_specs=out_specs,
        scratch_shapes=scratch,
        compiler_params=params(),
        cost_estimate=pl.CostEstimate(
            flops=6 * slots * count * heights * heights // pieces,
            bytes_accessed=slots * heights * heights * 4 // pieces, transcendentals=0,
        ),
        name="solve",
    )(*blocks, *matrices, *([] if partial is None else [partial]))


def restore_kernel(*refs):
    block_refs, (order_ref, out_ref) = (refs[:-2], refs[-2:])
    components, band_modes, rows, columns = out_ref.shape
    slots = columns // 2 // len(block_refs)
    per_slot = block_refs[0].shape[0] // slots
    for c in range(components):
        for mode in range(band_modes):
            for tile in range(rows // LANES):
                parts = []
                for p in range(2):
                    row = ((tile * 2 + p) * components + c) * band_modes + mode
                    for block_ref in block_refs:
                        parts.append(block_ref[pl.ds(row, slots, stride=per_slot), :])
                top, rest = two_parts(jnp.concatenate(parts, axis=0))
                both = jnp.concatenate([top, rest], axis=0)
                out_ref[c, mode, pl.ds(tile * LANES, LANES)] = dot(
                    both, order_ref[...], ((0,), (0,))
                )


def restore(blocks, order, components, band_modes, rows):
    columns = order.shape[1]
    return pl.pallas_call(
        restore_kernel,
        out_shape=jax.ShapeDtypeStruct((components, band_modes, rows, columns), jnp.float32),
        in_specs=[VMEM] * (len(blocks) + 1),
        out_specs=VMEM,
        compiler_params=params(),
        cost_estimate=cost(8 * components * band_modes * rows * columns),
        name="restore",
    )(*blocks, order)


def table_parts(value):
    top = lax.reduce_precision(value, 8, 7)
    return top.astype(jnp.bfloat16), (value - top).astype(jnp.bfloat16)


def slot_tables(owner_map, even_map, columns):
    forward, backward = spanwise_tables(columns // 2, 2 * columns)
    select, even_select = (
        (2 * order[None, :] + jnp.arange(2)[:, None]).reshape(1, columns)
        == jnp.arange(columns)[:, None]
        for order in (owner_map, even_map)
    )
    forward_top, forward_rest = table_parts(forward)
    first = jnp.concatenate([forward_top, select.astype(jnp.bfloat16)], axis=1)
    first = jnp.concatenate([first, first], axis=0)
    back = []
    for chosen in (select, even_select):
        slotted_back = jnp.dot(
            backward, chosen.astype(jnp.float32), precision=lax.Precision.HIGHEST
        )
        back += table_parts(slotted_back)
    back = jnp.concatenate(back, axis=1)
    order = select.T.astype(jnp.bfloat16)
    order = jnp.concatenate([order, order], axis=0)
    return (first, forward_rest, back), order


def slot_masks(owner_map, mode_counts, realizations):
    active = jnp.tile(owner_map, 2)[None, :] < mode_counts[:, None]
    mask = jnp.where(active, jnp.float32(dt_step), 0.0)[:, None, :]
    return mask, mask / realizations


def exchange(blocks, axes):
    count, realizations = (len(blocks), lax.axis_size("real"))
    result = list(blocks)
    for position in range(1, count):
        steps = [order[position] for order in steps_of(count)]
        pairs = [
            (index * realizations + r, (index ^ steps[r % 2]) * realizations + r)
            for index in range(count)
            for r in range(realizations)
        ]
        result[position] = lax.ppermute(blocks[position], axes + ("real",), pairs)
    return result


def local(velocity, low_index, neighbours, owner_map, mode_counts, helmholtz):
    components, reals_dev, band_modes, rows_ht, columns = velocity.shape
    kx_count, ht_count = (lax.axis_size("kx"), lax.axis_size("ht"))
    own_kx, own_ht = (lax.axis_index("kx"), lax.axis_index("ht"))
    owners, pieces, real_count = (kx_count * ht_count, PIECES, lax.axis_size("real"))
    rows = rows_ht // (kx_count * pieces)
    groups = LANES // rows if rows else 0
    slots = columns // 2 // owners
    if (
        columns != LANES or reals_dev != 1 or rows_ht % LANES or rows % 8 or LANES % rows or kx_count % groups or kx_count & (kx_count - 1)
        or (band_modes * 2 * components) % 8 or slots % 8 or owners & (owners - 1) or low_index.shape[0] >= kx_count * band_modes
        or low_index.shape[0] >= columns or real_count < 2 or real_count & (real_count - 1)
    ):
        return local_plain(velocity, low_index, neighbours, owner_map, mode_counts, helmholtz)
    realizations, members = (real_count, low_index.shape[0])
    chunks, modes = (components * band_modes, band_modes * kx_count)
    shape = (components, modes, rows, columns)
    extra_rows = -(-band_modes // 8) * 8
    split = velocity.reshape(chunks, pieces, kx_count, rows, columns)
    owner_map, even_map = (
        owner_map.reshape(owners, slots)[(own_kx * ht_count + own_ht) ^ order].reshape(-1)
        for order in (
            jnp.stack([step_at(owners, position) for position in range(owners)]),
            jnp.array(steps_of(owners)[0], jnp.int32),
        )
    )
    parts = [
        exchange(blocks, ("kx",)) for blocks in pack(split, neighbours, mode_counts, extra_rows)
    ]
    *matrices, after = split_matrix(helmholtz, pieces, kx_count, ht_count)
    small = 0.0
    for index, block in enumerate(parts[0]):
        lines = block[chunks * rows : chunks * rows + band_modes, : members + 1]
        here = (own_kx ^ step_at(kx_count, index)) == jnp.arange(kx_count)
        small = small + jnp.where(here[:, None, None], lines[None], 0.0)
    small = small.reshape(modes, members + 1).astype(jnp.int32)
    neighbours, mode_counts = (small[:, :-1], small[:, -1])
    tables, order = slot_tables(owner_map, even_map, columns)
    mask, low_mask = slot_masks(owner_map, mode_counts, realizations)
    received = []
    for part in parts:
        slotted, stress = nonlinear(part, shape, low_index, neighbours, tables, mask, after)
        step, other = (1, None)
        while step < realizations:
            stress = stress if other is None else stress + other
            other = lax.ppermute(
                stress, "real", [(index, index ^ step) for index in range(realizations)]
            )
            step *= 2
        after = other
        blocks = outgoing(
            slotted, stress, other, low_index, low_mask, groups, band_modes, owners
        )
        blocks = [block.reshape(slots, -1, LANES) for block in blocks]
        received.append(exchange(blocks, ("kx", "ht")))
    solved = None
    for piece, blocks in enumerate(received):
        solved = solve(blocks, matrices, piece, pieces, solved, groups, kx_count, ht_count)
    returned = [block.reshape(-1, LANES) for block in exchange(solved, ("kx", "ht"))]
    result = restore(returned, order, components, band_modes, rows_ht)
    return result.reshape(velocity.shape)


def solution(mesh):
    in_specs = (
        P(None, "real", "kx", "ht", None),
        P(),
        P("kx", None),
        P(),
        P("kx"),
        P(("kx", "ht"), None, None),
    )
    out_specs = P(None, "real", "kx", "ht", None)
    return jax.shard_map(local, mesh=mesh, in_specs=in_specs, out_specs=out_specs, check_vma=False)
```

```python
import functools

import jax
import jax.numpy as jnp
from jax import lax
from jax.experimental import pallas as pl
from jax.experimental.pallas import tpu as pltpu
from jax.sharding import PartitionSpec as P

dt_step = 0.1


def spanwise_tables(mode_count, point_count):
    column_ids = jnp.arange(2 * mode_count)
    wavenumber = (column_ids // 2).astype(jnp.float32)
    imag_part = column_ids % 2
    positions = 2.0 * jnp.pi * jnp.arange(point_count).astype(jnp.float32) / point_count
    phases = wavenumber[:, None] * positions[None, :]
    forward = jnp.where(imag_part[:, None] == 0, jnp.cos(phases), -jnp.sin(phases)) / jnp.sqrt(
        jnp.float32(mode_count)
    )
    backward = forward.T * (2.0 * mode_count / point_count)
    return (forward, backward)


def nonlinear_rows(fields, low_index, neighbours, mode_counts, forward, backward):
    precision = lax.Precision.HIGH
    realizations, modes, columns = (fields.shape[1], fields.shape[2], fields.shape[4])
    low_select = (low_index[:, None] == jnp.arange(modes)[None, :]).astype(jnp.float32)
    high_mask = 1.0 - jnp.sum(low_select, axis=0)
    high_rows = high_mask[None, None, :, None, None]
    column_mask = ((jnp.arange(columns) // 2)[None, :] < mode_counts[:, None]).astype(jnp.float32)
    physical = jnp.dot(fields, forward, precision=precision)
    low_fields = jnp.take(physical, low_index, axis=2)
    high_low = jnp.zeros_like(physical)
    stresses = []
    for member in range(low_index.shape[0]):
        partner = jnp.take(physical, neighbours[:, member], axis=2)
        low_one = low_fields[:, :, member : member + 1]
        high_low = high_low + low_one * partner[1:2] + partner * low_one[1:2]
        stresses.append(jnp.sum(physical * (partner[1:2] * high_rows), axis=(1, 2)))
    stress = jnp.stack(stresses, axis=1) / realizations
    forcing = jnp.dot(high_low, backward, precision=precision) * high_rows
    low_forcing = jnp.dot(stress, backward, precision=precision)
    low_rows = jnp.einsum("jm,cjyk->cmyk", low_select, low_forcing, precision=lax.Precision.HIGHEST)
    forcing = (forcing + low_rows[:, None]) * column_mask[None, None, :, None, :]
    return fields + dt_step * forcing


def local_plain(velocity, low_index, neighbours, owner_map, mode_counts, helmholtz):
    components, reals_dev, band_modes, rows_ht, columns = velocity.shape
    kz_modes = columns // 2
    forward, backward = spanwise_tables(kz_modes, 4 * kz_modes)
    kx_count, ht_count = (lax.axis_size("kx"), lax.axis_size("ht"))
    real_count = lax.axis_size("real")
    modes, realizations = (band_modes * kx_count, reals_dev * real_count)
    slots_dev = kz_modes // (kx_count * ht_count)
    rows_dev = rows_ht // (kx_count * real_count)
    small = jnp.concatenate([neighbours, mode_counts[:, None]], axis=1)
    small = lax.all_gather(small, "kx", axis=0, tiled=True)
    neighbours, mode_counts = (small[:, :-1], small[:, -1])
    inverse_map = (
        jnp.zeros((kz_modes,), jnp.int32).at[owner_map].set(jnp.arange(kz_modes, dtype=jnp.int32))
    )
    split = velocity.reshape(
        components, reals_dev, band_modes, kx_count * real_count, rows_dev, columns
    )
    split = split.transpose(3, 0, 1, 2, 4, 5)
    split = lax.all_to_all(split, ("kx", "real"), split_axis=0, concat_axis=0, tiled=True)
    fields = split.reshape(
        kx_count, real_count, components, reals_dev, band_modes, rows_dev, columns
    )
    fields = fields.transpose(2, 1, 3, 0, 4, 5, 6).reshape(
        components, realizations, modes, rows_dev, columns
    )
    updated = nonlinear_rows(fields, low_index, neighbours, mode_counts, forward, backward)
    slotted = jnp.take(
        updated.reshape(components, realizations, modes, rows_dev, kz_modes, 2), owner_map, axis=4
    )
    slotted = slotted.reshape(
        components, real_count, reals_dev, modes, rows_dev, kx_count * ht_count, slots_dev, 2
    )
    outgoing = slotted.transpose(5, 1, 6, 2, 0, 3, 7, 4).reshape(
        kx_count * ht_count * real_count, slots_dev, reals_dev * components * modes * 2, rows_dev
    )
    incoming = lax.all_to_all(
        outgoing, ("kx", "ht", "real"), split_axis=0, concat_axis=0, tiled=True
    )
    incoming = incoming.reshape(
        kx_count, ht_count, real_count, slots_dev, reals_dev * components * modes * 2, rows_dev
    )
    incoming = incoming.transpose(3, 4, 1, 0, 2, 5).reshape(
        slots_dev, reals_dev * components * modes * 2, ht_count * rows_ht
    )
    solved = jnp.einsum("syx,snx->sny", helmholtz, incoming, precision=lax.Precision.HIGH)
    solved = solved.reshape(
        slots_dev, reals_dev, components, kx_count, band_modes, 2, ht_count, rows_ht
    )
    solved = solved.transpose(3, 6, 0, 5, 1, 2, 4, 7).reshape(
        kx_count * ht_count, slots_dev * 2, reals_dev * components * band_modes, rows_ht
    )
    returned = lax.all_to_all(solved, ("kx", "ht"), split_axis=0, concat_axis=0, tiled=True)
    restored = returned.reshape(
        kz_modes, 2, reals_dev, components, band_modes, rows_ht
    )
    restored = jnp.take(restored, inverse_map, axis=0)
    return restored.transpose(3, 2, 4, 5, 0, 1).reshape(velocity.shape)


LANES = 128
PIECES = 2
VMEM = pl.BlockSpec(memory_space=pltpu.VMEM)
SMEM = pl.BlockSpec(memory_space=pltpu.SMEM)


def params():
    return pltpu.CompilerParams(vmem_limit_bytes=48 * 1024 * 1024)


ORDERS = {4: (1, 3, 2), 8: (4, 1, 2, 6, 5, 3, 7)}


def steps_of(count):
    even = ORDERS.get(count, tuple(range(1, count)))
    odd = list(even)
    for first in range(0, count - 2, 2):
        odd[first], odd[first + 1] = (even[first + 1], even[first])
    return (0,) + tuple(even), (0,) + tuple(odd)


def step_at(count, position):
    even, odd = steps_of(count)
    return jnp.where(lax.axis_index("real") % 2 == 0, even[position], odd[position])


def cost(size):
    return pl.CostEstimate(flops=0, bytes_accessed=size, transcendentals=0)


def two_parts(value):
    top = value.astype(jnp.bfloat16)
    rest = (value - top.astype(jnp.float32)).astype(jnp.bfloat16)
    return top, rest


def dot(left, right, dims=((1,), (0,))):
    return lax.dot_general(left, right, (dims, ((), ())), preferred_element_type=jnp.float32)


def pack_kernel(near_ref, count_ref, velocity_ref, *out_refs):
    chunks, pieces, kx_count, rows, columns = velocity_ref.shape
    own = lax.axis_index("kx")
    for index in range(kx_count):
        partner = own ^ step_at(kx_count, index)
        for chunk in range(chunks):
            place = slice(chunk * rows, (chunk + 1) * rows)
            out_refs[index][place] = velocity_ref[chunk, 0, partner]
            for piece in range(1, pieces):
                out_refs[kx_count + piece - 1][index, place] = velocity_ref[chunk, piece, index]
    shape = (out_refs[0].shape[0] - chunks * rows, columns)
    row = lax.broadcasted_iota(jnp.int32, shape, 0)
    lane = lax.broadcasted_iota(jnp.int32, shape, 1)
    extra = jnp.zeros(shape, jnp.int32)
    modes, members = near_ref.shape
    for mode in range(modes):
        line = jnp.where(lane == members, count_ref[mode], 0)
        for member in range(members):
            line = jnp.where(lane == member, near_ref[mode, member], line)
        extra = jnp.where(row == mode, line, extra)
    extra = extra.astype(jnp.float32)
    for out_ref in out_refs[:kx_count]:
        out_ref[chunks * rows :] = extra


def pack(velocity, neighbours, mode_counts, extra_rows):
    chunks, pieces, kx_count, rows, columns = velocity.shape
    size = chunks * rows
    shapes = [(size + extra_rows, columns)] * kx_count
    shapes += [(kx_count, size, columns)] * (pieces - 1)
    out = pl.pallas_call(
        pack_kernel,
        out_shape=tuple(jax.ShapeDtypeStruct(shape, jnp.float32) for shape in shapes),
        in_specs=[SMEM, SMEM, VMEM],
        out_specs=(VMEM,) * len(shapes),
        cost_estimate=cost(8 * velocity.size),
        name="pack",
    )(neighbours, mode_counts, velocity)
    return out[:kx_count], out[kx_count:]


def split_matrix_kernel(matrix_ref, top_ref, rest_ref, mark_ref, turned, *, pieces, kx_count):
    ht_count, heights, width = turned.shape
    rows = width // (pieces * kx_count)
    owners = kx_count * ht_count
    own_kx, own_ht = (lax.axis_index("kx"), lax.axis_index("ht"))
    for h in range(ht_count):
        turned[h] = matrix_ref[0, h * width : (h + 1) * width, :].T
    for position in range(owners):
        step = step_at(owners, position)
        kx, ht = (own_kx ^ (step // ht_count), own_ht ^ (step % ht_count))
        for piece in range(pieces):
            source = pl.multiple_of(((ht * pieces + piece) * kx_count + kx) * rows, rows)
            start = (piece * owners + position) * rows
            for h in range(ht_count):
                place = (0, slice(start, start + rows), slice(h * width, (h + 1) * width))
                value = turned[h, pl.ds(source, rows), :]
                top_ref[place], rest_ref[place] = two_parts(value)
    mark_ref[...] = jnp.zeros_like(mark_ref)


def split_matrix(helmholtz, pieces, kx_count, ht_count):
    slots, heights, _ = helmholtz.shape
    spec = pl.BlockSpec((1, heights, heights), lambda s: (s, 0, 0))
    shape = jax.ShapeDtypeStruct(helmholtz.shape, jnp.bfloat16)
    return pl.pallas_call(
        functools.partial(split_matrix_kernel, pieces=pieces, kx_count=kx_count),
        out_shape=(shape, shape, jax.ShapeDtypeStruct((8, LANES), jnp.float32)),
        grid=(slots,),
        in_specs=[spec],
        out_specs=(spec, spec, pl.BlockSpec((8, LANES), lambda s: (0, 0))),
        scratch_shapes=[pltpu.VMEM((ht_count, heights, heights // ht_count), jnp.float32)],
        compiler_params=params(),
        cost_estimate=cost(8 * helmholtz.size),
        name="split_matrix",
    )(helmholtz)


def nonlinear_kernel(low_ref, near_ref, *refs):
    block_refs, refs = (refs[:-12], refs[-12:])
    first_ref, second_ref, back_ref, mask_ref, _, slotted_ref, kept_ref, sent_ref = refs[:8]
    physical, products, sums, high_ref = refs[8:]
    components, modes, rows, columns = slotted_ref.shape
    if len(block_refs) > 1:
        bands = len(block_refs)
        places = [lax.axis_index("kx") ^ step_at(bands, index) for index in range(bands)]
    else:
        bands = block_refs[0].shape[0]
        places = list(range(bands))
        block_refs = [block_refs[0].at[index] for index in range(bands)]
    points, band_modes = (physical.shape[3], modes // bands)
    members, highs = (sums.shape[1], products.shape[1])
    odd = lax.axis_index("real") % 2 == 1
    found = jnp.int32(0)
    for mode in range(modes):
        is_low = jnp.int32(0)
        for member in range(members):
            is_low = is_low | (low_ref[member] == mode).astype(jnp.int32)
        high_ref[found] = mode
        found = found + 1 - is_low

    def transform(component, carry):
        size = band_modes * rows
        for index, block_ref in enumerate(block_refs):
            top, rest = two_parts(block_ref[pl.ds(pl.multiple_of(component * size, 8), size)])
            both = dot(jnp.concatenate([top, rest], axis=1), first_ref[...])
            fields = both[:, :points] + dot(top, second_ref[...])
            place = pl.ds(places[index] * band_modes, band_modes)
            physical[component, place] = fields.reshape(band_modes, rows, points)
            slotted_ref[component, place] = both[:, points:].reshape(band_modes, rows, columns)
        return carry

    lax.fori_loop(0, components, transform, 0)

    def pairs(step, carry):
        halves = points // LANES
        place = (
            pl.ds(pl.multiple_of((step // halves) * 8, 8), 8),
            pl.ds(pl.multiple_of((step % halves) * LANES, LANES), LANES),
        )

        def one_high(index, totals):
            mode = high_ref[index]
            own = [physical[(c, mode) + place] for c in range(components)]
            result = [jnp.zeros((8, LANES), jnp.float32) for _ in range(components)]
            totals = list(totals)
            for member in range(members):
                low = low_ref[member]
                near = near_ref[mode, member]
                partner = [physical[(c, near) + place] for c in range(components)]
                low_one = [physical[(c, low) + place] for c in range(components)]
                for c in range(components):
                    if c == 1:
                        result[c] = result[c] + low_one[1] * partner[1]
                    else:
                        result[c] = result[c] + (low_one[c] * partner[1] + partner[c] * low_one[1])
                    slot = member * components + c
                    totals[slot] = totals[slot] + own[c] * partner[1]
            for c in range(components):
                products[(c, index) + place] = result[c] * 2.0 if c == 1 else result[c]
            return tuple(totals)

        empty = tuple(jnp.zeros((8, LANES), jnp.float32) for _ in range(members * components))
        totals = lax.fori_loop(0, highs, one_high, empty)
        for member in range(members):
            for c in range(components):
                sums[(c, member) + place] = totals[member * components + c]
        return carry

    lax.fori_loop(0, (rows // 8) * (points // LANES), pairs, 0)

    def inverse(fields, start):
        top, rest = two_parts(fields)
        both = dot(top, back_ref[:, start : start + 2 * columns])
        return (
            both[:, :columns] + both[:, columns:]
            + dot(rest, back_ref[:, start : start + columns])
        )

    def finish(component, carry):
        forcing = inverse(products[component].reshape(highs * rows, points), 0)
        forcing = forcing.reshape(highs, rows, columns)
        for index in range(highs):
            mode = high_ref[index]
            slotted_ref[component, mode] += forcing[index] * mask_ref[mode]
        stress = inverse(sums[component].reshape(members * rows, points), 2 * columns)
        stress = stress.reshape(2, members // 2, rows, columns)
        kept_ref[component] = jnp.where(odd, stress[1], stress[0])
        sent_ref[component] = jnp.where(odd, stress[0], stress[1])
        return carry

    lax.fori_loop(0, components, finish, 0)


def nonlinear(blocks, shape, low_index, neighbours, tables, mask, after):
    components, modes, rows, columns = shape
    members, points = (low_index.shape[0], 2 * columns)
    highs = modes - members
    return pl.pallas_call(
        nonlinear_kernel,
        out_shape=(
            jax.ShapeDtypeStruct((components, modes, rows, columns), jnp.float32),
            jax.ShapeDtypeStruct((components, members // 2, rows, columns), jnp.float32),
            jax.ShapeDtypeStruct((components, members // 2, rows, columns), jnp.float32),
        ),
        in_specs=[SMEM, SMEM] + [VMEM] * (len(blocks) + 4) + [pl.BlockSpec(memory_space=pl.ANY)],
        out_specs=(VMEM, VMEM, VMEM),
        scratch_shapes=[
            pltpu.VMEM((components, modes, rows, points), jnp.float32),
            pltpu.VMEM((components, highs, rows, points), jnp.float32),
            pltpu.VMEM((components, members, rows, points), jnp.float32),
            pltpu.SMEM((modes + 1,), jnp.int32),
        ],
        compiler_params=params(),
        cost_estimate=cost(8 * components * modes * rows * points * members),
        name="nonlinear",
    )(low_index, neighbours, *blocks, *tables, mask, after)


def outgoing_kernel(
    low_ref, slotted_ref, kept_ref, other_ref, mask_ref, *refs, groups, band_modes
):
    out_refs, full = (refs[:-1], refs[-1])
    components, modes, rows, columns = slotted_ref.shape
    half, owners = (kept_ref.shape[1], len(out_refs))
    slots = columns // 2 // owners
    per_slot = out_refs[0].shape[0] // slots
    full[...] = slotted_ref[...]
    position = lax.broadcasted_iota(jnp.int32, (rows, columns), 1) // slots % owners
    own = lax.axis_index("real") % 2
    upper = (own == 1) & (position % 2 == 1) & (position < owners - 1)
    lower = (own == 1) & (position % 2 == 0) & (position > 0)
    for member in range(half):
        for part_ref, start in ((kept_ref, own * half), (other_ref, (1 - own) * half)):
            mode = low_ref[start + member]
            for c in range(components):
                stress = part_ref[c, member]
                stress = jnp.where(
                    upper, pltpu.roll(stress, columns - slots, 1),
                    jnp.where(lower, pltpu.roll(stress, slots, 1), stress),
                )
                full[c, mode] += stress * mask_ref[mode]
    inner = modes // groups
    for c in range(components):
        for part in range(inner):
            tile = jnp.concatenate([full[c, part + inner * g] for g in range(groups)], axis=0)
            turned = tile.T
            band_low, band_mode = (part // band_modes, part % band_modes)
            for p in range(2):
                row = ((band_low * 2 + p) * components + c) * band_modes + band_mode
                for owner in range(owners):
                    start = (p * owners + owner) * slots
                    out_refs[owner][pl.ds(row, slots, stride=per_slot), :] = turned[
                        start : start + slots
                    ]


def outgoing(slotted, kept, other, low_index, mask, groups, band_modes, owners):
    components, modes, rows, columns = slotted.shape
    total = (columns // 2 // owners) * (modes // groups) * 2 * components
    return pl.pallas_call(
        functools.partial(outgoing_kernel, groups=groups, band_modes=band_modes),
        out_shape=(jax.ShapeDtypeStruct((total, groups * rows), jnp.float32),) * owners,
        in_specs=[SMEM, VMEM, VMEM, VMEM, VMEM],
        out_specs=(VMEM,) * owners,
        scratch_shapes=[pltpu.VMEM(slotted.shape, jnp.float32)],
        compiler_params=params(),
        cost_estimate=cost(8 * slotted.size),
        name="outgoing",
    )(low_index, slotted, kept, other, mask)


def regroup(blocks, rows):
    count = len(blocks)
    lane = lax.broadcasted_iota(jnp.int32, blocks[0].shape, 1) // rows
    step = 1
    while step < count:
        take = (lane & step) == 0
        for i in range(count):
            if i & step == 0:
                here, there = (blocks[i], blocks[i + step])
                blocks[i] = jnp.where(take, here, pltpu.roll(there, step * rows, 1))
                blocks[i + step] = jnp.where(
                    take, pltpu.roll(here, LANES - step * rows, 1), there
                )
        step *= 2
    return blocks


def solve_kernel(*refs, groups, kx_count, ht_count, started, last):
    owners = kx_count * ht_count
    block_refs, (top_ref, rest_ref), refs = (
        refs[:owners], refs[owners : owners + 2], refs[owners + 2 :]
    )
    rows = LANES // groups
    tiles = []
    for first in range(0, owners, groups):
        blocks = [block_refs[first + g][0] for g in range(groups)]
        tiles.append(jnp.concatenate(regroup(blocks, rows), axis=0))
    top, rest = two_parts(jnp.concatenate(tiles, axis=1))
    count = top.shape[0]
    both = dot(jnp.concatenate([top, rest], axis=0), top_ref[0])
    solved = both[:count] + both[count:] + dot(top, rest_ref[0])
    if started:
        solved, refs = (solved + refs[0][0], refs[1:])
    if not last:
        refs[0][0] = solved
        return
    out_refs, full = (refs[:owners], refs[owners])
    for tile in range(full.shape[0]):
        full[tile] = solved[:, tile * LANES : (tile + 1) * LANES]
    own_kx, own_ht = (lax.axis_index("kx"), lax.axis_index("ht"))
    lane_tiles, per_band = out_refs[0].shape[1:3]
    for position, out_ref in enumerate(out_refs):
        step = step_at(owners, position)
        kx, ht = (own_kx ^ (step // ht_count), own_ht ^ (step % ht_count))
        band = pl.ds(pl.multiple_of(kx * per_band, 8), per_band)
        for tile in range(lane_tiles):
            out_ref[0, tile] = full[ht * lane_tiles + tile, band]


def solve(blocks, matrices, piece, pieces, partial, groups, kx_count, ht_count):
    slots, per_slot, lanes = blocks[0].shape
    heights, last = (matrices[0].shape[2], piece == pieces - 1)
    count, owners = (per_slot * groups, kx_count * ht_count)
    whole = pl.BlockSpec((1, count, heights), lambda s: (s, 0, 0))
    if last:
        shape = (slots, heights // ht_count // LANES, count // kx_count, LANES)
        out_shape = (jax.ShapeDtypeStruct(shape, jnp.float32),) * owners
        out_specs = (pl.BlockSpec((1,) + shape[1:], lambda s: (s, 0, 0, 0)),) * owners
        scratch = [pltpu.VMEM((heights // LANES, count, LANES), jnp.float32)]
    else:
        out_shape = jax.ShapeDtypeStruct((slots, count, heights), jnp.float32)
        out_specs, scratch = (whole, [])
    return pl.pallas_call(
        functools.partial(
            solve_kernel, groups=groups, kx_count=kx_count, ht_count=ht_count,
            started=partial is not None, last=last,
        ),
        out_shape=out_shape,
        grid=(slots,),
        in_specs=[pl.BlockSpec((1, per_slot, lanes), lambda s: (s, 0, 0))] * owners
        + [pl.BlockSpec((1, heights // pieces, heights), lambda s: (s, piece, 0))] * 2
        + ([] if partial is None else [whole]),
        out_specs=out_specs,
        scratch_shapes=scratch,
        compiler_params=params(),
        cost_estimate=pl.CostEstimate(
            flops=6 * slots * count * heights * heights // pieces,
            bytes_accessed=slots * heights * heights * 4 // pieces, transcendentals=0,
        ),
        name="solve",
    )(*blocks, *matrices, *([] if partial is None else [partial]))


def restore_kernel(*refs):
    block_refs, (order_ref, out_ref) = (refs[:-2], refs[-2:])
    components, band_modes, rows, columns = out_ref.shape
    slots = columns // 2 // len(block_refs)
    per_slot = block_refs[0].shape[0] // slots
    for c in range(components):
        for mode in range(band_modes):
            for tile in range(rows // LANES):
                parts = []
                for p in range(2):
                    row = ((tile * 2 + p) * components + c) * band_modes + mode
                    for block_ref in block_refs:
                        parts.append(block_ref[pl.ds(row, slots, stride=per_slot), :])
                top, rest = two_parts(jnp.concatenate(parts, axis=0))
                both = jnp.concatenate([top, rest], axis=0)
                out_ref[c, mode, pl.ds(tile * LANES, LANES)] = dot(
                    both, order_ref[...], ((0,), (0,))
                )


def restore(blocks, order, components, band_modes, rows):
    columns = order.shape[1]
    return pl.pallas_call(
        restore_kernel,
        out_shape=jax.ShapeDtypeStruct((components, band_modes, rows, columns), jnp.float32),
        in_specs=[VMEM] * (len(blocks) + 1),
        out_specs=VMEM,
        compiler_params=params(),
        cost_estimate=cost(8 * components * band_modes * rows * columns),
        name="restore",
    )(*blocks, order)


def table_parts(value):
    top = lax.reduce_precision(value, 8, 7)
    return top.astype(jnp.bfloat16), (value - top).astype(jnp.bfloat16)


def slot_tables(owner_map, even_map, columns):
    forward, backward = spanwise_tables(columns // 2, 2 * columns)
    select, even_select = (
        (2 * order[None, :] + jnp.arange(2)[:, None]).reshape(1, columns)
        == jnp.arange(columns)[:, None]
        for order in (owner_map, even_map)
    )
    forward_top, forward_rest = table_parts(forward)
    first = jnp.concatenate([forward_top, select.astype(jnp.bfloat16)], axis=1)
    first = jnp.concatenate([first, first], axis=0)
    back = []
    for chosen in (select, even_select):
        slotted_back = jnp.dot(
            backward, chosen.astype(jnp.float32), precision=lax.Precision.HIGHEST
        )
        back += table_parts(slotted_back)
    back = jnp.concatenate(back, axis=1)
    order = select.T.astype(jnp.bfloat16)
    order = jnp.concatenate([order, order], axis=0)
    return (first, forward_rest, back), order


def slot_masks(owner_map, mode_counts, realizations):
    active = jnp.tile(owner_map, 2)[None, :] < mode_counts[:, None]
    mask = jnp.where(active, jnp.float32(dt_step), 0.0)[:, None, :]
    return mask, mask / realizations


def exchange(blocks, axes):
    count, realizations = (len(blocks), lax.axis_size("real"))
    result = list(blocks)
    for position in range(1, count):
        steps = [order[position] for order in steps_of(count)]
        pairs = [
            (index * realizations + r, (index ^ steps[r % 2]) * realizations + r)
            for index in range(count)
            for r in range(realizations)
        ]
        result[position] = lax.ppermute(blocks[position], axes + ("real",), pairs)
    return result


def swap(value, step):
    pairs = [(index, index ^ step) for index in range(lax.axis_size("real"))]
    return lax.ppermute(value, "real", pairs)


def local(velocity, low_index, neighbours, owner_map, mode_counts, helmholtz):
    components, reals_dev, band_modes, rows_ht, columns = velocity.shape
    kx_count, ht_count = (lax.axis_size("kx"), lax.axis_size("ht"))
    own_kx, own_ht = (lax.axis_index("kx"), lax.axis_index("ht"))
    owners, pieces, real_count = (kx_count * ht_count, PIECES, lax.axis_size("real"))
    rows = rows_ht // (kx_count * pieces)
    groups = LANES // rows if rows else 0
    slots = columns // 2 // owners
    if (
        columns != LANES or reals_dev != 1 or rows_ht % LANES or rows % 8 or LANES % rows or kx_count % groups or kx_count & (kx_count - 1)
        or (band_modes * 2 * components) % 8 or slots % 8 or owners & (owners - 1) or low_index.shape[0] >= kx_count * band_modes
        or low_index.shape[0] >= columns or low_index.shape[0] % 2 or real_count < 2 or real_count & (real_count - 1)
    ):
        return local_plain(velocity, low_index, neighbours, owner_map, mode_counts, helmholtz)
    realizations, members = (real_count, low_index.shape[0])
    chunks, modes = (components * band_modes, band_modes * kx_count)
    shape = (components, modes, rows, columns)
    extra_rows = -(-band_modes // 8) * 8
    split = velocity.reshape(chunks, pieces, kx_count, rows, columns)
    owner_map, even_map = (
        owner_map.reshape(owners, slots)[(own_kx * ht_count + own_ht) ^ order].reshape(-1)
        for order in (
            jnp.stack([step_at(owners, position) for position in range(owners)]),
            jnp.array(steps_of(owners)[0], jnp.int32),
        )
    )
    first_blocks, rest = pack(split, neighbours, mode_counts, extra_rows)
    parts = [exchange(first_blocks, ("kx",))] + [
        (lax.all_to_all(block, "kx", split_axis=0, concat_axis=0, tiled=True),) for block in rest
    ]
    *matrices, after = split_matrix(helmholtz, pieces, kx_count, ht_count)
    small = 0.0
    for index, block in enumerate(parts[0]):
        lines = block[chunks * rows : chunks * rows + band_modes, : members + 1]
        here = (own_kx ^ step_at(kx_count, index)) == jnp.arange(kx_count)
        small = small + jnp.where(here[:, None, None], lines[None], 0.0)
    small = small.reshape(modes, members + 1).astype(jnp.int32)
    neighbours, mode_counts = (small[:, :-1], small[:, -1])
    tables, order = slot_tables(owner_map, even_map, columns)
    mask, low_mask = slot_masks(owner_map, mode_counts, realizations)
    received = []
    for part in parts:
        slotted, kept, sent = nonlinear(
            part, shape, low_index, neighbours, tables, mask, after
        )
        kept = kept + swap(sent, 1)
        step = 2
        while step < realizations:
            kept = kept + swap(kept, step)
            step *= 2
        after = swap(kept, 1)
        blocks = outgoing(
            slotted, kept, after, low_index, low_mask, groups, band_modes, owners
        )
        blocks = [block.reshape(slots, -1, LANES) for block in blocks]
        received.append(exchange(blocks, ("kx", "ht")))
    solved = None
    for piece, blocks in enumerate(received):
        solved = solve(blocks, matrices, piece, pieces, solved, groups, kx_count, ht_count)
    returned = [block.reshape(-1, LANES) for block in exchange(solved, ("kx", "ht"))]
    result = restore(returned, order, components, band_modes, rows_ht)
    return result.reshape(velocity.shape)


def solution(mesh):
    in_specs = (
        P(None, "real", "kx", "ht", None),
        P(),
        P("kx", None),
        P(),
        P("kx"),
        P(("kx", "ht"), None, None),
    )
    out_specs = P(None, "real", "kx", "ht", None)
    return jax.shard_map(local, mesh=mesh, in_specs=in_specs, out_specs=out_specs, check_vma=False)
```

```python
import functools

import jax
import jax.numpy as jnp
import numpy as np
from jax import lax
from jax.experimental import pallas as pl
from jax.experimental.pallas import tpu as pltpu
from jax.sharding import PartitionSpec as P

dt_step = 0.1


def spanwise_tables(mode_count, point_count):
    column_ids = jnp.arange(2 * mode_count)
    wavenumber = (column_ids // 2).astype(jnp.float32)
    imag_part = column_ids % 2
    positions = 2.0 * jnp.pi * jnp.arange(point_count).astype(jnp.float32) / point_count
    phases = wavenumber[:, None] * positions[None, :]
    forward = jnp.where(imag_part[:, None] == 0, jnp.cos(phases), -jnp.sin(phases)) / jnp.sqrt(
        jnp.float32(mode_count)
    )
    backward = forward.T * (2.0 * mode_count / point_count)
    return (forward, backward)


def nonlinear_rows(fields, low_index, neighbours, mode_counts, forward, backward):
    precision = lax.Precision.HIGH
    realizations, modes, columns = (fields.shape[1], fields.shape[2], fields.shape[4])
    low_select = (low_index[:, None] == jnp.arange(modes)[None, :]).astype(jnp.float32)
    high_mask = 1.0 - jnp.sum(low_select, axis=0)
    high_rows = high_mask[None, None, :, None, None]
    column_mask = ((jnp.arange(columns) // 2)[None, :] < mode_counts[:, None]).astype(jnp.float32)
    physical = jnp.dot(fields, forward, precision=precision)
    low_fields = jnp.take(physical, low_index, axis=2)
    high_low = jnp.zeros_like(physical)
    stresses = []
    for member in range(low_index.shape[0]):
        partner = jnp.take(physical, neighbours[:, member], axis=2)
        low_one = low_fields[:, :, member : member + 1]
        high_low = high_low + low_one * partner[1:2] + partner * low_one[1:2]
        stresses.append(jnp.sum(physical * (partner[1:2] * high_rows), axis=(1, 2)))
    stress = jnp.stack(stresses, axis=1) / realizations
    forcing = jnp.dot(high_low, backward, precision=precision) * high_rows
    low_forcing = jnp.dot(stress, backward, precision=precision)
    low_rows = jnp.einsum("jm,cjyk->cmyk", low_select, low_forcing, precision=lax.Precision.HIGHEST)
    forcing = (forcing + low_rows[:, None]) * column_mask[None, None, :, None, :]
    return fields + dt_step * forcing


def local_plain(velocity, low_index, neighbours, owner_map, mode_counts, helmholtz):
    components, reals_dev, band_modes, rows_ht, columns = velocity.shape
    kz_modes = columns // 2
    forward, backward = spanwise_tables(kz_modes, 4 * kz_modes)
    kx_count, ht_count = (lax.axis_size("kx"), lax.axis_size("ht"))
    real_count = lax.axis_size("real")
    modes, realizations = (band_modes * kx_count, reals_dev * real_count)
    slots_dev = kz_modes // (kx_count * ht_count)
    rows_dev = rows_ht // (kx_count * real_count)
    small = jnp.concatenate([neighbours, mode_counts[:, None]], axis=1)
    small = lax.all_gather(small, "kx", axis=0, tiled=True)
    neighbours, mode_counts = (small[:, :-1], small[:, -1])
    inverse_map = (
        jnp.zeros((kz_modes,), jnp.int32).at[owner_map].set(jnp.arange(kz_modes, dtype=jnp.int32))
    )
    split = velocity.reshape(
        components, reals_dev, band_modes, kx_count * real_count, rows_dev, columns
    )
    split = split.transpose(3, 0, 1, 2, 4, 5)
    split = lax.all_to_all(split, ("kx", "real"), split_axis=0, concat_axis=0, tiled=True)
    fields = split.reshape(
        kx_count, real_count, components, reals_dev, band_modes, rows_dev, columns
    )
    fields = fields.transpose(2, 1, 3, 0, 4, 5, 6).reshape(
        components, realizations, modes, rows_dev, columns
    )
    updated = nonlinear_rows(fields, low_index, neighbours, mode_counts, forward, backward)
    slotted = jnp.take(
        updated.reshape(components, realizations, modes, rows_dev, kz_modes, 2), owner_map, axis=4
    )
    slotted = slotted.reshape(
        components, real_count, reals_dev, modes, rows_dev, kx_count * ht_count, slots_dev, 2
    )
    outgoing = slotted.transpose(5, 1, 6, 2, 0, 3, 7, 4).reshape(
        kx_count * ht_count * real_count, slots_dev, reals_dev * components * modes * 2, rows_dev
    )
    incoming = lax.all_to_all(
        outgoing, ("kx", "ht", "real"), split_axis=0, concat_axis=0, tiled=True
    )
    incoming = incoming.reshape(
        kx_count, ht_count, real_count, slots_dev, reals_dev * components * modes * 2, rows_dev
    )
    incoming = incoming.transpose(3, 4, 1, 0, 2, 5).reshape(
        slots_dev, reals_dev * components * modes * 2, ht_count * rows_ht
    )
    solved = jnp.einsum("syx,snx->sny", helmholtz, incoming, precision=lax.Precision.HIGH)
    solved = solved.reshape(
        slots_dev, reals_dev, components, kx_count, band_modes, 2, ht_count, rows_ht
    )
    solved = solved.transpose(3, 6, 0, 5, 1, 2, 4, 7).reshape(
        kx_count * ht_count, slots_dev * 2, reals_dev * components * band_modes, rows_ht
    )
    returned = lax.all_to_all(solved, ("kx", "ht"), split_axis=0, concat_axis=0, tiled=True)
    restored = returned.reshape(
        kz_modes, 2, reals_dev, components, band_modes, rows_ht
    )
    restored = jnp.take(restored, inverse_map, axis=0)
    return restored.transpose(3, 2, 4, 5, 0, 1).reshape(velocity.shape)


LANES = 128
PIECES = 2
VMEM = pl.BlockSpec(memory_space=pltpu.VMEM)
SMEM = pl.BlockSpec(memory_space=pltpu.SMEM)


def params():
    return pltpu.CompilerParams(vmem_limit_bytes=48 * 1024 * 1024)


ORDERS = {4: (1, 3, 2), 8: (4, 1, 2, 6, 5, 3, 7)}


def steps_of(count):
    even = ORDERS.get(count, tuple(range(1, count)))
    odd = list(even)
    for first in range(0, count - 2, 2):
        odd[first], odd[first + 1] = (even[first + 1], even[first])
    return (0,) + tuple(even), (0,) + tuple(odd)


def step_at(count, position):
    even, odd = steps_of(count)
    return jnp.where((lax.axis_index("real") & 1) == 0, even[position], odd[position])


def cost(size):
    return pl.CostEstimate(flops=0, bytes_accessed=size, transcendentals=0)


def two_parts(value):
    top = value.astype(jnp.bfloat16)
    rest = (value - top.astype(jnp.float32)).astype(jnp.bfloat16)
    return top, rest


def dot(left, right, dims=((1,), (0,))):
    return lax.dot_general(left, right, (dims, ((), ())), preferred_element_type=jnp.float32)


def pack_kernel(near_ref, count_ref, velocity_ref, *out_refs):
    chunks, pieces, kx_count, rows, columns = velocity_ref.shape
    own = lax.axis_index("kx")
    for index in range(kx_count):
        partner = own ^ step_at(kx_count, index)
        for chunk in range(chunks):
            place = slice(chunk * rows, (chunk + 1) * rows)
            out_refs[index][place] = velocity_ref[chunk, 0, partner]
            for piece in range(1, pieces):
                out_refs[kx_count + piece - 1][index, place] = velocity_ref[chunk, piece, index]
    shape = (out_refs[0].shape[0] - chunks * rows, columns)
    row = lax.broadcasted_iota(jnp.int32, shape, 0)
    lane = lax.broadcasted_iota(jnp.int32, shape, 1)
    extra = jnp.zeros(shape, jnp.int32)
    modes, members = near_ref.shape
    for mode in range(modes):
        line = jnp.where(lane == members, count_ref[mode], 0)
        for member in range(members):
            line = jnp.where(lane == member, near_ref[mode, member], line)
        extra = jnp.where(row == mode, line, extra)
    extra = extra.astype(jnp.float32)
    for out_ref in out_refs[:kx_count]:
        out_ref[chunks * rows :] = extra


def pack(velocity, neighbours, mode_counts, extra_rows):
    chunks, pieces, kx_count, rows, columns = velocity.shape
    size = chunks * rows
    shapes = [(size + extra_rows, columns)] * kx_count
    shapes += [(kx_count, size, columns)] * (pieces - 1)
    out = pl.pallas_call(
        pack_kernel,
        out_shape=tuple(jax.ShapeDtypeStruct(shape, jnp.float32) for shape in shapes),
        in_specs=[SMEM, SMEM, VMEM],
        out_specs=(VMEM,) * len(shapes),
        cost_estimate=cost(8 * velocity.size),
        name="pack",
    )(neighbours, mode_counts, velocity)
    return out[:kx_count], out[kx_count:]


def tables_kernel(owner_ref, top_ref, rest_ref, first_ref, back_ref, order_ref, slot_ref):
    columns = slot_ref.shape[1]
    modes = columns // 2
    lane = lax.broadcasted_iota(jnp.int32, (8, columns), 1)
    mode = jnp.zeros((8, columns), jnp.int32)
    for slot in range(modes):
        mode = jnp.where(lane % modes == slot, owner_ref[slot], mode)
    slot_ref[...] = mode
    wanted = 2 * mode + lane // modes
    row = lax.broadcasted_iota(jnp.int32, (columns, columns), 0)
    chosen = (row == wanted[:1]).astype(jnp.float32)
    select = chosen.astype(jnp.bfloat16)
    points = top_ref.shape[1]
    for half in range(2):
        rows = slice(half * columns, (half + 1) * columns)
        first_ref[rows, :points] = top_ref[...]
        first_ref[rows, points:] = select
        order_ref[rows] = chosen.T.astype(jnp.bfloat16)
    for index, table_ref in enumerate((top_ref, rest_ref)):
        back = dot(table_ref[...], select, ((0,), (0,))) * (2.0 * modes / points)
        back_ref[:, index * columns : (index + 1) * columns] = back.astype(jnp.bfloat16)


def spanwise_constants(columns, points):
    mode = np.arange(columns) // 2
    phase = 2.0 * np.pi * ((mode[:, None] * np.arange(points)[None, :]) % points) / points
    forward = np.where(np.arange(columns)[:, None] % 2 == 0, np.cos(phase), -np.sin(phase))
    forward = (forward / np.sqrt(columns // 2)).astype(np.float32)
    top = forward.astype(jnp.bfloat16)
    rest = (forward - top.astype(np.float32)).astype(jnp.bfloat16)
    return jnp.asarray(top), jnp.asarray(rest)


def slot_tables(owner_map, columns):
    points = 2 * columns
    top, rest = spanwise_constants(columns, points)
    first, back, order, slot_modes = pl.pallas_call(
        tables_kernel,
        out_shape=(
            jax.ShapeDtypeStruct((2 * columns, points + columns), jnp.bfloat16),
            jax.ShapeDtypeStruct((points, 2 * columns), jnp.bfloat16),
            jax.ShapeDtypeStruct((2 * columns, columns), jnp.bfloat16),
            jax.ShapeDtypeStruct((8, columns), jnp.int32),
        ),
        in_specs=[SMEM, VMEM, VMEM],
        out_specs=(VMEM,) * 4,
        compiler_params=params(),
        cost_estimate=cost(16 * points * columns),
        name="tables",
    )(owner_map, top, rest)
    return (first, rest, back), order, slot_modes


def nonlinear_kernel(low_ref, near_ref, count_ref, *refs):
    block_refs, refs = (refs[:-12], refs[-12:])
    first_ref, second_ref, back_ref, slot_ref, _, slotted_ref, kept_ref, sent_ref = refs[:8]
    physical, products, sums, high_ref = refs[8:]
    components, modes, rows, columns = slotted_ref.shape
    if len(block_refs) > 1:
        bands = len(block_refs)
        places = [lax.axis_index("kx") ^ step_at(bands, index) for index in range(bands)]
    else:
        bands = block_refs[0].shape[0]
        places = list(range(bands))
        block_refs = [block_refs[0].at[index] for index in range(bands)]
    points, band_modes = (physical.shape[3], modes // bands)
    members, highs = (sums.shape[1], products.shape[1])
    odd = (lax.axis_index("real") & 1) == 1
    found = jnp.int32(0)
    for mode in range(modes):
        is_low = jnp.int32(0)
        for member in range(members):
            is_low = is_low | (low_ref[member] == mode).astype(jnp.int32)
        high_ref[found] = mode
        found = found + 1 - is_low

    def transform(component, carry):
        size = band_modes * rows
        for index, block_ref in enumerate(block_refs):
            top, rest = two_parts(block_ref[pl.ds(pl.multiple_of(component * size, 8), size)])
            both = dot(jnp.concatenate([top, rest], axis=1), first_ref[...])
            fields = both[:, :points] + dot(top, second_ref[...])
            place = pl.ds(places[index] * band_modes, band_modes)
            physical[component, place] = fields.reshape(band_modes, rows, points)
            slotted_ref[component, place] = both[:, points:].reshape(band_modes, rows, columns)
        return carry

    lax.fori_loop(0, components, transform, 0)

    def pairs(step, carry):
        halves = points // LANES
        place = (
            pl.ds(pl.multiple_of((step // halves) * 8, 8), 8),
            pl.ds(pl.multiple_of((step % halves) * LANES, LANES), LANES),
        )

        def one_high(index, totals):
            mode = high_ref[index]
            own = [physical[(c, mode) + place] for c in range(components)]
            result = [jnp.zeros((8, LANES), jnp.float32) for _ in range(components)]
            totals = list(totals)
            for member in range(members):
                low = low_ref[member]
                near = near_ref[mode, member]
                partner = [physical[(c, near) + place] for c in range(components)]
                low_one = [physical[(c, low) + place] for c in range(components)]
                for c in range(components):
                    if c == 1:
                        result[c] = result[c] + low_one[1] * partner[1]
                    else:
                        result[c] = result[c] + (low_one[c] * partner[1] + partner[c] * low_one[1])
                    slot = member * components + c
                    totals[slot] = totals[slot] + own[c] * partner[1]
            for c in range(components):
                products[(c, index) + place] = result[c] * 2.0 if c == 1 else result[c]
            return tuple(totals)

        empty = tuple(jnp.zeros((8, LANES), jnp.float32) for _ in range(members * components))
        totals = lax.fori_loop(0, highs, one_high, empty)
        for member in range(members):
            for c in range(components):
                sums[(c, member) + place] = totals[member * components + c]
        return carry

    lax.fori_loop(0, (rows // 8) * (points // LANES), pairs, 0)

    def inverse(fields):
        top, rest = two_parts(fields)
        both = dot(top, back_ref[...])
        return both[:, :columns] + both[:, columns:] + dot(rest, back_ref[:, :columns])

    def finish(component, carry):
        forcing = inverse(products[component].reshape(highs * rows, points))
        forcing = forcing.reshape(highs, rows, columns)
        for index in range(highs):
            mode = high_ref[index]
            active = slot_ref[:1] < count_ref[mode]
            slotted_ref[component, mode] += jnp.where(active, forcing[index] * dt_step, 0.0)
        stress = inverse(sums[component].reshape(members * rows, points))
        stress = stress.reshape(2, members // 2, rows, columns)
        kept_ref[component] = jnp.where(odd, stress[1], stress[0])
        sent_ref[component] = jnp.where(odd, stress[0], stress[1])
        return carry

    lax.fori_loop(0, components, finish, 0)


def nonlinear(blocks, shape, low_index, neighbours, mode_counts, tables, slot_modes, after):
    components, modes, rows, columns = shape
    members, points = (low_index.shape[0], 2 * columns)
    highs = modes - members
    return pl.pallas_call(
        nonlinear_kernel,
        out_shape=(
            jax.ShapeDtypeStruct((components, modes, rows, columns), jnp.float32),
            jax.ShapeDtypeStruct((components, members // 2, rows, columns), jnp.float32),
            jax.ShapeDtypeStruct((components, members // 2, rows, columns), jnp.float32),
        ),
        in_specs=[SMEM] * 3 + [VMEM] * (len(blocks) + 4) + [pl.BlockSpec(memory_space=pl.ANY)],
        out_specs=(VMEM, VMEM, VMEM),
        scratch_shapes=[
            pltpu.VMEM((components, modes, rows, points), jnp.float32),
            pltpu.VMEM((components, highs, rows, points), jnp.float32),
            pltpu.VMEM((components, members, rows, points), jnp.float32),
            pltpu.SMEM((modes + 1,), jnp.int32),
        ],
        compiler_params=params(),
        cost_estimate=cost(8 * components * modes * rows * points * members),
        name="nonlinear",
    )(low_index, neighbours, mode_counts, *blocks, *tables, slot_modes, after)


def outgoing_kernel(
    low_ref, count_ref, slotted_ref, kept_ref, other_ref, slot_ref, *refs,
    groups, band_modes, owners, scale
):
    out_refs, (full, turned) = (refs[:-2], refs[-2:])
    components, modes, rows, columns = slotted_ref.shape
    half, slots = (kept_ref.shape[1], columns // 2 // owners)
    per_slot = out_refs[0].shape[0] * len(out_refs) // (columns // 2)
    own = lax.axis_index("real") & 1
    full[...] = slotted_ref[...]
    for member in range(half):
        for part_ref, start in ((kept_ref, own * half), (other_ref, (1 - own) * half)):
            mode = low_ref[start + member]
            active = slot_ref[:1] < count_ref[mode]
            for c in range(components):
                full[c, mode] += jnp.where(active, part_ref[c, member] * scale, 0.0)
    inner = modes // groups
    if len(out_refs) > 1:
        me = lax.axis_index("kx") * lax.axis_size("ht") + lax.axis_index("ht")
        targets = [me ^ step_at(owners, position) for position in range(owners)]
    for c in range(components):
        for part in range(inner):
            tile = jnp.concatenate([full[c, part + inner * g] for g in range(groups)], axis=0)
            band_low, band_mode = (part // band_modes, part % band_modes)
            if len(out_refs) > 1:
                turned[...] = tile.T
            else:
                value = tile.T
            for p in range(2):
                row = ((band_low * 2 + p) * components + c) * band_modes + band_mode
                if len(out_refs) == 1:
                    out_refs[0][pl.ds(row, columns // 2, stride=per_slot), :] = value[
                        p * (columns // 2) : (p + 1) * (columns // 2)
                    ]
                    continue
                for out_ref, target in zip(out_refs, targets):
                    start = pl.multiple_of((p * owners + target) * slots, slots)
                    out_ref[pl.ds(row, slots, stride=per_slot), :] = turned[pl.ds(start, slots)]


def outgoing(
    slotted, kept, other, low_index, mode_counts, slot_modes, groups, band_modes, owners,
    realizations, separate,
):
    components, modes, rows, columns = slotted.shape
    total, lanes = ((columns // 2) * (modes // groups) * 2 * components, groups * rows)
    count = owners if separate else 1
    return pl.pallas_call(
        functools.partial(
            outgoing_kernel, groups=groups, band_modes=band_modes, owners=owners,
            scale=dt_step / realizations,
        ),
        out_shape=(jax.ShapeDtypeStruct((total // count, lanes), jnp.float32),) * count,
        in_specs=[SMEM, SMEM] + [VMEM] * 4,
        out_specs=(VMEM,) * count,
        scratch_shapes=[
            pltpu.VMEM(slotted.shape, jnp.float32), pltpu.VMEM((columns, lanes), jnp.float32)
        ],
        compiler_params=params(),
        cost_estimate=cost(8 * slotted.size),
        name="outgoing",
    )(low_index, mode_counts, slotted, kept, other, slot_modes)


def regroup(blocks, rows):
    count = len(blocks)
    lane = lax.broadcasted_iota(jnp.int32, blocks[0].shape, 1) // rows
    step = 1
    while step < count:
        take = (lane & step) == 0
        for i in range(count):
            if i & step == 0:
                here, there = (blocks[i], blocks[i + step])
                blocks[i] = jnp.where(take, here, pltpu.roll(there, step * rows, 1))
                blocks[i + step] = jnp.where(
                    take, pltpu.roll(here, LANES - step * rows, 1), there
                )
        step *= 2
    return blocks


def solve_kernel(*refs, groups, kx_count, ht_count, pieces):
    owners = kx_count * ht_count
    first_ref, refs = (refs[0], refs[1:])
    count = owners * (pieces - 1)
    block_refs, matrix_ref, refs = (refs[:count], refs[count], refs[count + 1 :])
    out_refs, (matrices, arrived, ordered, full) = (refs[:owners], refs[owners:])
    slots, heights = (matrix_ref.shape[0], matrix_ref.shape[1])
    copies = [
        pltpu.make_async_copy(matrix_ref.at[s], matrices.at[s], arrived.at[s])
        for s in range(slots)
    ]
    for copy in copies:
        copy.start()
    own_kx, own_ht = (lax.axis_index("kx"), lax.axis_index("ht"))
    partners = []
    for position in range(owners):
        step = step_at(owners, position)
        partners.append((own_kx ^ (step // ht_count), own_ht ^ (step % ht_count)))
    for index, block_ref in enumerate(block_refs):
        kx, ht = partners[index % owners]
        ordered[index // owners, kx * ht_count + ht] = block_ref[...]
    rows, (lane_tiles, per_band) = (LANES // groups, out_refs[0].shape[1:3])
    for s in range(slots):
        tiles = []
        for h in range(ht_count):
            for piece in range(pieces):
                source = first_ref if piece == 0 else ordered.at[piece - 1]
                for first in range(0, kx_count, groups):
                    blocks = [source[(first + g) * ht_count + h, s] for g in range(groups)]
                    tiles.append(jnp.concatenate(regroup(blocks, rows), axis=0))
        top, rest = two_parts(jnp.concatenate(tiles, axis=1))
        count = top.shape[0]
        copies[s].wait()
        matrix_top, matrix_rest = two_parts(matrices[s])
        last = ((1,), (1,))
        both = dot(matrix_top, jnp.concatenate([top, rest], axis=0), last)
        solved = both[:, :count] + both[:, count:] + dot(matrix_rest, top, last)
        for tile in range(heights // LANES):
            full[s % 2, tile] = solved[tile * LANES : (tile + 1) * LANES].T
        for out_ref, (kx, ht) in zip(out_refs, partners):
            band = pl.ds(pl.multiple_of(kx * per_band, 8), per_band)
            for tile in range(lane_tiles):
                out_ref[s, tile] = full[s % 2, ht * lane_tiles + tile, band]


def solve(first, blocks, helmholtz, pieces, groups, kx_count, ht_count):
    owners, slots, per_slot, lanes = first.shape
    heights, count = (helmholtz.shape[1], per_slot * groups)
    shape = (slots, heights // ht_count // LANES, count // kx_count, LANES)
    return pl.pallas_call(
        functools.partial(
            solve_kernel, groups=groups, kx_count=kx_count, ht_count=ht_count, pieces=pieces
        ),
        out_shape=(jax.ShapeDtypeStruct(shape, jnp.float32),) * owners,
        in_specs=[VMEM] * (1 + len(blocks)) + [pl.BlockSpec(memory_space=pl.ANY)],
        out_specs=(VMEM,) * owners,
        scratch_shapes=[
            pltpu.VMEM(helmholtz.shape, jnp.float32),
            pltpu.SemaphoreType.DMA((slots,)),
            pltpu.VMEM((max(pieces - 1, 1),) + first.shape, jnp.float32),
            pltpu.VMEM((2, heights // LANES, count, LANES), jnp.float32),
        ],
        compiler_params=params(),
        cost_estimate=cost(4 * helmholtz.size),
        name="solve",
    )(first, *blocks, helmholtz)


def restore_kernel(*refs, owners, ht_count):
    block_refs, (order_ref, out_ref, ordered) = (refs[:-3], refs[-3:])
    components, band_modes, rows, columns = out_ref.shape
    slots = columns // 2 // owners
    per_slot = block_refs[0].shape[0] // slots
    me = lax.axis_index("kx") * ht_count + lax.axis_index("ht")
    for position, block_ref in enumerate(block_refs):
        ordered[me ^ step_at(owners, position)] = block_ref[...]
    for c in range(components):
        for mode in range(band_modes):
            for tile in range(rows // LANES):
                parts = []
                for p in range(2):
                    row = ((tile * 2 + p) * components + c) * band_modes + mode
                    for owner in range(owners):
                        parts.append(ordered[owner, pl.ds(row, slots, stride=per_slot), :])
                top, rest = two_parts(jnp.concatenate(parts, axis=0))
                both = jnp.concatenate([top, rest], axis=0)
                out_ref[c, mode, pl.ds(tile * LANES, LANES)] = dot(
                    both, order_ref[...], ((0,), (0,))
                )


def restore(blocks, order, components, band_modes, rows, ht_count):
    columns = order.shape[1]
    return pl.pallas_call(
        functools.partial(restore_kernel, owners=len(blocks), ht_count=ht_count),
        out_shape=jax.ShapeDtypeStruct((components, band_modes, rows, columns), jnp.float32),
        in_specs=[VMEM] * (len(blocks) + 1),
        out_specs=VMEM,
        scratch_shapes=[pltpu.VMEM((len(blocks),) + blocks[0].shape, jnp.float32)],
        compiler_params=params(),
        cost_estimate=cost(8 * components * band_modes * rows * columns),
        name="restore",
    )(*blocks, order)


def exchange(blocks, axes):
    count, realizations = (len(blocks), lax.axis_size("real"))
    result = list(blocks)
    for position in range(1, count):
        steps = [order[position] for order in steps_of(count)]
        pairs = [
            (index * realizations + r, (index ^ steps[r % 2]) * realizations + r)
            for index in range(count)
            for r in range(realizations)
        ]
        result[position] = lax.ppermute(blocks[position], axes + ("real",), pairs)
    return result


def swap(value, step):
    pairs = [(index, index ^ step) for index in range(lax.axis_size("real"))]
    return lax.ppermute(value, "real", pairs)


def local(velocity, low_index, neighbours, owner_map, mode_counts, helmholtz):
    components, reals_dev, band_modes, rows_ht, columns = velocity.shape
    kx_count, ht_count = (lax.axis_size("kx"), lax.axis_size("ht"))
    own_kx, own_ht = (lax.axis_index("kx"), lax.axis_index("ht"))
    owners, pieces, real_count = (kx_count * ht_count, PIECES, lax.axis_size("real"))
    rows = rows_ht // (kx_count * pieces)
    groups = LANES // rows if rows else 0
    slots = columns // 2 // owners
    if (
        columns != LANES or reals_dev != 1 or rows_ht % LANES or rows % 8 or LANES % rows or kx_count % groups or kx_count & (kx_count - 1)
        or (band_modes * 2 * components) % 8 or slots % 8 or owners & (owners - 1) or low_index.shape[0] >= kx_count * band_modes
        or low_index.shape[0] >= columns or low_index.shape[0] % 2 or real_count < 2 or real_count & (real_count - 1)
    ):
        return local_plain(velocity, low_index, neighbours, owner_map, mode_counts, helmholtz)
    realizations, members = (real_count, low_index.shape[0])
    chunks, modes = (components * band_modes, band_modes * kx_count)
    shape = (components, modes, rows, columns)
    extra_rows = -(-band_modes // 8) * 8
    split = velocity.reshape(chunks, pieces, kx_count, rows, columns)
    first_blocks, rest = pack(split, neighbours, mode_counts, extra_rows)
    parts = [exchange(first_blocks, ("kx",))] + [
        (lax.all_to_all(block, "kx", split_axis=0, concat_axis=0, tiled=True),) for block in rest
    ]
    tables, order, slot_modes = slot_tables(owner_map, columns)
    small = 0.0
    for index, block in enumerate(parts[0]):
        lines = block[chunks * rows : chunks * rows + band_modes, : members + 1]
        here = (own_kx ^ step_at(kx_count, index)) == jnp.arange(kx_count)
        small = small + jnp.where(here[:, None, None], lines[None], 0.0)
    small = small.reshape(modes, members + 1).astype(jnp.int32)
    neighbours, mode_counts = (small[:, :-1], small[:, -1])
    after = slot_modes
    received = []
    for piece, part in enumerate(parts):
        slotted, kept, sent = nonlinear(
            part, shape, low_index, neighbours, mode_counts, tables, slot_modes, after
        )
        kept = after = kept + swap(sent, 1)
        step = 2
        while step < realizations:
            kept = kept + swap(kept, step)
            step *= 2
        blocks = outgoing(
            slotted, kept, swap(kept, 1), low_index, mode_counts, slot_modes, groups, band_modes,
            owners, realizations, piece > 0,
        )
        if piece:
            received += exchange([block.reshape(slots, -1, LANES) for block in blocks], ("kx", "ht"))
        else:
            block = blocks[0].reshape(owners, slots, -1, LANES)
            first = lax.all_to_all(block, ("kx", "ht"), split_axis=0, concat_axis=0, tiled=True)
    solved = solve(first, received, helmholtz, pieces, groups, kx_count, ht_count)
    returned = [block.reshape(-1, LANES) for block in exchange(solved, ("kx", "ht"))]
    result = restore(returned, order, components, band_modes, rows_ht, ht_count)
    return result.reshape(velocity.shape)


def solution(mesh):
    in_specs = (
        P(None, "real", "kx", "ht", None),
        P(),
        P("kx", None),
        P(),
        P("kx"),
        P(("kx", "ht"), None, None),
    )
    out_specs = P(None, "real", "kx", "ht", None)
    return jax.shard_map(local, mesh=mesh, in_specs=in_specs, out_specs=out_specs, check_vma=False)
```

```python
import functools

import jax
import jax.numpy as jnp
import numpy as np
from jax import lax
from jax.experimental import pallas as pl
from jax.experimental.pallas import tpu as pltpu
from jax.sharding import PartitionSpec as P

dt_step = 0.1


def spanwise_tables(mode_count, point_count):
    column_ids = jnp.arange(2 * mode_count)
    wavenumber = (column_ids // 2).astype(jnp.float32)
    imag_part = column_ids % 2
    positions = 2.0 * jnp.pi * jnp.arange(point_count).astype(jnp.float32) / point_count
    phases = wavenumber[:, None] * positions[None, :]
    forward = jnp.where(imag_part[:, None] == 0, jnp.cos(phases), -jnp.sin(phases)) / jnp.sqrt(
        jnp.float32(mode_count)
    )
    backward = forward.T * (2.0 * mode_count / point_count)
    return (forward, backward)


def nonlinear_rows(fields, low_index, neighbours, mode_counts, forward, backward):
    precision = lax.Precision.HIGH
    realizations, modes, columns = (fields.shape[1], fields.shape[2], fields.shape[4])
    low_select = (low_index[:, None] == jnp.arange(modes)[None, :]).astype(jnp.float32)
    high_mask = 1.0 - jnp.sum(low_select, axis=0)
    high_rows = high_mask[None, None, :, None, None]
    column_mask = ((jnp.arange(columns) // 2)[None, :] < mode_counts[:, None]).astype(jnp.float32)
    physical = jnp.dot(fields, forward, precision=precision)
    low_fields = jnp.take(physical, low_index, axis=2)
    high_low = jnp.zeros_like(physical)
    stresses = []
    for member in range(low_index.shape[0]):
        partner = jnp.take(physical, neighbours[:, member], axis=2)
        low_one = low_fields[:, :, member : member + 1]
        high_low = high_low + low_one * partner[1:2] + partner * low_one[1:2]
        stresses.append(jnp.sum(physical * (partner[1:2] * high_rows), axis=(1, 2)))
    stress = jnp.stack(stresses, axis=1) / realizations
    forcing = jnp.dot(high_low, backward, precision=precision) * high_rows
    low_forcing = jnp.dot(stress, backward, precision=precision)
    low_rows = jnp.einsum("jm,cjyk->cmyk", low_select, low_forcing, precision=lax.Precision.HIGHEST)
    forcing = (forcing + low_rows[:, None]) * column_mask[None, None, :, None, :]
    return fields + dt_step * forcing


def local_plain(velocity, low_index, neighbours, owner_map, mode_counts, helmholtz):
    components, reals_dev, band_modes, rows_ht, columns = velocity.shape
    kz_modes = columns // 2
    forward, backward = spanwise_tables(kz_modes, 4 * kz_modes)
    kx_count, ht_count = (lax.axis_size("kx"), lax.axis_size("ht"))
    real_count = lax.axis_size("real")
    modes, realizations = (band_modes * kx_count, reals_dev * real_count)
    slots_dev = kz_modes // (kx_count * ht_count)
    rows_dev = rows_ht // (kx_count * real_count)
    small = jnp.concatenate([neighbours, mode_counts[:, None]], axis=1)
    small = lax.all_gather(small, "kx", axis=0, tiled=True)
    neighbours, mode_counts = (small[:, :-1], small[:, -1])
    inverse_map = (
        jnp.zeros((kz_modes,), jnp.int32).at[owner_map].set(jnp.arange(kz_modes, dtype=jnp.int32))
    )
    split = velocity.reshape(
        components, reals_dev, band_modes, kx_count * real_count, rows_dev, columns
    )
    split = split.transpose(3, 0, 1, 2, 4, 5)
    split = lax.all_to_all(split, ("kx", "real"), split_axis=0, concat_axis=0, tiled=True)
    fields = split.reshape(
        kx_count, real_count, components, reals_dev, band_modes, rows_dev, columns
    )
    fields = fields.transpose(2, 1, 3, 0, 4, 5, 6).reshape(
        components, realizations, modes, rows_dev, columns
    )
    updated = nonlinear_rows(fields, low_index, neighbours, mode_counts, forward, backward)
    slotted = jnp.take(
        updated.reshape(components, realizations, modes, rows_dev, kz_modes, 2), owner_map, axis=4
    )
    slotted = slotted.reshape(
        components, real_count, reals_dev, modes, rows_dev, kx_count * ht_count, slots_dev, 2
    )
    outgoing = slotted.transpose(5, 1, 6, 2, 0, 3, 7, 4).reshape(
        kx_count * ht_count * real_count, slots_dev, reals_dev * components * modes * 2, rows_dev
    )
    incoming = lax.all_to_all(
        outgoing, ("kx", "ht", "real"), split_axis=0, concat_axis=0, tiled=True
    )
    incoming = incoming.reshape(
        kx_count, ht_count, real_count, slots_dev, reals_dev * components * modes * 2, rows_dev
    )
    incoming = incoming.transpose(3, 4, 1, 0, 2, 5).reshape(
        slots_dev, reals_dev * components * modes * 2, ht_count * rows_ht
    )
    solved = jnp.einsum("syx,snx->sny", helmholtz, incoming, precision=lax.Precision.HIGH)
    solved = solved.reshape(
        slots_dev, reals_dev, components, kx_count, band_modes, 2, ht_count, rows_ht
    )
    solved = solved.transpose(3, 6, 0, 5, 1, 2, 4, 7).reshape(
        kx_count * ht_count, slots_dev * 2, reals_dev * components * band_modes, rows_ht
    )
    returned = lax.all_to_all(solved, ("kx", "ht"), split_axis=0, concat_axis=0, tiled=True)
    restored = returned.reshape(
        kz_modes, 2, reals_dev, components, band_modes, rows_ht
    )
    restored = jnp.take(restored, inverse_map, axis=0)
    return restored.transpose(3, 2, 4, 5, 0, 1).reshape(velocity.shape)


LANES = 128
PIECES = 2
VMEM = pl.BlockSpec(memory_space=pltpu.VMEM)
SMEM = pl.BlockSpec(memory_space=pltpu.SMEM)


def params():
    return pltpu.CompilerParams(vmem_limit_bytes=48 * 1024 * 1024)


ORDERS = {4: (1, 3, 2), 8: (4, 1, 2, 6, 5, 3, 7)}


def steps_of(count):
    even = ORDERS.get(count, tuple(range(1, count)))
    odd = list(even)
    for first in range(0, count - 2, 2):
        odd[first], odd[first + 1] = (even[first + 1], even[first])
    return (0,) + tuple(even), (0,) + tuple(odd)


def step_at(count, position):
    even, odd = steps_of(count)
    return jnp.where((lax.axis_index("real") & 1) == 0, even[position], odd[position])


def cost(size):
    return pl.CostEstimate(flops=0, bytes_accessed=size, transcendentals=0)


def two_parts(value):
    top = value.astype(jnp.bfloat16)
    rest = (value - top.astype(jnp.float32)).astype(jnp.bfloat16)
    return top, rest


def dot(left, right, dims=((1,), (0,))):
    return lax.dot_general(left, right, (dims, ((), ())), preferred_element_type=jnp.float32)


def pack_kernel(near_ref, count_ref, velocity_ref, first_ref, *out_refs):
    chunks, pieces, kx_count, rows, columns = velocity_ref.shape
    shape = (first_ref.shape[1] - chunks * rows, columns)
    row = lax.broadcasted_iota(jnp.int32, shape, 0)
    lane = lax.broadcasted_iota(jnp.int32, shape, 1)
    extra = jnp.zeros(shape, jnp.int32)
    modes, members = near_ref.shape
    for mode in range(modes):
        line = jnp.where(lane == members, count_ref[mode], 0)
        for member in range(members):
            line = jnp.where(lane == member, near_ref[mode, member], line)
        extra = jnp.where(row == mode, line, extra)
    extra = extra.astype(jnp.float32)
    own = lax.axis_index("kx")
    for index in range(kx_count):
        first_ref[index, chunks * rows :] = extra
        partner = own ^ step_at(kx_count, index)
        for chunk in range(chunks):
            place = slice(chunk * rows, (chunk + 1) * rows)
            first_ref[index, place] = velocity_ref[chunk, 0, index]
            for piece in range(1, pieces):
                out_ref = out_refs[(piece - 1) * kx_count + index]
                out_ref[place] = velocity_ref[chunk, piece, partner]


def pack(velocity, neighbours, mode_counts, extra_rows):
    chunks, pieces, kx_count, rows, columns = velocity.shape
    size = chunks * rows
    shapes = [(kx_count, size + extra_rows, columns)]
    shapes += [(size, columns)] * (kx_count * (pieces - 1))
    first, *out = pl.pallas_call(
        pack_kernel,
        out_shape=tuple(jax.ShapeDtypeStruct(shape, jnp.float32) for shape in shapes),
        in_specs=[SMEM, SMEM, VMEM],
        out_specs=(VMEM,) * len(shapes),
        cost_estimate=cost(8 * velocity.size),
        name="pack",
    )(neighbours, mode_counts, velocity)
    return first, [out[i : i + kx_count] for i in range(0, len(out), kx_count)]


def tables_kernel(owner_ref, top_ref, rest_ref, first_ref, back_ref, order_ref, slot_ref):
    columns = slot_ref.shape[1]
    modes = columns // 2
    lane = lax.broadcasted_iota(jnp.int32, (8, columns), 1)
    mode = jnp.zeros((8, columns), jnp.int32)
    for slot in range(modes):
        mode = jnp.where(lane % modes == slot, owner_ref[slot], mode)
    slot_ref[...] = mode
    wanted = 2 * mode + lane // modes
    row = lax.broadcasted_iota(jnp.int32, (columns, columns), 0)
    chosen = (row == wanted[:1]).astype(jnp.float32)
    select = chosen.astype(jnp.bfloat16)
    points = top_ref.shape[1]
    for half in range(2):
        rows = slice(half * columns, (half + 1) * columns)
        first_ref[rows, :points] = top_ref[...]
        first_ref[rows, points:] = select
        order_ref[rows] = chosen.T.astype(jnp.bfloat16)
    for index, table_ref in enumerate((top_ref, rest_ref)):
        back = dot(table_ref[...], select, ((0,), (0,))) * (2.0 * modes / points)
        back_ref[:, index * columns : (index + 1) * columns] = back.astype(jnp.bfloat16)


def spanwise_constants(columns, points):
    mode = np.arange(columns) // 2
    phase = 2.0 * np.pi * ((mode[:, None] * np.arange(points)[None, :]) % points) / points
    forward = np.where(np.arange(columns)[:, None] % 2 == 0, np.cos(phase), -np.sin(phase))
    forward = (forward / np.sqrt(columns // 2)).astype(np.float32)
    top = forward.astype(jnp.bfloat16)
    rest = (forward - top.astype(np.float32)).astype(jnp.bfloat16)
    return jnp.asarray(top), jnp.asarray(rest)


def slot_tables(owner_map, columns):
    points = 2 * columns
    top, rest = spanwise_constants(columns, points)
    first, back, order, slot_modes = pl.pallas_call(
        tables_kernel,
        out_shape=(
            jax.ShapeDtypeStruct((2 * columns, points + columns), jnp.bfloat16),
            jax.ShapeDtypeStruct((points, 2 * columns), jnp.bfloat16),
            jax.ShapeDtypeStruct((2 * columns, columns), jnp.bfloat16),
            jax.ShapeDtypeStruct((8, columns), jnp.int32),
        ),
        in_specs=[SMEM, VMEM, VMEM],
        out_specs=(VMEM,) * 4,
        compiler_params=params(),
        cost_estimate=cost(16 * points * columns),
        name="tables",
    )(owner_map, top, rest)
    return (first, rest, back), order, slot_modes


def nonlinear_kernel(low_ref, near_ref, count_ref, *refs):
    block_refs, refs = (refs[:-12], refs[-12:])
    first_ref, second_ref, back_ref, slot_ref, _, slotted_ref, kept_ref, sent_ref = refs[:8]
    physical, products, sums, high_ref = refs[8:]
    components, modes, rows, columns = slotted_ref.shape
    if len(block_refs) > 1:
        bands = len(block_refs)
        places = [lax.axis_index("kx") ^ step_at(bands, index) for index in range(bands)]
    else:
        bands = block_refs[0].shape[0]
        places = list(range(bands))
        block_refs = [block_refs[0].at[index] for index in range(bands)]
    points, band_modes = (physical.shape[3], modes // bands)
    members, highs = (sums.shape[1], products.shape[1])
    odd = (lax.axis_index("real") & 1) == 1
    found = jnp.int32(0)
    for mode in range(modes):
        is_low = jnp.int32(0)
        for member in range(members):
            is_low = is_low | (low_ref[member] == mode).astype(jnp.int32)
        high_ref[found] = mode
        found = found + 1 - is_low

    def transform(component, carry):
        size = band_modes * rows
        for index, block_ref in enumerate(block_refs):
            top, rest = two_parts(block_ref[pl.ds(pl.multiple_of(component * size, 8), size)])
            both = dot(jnp.concatenate([top, rest], axis=1), first_ref[...])
            fields = both[:, :points] + dot(top, second_ref[...])
            place = pl.ds(places[index] * band_modes, band_modes)
            physical[component, place] = fields.reshape(band_modes, rows, points)
            slotted_ref[component, place] = both[:, points:].reshape(band_modes, rows, columns)
        return carry

    lax.fori_loop(0, components, transform, 0)

    def pairs(step, carry):
        halves = points // LANES
        place = (
            pl.ds(pl.multiple_of((step // halves) * 8, 8), 8),
            pl.ds(pl.multiple_of((step % halves) * LANES, LANES), LANES),
        )

        def one_high(index, totals):
            mode = high_ref[index]
            own = [physical[(c, mode) + place] for c in range(components)]
            result = [jnp.zeros((8, LANES), jnp.float32) for _ in range(components)]
            totals = list(totals)
            for member in range(members):
                low = low_ref[member]
                near = near_ref[mode, member]
                partner = [physical[(c, near) + place] for c in range(components)]
                low_one = [physical[(c, low) + place] for c in range(components)]
                for c in range(components):
                    if c == 1:
                        result[c] = result[c] + low_one[1] * partner[1]
                    else:
                        result[c] = result[c] + (low_one[c] * partner[1] + partner[c] * low_one[1])
                    slot = member * components + c
                    totals[slot] = totals[slot] + own[c] * partner[1]
            for c in range(components):
                products[(c, index) + place] = result[c] * 2.0 if c == 1 else result[c]
            return tuple(totals)

        empty = tuple(jnp.zeros((8, LANES), jnp.float32) for _ in range(members * components))
        totals = lax.fori_loop(0, highs, one_high, empty)
        for member in range(members):
            for c in range(components):
                sums[(c, member) + place] = totals[member * components + c]
        return carry

    lax.fori_loop(0, (rows // 8) * (points // LANES), pairs, 0)

    def inverse(fields):
        top, rest = two_parts(fields)
        both = dot(top, back_ref[...])
        return both[:, :columns] + both[:, columns:] + dot(rest, back_ref[:, :columns])

    def finish(component, carry):
        forcing = inverse(products[component].reshape(highs * rows, points))
        forcing = forcing.reshape(highs, rows, columns)
        for index in range(highs):
            mode = high_ref[index]
            active = slot_ref[:1] < count_ref[mode]
            slotted_ref[component, mode] += jnp.where(active, forcing[index] * dt_step, 0.0)
        stress = inverse(sums[component].reshape(members * rows, points))
        stress = stress.reshape(2, members // 2, rows, columns)
        kept_ref[component] = jnp.where(odd, stress[1], stress[0])
        sent_ref[component] = jnp.where(odd, stress[0], stress[1])
        return carry

    lax.fori_loop(0, components, finish, 0)


def nonlinear(blocks, shape, low_index, neighbours, mode_counts, tables, slot_modes, after):
    components, modes, rows, columns = shape
    members, points = (low_index.shape[0], 2 * columns)
    highs = modes - members
    return pl.pallas_call(
        nonlinear_kernel,
        out_shape=(
            jax.ShapeDtypeStruct((components, modes, rows, columns), jnp.float32),
            jax.ShapeDtypeStruct((components, members // 2, rows, columns), jnp.float32),
            jax.ShapeDtypeStruct((components, members // 2, rows, columns), jnp.float32),
        ),
        in_specs=[SMEM] * 3 + [VMEM] * (len(blocks) + 4) + [pl.BlockSpec(memory_space=pl.ANY)],
        out_specs=(VMEM, VMEM, VMEM),
        scratch_shapes=[
            pltpu.VMEM((components, modes, rows, points), jnp.float32),
            pltpu.VMEM((components, highs, rows, points), jnp.float32),
            pltpu.VMEM((components, members, rows, points), jnp.float32),
            pltpu.SMEM((modes + 1,), jnp.int32),
        ],
        compiler_params=params(),
        cost_estimate=cost(8 * components * modes * rows * points * members),
        name="nonlinear",
    )(low_index, neighbours, mode_counts, *blocks, *tables, slot_modes, after)


def outgoing_kernel(
    low_ref, count_ref, slotted_ref, kept_ref, other_ref, slot_ref, *refs,
    groups, band_modes, owners, scale
):
    out_refs, (full, turned) = (refs[:-2], refs[-2:])
    components, modes, rows, columns = slotted_ref.shape
    half, slots = (kept_ref.shape[1], columns // 2 // owners)
    per_slot = out_refs[0].shape[0] * len(out_refs) // (columns // 2)
    own = lax.axis_index("real") & 1
    full[...] = slotted_ref[...]
    for member in range(half):
        for part_ref, start in ((kept_ref, own * half), (other_ref, (1 - own) * half)):
            mode = low_ref[start + member]
            active = slot_ref[:1] < count_ref[mode]
            for c in range(components):
                full[c, mode] += jnp.where(active, part_ref[c, member] * scale, 0.0)
    inner = modes // groups
    if len(out_refs) > 1:
        me = lax.axis_index("kx") * lax.axis_size("ht") + lax.axis_index("ht")
        targets = [me ^ step_at(owners, position) for position in range(owners)]
    for c in range(components):
        for part in range(inner):
            tile = jnp.concatenate([full[c, part + inner * g] for g in range(groups)], axis=0)
            band_low, band_mode = (part // band_modes, part % band_modes)
            if len(out_refs) > 1:
                turned[...] = tile.T
            else:
                value = tile.T
            for p in range(2):
                row = ((band_low * 2 + p) * components + c) * band_modes + band_mode
                if len(out_refs) == 1:
                    out_refs[0][pl.ds(row, columns // 2, stride=per_slot), :] = value[
                        p * (columns // 2) : (p + 1) * (columns // 2)
                    ]
                    continue
                for out_ref, target in zip(out_refs, targets):
                    start = pl.multiple_of((p * owners + target) * slots, slots)
                    out_ref[pl.ds(row, slots, stride=per_slot), :] = turned[pl.ds(start, slots)]


def outgoing(
    slotted, kept, other, low_index, mode_counts, slot_modes, groups, band_modes, owners,
    realizations, separate,
):
    components, modes, rows, columns = slotted.shape
    total, lanes = ((columns // 2) * (modes // groups) * 2 * components, groups * rows)
    count = owners if separate else 1
    return pl.pallas_call(
        functools.partial(
            outgoing_kernel, groups=groups, band_modes=band_modes, owners=owners,
            scale=dt_step / realizations,
        ),
        out_shape=(jax.ShapeDtypeStruct((total // count, lanes), jnp.float32),) * count,
        in_specs=[SMEM, SMEM] + [VMEM] * 4,
        out_specs=(VMEM,) * count,
        scratch_shapes=[
            pltpu.VMEM(slotted.shape, jnp.float32), pltpu.VMEM((columns, lanes), jnp.float32)
        ],
        compiler_params=params(),
        cost_estimate=cost(8 * slotted.size),
        name="outgoing",
    )(low_index, mode_counts, slotted, kept, other, slot_modes)


def regroup(blocks, rows):
    count = len(blocks)
    lane = lax.broadcasted_iota(jnp.int32, blocks[0].shape, 1) // rows
    step = 1
    while step < count:
        take = (lane & step) == 0
        for i in range(count):
            if i & step == 0:
                here, there = (blocks[i], blocks[i + step])
                blocks[i] = jnp.where(take, here, pltpu.roll(there, step * rows, 1))
                blocks[i + step] = jnp.where(
                    take, pltpu.roll(here, LANES - step * rows, 1), there
                )
        step *= 2
    return blocks


def solve_kernel(*refs, groups, kx_count, ht_count, pieces):
    owners = kx_count * ht_count
    first_ref, refs = (refs[0], refs[1:])
    count = owners * (pieces - 1)
    block_refs, matrix_ref, refs = (refs[:count], refs[count], refs[count + 1 :])
    out_refs, (matrices, arrived, ordered, full) = (refs[:owners], refs[owners:])
    slots, heights = (matrix_ref.shape[0], matrix_ref.shape[1])
    copies = [
        pltpu.make_async_copy(matrix_ref.at[s], matrices.at[s], arrived.at[s])
        for s in range(slots)
    ]
    for copy in copies:
        copy.start()
    own_kx, own_ht = (lax.axis_index("kx"), lax.axis_index("ht"))
    partners = []
    for position in range(owners):
        step = step_at(owners, position)
        partners.append((own_kx ^ (step // ht_count), own_ht ^ (step % ht_count)))
    for index, block_ref in enumerate(block_refs):
        kx, ht = partners[index % owners]
        ordered[index // owners, kx * ht_count + ht] = block_ref[...]
    rows, (lane_tiles, per_band) = (LANES // groups, out_refs[0].shape[1:3])
    for s in range(slots):
        tiles = []
        for h in range(ht_count):
            for piece in range(pieces):
                source = first_ref if piece == 0 else ordered.at[piece - 1]
                for first in range(0, kx_count, groups):
                    blocks = [source[(first + g) * ht_count + h, s] for g in range(groups)]
                    tiles.append(jnp.concatenate(regroup(blocks, rows), axis=0))
        top, rest = two_parts(jnp.concatenate(tiles, axis=1))
        count = top.shape[0]
        copies[s].wait()
        matrix_top, matrix_rest = two_parts(matrices[s])
        last = ((1,), (1,))
        both = dot(matrix_top, jnp.concatenate([top, rest], axis=0), last)
        solved = both[:, :count] + both[:, count:] + dot(matrix_rest, top, last)
        for tile in range(heights // LANES):
            full[s % 2, tile] = solved[tile * LANES : (tile + 1) * LANES].T
        for out_ref, (kx, ht) in zip(out_refs, partners):
            band = pl.ds(pl.multiple_of(kx * per_band, 8), per_band)
            for tile in range(lane_tiles):
                out_ref[s, tile] = full[s % 2, ht * lane_tiles + tile, band]


def solve(first, blocks, helmholtz, pieces, groups, kx_count, ht_count):
    owners, slots, per_slot, lanes = first.shape
    heights, count = (helmholtz.shape[1], per_slot * groups)
    shape = (slots, heights // ht_count // LANES, count // kx_count, LANES)
    return pl.pallas_call(
        functools.partial(
            solve_kernel, groups=groups, kx_count=kx_count, ht_count=ht_count, pieces=pieces
        ),
        out_shape=(jax.ShapeDtypeStruct(shape, jnp.float32),) * owners,
        in_specs=[VMEM] * (1 + len(blocks)) + [pl.BlockSpec(memory_space=pl.ANY)],
        out_specs=(VMEM,) * owners,
        scratch_shapes=[
            pltpu.VMEM(helmholtz.shape, jnp.float32),
            pltpu.SemaphoreType.DMA((slots,)),
            pltpu.VMEM((max(pieces - 1, 1),) + first.shape, jnp.float32),
            pltpu.VMEM((2, heights // LANES, count, LANES), jnp.float32),
        ],
        compiler_params=params(),
        cost_estimate=cost(4 * helmholtz.size),
        name="solve",
    )(first, *blocks, helmholtz)


def restore_kernel(*refs, owners, ht_count):
    block_refs, (order_ref, out_ref, ordered) = (refs[:-3], refs[-3:])
    components, band_modes, rows, columns = out_ref.shape
    slots = columns // 2 // owners
    per_slot = block_refs[0].shape[0] // slots
    me = lax.axis_index("kx") * ht_count + lax.axis_index("ht")
    for position, block_ref in enumerate(block_refs):
        ordered[me ^ step_at(owners, position)] = block_ref[...]
    for c in range(components):
        for mode in range(band_modes):
            for tile in range(rows // LANES):
                parts = []
                for p in range(2):
                    row = ((tile * 2 + p) * components + c) * band_modes + mode
                    for owner in range(owners):
                        parts.append(ordered[owner, pl.ds(row, slots, stride=per_slot), :])
                top, rest = two_parts(jnp.concatenate(parts, axis=0))
                both = jnp.concatenate([top, rest], axis=0)
                out_ref[c, mode, pl.ds(tile * LANES, LANES)] = dot(
                    both, order_ref[...], ((0,), (0,))
                )


def restore(blocks, order, components, band_modes, rows, ht_count):
    columns = order.shape[1]
    return pl.pallas_call(
        functools.partial(restore_kernel, owners=len(blocks), ht_count=ht_count),
        out_shape=jax.ShapeDtypeStruct((components, band_modes, rows, columns), jnp.float32),
        in_specs=[VMEM] * (len(blocks) + 1),
        out_specs=VMEM,
        scratch_shapes=[pltpu.VMEM((len(blocks),) + blocks[0].shape, jnp.float32)],
        compiler_params=params(),
        cost_estimate=cost(8 * components * band_modes * rows * columns),
        name="restore",
    )(*blocks, order)


def exchange(blocks, axes):
    count, realizations = (len(blocks), lax.axis_size("real"))
    result = list(blocks)
    for position in range(1, count):
        steps = [order[position] for order in steps_of(count)]
        pairs = [
            (index * realizations + r, (index ^ steps[r % 2]) * realizations + r)
            for index in range(count)
            for r in range(realizations)
        ]
        result[position] = lax.ppermute(blocks[position], axes + ("real",), pairs)
    return result


def swap(value, step):
    pairs = [(index, index ^ step) for index in range(lax.axis_size("real"))]
    return lax.ppermute(value, "real", pairs)


def local(velocity, low_index, neighbours, owner_map, mode_counts, helmholtz):
    components, reals_dev, band_modes, rows_ht, columns = velocity.shape
    kx_count, ht_count = (lax.axis_size("kx"), lax.axis_size("ht"))
    own_kx, own_ht = (lax.axis_index("kx"), lax.axis_index("ht"))
    owners, pieces, real_count = (kx_count * ht_count, PIECES, lax.axis_size("real"))
    rows = rows_ht // (kx_count * pieces)
    groups = LANES // rows if rows else 0
    slots = columns // 2 // owners
    if (
        columns != LANES or reals_dev != 1 or rows_ht % LANES or rows % 8 or LANES % rows or kx_count % groups or kx_count & (kx_count - 1)
        or (band_modes * 2 * components) % 8 or slots % 8 or owners & (owners - 1) or low_index.shape[0] >= kx_count * band_modes
        or low_index.shape[0] >= columns or low_index.shape[0] % 2 or real_count < 2 or real_count & (real_count - 1)
    ):
        return local_plain(velocity, low_index, neighbours, owner_map, mode_counts, helmholtz)
    realizations, members = (real_count, low_index.shape[0])
    chunks, modes = (components * band_modes, band_modes * kx_count)
    shape = (components, modes, rows, columns)
    extra_rows = -(-band_modes // 8) * 8
    split = velocity.reshape(chunks, pieces, kx_count, rows, columns)
    block, rest = pack(split, neighbours, mode_counts, extra_rows)
    block = lax.all_to_all(block, "kx", split_axis=0, concat_axis=0, tiled=True)
    parts = [(block,)] + [exchange(blocks, ("kx",)) for blocks in rest]
    tables, order, slot_modes = slot_tables(owner_map, columns)
    small = block[:, chunks * rows : chunks * rows + band_modes, : members + 1]
    small = small.reshape(modes, members + 1).astype(jnp.int32)
    neighbours, mode_counts = (small[:, :-1], small[:, -1])
    after = slot_modes
    received = []
    for piece, part in enumerate(parts):
        slotted, kept, sent = nonlinear(
            part, shape, low_index, neighbours, mode_counts, tables, slot_modes, after
        )
        kept = after = kept + swap(sent, 1)
        step = 2
        while step < realizations:
            kept = kept + swap(kept, step)
            step *= 2
        blocks = outgoing(
            slotted, kept, swap(kept, 1), low_index, mode_counts, slot_modes, groups, band_modes,
            owners, realizations, piece > 0,
        )
        if piece:
            received += exchange([block.reshape(slots, -1, LANES) for block in blocks], ("kx", "ht"))
        else:
            block = blocks[0].reshape(owners, slots, -1, LANES)
            first = lax.all_to_all(block, ("kx", "ht"), split_axis=0, concat_axis=0, tiled=True)
    solved = solve(first, received, helmholtz, pieces, groups, kx_count, ht_count)
    returned = [block.reshape(-1, LANES) for block in exchange(solved, ("kx", "ht"))]
    result = restore(returned, order, components, band_modes, rows_ht, ht_count)
    return result.reshape(velocity.shape)


def solution(mesh):
    in_specs = (
        P(None, "real", "kx", "ht", None),
        P(),
        P("kx", None),
        P(),
        P("kx"),
        P(("kx", "ht"), None, None),
    )
    out_specs = P(None, "real", "kx", "ht", None)
    return jax.shard_map(local, mesh=mesh, in_specs=in_specs, out_specs=out_specs, check_vma=False)
```

```python
import functools

import jax
import jax.numpy as jnp
import numpy as np
from jax import lax
from jax.experimental import pallas as pl
from jax.experimental.pallas import tpu as pltpu
from jax.sharding import PartitionSpec as P

dt_step = 0.1


def spanwise_tables(mode_count, point_count):
    column_ids = jnp.arange(2 * mode_count)
    wavenumber = (column_ids // 2).astype(jnp.float32)
    imag_part = column_ids % 2
    positions = 2.0 * jnp.pi * jnp.arange(point_count).astype(jnp.float32) / point_count
    phases = wavenumber[:, None] * positions[None, :]
    forward = jnp.where(imag_part[:, None] == 0, jnp.cos(phases), -jnp.sin(phases)) / jnp.sqrt(
        jnp.float32(mode_count)
    )
    backward = forward.T * (2.0 * mode_count / point_count)
    return (forward, backward)


def nonlinear_rows(fields, low_index, neighbours, mode_counts, forward, backward):
    precision = lax.Precision.HIGH
    realizations, modes, columns = (fields.shape[1], fields.shape[2], fields.shape[4])
    low_select = (low_index[:, None] == jnp.arange(modes)[None, :]).astype(jnp.float32)
    high_mask = 1.0 - jnp.sum(low_select, axis=0)
    high_rows = high_mask[None, None, :, None, None]
    column_mask = ((jnp.arange(columns) // 2)[None, :] < mode_counts[:, None]).astype(jnp.float32)
    physical = jnp.dot(fields, forward, precision=precision)
    low_fields = jnp.take(physical, low_index, axis=2)
    high_low = jnp.zeros_like(physical)
    stresses = []
    for member in range(low_index.shape[0]):
        partner = jnp.take(physical, neighbours[:, member], axis=2)
        low_one = low_fields[:, :, member : member + 1]
        high_low = high_low + low_one * partner[1:2] + partner * low_one[1:2]
        stresses.append(jnp.sum(physical * (partner[1:2] * high_rows), axis=(1, 2)))
    stress = jnp.stack(stresses, axis=1) / realizations
    forcing = jnp.dot(high_low, backward, precision=precision) * high_rows
    low_forcing = jnp.dot(stress, backward, precision=precision)
    low_rows = jnp.einsum("jm,cjyk->cmyk", low_select, low_forcing, precision=lax.Precision.HIGHEST)
    forcing = (forcing + low_rows[:, None]) * column_mask[None, None, :, None, :]
    return fields + dt_step * forcing


def local_plain(velocity, low_index, neighbours, owner_map, mode_counts, helmholtz):
    components, reals_dev, band_modes, rows_ht, columns = velocity.shape
    kz_modes = columns // 2
    forward, backward = spanwise_tables(kz_modes, 4 * kz_modes)
    kx_count, ht_count = (lax.axis_size("kx"), lax.axis_size("ht"))
    real_count = lax.axis_size("real")
    modes, realizations = (band_modes * kx_count, reals_dev * real_count)
    slots_dev = kz_modes // (kx_count * ht_count)
    rows_dev = rows_ht // (kx_count * real_count)
    small = jnp.concatenate([neighbours, mode_counts[:, None]], axis=1)
    small = lax.all_gather(small, "kx", axis=0, tiled=True)
    neighbours, mode_counts = (small[:, :-1], small[:, -1])
    inverse_map = (
        jnp.zeros((kz_modes,), jnp.int32).at[owner_map].set(jnp.arange(kz_modes, dtype=jnp.int32))
    )
    split = velocity.reshape(
        components, reals_dev, band_modes, kx_count * real_count, rows_dev, columns
    )
    split = split.transpose(3, 0, 1, 2, 4, 5)
    split = lax.all_to_all(split, ("kx", "real"), split_axis=0, concat_axis=0, tiled=True)
    fields = split.reshape(
        kx_count, real_count, components, reals_dev, band_modes, rows_dev, columns
    )
    fields = fields.transpose(2, 1, 3, 0, 4, 5, 6).reshape(
        components, realizations, modes, rows_dev, columns
    )
    updated = nonlinear_rows(fields, low_index, neighbours, mode_counts, forward, backward)
    slotted = jnp.take(
        updated.reshape(components, realizations, modes, rows_dev, kz_modes, 2), owner_map, axis=4
    )
    slotted = slotted.reshape(
        components, real_count, reals_dev, modes, rows_dev, kx_count * ht_count, slots_dev, 2
    )
    outgoing = slotted.transpose(5, 1, 6, 2, 0, 3, 7, 4).reshape(
        kx_count * ht_count * real_count, slots_dev, reals_dev * components * modes * 2, rows_dev
    )
    incoming = lax.all_to_all(
        outgoing, ("kx", "ht", "real"), split_axis=0, concat_axis=0, tiled=True
    )
    incoming = incoming.reshape(
        kx_count, ht_count, real_count, slots_dev, reals_dev * components * modes * 2, rows_dev
    )
    incoming = incoming.transpose(3, 4, 1, 0, 2, 5).reshape(
        slots_dev, reals_dev * components * modes * 2, ht_count * rows_ht
    )
    solved = jnp.einsum("syx,snx->sny", helmholtz, incoming, precision=lax.Precision.HIGH)
    solved = solved.reshape(
        slots_dev, reals_dev, components, kx_count, band_modes, 2, ht_count, rows_ht
    )
    solved = solved.transpose(3, 6, 0, 5, 1, 2, 4, 7).reshape(
        kx_count * ht_count, slots_dev * 2, reals_dev * components * band_modes, rows_ht
    )
    returned = lax.all_to_all(solved, ("kx", "ht"), split_axis=0, concat_axis=0, tiled=True)
    restored = returned.reshape(
        kz_modes, 2, reals_dev, components, band_modes, rows_ht
    )
    restored = jnp.take(restored, inverse_map, axis=0)
    return restored.transpose(3, 2, 4, 5, 0, 1).reshape(velocity.shape)


LANES = 128
PIECES = 2
VMEM = pl.BlockSpec(memory_space=pltpu.VMEM)
SMEM = pl.BlockSpec(memory_space=pltpu.SMEM)


def params():
    return pltpu.CompilerParams(vmem_limit_bytes=48 * 1024 * 1024)


ORDERS = {4: (1, 3, 2), 8: (4, 1, 2, 6, 5, 3, 7)}


def steps_of(count):
    even = ORDERS.get(count, tuple(range(1, count)))
    odd = list(even)
    for first in range(0, count - 2, 2):
        odd[first], odd[first + 1] = (even[first + 1], even[first])
    return (0,) + tuple(even), (0,) + tuple(odd)


def step_at(count, position):
    even, odd = steps_of(count)
    return jnp.where((lax.axis_index("real") & 1) == 0, even[position], odd[position])


def cost(size):
    return pl.CostEstimate(flops=0, bytes_accessed=size, transcendentals=0)


def two_parts(value):
    top = value.astype(jnp.bfloat16)
    rest = (value - top.astype(jnp.float32)).astype(jnp.bfloat16)
    return top, rest


def dot(left, right, dims=((1,), (0,))):
    return lax.dot_general(left, right, (dims, ((), ())), preferred_element_type=jnp.float32)


def pack_kernel(near_ref, count_ref, velocity_ref, *out_refs):
    chunks, pieces, kx_count, rows, columns = velocity_ref.shape
    own = lax.axis_index("kx")
    for index in range(kx_count):
        partner = own ^ step_at(kx_count, index)
        for chunk in range(chunks):
            place = slice(chunk * rows, (chunk + 1) * rows)
            out_refs[index][place] = velocity_ref[chunk, 0, partner]
            for piece in range(1, pieces):
                out_refs[kx_count + piece - 1][index, place] = velocity_ref[chunk, piece, index]
    shape = (out_refs[0].shape[0] - chunks * rows, columns)
    row = lax.broadcasted_iota(jnp.int32, shape, 0)
    lane = lax.broadcasted_iota(jnp.int32, shape, 1)
    extra = jnp.zeros(shape, jnp.int32)
    modes, members = near_ref.shape
    for mode in range(modes):
        line = jnp.where(lane == members, count_ref[mode], 0)
        for member in range(members):
            line = jnp.where(lane == member, near_ref[mode, member], line)
        extra = jnp.where(row == mode, line, extra)
    extra = extra.astype(jnp.float32)
    for out_ref in out_refs[:kx_count]:
        out_ref[chunks * rows :] = extra


def pack(velocity, neighbours, mode_counts, extra_rows):
    chunks, pieces, kx_count, rows, columns = velocity.shape
    size = chunks * rows
    shapes = [(size + extra_rows, columns)] * kx_count
    shapes += [(kx_count, size, columns)] * (pieces - 1)
    out = pl.pallas_call(
        pack_kernel,
        out_shape=tuple(jax.ShapeDtypeStruct(shape, jnp.float32) for shape in shapes),
        in_specs=[SMEM, SMEM, VMEM],
        out_specs=(VMEM,) * len(shapes),
        cost_estimate=cost(8 * velocity.size),
        name="pack",
    )(neighbours, mode_counts, velocity)
    return out[:kx_count], out[kx_count:]


def tables_kernel(owner_ref, top_ref, rest_ref, first_ref, back_ref, order_ref, slot_ref):
    columns = slot_ref.shape[1]
    modes = columns // 2
    lane = lax.broadcasted_iota(jnp.int32, (8, columns), 1)
    mode = jnp.zeros((8, columns), jnp.int32)
    for slot in range(modes):
        mode = jnp.where(lane % modes == slot, owner_ref[slot], mode)
    slot_ref[...] = mode
    wanted = 2 * mode + lane // modes
    row = lax.broadcasted_iota(jnp.int32, (columns, columns), 0)
    chosen = (row == wanted[:1]).astype(jnp.float32)
    select = chosen.astype(jnp.bfloat16)
    points = top_ref.shape[1]
    for half in range(2):
        rows = slice(half * columns, (half + 1) * columns)
        first_ref[rows, :points] = top_ref[...]
        first_ref[rows, points:] = select
        order_ref[rows] = chosen.T.astype(jnp.bfloat16)
    for index, table_ref in enumerate((top_ref, rest_ref)):
        back = dot(table_ref[...], select, ((0,), (0,))) * (2.0 * modes / points)
        back_ref[:, index * columns : (index + 1) * columns] = back.astype(jnp.bfloat16)


def spanwise_constants(columns, points):
    mode = np.arange(columns) // 2
    phase = 2.0 * np.pi * ((mode[:, None] * np.arange(points)[None, :]) % points) / points
    forward = np.where(np.arange(columns)[:, None] % 2 == 0, np.cos(phase), -np.sin(phase))
    forward = (forward / np.sqrt(columns // 2)).astype(np.float32)
    top = forward.astype(jnp.bfloat16)
    rest = (forward - top.astype(np.float32)).astype(jnp.bfloat16)
    return jnp.asarray(top), jnp.asarray(rest)


def slot_tables(owner_map, columns):
    points = 2 * columns
    top, rest = spanwise_constants(columns, points)
    first, back, order, slot_modes = pl.pallas_call(
        tables_kernel,
        out_shape=(
            jax.ShapeDtypeStruct((2 * columns, points + columns), jnp.bfloat16),
            jax.ShapeDtypeStruct((points, 2 * columns), jnp.bfloat16),
            jax.ShapeDtypeStruct((2 * columns, columns), jnp.bfloat16),
            jax.ShapeDtypeStruct((8, columns), jnp.int32),
        ),
        in_specs=[SMEM, VMEM, VMEM],
        out_specs=(VMEM,) * 4,
        compiler_params=params(),
        cost_estimate=cost(640 * points * columns),
        name="tables",
    )(owner_map, top, rest)
    return (first, rest, back), order, slot_modes


def nonlinear_kernel(low_ref, near_ref, count_ref, *refs):
    block_refs, refs = (refs[:-12], refs[-12:])
    first_ref, second_ref, back_ref, slot_ref, _, slotted_ref, kept_ref, sent_ref = refs[:8]
    physical, products, sums, high_ref = refs[8:]
    components, modes, rows, columns = slotted_ref.shape
    if len(block_refs) > 1:
        bands = len(block_refs)
        places = [lax.axis_index("kx") ^ step_at(bands, index) for index in range(bands)]
    else:
        bands = block_refs[0].shape[0]
        places = list(range(bands))
        block_refs = [block_refs[0].at[index] for index in range(bands)]
    points, band_modes = (physical.shape[3], modes // bands)
    members, highs = (sums.shape[1], products.shape[1])
    odd = (lax.axis_index("real") & 1) == 1
    found = jnp.int32(0)
    for mode in range(modes):
        is_low = jnp.int32(0)
        for member in range(members):
            is_low = is_low | (low_ref[member] == mode).astype(jnp.int32)
        high_ref[found] = mode
        found = found + 1 - is_low

    def transform(component, carry):
        size = band_modes * rows
        for index, block_ref in enumerate(block_refs):
            top, rest = two_parts(block_ref[pl.ds(pl.multiple_of(component * size, 8), size)])
            both = dot(jnp.concatenate([top, rest], axis=1), first_ref[...])
            fields = both[:, :points] + dot(top, second_ref[...])
            place = pl.ds(places[index] * band_modes, band_modes)
            physical[component, place] = fields.reshape(band_modes, rows, points)
            slotted_ref[component, place] = both[:, points:].reshape(band_modes, rows, columns)
        return carry

    lax.fori_loop(0, components, transform, 0)

    def pairs(step, carry):
        halves = points // LANES
        place = (
            pl.ds(pl.multiple_of((step // halves) * 8, 8), 8),
            pl.ds(pl.multiple_of((step % halves) * LANES, LANES), LANES),
        )

        def one_high(index, totals):
            mode = high_ref[index]
            own = [physical[(c, mode) + place] for c in range(components)]
            result = [jnp.zeros((8, LANES), jnp.float32) for _ in range(components)]
            totals = list(totals)
            for member in range(members):
                low = low_ref[member]
                near = near_ref[mode, member]
                partner = [physical[(c, near) + place] for c in range(components)]
                low_one = [physical[(c, low) + place] for c in range(components)]
                for c in range(components):
                    if c == 1:
                        result[c] = result[c] + low_one[1] * partner[1]
                    else:
                        result[c] = result[c] + (low_one[c] * partner[1] + partner[c] * low_one[1])
                    slot = member * components + c
                    totals[slot] = totals[slot] + own[c] * partner[1]
            for c in range(components):
                products[(c, index) + place] = result[c] * 2.0 if c == 1 else result[c]
            return tuple(totals)

        empty = tuple(jnp.zeros((8, LANES), jnp.float32) for _ in range(members * components))
        totals = lax.fori_loop(0, highs, one_high, empty)
        for member in range(members):
            for c in range(components):
                sums[(c, member) + place] = totals[member * components + c]
        return carry

    lax.fori_loop(0, (rows // 8) * (points // LANES), pairs, 0)

    def inverse(fields):
        top, rest = two_parts(fields)
        both = dot(top, back_ref[...])
        return both[:, :columns] + both[:, columns:] + dot(rest, back_ref[:, :columns])

    def finish(component, carry):
        forcing = inverse(products[component].reshape(highs * rows, points))
        forcing = forcing.reshape(highs, rows, columns)
        for index in range(highs):
            mode = high_ref[index]
            active = slot_ref[:1] < count_ref[mode]
            slotted_ref[component, mode] += jnp.where(active, forcing[index] * dt_step, 0.0)
        stress = inverse(sums[component].reshape(members * rows, points))
        stress = stress.reshape(2, members // 2, rows, columns)
        kept_ref[component] = jnp.where(odd, stress[1], stress[0])
        sent_ref[component] = jnp.where(odd, stress[0], stress[1])
        return carry

    lax.fori_loop(0, components, finish, 0)


def nonlinear(blocks, shape, low_index, neighbours, mode_counts, tables, slot_modes, after):
    components, modes, rows, columns = shape
    members, points = (low_index.shape[0], 2 * columns)
    highs = modes - members
    return pl.pallas_call(
        nonlinear_kernel,
        out_shape=(
            jax.ShapeDtypeStruct((components, modes, rows, columns), jnp.float32),
            jax.ShapeDtypeStruct((components, members // 2, rows, columns), jnp.float32),
            jax.ShapeDtypeStruct((components, members // 2, rows, columns), jnp.float32),
        ),
        in_specs=[SMEM] * 3 + [VMEM] * (len(blocks) + 4) + [pl.BlockSpec(memory_space=pl.ANY)],
        out_specs=(VMEM, VMEM, VMEM),
        scratch_shapes=[
            pltpu.VMEM((components, modes, rows, points), jnp.float32),
            pltpu.VMEM((components, highs, rows, points), jnp.float32),
            pltpu.VMEM((components, members, rows, points), jnp.float32),
            pltpu.SMEM((modes + 1,), jnp.int32),
        ],
        compiler_params=params(),
        cost_estimate=cost(8 * components * modes * rows * points * members),
        name="nonlinear",
    )(low_index, neighbours, mode_counts, *blocks, *tables, slot_modes, after)


def outgoing_kernel(
    low_ref, count_ref, slotted_ref, kept_ref, other_ref, slot_ref, *refs,
    groups, band_modes, owners, scale
):
    out_refs, (full, turned) = (refs[:-2], refs[-2:])
    components, modes, rows, columns = slotted_ref.shape
    half, slots = (kept_ref.shape[1], columns // 2 // owners)
    per_slot = out_refs[0].shape[0] * len(out_refs) // (columns // 2)
    own = lax.axis_index("real") & 1
    full[...] = slotted_ref[...]
    for member in range(half):
        for part_ref, start in ((kept_ref, own * half), (other_ref, (1 - own) * half)):
            mode = low_ref[start + member]
            active = slot_ref[:1] < count_ref[mode]
            for c in range(components):
                full[c, mode] += jnp.where(active, part_ref[c, member] * scale, 0.0)
    inner = modes // groups
    if len(out_refs) > 1:
        me = lax.axis_index("kx") * lax.axis_size("ht") + lax.axis_index("ht")
        targets = [me ^ step_at(owners, position) for position in range(owners)]
    for c in range(components):
        for part in range(inner):
            tile = jnp.concatenate([full[c, part + inner * g] for g in range(groups)], axis=0)
            band_low, band_mode = (part // band_modes, part % band_modes)
            if len(out_refs) > 1:
                turned[...] = tile.T
            else:
                value = tile.T
            for p in range(2):
                row = ((band_low * 2 + p) * components + c) * band_modes + band_mode
                if len(out_refs) == 1:
                    out_refs[0][pl.ds(row, columns // 2, stride=per_slot), :] = value[
                        p * (columns // 2) : (p + 1) * (columns // 2)
                    ]
                    continue
                for out_ref, target in zip(out_refs, targets):
                    start = pl.multiple_of((p * owners + target) * slots, slots)
                    out_ref[pl.ds(row, slots, stride=per_slot), :] = turned[pl.ds(start, slots)]


def outgoing(
    slotted, kept, other, low_index, mode_counts, slot_modes, groups, band_modes, owners,
    realizations, separate,
):
    components, modes, rows, columns = slotted.shape
    total, lanes = ((columns // 2) * (modes // groups) * 2 * components, groups * rows)
    count = owners if separate else 1
    return pl.pallas_call(
        functools.partial(
            outgoing_kernel, groups=groups, band_modes=band_modes, owners=owners,
            scale=dt_step / realizations,
        ),
        out_shape=(jax.ShapeDtypeStruct((total // count, lanes), jnp.float32),) * count,
        in_specs=[SMEM, SMEM] + [VMEM] * 4,
        out_specs=(VMEM,) * count,
        scratch_shapes=[
            pltpu.VMEM(slotted.shape, jnp.float32), pltpu.VMEM((columns, lanes), jnp.float32)
        ],
        compiler_params=params(),
        cost_estimate=cost(8 * slotted.size),
        name="outgoing",
    )(low_index, mode_counts, slotted, kept, other, slot_modes)


def regroup(blocks, rows):
    count = len(blocks)
    lane = lax.broadcasted_iota(jnp.int32, blocks[0].shape, 1) // rows
    step = 1
    while step < count:
        take = (lane & step) == 0
        for i in range(count):
            if i & step == 0:
                here, there = (blocks[i], blocks[i + step])
                blocks[i] = jnp.where(take, here, pltpu.roll(there, step * rows, 1))
                blocks[i + step] = jnp.where(
                    take, pltpu.roll(here, LANES - step * rows, 1), there
                )
        step *= 2
    return blocks


def solve_kernel(*refs, groups, kx_count, ht_count, pieces):
    owners = kx_count * ht_count
    first_ref, refs = (refs[0], refs[1:])
    count = owners * (pieces - 1)
    block_refs, matrix_ref, refs = (refs[:count], refs[count], refs[count + 1 :])
    out_refs, (matrices, arrived, ordered, full) = (refs[:owners], refs[owners:])
    slots, heights = (matrix_ref.shape[0], matrix_ref.shape[1])
    copies = [
        pltpu.make_async_copy(matrix_ref.at[s], matrices.at[s], arrived.at[s])
        for s in range(slots)
    ]
    for copy in copies:
        copy.start()
    own_kx, own_ht = (lax.axis_index("kx"), lax.axis_index("ht"))
    partners = []
    for position in range(owners):
        step = step_at(owners, position)
        partners.append((own_kx ^ (step // ht_count), own_ht ^ (step % ht_count)))
    for index, block_ref in enumerate(block_refs):
        kx, ht = partners[index % owners]
        ordered[index // owners, kx * ht_count + ht] = block_ref[...]
    rows, (lane_tiles, per_band) = (LANES // groups, out_refs[0].shape[1:3])
    for s in range(slots):
        tiles = []
        for h in range(ht_count):
            for piece in range(pieces):
                source = first_ref if piece == 0 else ordered.at[piece - 1]
                for first in range(0, kx_count, groups):
                    blocks = [source[(first + g) * ht_count + h, s] for g in range(groups)]
                    tiles.append(jnp.concatenate(regroup(blocks, rows), axis=0))
        top, rest = two_parts(jnp.concatenate(tiles, axis=1))
        count = top.shape[0]
        copies[s].wait()
        matrix_top, matrix_rest = two_parts(matrices[s])
        last = ((1,), (1,))
        both = dot(matrix_top, jnp.concatenate([top, rest], axis=0), last)
        solved = both[:, :count] + both[:, count:] + dot(matrix_rest, top, last)
        for tile in range(heights // LANES):
            full[s % 2, tile] = solved[tile * LANES : (tile + 1) * LANES].T
        for out_ref, (kx, ht) in zip(out_refs, partners):
            band = pl.ds(pl.multiple_of(kx * per_band, 8), per_band)
            for tile in range(lane_tiles):
                out_ref[s, tile] = full[s % 2, ht * lane_tiles + tile, band]


def solve(first, blocks, helmholtz, pieces, groups, kx_count, ht_count):
    owners, slots, per_slot, lanes = first.shape
    heights, count = (helmholtz.shape[1], per_slot * groups)
    shape = (slots, heights // ht_count // LANES, count // kx_count, LANES)
    return pl.pallas_call(
        functools.partial(
            solve_kernel, groups=groups, kx_count=kx_count, ht_count=ht_count, pieces=pieces
        ),
        out_shape=(jax.ShapeDtypeStruct(shape, jnp.float32),) * owners,
        in_specs=[VMEM] * (1 + len(blocks)) + [pl.BlockSpec(memory_space=pl.ANY)],
        out_specs=(VMEM,) * owners,
        scratch_shapes=[
            pltpu.VMEM(helmholtz.shape, jnp.float32),
            pltpu.SemaphoreType.DMA((slots,)),
            pltpu.VMEM((max(pieces - 1, 1),) + first.shape, jnp.float32),
            pltpu.VMEM((2, heights // LANES, count, LANES), jnp.float32),
        ],
        compiler_params=params(),
        cost_estimate=cost(4 * helmholtz.size),
        name="solve",
    )(first, *blocks, helmholtz)


def restore_kernel(*refs, owners, ht_count):
    block_refs, (order_ref, out_ref, ordered) = (refs[:-3], refs[-3:])
    components, band_modes, rows, columns = out_ref.shape
    slots = columns // 2 // owners
    per_slot = block_refs[0].shape[0] // slots
    me = lax.axis_index("kx") * ht_count + lax.axis_index("ht")
    for position, block_ref in enumerate(block_refs):
        ordered[me ^ step_at(owners, position)] = block_ref[...]
    for c in range(components):
        for mode in range(band_modes):
            for tile in range(rows // LANES):
                parts = []
                for p in range(2):
                    row = ((tile * 2 + p) * components + c) * band_modes + mode
                    for owner in range(owners):
                        parts.append(ordered[owner, pl.ds(row, slots, stride=per_slot), :])
                top, rest = two_parts(jnp.concatenate(parts, axis=0))
                both = jnp.concatenate([top, rest], axis=0)
                out_ref[c, mode, pl.ds(tile * LANES, LANES)] = dot(
                    both, order_ref[...], ((0,), (0,))
                )


def restore(blocks, order, components, band_modes, rows, ht_count):
    columns = order.shape[1]
    return pl.pallas_call(
        functools.partial(restore_kernel, owners=len(blocks), ht_count=ht_count),
        out_shape=jax.ShapeDtypeStruct((components, band_modes, rows, columns), jnp.float32),
        in_specs=[VMEM] * (len(blocks) + 1),
        out_specs=VMEM,
        scratch_shapes=[pltpu.VMEM((len(blocks),) + blocks[0].shape, jnp.float32)],
        compiler_params=params(),
        cost_estimate=cost(8 * components * band_modes * rows * columns),
        name="restore",
    )(*blocks, order)


def exchange(blocks, axes):
    count, realizations = (len(blocks), lax.axis_size("real"))
    result = list(blocks)
    for position in range(1, count):
        steps = [order[position] for order in steps_of(count)]
        pairs = [
            (index * realizations + r, (index ^ steps[r % 2]) * realizations + r)
            for index in range(count)
            for r in range(realizations)
        ]
        result[position] = lax.ppermute(blocks[position], axes + ("real",), pairs)
    return result


def swap(value, step):
    pairs = [(index, index ^ step) for index in range(lax.axis_size("real"))]
    return lax.ppermute(value, "real", pairs)


def local(velocity, low_index, neighbours, owner_map, mode_counts, helmholtz):
    components, reals_dev, band_modes, rows_ht, columns = velocity.shape
    kx_count, ht_count = (lax.axis_size("kx"), lax.axis_size("ht"))
    own_kx, own_ht = (lax.axis_index("kx"), lax.axis_index("ht"))
    owners, pieces, real_count = (kx_count * ht_count, PIECES, lax.axis_size("real"))
    rows = rows_ht // (kx_count * pieces)
    groups = LANES // rows if rows else 0
    slots = columns // 2 // owners
    if (
        columns != LANES or reals_dev != 1 or rows_ht % LANES or rows % 8 or LANES % rows or kx_count % groups or kx_count & (kx_count - 1)
        or (band_modes * 2 * components) % 8 or slots % 8 or owners & (owners - 1) or low_index.shape[0] >= kx_count * band_modes
        or low_index.shape[0] >= columns or low_index.shape[0] % 2 or real_count < 2 or real_count & (real_count - 1)
    ):
        return local_plain(velocity, low_index, neighbours, owner_map, mode_counts, helmholtz)
    realizations, members = (real_count, low_index.shape[0])
    chunks, modes = (components * band_modes, band_modes * kx_count)
    shape = (components, modes, rows, columns)
    extra_rows = -(-band_modes // 8) * 8
    split = velocity.reshape(chunks, pieces, kx_count, rows, columns)
    first_blocks, rest = pack(split, neighbours, mode_counts, extra_rows)
    parts = [exchange(first_blocks, ("kx",))] + [
        (lax.all_to_all(block, "kx", split_axis=0, concat_axis=0, tiled=True),) for block in rest
    ]
    tables, order, slot_modes = slot_tables(owner_map, columns)
    small = 0.0
    for index, block in enumerate(parts[0]):
        lines = block[chunks * rows : chunks * rows + band_modes, : members + 1]
        here = (own_kx ^ step_at(kx_count, index)) == jnp.arange(kx_count)
        small = small + jnp.where(here[:, None, None], lines[None], 0.0)
    small = small.reshape(modes, members + 1).astype(jnp.int32)
    neighbours, mode_counts = (small[:, :-1], small[:, -1])
    after = slot_modes
    received = []
    for piece, part in enumerate(parts):
        slotted, kept, sent = nonlinear(
            part, shape, low_index, neighbours, mode_counts, tables, slot_modes, after
        )
        kept = after = kept + swap(sent, 1)
        step = 2
        while step < realizations:
            kept = kept + swap(kept, step)
            step *= 2
        blocks = outgoing(
            slotted, kept, swap(kept, 1), low_index, mode_counts, slot_modes, groups, band_modes,
            owners, realizations, piece > 0,
        )
        if piece:
            received += exchange([block.reshape(slots, -1, LANES) for block in blocks], ("kx", "ht"))
        else:
            block = blocks[0].reshape(owners, slots, -1, LANES)
            first = lax.all_to_all(block, ("kx", "ht"), split_axis=0, concat_axis=0, tiled=True)
    solved = solve(first, received, helmholtz, pieces, groups, kx_count, ht_count)
    returned = [block.reshape(-1, LANES) for block in exchange(solved, ("kx", "ht"))]
    result = restore(returned, order, components, band_modes, rows_ht, ht_count)
    return result.reshape(velocity.shape)


def solution(mesh):
    in_specs = (
        P(None, "real", "kx", "ht", None),
        P(),
        P("kx", None),
        P(),
        P("kx"),
        P(("kx", "ht"), None, None),
    )
    out_specs = P(None, "real", "kx", "ht", None)
    return jax.shard_map(local, mesh=mesh, in_specs=in_specs, out_specs=out_specs, check_vma=False)
```

```python
import functools

import jax
import jax.numpy as jnp
import numpy as np
from jax import lax
from jax.experimental import pallas as pl
from jax.experimental.pallas import tpu as pltpu
from jax.sharding import PartitionSpec as P

dt_step = 0.1


def spanwise_tables(mode_count, point_count):
    column_ids = jnp.arange(2 * mode_count)
    wavenumber = (column_ids // 2).astype(jnp.float32)
    imag_part = column_ids % 2
    positions = 2.0 * jnp.pi * jnp.arange(point_count).astype(jnp.float32) / point_count
    phases = wavenumber[:, None] * positions[None, :]
    forward = jnp.where(imag_part[:, None] == 0, jnp.cos(phases), -jnp.sin(phases)) / jnp.sqrt(
        jnp.float32(mode_count)
    )
    backward = forward.T * (2.0 * mode_count / point_count)
    return (forward, backward)


def nonlinear_rows(fields, low_index, neighbours, mode_counts, forward, backward):
    precision = lax.Precision.HIGH
    realizations, modes, columns = (fields.shape[1], fields.shape[2], fields.shape[4])
    low_select = (low_index[:, None] == jnp.arange(modes)[None, :]).astype(jnp.float32)
    high_mask = 1.0 - jnp.sum(low_select, axis=0)
    high_rows = high_mask[None, None, :, None, None]
    column_mask = ((jnp.arange(columns) // 2)[None, :] < mode_counts[:, None]).astype(jnp.float32)
    physical = jnp.dot(fields, forward, precision=precision)
    low_fields = jnp.take(physical, low_index, axis=2)
    high_low = jnp.zeros_like(physical)
    stresses = []
    for member in range(low_index.shape[0]):
        partner = jnp.take(physical, neighbours[:, member], axis=2)
        low_one = low_fields[:, :, member : member + 1]
        high_low = high_low + low_one * partner[1:2] + partner * low_one[1:2]
        stresses.append(jnp.sum(physical * (partner[1:2] * high_rows), axis=(1, 2)))
    stress = jnp.stack(stresses, axis=1) / realizations
    forcing = jnp.dot(high_low, backward, precision=precision) * high_rows
    low_forcing = jnp.dot(stress, backward, precision=precision)
    low_rows = jnp.einsum("jm,cjyk->cmyk", low_select, low_forcing, precision=lax.Precision.HIGHEST)
    forcing = (forcing + low_rows[:, None]) * column_mask[None, None, :, None, :]
    return fields + dt_step * forcing


def local_plain(velocity, low_index, neighbours, owner_map, mode_counts, helmholtz):
    components, reals_dev, band_modes, rows_ht, columns = velocity.shape
    kz_modes = columns // 2
    forward, backward = spanwise_tables(kz_modes, 4 * kz_modes)
    kx_count, ht_count = (lax.axis_size("kx"), lax.axis_size("ht"))
    real_count = lax.axis_size("real")
    modes, realizations = (band_modes * kx_count, reals_dev * real_count)
    slots_dev = kz_modes // (kx_count * ht_count)
    rows_dev = rows_ht // (kx_count * real_count)
    small = jnp.concatenate([neighbours, mode_counts[:, None]], axis=1)
    small = lax.all_gather(small, "kx", axis=0, tiled=True)
    neighbours, mode_counts = (small[:, :-1], small[:, -1])
    inverse_map = (
        jnp.zeros((kz_modes,), jnp.int32).at[owner_map].set(jnp.arange(kz_modes, dtype=jnp.int32))
    )
    split = velocity.reshape(
        components, reals_dev, band_modes, kx_count * real_count, rows_dev, columns
    )
    split = split.transpose(3, 0, 1, 2, 4, 5)
    split = lax.all_to_all(split, ("kx", "real"), split_axis=0, concat_axis=0, tiled=True)
    fields = split.reshape(
        kx_count, real_count, components, reals_dev, band_modes, rows_dev, columns
    )
    fields = fields.transpose(2, 1, 3, 0, 4, 5, 6).reshape(
        components, realizations, modes, rows_dev, columns
    )
    updated = nonlinear_rows(fields, low_index, neighbours, mode_counts, forward, backward)
    slotted = jnp.take(
        updated.reshape(components, realizations, modes, rows_dev, kz_modes, 2), owner_map, axis=4
    )
    slotted = slotted.reshape(
        components, real_count, reals_dev, modes, rows_dev, kx_count * ht_count, slots_dev, 2
    )
    outgoing = slotted.transpose(5, 1, 6, 2, 0, 3, 7, 4).reshape(
        kx_count * ht_count * real_count, slots_dev, reals_dev * components * modes * 2, rows_dev
    )
    incoming = lax.all_to_all(
        outgoing, ("kx", "ht", "real"), split_axis=0, concat_axis=0, tiled=True
    )
    incoming = incoming.reshape(
        kx_count, ht_count, real_count, slots_dev, reals_dev * components * modes * 2, rows_dev
    )
    incoming = incoming.transpose(3, 4, 1, 0, 2, 5).reshape(
        slots_dev, reals_dev * components * modes * 2, ht_count * rows_ht
    )
    solved = jnp.einsum("syx,snx->sny", helmholtz, incoming, precision=lax.Precision.HIGH)
    solved = solved.reshape(
        slots_dev, reals_dev, components, kx_count, band_modes, 2, ht_count, rows_ht
    )
    solved = solved.transpose(3, 6, 0, 5, 1, 2, 4, 7).reshape(
        kx_count * ht_count, slots_dev * 2, reals_dev * components * band_modes, rows_ht
    )
    returned = lax.all_to_all(solved, ("kx", "ht"), split_axis=0, concat_axis=0, tiled=True)
    restored = returned.reshape(
        kz_modes, 2, reals_dev, components, band_modes, rows_ht
    )
    restored = jnp.take(restored, inverse_map, axis=0)
    return restored.transpose(3, 2, 4, 5, 0, 1).reshape(velocity.shape)


LANES = 128
PIECES = 2
VMEM = pl.BlockSpec(memory_space=pltpu.VMEM)
SMEM = pl.BlockSpec(memory_space=pltpu.SMEM)


def params():
    return pltpu.CompilerParams(vmem_limit_bytes=48 * 1024 * 1024)


ORDERS = {4: (1, 3, 2), 8: (4, 1, 2, 6, 5, 3, 7)}


def steps_of(count):
    even = ORDERS.get(count, tuple(range(1, count)))
    odd = list(even)
    for first in range(0, count - 2, 2):
        odd[first], odd[first + 1] = (even[first + 1], even[first])
    return (0,) + tuple(even), (0,) + tuple(odd)


def step_at(count, position):
    even, odd = steps_of(count)
    return jnp.where((lax.axis_index("real") & 1) == 0, even[position], odd[position])


def cost(size):
    return pl.CostEstimate(flops=0, bytes_accessed=size, transcendentals=0)


def two_parts(value):
    top = value.astype(jnp.bfloat16)
    rest = (value - top.astype(jnp.float32)).astype(jnp.bfloat16)
    return top, rest


def dot(left, right, dims=((1,), (0,))):
    return lax.dot_general(left, right, (dims, ((), ())), preferred_element_type=jnp.float32)


def pack_first_kernel(near_ref, count_ref, velocity_ref, *out_refs):
    chunks, _, kx_count, rows, columns = velocity_ref.shape
    shape = (out_refs[0].shape[0] - chunks * rows, columns)
    row = lax.broadcasted_iota(jnp.int32, shape, 0)
    lane = lax.broadcasted_iota(jnp.int32, shape, 1)
    extra = jnp.zeros(shape, jnp.int32)
    modes, members = near_ref.shape
    for mode in range(modes):
        line = jnp.where(lane == members, count_ref[mode], 0)
        for member in range(members):
            line = jnp.where(lane == member, near_ref[mode, member], line)
        extra = jnp.where(row == mode, line, extra)
    extra = extra.astype(jnp.float32)
    own = lax.axis_index("kx")
    for index, out_ref in enumerate(out_refs):
        partner = own ^ step_at(kx_count, index)
        for chunk in range(chunks):
            out_ref[chunk * rows : (chunk + 1) * rows] = velocity_ref[chunk, 0, partner]
        out_ref[chunks * rows :] = extra


def pack_first(velocity, neighbours, mode_counts, extra_rows):
    chunks, _, kx_count, rows, columns = velocity.shape
    shape = jax.ShapeDtypeStruct((chunks * rows + extra_rows, columns), jnp.float32)
    return pl.pallas_call(
        pack_first_kernel,
        out_shape=(shape,) * kx_count,
        grid=(1,),
        in_specs=[
            SMEM,
            SMEM,
            pl.BlockSpec((chunks, 1, kx_count, rows, columns), lambda i: (0, 0, 0, 0, 0)),
        ],
        out_specs=(pl.BlockSpec(shape.shape, lambda i: (0, 0)),) * kx_count,
        cost_estimate=cost(4 * velocity.size),
        name="pack_first",
    )(neighbours, mode_counts, velocity)


def pack_kernel(velocity_ref, _, out_ref):
    chunks, _, kx_count, rows, columns = velocity_ref.shape
    for index in range(kx_count):
        for chunk in range(chunks):
            place = slice(chunk * rows, (chunk + 1) * rows)
            out_ref[index, place] = velocity_ref[chunk, 0, index]


def pack(velocity, piece, after):
    chunks, _, kx_count, rows, columns = velocity.shape
    shape = (kx_count, chunks * rows, columns)
    return pl.pallas_call(
        pack_kernel,
        out_shape=jax.ShapeDtypeStruct(shape, jnp.float32),
        grid=(1,),
        in_specs=[
            pl.BlockSpec((chunks, 1, kx_count, rows, columns), lambda i: (0, piece, 0, 0, 0)),
            pl.BlockSpec(memory_space=pl.ANY),
        ],
        out_specs=pl.BlockSpec(shape, lambda i: (0, 0, 0)),
        cost_estimate=cost(4 * velocity.size),
        name="pack",
    )(velocity, after)


def tables_kernel(owner_ref, top_ref, rest_ref, first_ref, back_ref, order_ref, slot_ref):
    columns = slot_ref.shape[1]
    modes = columns // 2
    lane = lax.broadcasted_iota(jnp.int32, (8, columns), 1)
    mode = jnp.zeros((8, columns), jnp.int32)
    for slot in range(modes):
        mode = jnp.where(lane % modes == slot, owner_ref[slot], mode)
    slot_ref[...] = mode
    wanted = 2 * mode + lane // modes
    row = lax.broadcasted_iota(jnp.int32, (columns, columns), 0)
    chosen = (row == wanted[:1]).astype(jnp.float32)
    select = chosen.astype(jnp.bfloat16)
    points = top_ref.shape[1]
    for half in range(2):
        rows = slice(half * columns, (half + 1) * columns)
        first_ref[rows, :points] = top_ref[...]
        first_ref[rows, points:] = select
        order_ref[rows] = chosen.T.astype(jnp.bfloat16)
    for index, table_ref in enumerate((top_ref, rest_ref)):
        back = dot(table_ref[...], select, ((0,), (0,))) * (2.0 * modes / points)
        back_ref[:, index * columns : (index + 1) * columns] = back.astype(jnp.bfloat16)


def spanwise_constants(columns, points):
    mode = np.arange(columns) // 2
    phase = 2.0 * np.pi * ((mode[:, None] * np.arange(points)[None, :]) % points) / points
    forward = np.where(np.arange(columns)[:, None] % 2 == 0, np.cos(phase), -np.sin(phase))
    forward = (forward / np.sqrt(columns // 2)).astype(np.float32)
    top = forward.astype(jnp.bfloat16)
    rest = (forward - top.astype(np.float32)).astype(jnp.bfloat16)
    return jnp.asarray(top), jnp.asarray(rest)


def slot_tables(owner_map, columns):
    points = 2 * columns
    top, rest = spanwise_constants(columns, points)
    first, back, order, slot_modes = pl.pallas_call(
        tables_kernel,
        out_shape=(
            jax.ShapeDtypeStruct((2 * columns, points + columns), jnp.bfloat16),
            jax.ShapeDtypeStruct((points, 2 * columns), jnp.bfloat16),
            jax.ShapeDtypeStruct((2 * columns, columns), jnp.bfloat16),
            jax.ShapeDtypeStruct((8, columns), jnp.int32),
        ),
        in_specs=[SMEM, VMEM, VMEM],
        out_specs=(VMEM,) * 4,
        compiler_params=params(),
        cost_estimate=cost(16 * points * columns),
        name="tables",
    )(owner_map, top, rest)
    return (first, rest, back), order, slot_modes


def nonlinear_kernel(low_ref, near_ref, count_ref, *refs):
    block_refs, refs = (refs[:-12], refs[-12:])
    first_ref, second_ref, back_ref, slot_ref, _, slotted_ref, kept_ref, sent_ref = refs[:8]
    physical, products, sums, high_ref = refs[8:]
    components, modes, rows, columns = slotted_ref.shape
    if len(block_refs) > 1:
        bands = len(block_refs)
        places = [lax.axis_index("kx") ^ step_at(bands, index) for index in range(bands)]
    else:
        bands = block_refs[0].shape[0]
        places = list(range(bands))
        block_refs = [block_refs[0].at[index] for index in range(bands)]
    points, band_modes = (physical.shape[3], modes // bands)
    members, highs = (sums.shape[1], products.shape[1])
    odd = (lax.axis_index("real") & 1) == 1
    found = jnp.int32(0)
    for mode in range(modes):
        is_low = jnp.int32(0)
        for member in range(members):
            is_low = is_low | (low_ref[member] == mode).astype(jnp.int32)
        high_ref[found] = mode
        found = found + 1 - is_low

    def transform(component, carry):
        size = band_modes * rows
        for index, block_ref in enumerate(block_refs):
            top, rest = two_parts(block_ref[pl.ds(pl.multiple_of(component * size, 8), size)])
            both = dot(jnp.concatenate([top, rest], axis=1), first_ref[...])
            fields = both[:, :points] + dot(top, second_ref[...])
            place = pl.ds(places[index] * band_modes, band_modes)
            physical[component, place] = fields.reshape(band_modes, rows, points)
            slotted_ref[component, place] = both[:, points:].reshape(band_modes, rows, columns)
        return carry

    lax.fori_loop(0, components, transform, 0)

    def pairs(step, carry):
        halves = points // LANES
        place = (
            pl.ds(pl.multiple_of((step // halves) * 8, 8), 8),
            pl.ds(pl.multiple_of((step % halves) * LANES, LANES), LANES),
        )

        def one_high(index, totals):
            mode = high_ref[index]
            own = [physical[(c, mode) + place] for c in range(components)]
            result = [jnp.zeros((8, LANES), jnp.float32) for _ in range(components)]
            totals = list(totals)
            for member in range(members):
                low = low_ref[member]
                near = near_ref[mode, member]
                partner = [physical[(c, near) + place] for c in range(components)]
                low_one = [physical[(c, low) + place] for c in range(components)]
                for c in range(components):
                    if c == 1:
                        result[c] = result[c] + low_one[1] * partner[1]
                    else:
                        result[c] = result[c] + (low_one[c] * partner[1] + partner[c] * low_one[1])
                    slot = member * components + c
                    totals[slot] = totals[slot] + own[c] * partner[1]
            for c in range(components):
                products[(c, index) + place] = result[c] * 2.0 if c == 1 else result[c]
            return tuple(totals)

        empty = tuple(jnp.zeros((8, LANES), jnp.float32) for _ in range(members * components))
        totals = lax.fori_loop(0, highs, one_high, empty)
        for member in range(members):
            for c in range(components):
                sums[(c, member) + place] = totals[member * components + c]
        return carry

    lax.fori_loop(0, (rows // 8) * (points // LANES), pairs, 0)

    def inverse(fields):
        top, rest = two_parts(fields)
        both = dot(top, back_ref[...])
        return both[:, :columns] + both[:, columns:] + dot(rest, back_ref[:, :columns])

    def finish(component, carry):
        forcing = inverse(products[component].reshape(highs * rows, points))
        forcing = forcing.reshape(highs, rows, columns)
        for index in range(highs):
            mode = high_ref[index]
            active = slot_ref[:1] < count_ref[mode]
            slotted_ref[component, mode] += jnp.where(active, forcing[index] * dt_step, 0.0)
        stress = inverse(sums[component].reshape(members * rows, points))
        stress = stress.reshape(2, members // 2, rows, columns)
        kept_ref[component] = jnp.where(odd, stress[1], stress[0])
        sent_ref[component] = jnp.where(odd, stress[0], stress[1])
        return carry

    lax.fori_loop(0, components, finish, 0)


def nonlinear(blocks, shape, low_index, neighbours, mode_counts, tables, slot_modes, after):
    components, modes, rows, columns = shape
    members, points = (low_index.shape[0], 2 * columns)
    highs = modes - members
    return pl.pallas_call(
        nonlinear_kernel,
        out_shape=(
            jax.ShapeDtypeStruct((components, modes, rows, columns), jnp.float32),
            jax.ShapeDtypeStruct((components, members // 2, rows, columns), jnp.float32),
            jax.ShapeDtypeStruct((components, members // 2, rows, columns), jnp.float32),
        ),
        in_specs=[SMEM] * 3 + [VMEM] * (len(blocks) + 4) + [pl.BlockSpec(memory_space=pl.ANY)],
        out_specs=(VMEM, VMEM, VMEM),
        scratch_shapes=[
            pltpu.VMEM((components, modes, rows, points), jnp.float32),
            pltpu.VMEM((components, highs, rows, points), jnp.float32),
            pltpu.VMEM((components, members, rows, points), jnp.float32),
            pltpu.SMEM((modes + 1,), jnp.int32),
        ],
        compiler_params=params(),
        cost_estimate=cost(8 * components * modes * rows * points * members),
        name="nonlinear",
    )(low_index, neighbours, mode_counts, *blocks, *tables, slot_modes, after)


def outgoing_kernel(
    low_ref, count_ref, slotted_ref, kept_ref, other_ref, slot_ref, *refs,
    groups, band_modes, owners, scale
):
    out_refs, (full, turned) = (refs[:-2], refs[-2:])
    components, modes, rows, columns = slotted_ref.shape
    half, slots = (kept_ref.shape[1], columns // 2 // owners)
    per_slot = out_refs[0].shape[0] * len(out_refs) // (columns // 2)
    own = lax.axis_index("real") & 1
    full[...] = slotted_ref[...]
    for member in range(half):
        for part_ref, start in ((kept_ref, own * half), (other_ref, (1 - own) * half)):
            mode = low_ref[start + member]
            active = slot_ref[:1] < count_ref[mode]
            for c in range(components):
                full[c, mode] += jnp.where(active, part_ref[c, member] * scale, 0.0)
    inner = modes // groups
    if len(out_refs) > 1:
        me = lax.axis_index("kx") * lax.axis_size("ht") + lax.axis_index("ht")
        targets = [me ^ step_at(owners, position) for position in range(owners)]
    for c in range(components):
        for part in range(inner):
            tile = jnp.concatenate([full[c, part + inner * g] for g in range(groups)], axis=0)
            band_low, band_mode = (part // band_modes, part % band_modes)
            if len(out_refs) > 1:
                turned[...] = tile.T
            else:
                value = tile.T
            for p in range(2):
                row = ((band_low * 2 + p) * components + c) * band_modes + band_mode
                if len(out_refs) == 1:
                    out_refs[0][pl.ds(row, columns // 2, stride=per_slot), :] = value[
                        p * (columns // 2) : (p + 1) * (columns // 2)
                    ]
                    continue
                for out_ref, target in zip(out_refs, targets):
                    start = pl.multiple_of((p * owners + target) * slots, slots)
                    out_ref[pl.ds(row, slots, stride=per_slot), :] = turned[pl.ds(start, slots)]


def outgoing(
    slotted, kept, other, low_index, mode_counts, slot_modes, groups, band_modes, owners,
    realizations, separate,
):
    components, modes, rows, columns = slotted.shape
    total, lanes = ((columns // 2) * (modes // groups) * 2 * components, groups * rows)
    count = owners if separate else 1
    return pl.pallas_call(
        functools.partial(
            outgoing_kernel, groups=groups, band_modes=band_modes, owners=owners,
            scale=dt_step / realizations,
        ),
        out_shape=(jax.ShapeDtypeStruct((total // count, lanes), jnp.float32),) * count,
        in_specs=[SMEM, SMEM] + [VMEM] * 4,
        out_specs=(VMEM,) * count,
        scratch_shapes=[
            pltpu.VMEM(slotted.shape, jnp.float32), pltpu.VMEM((columns, lanes), jnp.float32)
        ],
        compiler_params=params(),
        cost_estimate=cost(8 * slotted.size),
        name="outgoing",
    )(low_index, mode_counts, slotted, kept, other, slot_modes)


def regroup(blocks, rows):
    count = len(blocks)
    lane = lax.broadcasted_iota(jnp.int32, blocks[0].shape, 1) // rows
    step = 1
    while step < count:
        take = (lane & step) == 0
        for i in range(count):
            if i & step == 0:
                here, there = (blocks[i], blocks[i + step])
                blocks[i] = jnp.where(take, here, pltpu.roll(there, step * rows, 1))
                blocks[i + step] = jnp.where(
                    take, pltpu.roll(here, LANES - step * rows, 1), there
                )
        step *= 2
    return blocks


def solve_kernel(*refs, groups, kx_count, ht_count, pieces):
    owners = kx_count * ht_count
    first_ref, refs = (refs[0], refs[1:])
    count = owners * (pieces - 1)
    block_refs, matrix_ref, refs = (refs[:count], refs[count], refs[count + 1 :])
    out_refs, (matrices, arrived, ordered, full) = (refs[:owners], refs[owners:])
    slots, heights = (matrix_ref.shape[0], matrix_ref.shape[1])
    copies = [
        pltpu.make_async_copy(matrix_ref.at[s], matrices.at[s], arrived.at[s])
        for s in range(slots)
    ]
    for copy in copies:
        copy.start()
    own_kx, own_ht = (lax.axis_index("kx"), lax.axis_index("ht"))
    partners = []
    for position in range(owners):
        step = step_at(owners, position)
        partners.append((own_kx ^ (step // ht_count), own_ht ^ (step % ht_count)))
    for index, block_ref in enumerate(block_refs):
        kx, ht = partners[index % owners]
        ordered[index // owners, kx * ht_count + ht] = block_ref[...]
    rows, (lane_tiles, per_band) = (LANES // groups, out_refs[0].shape[1:3])
    for s in range(slots):
        tiles = []
        for h in range(ht_count):
            for piece in range(pieces):
                source = first_ref if piece == 0 else ordered.at[piece - 1]
                for first in range(0, kx_count, groups):
                    blocks = [source[(first + g) * ht_count + h, s] for g in range(groups)]
                    tiles.append(jnp.concatenate(regroup(blocks, rows), axis=0))
        top, rest = two_parts(jnp.concatenate(tiles, axis=1))
        count = top.shape[0]
        copies[s].wait()
        matrix_top, matrix_rest = two_parts(matrices[s])
        last = ((1,), (1,))
        both = dot(matrix_top, jnp.concatenate([top, rest], axis=0), last)
        solved = both[:, :count] + both[:, count:] + dot(matrix_rest, top, last)
        for tile in range(heights // LANES):
            full[s % 2, tile] = solved[tile * LANES : (tile + 1) * LANES].T
        for out_ref, (kx, ht) in zip(out_refs, partners):
            band = pl.ds(pl.multiple_of(kx * per_band, 8), per_band)
            for tile in range(lane_tiles):
                out_ref[s, tile] = full[s % 2, ht * lane_tiles + tile, band]


def solve(first, blocks, helmholtz, pieces, groups, kx_count, ht_count):
    owners, slots, per_slot, lanes = first.shape
    heights, count = (helmholtz.shape[1], per_slot * groups)
    shape = (slots, heights // ht_count // LANES, count // kx_count, LANES)
    return pl.pallas_call(
        functools.partial(
            solve_kernel, groups=groups, kx_count=kx_count, ht_count=ht_count, pieces=pieces
        ),
        out_shape=(jax.ShapeDtypeStruct(shape, jnp.float32),) * owners,
        in_specs=[VMEM] * (1 + len(blocks)) + [pl.BlockSpec(memory_space=pl.ANY)],
        out_specs=(VMEM,) * owners,
        scratch_shapes=[
            pltpu.VMEM(helmholtz.shape, jnp.float32),
            pltpu.SemaphoreType.DMA((slots,)),
            pltpu.VMEM((max(pieces - 1, 1),) + first.shape, jnp.float32),
            pltpu.VMEM((2, heights // LANES, count, LANES), jnp.float32),
        ],
        compiler_params=params(),
        cost_estimate=cost(4 * helmholtz.size),
        name="solve",
    )(first, *blocks, helmholtz)


def restore_kernel(*refs, owners, ht_count):
    block_refs, (order_ref, out_ref, ordered) = (refs[:-3], refs[-3:])
    components, band_modes, rows, columns = out_ref.shape
    slots = columns // 2 // owners
    per_slot = block_refs[0].shape[0] // slots
    me = lax.axis_index("kx") * ht_count + lax.axis_index("ht")
    for position, block_ref in enumerate(block_refs):
        ordered[me ^ step_at(owners, position)] = block_ref[...]
    for c in range(components):
        for mode in range(band_modes):
            for tile in range(rows // LANES):
                parts = []
                for p in range(2):
                    row = ((tile * 2 + p) * components + c) * band_modes + mode
                    for owner in range(owners):
                        parts.append(ordered[owner, pl.ds(row, slots, stride=per_slot), :])
                top, rest = two_parts(jnp.concatenate(parts, axis=0))
                both = jnp.concatenate([top, rest], axis=0)
                out_ref[c, mode, pl.ds(tile * LANES, LANES)] = dot(
                    both, order_ref[...], ((0,), (0,))
                )


def restore(blocks, order, components, band_modes, rows, ht_count):
    columns = order.shape[1]
    return pl.pallas_call(
        functools.partial(restore_kernel, owners=len(blocks), ht_count=ht_count),
        out_shape=jax.ShapeDtypeStruct((components, band_modes, rows, columns), jnp.float32),
        in_specs=[VMEM] * (len(blocks) + 1),
        out_specs=VMEM,
        scratch_shapes=[pltpu.VMEM((len(blocks),) + blocks[0].shape, jnp.float32)],
        compiler_params=params(),
        cost_estimate=cost(8 * components * band_modes * rows * columns),
        name="restore",
    )(*blocks, order)


def exchange(blocks, axes):
    count, realizations = (len(blocks), lax.axis_size("real"))
    result = list(blocks)
    for position in range(1, count):
        steps = [order[position] for order in steps_of(count)]
        pairs = [
            (index * realizations + r, (index ^ steps[r % 2]) * realizations + r)
            for index in range(count)
            for r in range(realizations)
        ]
        result[position] = lax.ppermute(blocks[position], axes + ("real",), pairs)
    return result


def swap(value, step):
    pairs = [(index, index ^ step) for index in range(lax.axis_size("real"))]
    return lax.ppermute(value, "real", pairs)


def local(velocity, low_index, neighbours, owner_map, mode_counts, helmholtz):
    components, reals_dev, band_modes, rows_ht, columns = velocity.shape
    kx_count, ht_count = (lax.axis_size("kx"), lax.axis_size("ht"))
    own_kx, own_ht = (lax.axis_index("kx"), lax.axis_index("ht"))
    owners, pieces, real_count = (kx_count * ht_count, PIECES, lax.axis_size("real"))
    rows = rows_ht // (kx_count * pieces)
    groups = LANES // rows if rows else 0
    slots = columns // 2 // owners
    if (
        columns != LANES or reals_dev != 1 or rows_ht % LANES or rows % 8 or LANES % rows or kx_count % groups or kx_count & (kx_count - 1)
        or (band_modes * 2 * components) % 8 or slots % 8 or owners & (owners - 1) or low_index.shape[0] >= kx_count * band_modes
        or low_index.shape[0] >= columns or low_index.shape[0] % 2 or real_count < 2 or real_count & (real_count - 1)
    ):
        return local_plain(velocity, low_index, neighbours, owner_map, mode_counts, helmholtz)
    realizations, members = (real_count, low_index.shape[0])
    chunks, modes = (components * band_modes, band_modes * kx_count)
    shape = (components, modes, rows, columns)
    extra_rows = -(-band_modes // 8) * 8
    split = velocity.reshape(chunks, pieces, kx_count, rows, columns)
    blocks = pack_first(split, neighbours, mode_counts, extra_rows)
    parts = [exchange(blocks, ("kx",))]
    for piece in range(1, pieces):
        block = pack(split, piece, parts[0][1])
        block = lax.all_to_all(block, "kx", split_axis=0, concat_axis=0, tiled=True)
        parts.append((block,))
    tables, order, slot_modes = slot_tables(owner_map, columns)
    small = 0.0
    for index, block in enumerate(parts[0]):
        lines = block[chunks * rows : chunks * rows + band_modes, : members + 1]
        here = (own_kx ^ step_at(kx_count, index)) == jnp.arange(kx_count)
        small = small + jnp.where(here[:, None, None], lines[None], 0.0)
    small = small.reshape(modes, members + 1).astype(jnp.int32)
    neighbours, mode_counts = (small[:, :-1], small[:, -1])
    after = slot_modes
    received = []
    for piece, part in enumerate(parts):
        slotted, kept, sent = nonlinear(
            part, shape, low_index, neighbours, mode_counts, tables, slot_modes, after
        )
        kept = after = kept + swap(sent, 1)
        step = 2
        while step < realizations:
            kept = kept + swap(kept, step)
            step *= 2
        blocks = outgoing(
            slotted, kept, swap(kept, 1), low_index, mode_counts, slot_modes, groups, band_modes,
            owners, realizations, piece > 0,
        )
        if piece:
            received += exchange([block.reshape(slots, -1, LANES) for block in blocks], ("kx", "ht"))
        else:
            block = blocks[0].reshape(owners, slots, -1, LANES)
            first = lax.all_to_all(block, ("kx", "ht"), split_axis=0, concat_axis=0, tiled=True)
    solved = solve(first, received, helmholtz, pieces, groups, kx_count, ht_count)
    returned = [block.reshape(-1, LANES) for block in exchange(solved, ("kx", "ht"))]
    result = restore(returned, order, components, band_modes, rows_ht, ht_count)
    return result.reshape(velocity.shape)


def solution(mesh):
    in_specs = (
        P(None, "real", "kx", "ht", None),
        P(),
        P("kx", None),
        P(),
        P("kx"),
        P(("kx", "ht"), None, None),
    )
    out_specs = P(None, "real", "kx", "ht", None)
    return jax.shard_map(local, mesh=mesh, in_specs=in_specs, out_specs=out_specs, check_vma=False)
```

```python
import functools

import jax
import jax.numpy as jnp
import numpy as np
from jax import lax
from jax.experimental import pallas as pl
from jax.experimental.pallas import tpu as pltpu
from jax.sharding import PartitionSpec as P

dt_step = 0.1


def spanwise_tables(mode_count, point_count):
    column_ids = jnp.arange(2 * mode_count)
    wavenumber = (column_ids // 2).astype(jnp.float32)
    imag_part = column_ids % 2
    positions = 2.0 * jnp.pi * jnp.arange(point_count).astype(jnp.float32) / point_count
    phases = wavenumber[:, None] * positions[None, :]
    forward = jnp.where(imag_part[:, None] == 0, jnp.cos(phases), -jnp.sin(phases)) / jnp.sqrt(
        jnp.float32(mode_count)
    )
    backward = forward.T * (2.0 * mode_count / point_count)
    return (forward, backward)


def nonlinear_rows(fields, low_index, neighbours, mode_counts, forward, backward):
    precision = lax.Precision.HIGH
    realizations, modes, columns = (fields.shape[1], fields.shape[2], fields.shape[4])
    low_select = (low_index[:, None] == jnp.arange(modes)[None, :]).astype(jnp.float32)
    high_mask = 1.0 - jnp.sum(low_select, axis=0)
    high_rows = high_mask[None, None, :, None, None]
    column_mask = ((jnp.arange(columns) // 2)[None, :] < mode_counts[:, None]).astype(jnp.float32)
    physical = jnp.dot(fields, forward, precision=precision)
    low_fields = jnp.take(physical, low_index, axis=2)
    high_low = jnp.zeros_like(physical)
    stresses = []
    for member in range(low_index.shape[0]):
        partner = jnp.take(physical, neighbours[:, member], axis=2)
        low_one = low_fields[:, :, member : member + 1]
        high_low = high_low + low_one * partner[1:2] + partner * low_one[1:2]
        stresses.append(jnp.sum(physical * (partner[1:2] * high_rows), axis=(1, 2)))
    stress = jnp.stack(stresses, axis=1) / realizations
    forcing = jnp.dot(high_low, backward, precision=precision) * high_rows
    low_forcing = jnp.dot(stress, backward, precision=precision)
    low_rows = jnp.einsum("jm,cjyk->cmyk", low_select, low_forcing, precision=lax.Precision.HIGHEST)
    forcing = (forcing + low_rows[:, None]) * column_mask[None, None, :, None, :]
    return fields + dt_step * forcing


def local_plain(velocity, low_index, neighbours, owner_map, mode_counts, helmholtz):
    components, reals_dev, band_modes, rows_ht, columns = velocity.shape
    kz_modes = columns // 2
    forward, backward = spanwise_tables(kz_modes, 4 * kz_modes)
    kx_count, ht_count = (lax.axis_size("kx"), lax.axis_size("ht"))
    real_count = lax.axis_size("real")
    modes, realizations = (band_modes * kx_count, reals_dev * real_count)
    slots_dev = kz_modes // (kx_count * ht_count)
    rows_dev = rows_ht // (kx_count * real_count)
    small = jnp.concatenate([neighbours, mode_counts[:, None]], axis=1)
    small = lax.all_gather(small, "kx", axis=0, tiled=True)
    neighbours, mode_counts = (small[:, :-1], small[:, -1])
    inverse_map = (
        jnp.zeros((kz_modes,), jnp.int32).at[owner_map].set(jnp.arange(kz_modes, dtype=jnp.int32))
    )
    split = velocity.reshape(
        components, reals_dev, band_modes, kx_count * real_count, rows_dev, columns
    )
    split = split.transpose(3, 0, 1, 2, 4, 5)
    split = lax.all_to_all(split, ("kx", "real"), split_axis=0, concat_axis=0, tiled=True)
    fields = split.reshape(
        kx_count, real_count, components, reals_dev, band_modes, rows_dev, columns
    )
    fields = fields.transpose(2, 1, 3, 0, 4, 5, 6).reshape(
        components, realizations, modes, rows_dev, columns
    )
    updated = nonlinear_rows(fields, low_index, neighbours, mode_counts, forward, backward)
    slotted = jnp.take(
        updated.reshape(components, realizations, modes, rows_dev, kz_modes, 2), owner_map, axis=4
    )
    slotted = slotted.reshape(
        components, real_count, reals_dev, modes, rows_dev, kx_count * ht_count, slots_dev, 2
    )
    outgoing = slotted.transpose(5, 1, 6, 2, 0, 3, 7, 4).reshape(
        kx_count * ht_count * real_count, slots_dev, reals_dev * components * modes * 2, rows_dev
    )
    incoming = lax.all_to_all(
        outgoing, ("kx", "ht", "real"), split_axis=0, concat_axis=0, tiled=True
    )
    incoming = incoming.reshape(
        kx_count, ht_count, real_count, slots_dev, reals_dev * components * modes * 2, rows_dev
    )
    incoming = incoming.transpose(3, 4, 1, 0, 2, 5).reshape(
        slots_dev, reals_dev * components * modes * 2, ht_count * rows_ht
    )
    solved = jnp.einsum("syx,snx->sny", helmholtz, incoming, precision=lax.Precision.HIGH)
    solved = solved.reshape(
        slots_dev, reals_dev, components, kx_count, band_modes, 2, ht_count, rows_ht
    )
    solved = solved.transpose(3, 6, 0, 5, 1, 2, 4, 7).reshape(
        kx_count * ht_count, slots_dev * 2, reals_dev * components * band_modes, rows_ht
    )
    returned = lax.all_to_all(solved, ("kx", "ht"), split_axis=0, concat_axis=0, tiled=True)
    restored = returned.reshape(
        kz_modes, 2, reals_dev, components, band_modes, rows_ht
    )
    restored = jnp.take(restored, inverse_map, axis=0)
    return restored.transpose(3, 2, 4, 5, 0, 1).reshape(velocity.shape)


LANES = 128
PIECES = 2
VMEM = pl.BlockSpec(memory_space=pltpu.VMEM)
SMEM = pl.BlockSpec(memory_space=pltpu.SMEM)


def params():
    return pltpu.CompilerParams(vmem_limit_bytes=48 * 1024 * 1024)


ORDERS = {4: (1, 3, 2), 8: (4, 1, 2, 6, 5, 3, 7)}


def steps_of(count):
    even = ORDERS.get(count, tuple(range(1, count)))
    odd = list(even)
    for first in range(0, count - 2, 2):
        odd[first], odd[first + 1] = (even[first + 1], even[first])
    return (0,) + tuple(even), (0,) + tuple(odd)


def step_at(count, position):
    even, odd = steps_of(count)
    return jnp.where((lax.axis_index("real") & 1) == 0, even[position], odd[position])


def cost(size):
    return pl.CostEstimate(flops=0, bytes_accessed=size, transcendentals=0)


def two_parts(value):
    top = value.astype(jnp.bfloat16)
    rest = (value - top.astype(jnp.float32)).astype(jnp.bfloat16)
    return top, rest


def dot(left, right, dims=((1,), (0,))):
    return lax.dot_general(left, right, (dims, ((), ())), preferred_element_type=jnp.float32)


def pack_first_kernel(near_ref, count_ref, velocity_ref, *out_refs):
    chunks, _, kx_count, rows, columns = velocity_ref.shape
    shape = (out_refs[0].shape[0] - chunks * rows, columns)
    row = lax.broadcasted_iota(jnp.int32, shape, 0)
    lane = lax.broadcasted_iota(jnp.int32, shape, 1)
    extra = jnp.zeros(shape, jnp.int32)
    modes, members = near_ref.shape
    for mode in range(modes):
        line = jnp.where(lane == members, count_ref[mode], 0)
        for member in range(members):
            line = jnp.where(lane == member, near_ref[mode, member], line)
        extra = jnp.where(row == mode, line, extra)
    extra = extra.astype(jnp.float32)
    own = lax.axis_index("kx")
    for index, out_ref in enumerate(out_refs):
        partner = own ^ step_at(kx_count, index)
        for chunk in range(chunks):
            out_ref[chunk * rows : (chunk + 1) * rows] = velocity_ref[chunk, 0, partner]
        out_ref[chunks * rows :] = extra


def pack_first(velocity, neighbours, mode_counts, extra_rows):
    chunks, _, kx_count, rows, columns = velocity.shape
    shape = jax.ShapeDtypeStruct((chunks * rows + extra_rows, columns), jnp.float32)
    return pl.pallas_call(
        pack_first_kernel,
        out_shape=(shape,) * kx_count,
        grid=(1,),
        in_specs=[
            SMEM,
            SMEM,
            pl.BlockSpec((chunks, 1, kx_count, rows, columns), lambda i: (0, 0, 0, 0, 0)),
        ],
        out_specs=(pl.BlockSpec(shape.shape, lambda i: (0, 0)),) * kx_count,
        cost_estimate=cost(4 * velocity.size),
        name="pack_first",
    )(neighbours, mode_counts, velocity)


def pack_kernel(velocity_ref, _, out_ref):
    chunks, _, kx_count, rows, columns = velocity_ref.shape
    for index in range(kx_count):
        for chunk in range(chunks):
            place = slice(chunk * rows, (chunk + 1) * rows)
            out_ref[index, place] = velocity_ref[chunk, 0, index]


def pack(velocity, piece, after):
    chunks, _, kx_count, rows, columns = velocity.shape
    shape = (kx_count, chunks * rows, columns)
    return pl.pallas_call(
        pack_kernel,
        out_shape=jax.ShapeDtypeStruct(shape, jnp.float32),
        grid=(1,),
        in_specs=[
            pl.BlockSpec((chunks, 1, kx_count, rows, columns), lambda i: (0, piece, 0, 0, 0)),
            pl.BlockSpec(memory_space=pl.ANY),
        ],
        out_specs=pl.BlockSpec(shape, lambda i: (0, 0, 0)),
        cost_estimate=cost(4 * velocity.size),
        name="pack",
    )(velocity, after)


def tables_kernel(owner_ref, top_ref, rest_ref, first_ref, back_ref, order_ref, slot_ref):
    columns = slot_ref.shape[1]
    modes = columns // 2
    lane = lax.broadcasted_iota(jnp.int32, (8, columns), 1)
    mode = jnp.zeros((8, columns), jnp.int32)
    for slot in range(modes):
        mode = jnp.where(lane % modes == slot, owner_ref[slot], mode)
    slot_ref[...] = mode
    wanted = 2 * mode + lane // modes
    row = lax.broadcasted_iota(jnp.int32, (columns, columns), 0)
    chosen = (row == wanted[:1]).astype(jnp.float32)
    select = chosen.astype(jnp.bfloat16)
    points = top_ref.shape[1]
    for half in range(2):
        rows = slice(half * columns, (half + 1) * columns)
        first_ref[rows, :points] = top_ref[...]
        first_ref[rows, points:] = select
        order_ref[rows] = chosen.T.astype(jnp.bfloat16)
    for index, table_ref in enumerate((top_ref, rest_ref)):
        back = dot(table_ref[...], select, ((0,), (0,))) * (2.0 * modes / points)
        back_ref[:, index * columns : (index + 1) * columns] = back.astype(jnp.bfloat16)


def spanwise_constants(columns, points):
    mode = np.arange(columns) // 2
    phase = 2.0 * np.pi * ((mode[:, None] * np.arange(points)[None, :]) % points) / points
    forward = np.where(np.arange(columns)[:, None] % 2 == 0, np.cos(phase), -np.sin(phase))
    forward = (forward / np.sqrt(columns // 2)).astype(np.float32)
    top = forward.astype(jnp.bfloat16)
    rest = (forward - top.astype(np.float32)).astype(jnp.bfloat16)
    return jnp.asarray(top), jnp.asarray(rest)


def slot_tables(owner_map, columns):
    points = 2 * columns
    top, rest = spanwise_constants(columns, points)
    first, back, order, slot_modes = pl.pallas_call(
        tables_kernel,
        out_shape=(
            jax.ShapeDtypeStruct((2 * columns, points + columns), jnp.bfloat16),
            jax.ShapeDtypeStruct((points, 2 * columns), jnp.bfloat16),
            jax.ShapeDtypeStruct((2 * columns, columns), jnp.bfloat16),
            jax.ShapeDtypeStruct((8, columns), jnp.int32),
        ),
        in_specs=[SMEM, VMEM, VMEM],
        out_specs=(VMEM,) * 4,
        compiler_params=params(),
        cost_estimate=cost(16 * points * columns),
        name="tables",
    )(owner_map, top, rest)
    return (first, rest, back), order, slot_modes


def list_high(low_ref, high_ref, modes):
    found = jnp.int32(0)
    for mode in range(modes):
        is_low = jnp.int32(0)
        for member in range(low_ref.shape[0]):
            is_low = is_low | (low_ref[member] == mode).astype(jnp.int32)
        high_ref[found] = mode
        found = found + 1 - is_low


def tile_at(step, points):
    halves = points // LANES
    return (
        pl.ds(pl.multiple_of((step // halves) * 8, 8), 8),
        pl.ds(pl.multiple_of((step % halves) * LANES, LANES), LANES),
    )


def inverse(fields, back_ref):
    columns = back_ref.shape[1] // 2
    top, rest = two_parts(fields)
    both = dot(top, back_ref[...])
    return both[:, :columns] + both[:, columns:] + dot(rest, back_ref[:, :columns])


def stress_kernel(low_ref, near_ref, *refs):
    block_refs, refs = (refs[:-10], refs[-10:])
    first_ref, second_ref, back_ref, _ = refs[:4]
    slotted_ref, physical, kept_ref, sent_ref, sums, high_ref = refs[4:]
    components, modes, rows, columns = slotted_ref.shape
    if len(block_refs) > 1:
        bands = len(block_refs)
        places = [lax.axis_index("kx") ^ step_at(bands, index) for index in range(bands)]
    else:
        bands = block_refs[0].shape[0]
        places = list(range(bands))
        block_refs = [block_refs[0].at[index] for index in range(bands)]
    points, band_modes = (physical.shape[3], modes // bands)
    members = sums.shape[1]
    odd = (lax.axis_index("real") & 1) == 1
    list_high(low_ref, high_ref, modes)
    size = band_modes * rows
    for c in range(components):
        joined = [block_ref[c * size : (c + 1) * size] for block_ref in block_refs]
        top, rest = two_parts(jnp.concatenate(joined, axis=0))
        both = dot(jnp.concatenate([top, rest], axis=1), first_ref[...])
        fields = both[:, :points] + dot(top, second_ref[...])
        for index in range(bands):
            place = pl.ds(places[index] * band_modes, band_modes)
            part = slice(index * size, (index + 1) * size)
            physical[c, place] = fields[part].reshape(band_modes, rows, points)
            slotted_ref[c, place] = both[part, points:].reshape(band_modes, rows, columns)

    def pairs(step, carry):
        place = tile_at(step, points)

        def one_high(index, totals):
            mode = high_ref[index]
            own = [physical[(c, mode) + place] for c in range(components)]
            totals = list(totals)
            for member in range(members):
                partner = physical[(1, near_ref[mode, member]) + place]
                for c in range(components):
                    slot = member * components + c
                    totals[slot] = totals[slot] + own[c] * partner
            return tuple(totals)

        empty = tuple(jnp.zeros((8, LANES), jnp.float32) for _ in range(members * components))
        totals = lax.fori_loop(0, modes - members, one_high, empty)
        for member in range(members):
            for c in range(components):
                sums[(c, member) + place] = totals[member * components + c]
        return carry

    lax.fori_loop(0, (rows // 8) * (points // LANES), pairs, 0)
    stress = inverse(sums[...].reshape(components * members * rows, points), back_ref)
    stress = stress.reshape(components, 2, members // 2, rows, columns)
    kept_ref[...] = jnp.where(odd, stress[:, 1], stress[:, 0])
    sent_ref[...] = jnp.where(odd, stress[:, 0], stress[:, 1])


def stress_terms(blocks, shape, low_index, neighbours, tables, after):
    components, modes, rows, columns = shape
    members, points = (low_index.shape[0], 2 * columns)
    half = jax.ShapeDtypeStruct((components, members // 2, rows, columns), jnp.float32)
    return pl.pallas_call(
        stress_kernel,
        out_shape=(
            jax.ShapeDtypeStruct(shape, jnp.float32),
            jax.ShapeDtypeStruct((components, modes, rows, points), jnp.float32),
            half,
            half,
        ),
        in_specs=[SMEM] * 2 + [VMEM] * (len(blocks) + 3) + [pl.BlockSpec(memory_space=pl.ANY)],
        out_specs=(VMEM,) * 4,
        scratch_shapes=[
            pltpu.VMEM((components, members, rows, points), jnp.float32),
            pltpu.SMEM((modes + 1,), jnp.int32),
        ],
        compiler_params=params(),
        cost_estimate=cost(4 * components * modes * rows * points * members),
        name="stress",
    )(low_index, neighbours, *blocks, *tables, after)


def products_kernel(
    low_ref, near_ref, count_ref, physical, back_ref, slot_ref, out_ref, products, high_ref
):
    components, modes, rows, points = physical.shape
    members, highs = (low_ref.shape[0], out_ref.shape[1])
    list_high(low_ref, high_ref, modes)

    def pairs(step, carry):
        place = tile_at(step, points)
        low = [
            [physical[(c, low_ref[member]) + place] for c in range(components)]
            for member in range(members)
        ]

        def one_high(index, inner):
            mode = high_ref[index]
            result = [jnp.zeros((8, LANES), jnp.float32) for _ in range(components)]
            for member in range(members):
                near = near_ref[mode, member]
                partner = [physical[(c, near) + place] for c in range(components)]
                for c in range(components):
                    if c == 1:
                        result[c] = result[c] + low[member][1] * partner[1]
                    else:
                        result[c] = result[c] + (
                            low[member][c] * partner[1] + partner[c] * low[member][1]
                        )
            for c in range(components):
                products[(c, index) + place] = result[c] * 2.0 if c == 1 else result[c]
            return inner

        lax.fori_loop(0, highs, one_high, 0)
        return carry

    lax.fori_loop(0, (rows // 8) * (points // LANES), pairs, 0)
    forcing = inverse(products[...].reshape(components * highs * rows, points), back_ref)
    forcing = forcing.reshape(out_ref.shape)
    for index in range(highs):
        active = slot_ref[:1] < count_ref[high_ref[index]]
        out_ref[:, index] = jnp.where(active, forcing[:, index] * dt_step, 0.0)


def high_terms(physical, low_index, neighbours, mode_counts, back, slot_modes):
    components, modes, rows, points = physical.shape
    highs = modes - low_index.shape[0]
    return pl.pallas_call(
        products_kernel,
        out_shape=jax.ShapeDtypeStruct((components, highs, rows, points // 2), jnp.float32),
        in_specs=[SMEM] * 3 + [VMEM] * 3,
        out_specs=VMEM,
        scratch_shapes=[
            pltpu.VMEM((components, highs, rows, points), jnp.float32),
            pltpu.SMEM((modes + 1,), jnp.int32),
        ],
        compiler_params=params(),
        cost_estimate=cost(4 * physical.size * low_index.shape[0]),
        name="products",
    )(low_index, neighbours, mode_counts, physical, back, slot_modes)


def outgoing_kernel(
    low_ref, count_ref, slotted_ref, forcing_ref, kept_ref, other_ref, slot_ref, *refs,
    groups, band_modes, owners, scale
):
    out_refs, (full, turned, high_ref) = (refs[:-3], refs[-3:])
    components, modes, rows, columns = slotted_ref.shape
    half, slots = (kept_ref.shape[1], columns // 2 // owners)
    per_slot = out_refs[0].shape[0] * len(out_refs) // (columns // 2)
    own = lax.axis_index("real") & 1
    list_high(low_ref, high_ref, modes)
    full[...] = slotted_ref[...]
    for index in range(forcing_ref.shape[1]):
        for c in range(components):
            full[c, high_ref[index]] += forcing_ref[c, index]
    for member in range(half):
        for part_ref, start in ((kept_ref, own * half), (other_ref, (1 - own) * half)):
            mode = low_ref[start + member]
            active = slot_ref[:1] < count_ref[mode]
            for c in range(components):
                full[c, mode] += jnp.where(active, part_ref[c, member] * scale, 0.0)
    inner = modes // groups
    if len(out_refs) > 1:
        me = lax.axis_index("kx") * lax.axis_size("ht") + lax.axis_index("ht")
        targets = [me ^ step_at(owners, position) for position in range(owners)]
    for c in range(components):
        for part in range(inner):
            tile = jnp.concatenate([full[c, part + inner * g] for g in range(groups)], axis=0)
            band_low, band_mode = (part // band_modes, part % band_modes)
            if len(out_refs) > 1:
                turned[...] = tile.T
            else:
                value = tile.T
            for p in range(2):
                row = ((band_low * 2 + p) * components + c) * band_modes + band_mode
                if len(out_refs) == 1:
                    out_refs[0][pl.ds(row, columns // 2, stride=per_slot), :] = value[
                        p * (columns // 2) : (p + 1) * (columns // 2)
                    ]
                    continue
                for out_ref, target in zip(out_refs, targets):
                    start = pl.multiple_of((p * owners + target) * slots, slots)
                    out_ref[pl.ds(row, slots, stride=per_slot), :] = turned[pl.ds(start, slots)]


def outgoing(
    slotted, forcing, kept, other, low_index, mode_counts, slot_modes, groups, band_modes, owners,
    realizations, separate,
):
    components, modes, rows, columns = slotted.shape
    total, lanes = ((columns // 2) * (modes // groups) * 2 * components, groups * rows)
    count = owners if separate else 1
    return pl.pallas_call(
        functools.partial(
            outgoing_kernel, groups=groups, band_modes=band_modes, owners=owners,
            scale=dt_step / realizations,
        ),
        out_shape=(jax.ShapeDtypeStruct((total // count, lanes), jnp.float32),) * count,
        in_specs=[SMEM, SMEM] + [VMEM] * 5,
        out_specs=(VMEM,) * count,
        scratch_shapes=[
            pltpu.VMEM(slotted.shape, jnp.float32), pltpu.VMEM((columns, lanes), jnp.float32),
            pltpu.SMEM((modes + 1,), jnp.int32),
        ],
        compiler_params=params(),
        cost_estimate=cost(8 * slotted.size),
        name="outgoing",
    )(low_index, mode_counts, slotted, forcing, kept, other, slot_modes)


def regroup(blocks, rows):
    count = len(blocks)
    lane = lax.broadcasted_iota(jnp.int32, blocks[0].shape, 1) // rows
    step = 1
    while step < count:
        take = (lane & step) == 0
        for i in range(count):
            if i & step == 0:
                here, there = (blocks[i], blocks[i + step])
                blocks[i] = jnp.where(take, here, pltpu.roll(there, step * rows, 1))
                blocks[i + step] = jnp.where(
                    take, pltpu.roll(here, LANES - step * rows, 1), there
                )
        step *= 2
    return blocks


def solve_kernel(*refs, groups, kx_count, ht_count, pieces):
    owners = kx_count * ht_count
    first_ref, refs = (refs[0], refs[1:])
    count = owners * (pieces - 1)
    block_refs, matrix_ref, refs = (refs[:count], refs[count], refs[count + 1 :])
    out_refs, (matrices, arrived, ordered, full) = (refs[:owners], refs[owners:])
    slots, heights = (matrix_ref.shape[0], matrix_ref.shape[1])
    copies = [
        pltpu.make_async_copy(matrix_ref.at[s], matrices.at[s], arrived.at[s])
        for s in range(slots)
    ]
    for copy in copies:
        copy.start()
    own_kx, own_ht = (lax.axis_index("kx"), lax.axis_index("ht"))
    partners = []
    for position in range(owners):
        step = step_at(owners, position)
        partners.append((own_kx ^ (step // ht_count), own_ht ^ (step % ht_count)))
    for index, block_ref in enumerate(block_refs):
        kx, ht = partners[index % owners]
        ordered[index // owners, kx * ht_count + ht] = block_ref[...]
    rows, (lane_tiles, per_band) = (LANES // groups, out_refs[0].shape[1:3])
    for s in range(slots):
        tiles = []
        for h in range(ht_count):
            for piece in range(pieces):
                source = first_ref if piece == 0 else ordered.at[piece - 1]
                for first in range(0, kx_count, groups):
                    blocks = [source[(first + g) * ht_count + h, s] for g in range(groups)]
                    tiles.append(jnp.concatenate(regroup(blocks, rows), axis=0))
        top, rest = two_parts(jnp.concatenate(tiles, axis=1))
        count = top.shape[0]
        copies[s].wait()
        matrix_top, matrix_rest = two_parts(matrices[s])
        last = ((1,), (1,))
        both = dot(matrix_top, jnp.concatenate([top, rest], axis=0), last)
        solved = both[:, :count] + both[:, count:] + dot(matrix_rest, top, last)
        for tile in range(heights // LANES):
            full[s % 2, tile] = solved[tile * LANES : (tile + 1) * LANES].T
        for out_ref, (kx, ht) in zip(out_refs, partners):
            band = pl.ds(pl.multiple_of(kx * per_band, 8), per_band)
            for tile in range(lane_tiles):
                out_ref[s, tile] = full[s % 2, ht * lane_tiles + tile, band]


def solve(first, blocks, helmholtz, pieces, groups, kx_count, ht_count):
    owners, slots, per_slot, lanes = first.shape
    heights, count = (helmholtz.shape[1], per_slot * groups)
    shape = (slots, heights // ht_count // LANES, count // kx_count, LANES)
    return pl.pallas_call(
        functools.partial(
            solve_kernel, groups=groups, kx_count=kx_count, ht_count=ht_count, pieces=pieces
        ),
        out_shape=(jax.ShapeDtypeStruct(shape, jnp.float32),) * owners,
        in_specs=[VMEM] * (1 + len(blocks)) + [pl.BlockSpec(memory_space=pl.ANY)],
        out_specs=(VMEM,) * owners,
        scratch_shapes=[
            pltpu.VMEM(helmholtz.shape, jnp.float32),
            pltpu.SemaphoreType.DMA((slots,)),
            pltpu.VMEM((max(pieces - 1, 1),) + first.shape, jnp.float32),
            pltpu.VMEM((2, heights // LANES, count, LANES), jnp.float32),
        ],
        compiler_params=params(),
        cost_estimate=cost(4 * helmholtz.size),
        name="solve",
    )(first, *blocks, helmholtz)


def restore_kernel(*refs, owners, ht_count):
    block_refs, (order_ref, out_ref, ordered) = (refs[:-3], refs[-3:])
    components, band_modes, rows, columns = out_ref.shape
    slots = columns // 2 // owners
    per_slot = block_refs[0].shape[0] // slots
    me = lax.axis_index("kx") * ht_count + lax.axis_index("ht")
    for position, block_ref in enumerate(block_refs):
        ordered[me ^ step_at(owners, position)] = block_ref[...]
    for c in range(components):
        for mode in range(band_modes):
            for tile in range(rows // LANES):
                parts = []
                for p in range(2):
                    row = ((tile * 2 + p) * components + c) * band_modes + mode
                    for owner in range(owners):
                        parts.append(ordered[owner, pl.ds(row, slots, stride=per_slot), :])
                top, rest = two_parts(jnp.concatenate(parts, axis=0))
                both = jnp.concatenate([top, rest], axis=0)
                out_ref[c, mode, pl.ds(tile * LANES, LANES)] = dot(
                    both, order_ref[...], ((0,), (0,))
                )


def restore(blocks, order, components, band_modes, rows, ht_count):
    columns = order.shape[1]
    return pl.pallas_call(
        functools.partial(restore_kernel, owners=len(blocks), ht_count=ht_count),
        out_shape=jax.ShapeDtypeStruct((components, band_modes, rows, columns), jnp.float32),
        in_specs=[VMEM] * (len(blocks) + 1),
        out_specs=VMEM,
        scratch_shapes=[pltpu.VMEM((len(blocks),) + blocks[0].shape, jnp.float32)],
        compiler_params=params(),
        cost_estimate=cost(8 * components * band_modes * rows * columns),
        name="restore",
    )(*blocks, order)


def exchange(blocks, axes):
    count, realizations = (len(blocks), lax.axis_size("real"))
    result = list(blocks)
    for position in range(1, count):
        steps = [order[position] for order in steps_of(count)]
        pairs = [
            (index * realizations + r, (index ^ steps[r % 2]) * realizations + r)
            for index in range(count)
            for r in range(realizations)
        ]
        result[position] = lax.ppermute(blocks[position], axes + ("real",), pairs)
    return result


def swap(value, step):
    pairs = [(index, index ^ step) for index in range(lax.axis_size("real"))]
    return lax.ppermute(value, "real", pairs)


def local(velocity, low_index, neighbours, owner_map, mode_counts, helmholtz):
    components, reals_dev, band_modes, rows_ht, columns = velocity.shape
    kx_count, ht_count = (lax.axis_size("kx"), lax.axis_size("ht"))
    own_kx, own_ht = (lax.axis_index("kx"), lax.axis_index("ht"))
    owners, pieces, real_count = (kx_count * ht_count, PIECES, lax.axis_size("real"))
    rows = rows_ht // (kx_count * pieces)
    groups = LANES // rows if rows else 0
    slots = columns // 2 // owners
    if (
        columns != LANES or reals_dev != 1 or rows_ht % LANES or rows % 8 or LANES % rows or kx_count % groups or kx_count & (kx_count - 1)
        or (band_modes * 2 * components) % 8 or slots % 8 or owners & (owners - 1) or low_index.shape[0] >= kx_count * band_modes
        or low_index.shape[0] >= columns or low_index.shape[0] % 2 or real_count < 2 or real_count & (real_count - 1)
    ):
        return local_plain(velocity, low_index, neighbours, owner_map, mode_counts, helmholtz)
    realizations, members = (real_count, low_index.shape[0])
    chunks, modes = (components * band_modes, band_modes * kx_count)
    shape = (components, modes, rows, columns)
    extra_rows = -(-band_modes // 8) * 8
    split = velocity.reshape(chunks, pieces, kx_count, rows, columns)
    blocks = pack_first(split, neighbours, mode_counts, extra_rows)
    parts = [exchange(blocks, ("kx",))]
    for piece in range(1, pieces):
        block = pack(split, piece, parts[0][1])
        block = lax.all_to_all(block, "kx", split_axis=0, concat_axis=0, tiled=True)
        parts.append((block,))
    tables, order, slot_modes = slot_tables(owner_map, columns)
    small = 0.0
    for index, block in enumerate(parts[0]):
        lines = block[chunks * rows : chunks * rows + band_modes, : members + 1]
        here = (own_kx ^ step_at(kx_count, index)) == jnp.arange(kx_count)
        small = small + jnp.where(here[:, None, None], lines[None], 0.0)
    small = small.reshape(modes, members + 1).astype(jnp.int32)
    neighbours, mode_counts = (small[:, :-1], small[:, -1])
    after = slot_modes
    received = []
    for piece, part in enumerate(parts):
        slotted, physical, kept, sent = stress_terms(
            part, shape, low_index, neighbours, tables, after
        )
        forcing = high_terms(physical, low_index, neighbours, mode_counts, tables[2], slot_modes)
        kept = after = kept + swap(sent, 1)
        step = 2
        while step < realizations:
            kept = kept + swap(kept, step)
            step *= 2
        blocks = outgoing(
            slotted, forcing, kept, swap(kept, 1), low_index, mode_counts, slot_modes, groups, band_modes,
            owners, realizations, piece > 0,
        )
        if piece:
            received += exchange([block.reshape(slots, -1, LANES) for block in blocks], ("kx", "ht"))
        else:
            block = blocks[0].reshape(owners, slots, -1, LANES)
            first = lax.all_to_all(block, ("kx", "ht"), split_axis=0, concat_axis=0, tiled=True)
    solved = solve(first, received, helmholtz, pieces, groups, kx_count, ht_count)
    returned = [block.reshape(-1, LANES) for block in exchange(solved, ("kx", "ht"))]
    result = restore(returned, order, components, band_modes, rows_ht, ht_count)
    return result.reshape(velocity.shape)


def solution(mesh):
    in_specs = (
        P(None, "real", "kx", "ht", None),
        P(),
        P("kx", None),
        P(),
        P("kx"),
        P(("kx", "ht"), None, None),
    )
    out_specs = P(None, "real", "kx", "ht", None)
    return jax.shard_map(local, mesh=mesh, in_specs=in_specs, out_specs=out_specs, check_vma=False)
```

```python
import functools

import jax
import jax.numpy as jnp
import numpy as np
from jax import lax
from jax.experimental import pallas as pl
from jax.experimental.pallas import tpu as pltpu
from jax.sharding import PartitionSpec as P

dt_step = 0.1


def spanwise_tables(mode_count, point_count):
    column_ids = jnp.arange(2 * mode_count)
    wavenumber = (column_ids // 2).astype(jnp.float32)
    imag_part = column_ids % 2
    positions = 2.0 * jnp.pi * jnp.arange(point_count).astype(jnp.float32) / point_count
    phases = wavenumber[:, None] * positions[None, :]
    forward = jnp.where(imag_part[:, None] == 0, jnp.cos(phases), -jnp.sin(phases)) / jnp.sqrt(
        jnp.float32(mode_count)
    )
    backward = forward.T * (2.0 * mode_count / point_count)
    return (forward, backward)


def nonlinear_rows(fields, low_index, neighbours, mode_counts, forward, backward):
    precision = lax.Precision.HIGH
    realizations, modes, columns = (fields.shape[1], fields.shape[2], fields.shape[4])
    low_select = (low_index[:, None] == jnp.arange(modes)[None, :]).astype(jnp.float32)
    high_mask = 1.0 - jnp.sum(low_select, axis=0)
    high_rows = high_mask[None, None, :, None, None]
    column_mask = ((jnp.arange(columns) // 2)[None, :] < mode_counts[:, None]).astype(jnp.float32)
    physical = jnp.dot(fields, forward, precision=precision)
    low_fields = jnp.take(physical, low_index, axis=2)
    high_low = jnp.zeros_like(physical)
    stresses = []
    for member in range(low_index.shape[0]):
        partner = jnp.take(physical, neighbours[:, member], axis=2)
        low_one = low_fields[:, :, member : member + 1]
        high_low = high_low + low_one * partner[1:2] + partner * low_one[1:2]
        stresses.append(jnp.sum(physical * (partner[1:2] * high_rows), axis=(1, 2)))
    stress = jnp.stack(stresses, axis=1) / realizations
    forcing = jnp.dot(high_low, backward, precision=precision) * high_rows
    low_forcing = jnp.dot(stress, backward, precision=precision)
    low_rows = jnp.einsum("jm,cjyk->cmyk", low_select, low_forcing, precision=lax.Precision.HIGHEST)
    forcing = (forcing + low_rows[:, None]) * column_mask[None, None, :, None, :]
    return fields + dt_step * forcing


def local_plain(velocity, low_index, neighbours, owner_map, mode_counts, helmholtz):
    components, reals_dev, band_modes, rows_ht, columns = velocity.shape
    kz_modes = columns // 2
    forward, backward = spanwise_tables(kz_modes, 4 * kz_modes)
    kx_count, ht_count = (lax.axis_size("kx"), lax.axis_size("ht"))
    real_count = lax.axis_size("real")
    modes, realizations = (band_modes * kx_count, reals_dev * real_count)
    slots_dev = kz_modes // (kx_count * ht_count)
    rows_dev = rows_ht // (kx_count * real_count)
    small = jnp.concatenate([neighbours, mode_counts[:, None]], axis=1)
    small = lax.all_gather(small, "kx", axis=0, tiled=True)
    neighbours, mode_counts = (small[:, :-1], small[:, -1])
    inverse_map = (
        jnp.zeros((kz_modes,), jnp.int32).at[owner_map].set(jnp.arange(kz_modes, dtype=jnp.int32))
    )
    split = velocity.reshape(
        components, reals_dev, band_modes, kx_count * real_count, rows_dev, columns
    )
    split = split.transpose(3, 0, 1, 2, 4, 5)
    split = lax.all_to_all(split, ("kx", "real"), split_axis=0, concat_axis=0, tiled=True)
    fields = split.reshape(
        kx_count, real_count, components, reals_dev, band_modes, rows_dev, columns
    )
    fields = fields.transpose(2, 1, 3, 0, 4, 5, 6).reshape(
        components, realizations, modes, rows_dev, columns
    )
    updated = nonlinear_rows(fields, low_index, neighbours, mode_counts, forward, backward)
    slotted = jnp.take(
        updated.reshape(components, realizations, modes, rows_dev, kz_modes, 2), owner_map, axis=4
    )
    slotted = slotted.reshape(
        components, real_count, reals_dev, modes, rows_dev, kx_count * ht_count, slots_dev, 2
    )
    outgoing = slotted.transpose(5, 1, 6, 2, 0, 3, 7, 4).reshape(
        kx_count * ht_count * real_count, slots_dev, reals_dev * components * modes * 2, rows_dev
    )
    incoming = lax.all_to_all(
        outgoing, ("kx", "ht", "real"), split_axis=0, concat_axis=0, tiled=True
    )
    incoming = incoming.reshape(
        kx_count, ht_count, real_count, slots_dev, reals_dev * components * modes * 2, rows_dev
    )
    incoming = incoming.transpose(3, 4, 1, 0, 2, 5).reshape(
        slots_dev, reals_dev * components * modes * 2, ht_count * rows_ht
    )
    solved = jnp.einsum("syx,snx->sny", helmholtz, incoming, precision=lax.Precision.HIGH)
    solved = solved.reshape(
        slots_dev, reals_dev, components, kx_count, band_modes, 2, ht_count, rows_ht
    )
    solved = solved.transpose(3, 6, 0, 5, 1, 2, 4, 7).reshape(
        kx_count * ht_count, slots_dev * 2, reals_dev * components * band_modes, rows_ht
    )
    returned = lax.all_to_all(solved, ("kx", "ht"), split_axis=0, concat_axis=0, tiled=True)
    restored = returned.reshape(
        kz_modes, 2, reals_dev, components, band_modes, rows_ht
    )
    restored = jnp.take(restored, inverse_map, axis=0)
    return restored.transpose(3, 2, 4, 5, 0, 1).reshape(velocity.shape)


LANES = 128
PIECES = 2
VMEM = pl.BlockSpec(memory_space=pltpu.VMEM)
SMEM = pl.BlockSpec(memory_space=pltpu.SMEM)


def params():
    return pltpu.CompilerParams(vmem_limit_bytes=48 * 1024 * 1024)


ORDERS = {4: (1, 3, 2), 8: (4, 1, 2, 6, 5, 3, 7)}


def steps_of(count):
    even = ORDERS.get(count, tuple(range(1, count)))
    odd = list(even)
    for first in range(0, count - 2, 2):
        odd[first], odd[first + 1] = (even[first + 1], even[first])
    return (0,) + tuple(even), (0,) + tuple(odd)


def step_at(count, position):
    even, odd = steps_of(count)
    return jnp.where((lax.axis_index("real") & 1) == 0, even[position], odd[position])


def cost(size):
    return pl.CostEstimate(flops=0, bytes_accessed=size, transcendentals=0)


def two_parts(value):
    top = value.astype(jnp.bfloat16)
    rest = (value - top.astype(jnp.float32)).astype(jnp.bfloat16)
    return top, rest


def dot(left, right, dims=((1,), (0,))):
    return lax.dot_general(left, right, (dims, ((), ())), preferred_element_type=jnp.float32)


def pack_first_kernel(near_ref, count_ref, velocity_ref, *out_refs):
    chunks, _, kx_count, rows, columns = velocity_ref.shape
    shape = (out_refs[0].shape[0] - chunks * rows, columns)
    row = lax.broadcasted_iota(jnp.int32, shape, 0)
    lane = lax.broadcasted_iota(jnp.int32, shape, 1)
    extra = jnp.zeros(shape, jnp.int32)
    modes, members = near_ref.shape
    for mode in range(modes):
        line = jnp.where(lane == members, count_ref[mode], 0)
        for member in range(members):
            line = jnp.where(lane == member, near_ref[mode, member], line)
        extra = jnp.where(row == mode, line, extra)
    extra = extra.astype(jnp.float32)
    own = lax.axis_index("kx")
    for index, out_ref in enumerate(out_refs):
        partner = own ^ step_at(kx_count, index)
        for chunk in range(chunks):
            out_ref[chunk * rows : (chunk + 1) * rows] = velocity_ref[chunk, 0, partner]
        out_ref[chunks * rows :] = extra


def pack_first(velocity, neighbours, mode_counts, extra_rows):
    chunks, _, kx_count, rows, columns = velocity.shape
    shape = jax.ShapeDtypeStruct((chunks * rows + extra_rows, columns), jnp.float32)
    return pl.pallas_call(
        pack_first_kernel,
        out_shape=(shape,) * kx_count,
        grid=(1,),
        in_specs=[
            SMEM,
            SMEM,
            pl.BlockSpec((chunks, 1, kx_count, rows, columns), lambda i: (0, 0, 0, 0, 0)),
        ],
        out_specs=(pl.BlockSpec(shape.shape, lambda i: (0, 0)),) * kx_count,
        cost_estimate=cost(4 * velocity.size),
        name="pack_first",
    )(neighbours, mode_counts, velocity)


def pack_kernel(velocity_ref, _, out_ref):
    chunks, _, kx_count, rows, columns = velocity_ref.shape
    for index in range(kx_count):
        for chunk in range(chunks):
            place = slice(chunk * rows, (chunk + 1) * rows)
            out_ref[index, place] = velocity_ref[chunk, 0, index]


def pack(velocity, piece, after):
    chunks, _, kx_count, rows, columns = velocity.shape
    shape = (kx_count, chunks * rows, columns)
    return pl.pallas_call(
        pack_kernel,
        out_shape=jax.ShapeDtypeStruct(shape, jnp.float32),
        grid=(1,),
        in_specs=[
            pl.BlockSpec((chunks, 1, kx_count, rows, columns), lambda i: (0, piece, 0, 0, 0)),
            pl.BlockSpec(memory_space=pl.ANY),
        ],
        out_specs=pl.BlockSpec(shape, lambda i: (0, 0, 0)),
        cost_estimate=cost(4 * velocity.size),
        name="pack",
    )(velocity, after)


def tables_kernel(owner_ref, top_ref, rest_ref, first_ref, back_ref, order_ref, slot_ref):
    columns = slot_ref.shape[1]
    modes = columns // 2
    lane = lax.broadcasted_iota(jnp.int32, (8, columns), 1)
    mode = jnp.zeros((8, columns), jnp.int32)
    for slot in range(modes):
        mode = jnp.where(lane % modes == slot, owner_ref[slot], mode)
    slot_ref[...] = mode
    wanted = 2 * mode + lane // modes
    row = lax.broadcasted_iota(jnp.int32, (columns, columns), 0)
    chosen = (row == wanted[:1]).astype(jnp.float32)
    select = chosen.astype(jnp.bfloat16)
    points = top_ref.shape[1]
    for half in range(2):
        rows = slice(half * columns, (half + 1) * columns)
        first_ref[rows, :points] = top_ref[...]
        first_ref[rows, points:] = select
        order_ref[rows] = chosen.T.astype(jnp.bfloat16)
    for index, table_ref in enumerate((top_ref, rest_ref)):
        back = dot(table_ref[...], select, ((0,), (0,))) * (2.0 * modes / points)
        back_ref[:, index * columns : (index + 1) * columns] = back.astype(jnp.bfloat16)


def spanwise_constants(columns, points):
    mode = np.arange(columns) // 2
    phase = 2.0 * np.pi * ((mode[:, None] * np.arange(points)[None, :]) % points) / points
    forward = np.where(np.arange(columns)[:, None] % 2 == 0, np.cos(phase), -np.sin(phase))
    forward = (forward / np.sqrt(columns // 2)).astype(np.float32)
    top = forward.astype(jnp.bfloat16)
    rest = (forward - top.astype(np.float32)).astype(jnp.bfloat16)
    return jnp.asarray(top), jnp.asarray(rest)


def slot_tables(owner_map, columns):
    points = 2 * columns
    top, rest = spanwise_constants(columns, points)
    first, back, order, slot_modes = pl.pallas_call(
        tables_kernel,
        out_shape=(
            jax.ShapeDtypeStruct((2 * columns, points + columns), jnp.bfloat16),
            jax.ShapeDtypeStruct((points, 2 * columns), jnp.bfloat16),
            jax.ShapeDtypeStruct((2 * columns, columns), jnp.bfloat16),
            jax.ShapeDtypeStruct((8, columns), jnp.int32),
        ),
        in_specs=[SMEM, VMEM, VMEM],
        out_specs=(VMEM,) * 4,
        compiler_params=params(),
        cost_estimate=cost(16 * points * columns),
        name="tables",
    )(owner_map, top, rest)
    return (first, rest, back), order, slot_modes


def list_high(low_ref, high_ref, modes):
    found = jnp.int32(0)
    for mode in range(modes):
        is_low = jnp.int32(0)
        for member in range(low_ref.shape[0]):
            is_low = is_low | (low_ref[member] == mode).astype(jnp.int32)
        high_ref[found] = mode
        found = found + 1 - is_low


def tile_at(step, points):
    halves = points // LANES
    return (
        pl.ds(pl.multiple_of((step // halves) * 8, 8), 8),
        pl.ds(pl.multiple_of((step % halves) * LANES, LANES), LANES),
    )


def inverse(fields, back_ref):
    columns = back_ref.shape[1] // 2
    top, rest = two_parts(fields)
    both = dot(top, back_ref[...])
    return both[:, :columns] + both[:, columns:] + dot(rest, back_ref[:, :columns])


def stress_kernel(low_ref, near_ref, *refs):
    block_refs, refs = (refs[:-10], refs[-10:])
    first_ref, second_ref, back_ref, _ = refs[:4]
    slotted_ref, physical, kept_ref, sent_ref, sums, high_ref = refs[4:]
    components, modes, rows, columns = slotted_ref.shape
    if len(block_refs) > 1:
        bands = len(block_refs)
        places = [lax.axis_index("kx") ^ step_at(bands, index) for index in range(bands)]
    else:
        bands = block_refs[0].shape[0]
        places = list(range(bands))
        block_refs = [block_refs[0].at[index] for index in range(bands)]
    points, band_modes = (physical.shape[3], modes // bands)
    members = sums.shape[1]
    odd = (lax.axis_index("real") & 1) == 1
    list_high(low_ref, high_ref, modes)
    size = band_modes * rows
    for c in range(components):
        joined = [block_ref[c * size : (c + 1) * size] for block_ref in block_refs]
        top, rest = two_parts(jnp.concatenate(joined, axis=0))
        both = dot(jnp.concatenate([top, rest], axis=1), first_ref[...])
        fields = both[:, :points] + dot(top, second_ref[...])
        for index in range(bands):
            place = pl.ds(places[index] * band_modes, band_modes)
            part = slice(index * size, (index + 1) * size)
            physical[c, place] = fields[part].reshape(band_modes, rows, points)
            slotted_ref[c, place] = both[part, points:].reshape(band_modes, rows, columns)

    def pairs(step, carry):
        place = tile_at(step, points)

        def one_high(index, totals):
            mode = high_ref[index]
            own = [physical[(c, mode) + place] for c in range(components)]
            totals = list(totals)
            for member in range(members):
                partner = physical[(1, near_ref[mode, member]) + place]
                for c in range(components):
                    slot = member * components + c
                    totals[slot] = totals[slot] + own[c] * partner
            return tuple(totals)

        empty = tuple(jnp.zeros((8, LANES), jnp.float32) for _ in range(members * components))
        totals = lax.fori_loop(0, modes - members, one_high, empty)
        for member in range(members):
            for c in range(components):
                sums[(c, member) + place] = totals[member * components + c]
        return carry

    lax.fori_loop(0, (rows // 8) * (points // LANES), pairs, 0)
    stress = inverse(sums[...].reshape(components * members * rows, points), back_ref)
    stress = stress.reshape(components, 2, members // 2, rows, columns)
    kept_ref[...] = jnp.where(odd, stress[:, 1], stress[:, 0])
    sent_ref[...] = jnp.where(odd, stress[:, 0], stress[:, 1])


def stress_terms(blocks, shape, low_index, neighbours, tables, after):
    components, modes, rows, columns = shape
    members, points = (low_index.shape[0], 2 * columns)
    half = jax.ShapeDtypeStruct((components, members // 2, rows, columns), jnp.float32)
    return pl.pallas_call(
        stress_kernel,
        out_shape=(
            jax.ShapeDtypeStruct(shape, jnp.float32),
            jax.ShapeDtypeStruct((components, modes, rows, points), jnp.float32),
            half,
            half,
        ),
        in_specs=[SMEM] * 2 + [VMEM] * (len(blocks) + 3) + [pl.BlockSpec(memory_space=pl.ANY)],
        out_specs=(VMEM,) * 4,
        scratch_shapes=[
            pltpu.VMEM((components, members, rows, points), jnp.float32),
            pltpu.SMEM((modes + 1,), jnp.int32),
        ],
        compiler_params=params(),
        cost_estimate=cost(4 * components * modes * rows * points * members),
        name="stress",
    )(low_index, neighbours, *blocks, *tables, after)


def products_kernel(
    low_ref, near_ref, count_ref, physical, back_ref, slot_ref, out_ref, products, high_ref
):
    components, modes, rows, points = physical.shape
    members, highs = (low_ref.shape[0], out_ref.shape[1])
    list_high(low_ref, high_ref, modes)

    def pairs(step, carry):
        place = tile_at(step, points)
        low = [
            [physical[(c, low_ref[member]) + place] for c in range(components)]
            for member in range(members)
        ]

        def one_high(index, inner):
            mode = high_ref[index]
            result = [jnp.zeros((8, LANES), jnp.float32) for _ in range(components)]
            for member in range(members):
                near = near_ref[mode, member]
                partner = [physical[(c, near) + place] for c in range(components)]
                for c in range(components):
                    if c == 1:
                        result[c] = result[c] + low[member][1] * partner[1]
                    else:
                        result[c] = result[c] + (
                            low[member][c] * partner[1] + partner[c] * low[member][1]
                        )
            for c in range(components):
                products[(c, index) + place] = result[c] * 2.0 if c == 1 else result[c]
            return inner

        lax.fori_loop(0, highs, one_high, 0)
        return carry

    lax.fori_loop(0, (rows // 8) * (points // LANES), pairs, 0)
    forcing = inverse(products[...].reshape(components * highs * rows, points), back_ref)
    forcing = forcing.reshape(out_ref.shape)
    for index in range(highs):
        active = slot_ref[:1] < count_ref[high_ref[index]]
        out_ref[:, index] = jnp.where(active, forcing[:, index] * dt_step, 0.0)


def high_terms(physical, low_index, neighbours, mode_counts, back, slot_modes):
    components, modes, rows, points = physical.shape
    highs = modes - low_index.shape[0]
    return pl.pallas_call(
        products_kernel,
        out_shape=jax.ShapeDtypeStruct((components, highs, rows, points // 2), jnp.float32),
        in_specs=[SMEM] * 3 + [VMEM] * 3,
        out_specs=VMEM,
        scratch_shapes=[
            pltpu.VMEM((components, highs, rows, points), jnp.float32),
            pltpu.SMEM((modes + 1,), jnp.int32),
        ],
        compiler_params=params(),
        cost_estimate=cost(4 * physical.size * low_index.shape[0]),
        name="products",
    )(low_index, neighbours, mode_counts, physical, back, slot_modes)


def outgoing_kernel(
    low_ref, count_ref, slotted_ref, forcing_ref, kept_ref, other_ref, slot_ref, *refs,
    groups, band_modes, owners, scale
):
    out_refs, (full, turned, high_ref) = (refs[:-3], refs[-3:])
    components, modes, rows, columns = slotted_ref.shape
    half, slots = (kept_ref.shape[1], columns // 2 // owners)
    per_slot = out_refs[0].shape[0] * len(out_refs) // (columns // 2)
    own = lax.axis_index("real") & 1
    list_high(low_ref, high_ref, modes)
    full[...] = slotted_ref[...]
    for index in range(forcing_ref.shape[1]):
        for c in range(components):
            full[c, high_ref[index]] += forcing_ref[c, index]
    for member in range(half):
        for part_ref, start in ((kept_ref, own * half), (other_ref, (1 - own) * half)):
            mode = low_ref[start + member]
            active = slot_ref[:1] < count_ref[mode]
            for c in range(components):
                full[c, mode] += jnp.where(active, part_ref[c, member] * scale, 0.0)
    inner = modes // groups
    if len(out_refs) > 1:
        me = lax.axis_index("kx") * lax.axis_size("ht") + lax.axis_index("ht")
        targets = [me ^ step_at(owners, position) for position in range(owners)]
    for c in range(components):
        for part in range(inner):
            tile = jnp.concatenate([full[c, part + inner * g] for g in range(groups)], axis=0)
            band_low, band_mode = (part // band_modes, part % band_modes)
            if len(out_refs) > 1:
                turned[...] = tile.T
            else:
                value = tile.T
            for p in range(2):
                row = ((band_low * 2 + p) * components + c) * band_modes + band_mode
                if len(out_refs) == 1:
                    out_refs[0][pl.ds(row, columns // 2, stride=per_slot), :] = value[
                        p * (columns // 2) : (p + 1) * (columns // 2)
                    ]
                    continue
                for out_ref, target in zip(out_refs, targets):
                    start = pl.multiple_of((p * owners + target) * slots, slots)
                    out_ref[pl.ds(row, slots, stride=per_slot), :] = turned[pl.ds(start, slots)]


def outgoing(
    slotted, forcing, kept, other, low_index, mode_counts, slot_modes, groups, band_modes, owners,
    realizations, separate,
):
    components, modes, rows, columns = slotted.shape
    total, lanes = ((columns // 2) * (modes // groups) * 2 * components, groups * rows)
    count = owners if separate else 1
    return pl.pallas_call(
        functools.partial(
            outgoing_kernel, groups=groups, band_modes=band_modes, owners=owners,
            scale=dt_step / realizations,
        ),
        out_shape=(jax.ShapeDtypeStruct((total // count, lanes), jnp.float32),) * count,
        in_specs=[SMEM, SMEM] + [VMEM] * 5,
        out_specs=(VMEM,) * count,
        scratch_shapes=[
            pltpu.VMEM(slotted.shape, jnp.float32), pltpu.VMEM((columns, lanes), jnp.float32),
            pltpu.SMEM((modes + 1,), jnp.int32),
        ],
        compiler_params=params(),
        cost_estimate=cost(8 * slotted.size),
        name="outgoing",
    )(low_index, mode_counts, slotted, forcing, kept, other, slot_modes)


def regroup(blocks, rows):
    count = len(blocks)
    lane = lax.broadcasted_iota(jnp.int32, blocks[0].shape, 1) // rows
    step = 1
    while step < count:
        take = (lane & step) == 0
        for i in range(count):
            if i & step == 0:
                here, there = (blocks[i], blocks[i + step])
                blocks[i] = jnp.where(take, here, pltpu.roll(there, step * rows, 1))
                blocks[i + step] = jnp.where(
                    take, pltpu.roll(here, LANES - step * rows, 1), there
                )
        step *= 2
    return blocks


def solve_kernel(*refs, groups, kx_count, ht_count, pieces):
    owners = kx_count * ht_count
    first_ref, refs = (refs[0], refs[1:])
    count = owners * (pieces - 1)
    block_refs, matrix_ref, refs = (refs[:count], refs[count], refs[count + 1 :])
    out_refs, (matrices, arrived, ordered, full) = (refs[:owners], refs[owners:])
    slots, heights = (matrix_ref.shape[0], matrix_ref.shape[1])
    copies = [
        pltpu.make_async_copy(matrix_ref.at[s], matrices.at[s], arrived.at[s])
        for s in range(slots)
    ]
    for copy in copies:
        copy.start()
    own_kx, own_ht = (lax.axis_index("kx"), lax.axis_index("ht"))
    partners = []
    for position in range(owners):
        step = step_at(owners, position)
        partners.append((own_kx ^ (step // ht_count), own_ht ^ (step % ht_count)))
    for index, block_ref in enumerate(block_refs):
        kx, ht = partners[index % owners]
        ordered[index // owners, kx * ht_count + ht] = block_ref[...]
    rows, (lane_tiles, per_band) = (LANES // groups, out_refs[0].shape[1:3])
    for s in range(slots):
        tiles = []
        for h in range(ht_count):
            for piece in range(pieces):
                source = first_ref if piece == 0 else ordered.at[piece - 1]
                for first in range(0, kx_count, groups):
                    blocks = [source[(first + g) * ht_count + h, s] for g in range(groups)]
                    tiles.append(jnp.concatenate(regroup(blocks, rows), axis=0))
        top, rest = two_parts(jnp.concatenate(tiles, axis=1))
        count = top.shape[0]
        copies[s].wait()
        matrix_top, matrix_rest = two_parts(matrices[s])
        last = ((1,), (1,))
        both = dot(matrix_top, jnp.concatenate([top, rest], axis=0), last)
        solved = both[:, :count] + both[:, count:] + dot(matrix_rest, top, last)
        for tile in range(heights // LANES):
            full[s % 2, tile] = solved[tile * LANES : (tile + 1) * LANES].T
        for out_ref, (kx, ht) in zip(out_refs, partners):
            band = pl.ds(pl.multiple_of(kx * per_band, 8), per_band)
            for tile in range(lane_tiles):
                out_ref[s, tile] = full[s % 2, ht * lane_tiles + tile, band]


def solve(first, blocks, helmholtz, pieces, groups, kx_count, ht_count):
    owners, slots, per_slot, lanes = first.shape
    heights, count = (helmholtz.shape[1], per_slot * groups)
    shape = (slots, heights // ht_count // LANES, count // kx_count, LANES)
    return pl.pallas_call(
        functools.partial(
            solve_kernel, groups=groups, kx_count=kx_count, ht_count=ht_count, pieces=pieces
        ),
        out_shape=(jax.ShapeDtypeStruct(shape, jnp.float32),) * owners,
        in_specs=[VMEM] * (1 + len(blocks)) + [pl.BlockSpec(memory_space=pl.ANY)],
        out_specs=(VMEM,) * owners,
        scratch_shapes=[
            pltpu.VMEM(helmholtz.shape, jnp.float32),
            pltpu.SemaphoreType.DMA((slots,)),
            pltpu.VMEM((max(pieces - 1, 1),) + first.shape, jnp.float32),
            pltpu.VMEM((2, heights // LANES, count, LANES), jnp.float32),
        ],
        compiler_params=params(),
        cost_estimate=cost(4 * helmholtz.size),
        name="solve",
    )(first, *blocks, helmholtz)


def restore_kernel(*refs, owners, ht_count):
    block_refs, (order_ref, out_ref, ordered) = (refs[:-3], refs[-3:])
    components, band_modes, rows, columns = out_ref.shape
    slots = columns // 2 // owners
    per_slot = block_refs[0].shape[0] // slots
    me = lax.axis_index("kx") * ht_count + lax.axis_index("ht")
    for position, block_ref in enumerate(block_refs):
        ordered[me ^ step_at(owners, position)] = block_ref[...]
    for c in range(components):
        for mode in range(band_modes):
            for tile in range(rows // LANES):
                parts = []
                for p in range(2):
                    row = ((tile * 2 + p) * components + c) * band_modes + mode
                    for owner in range(owners):
                        parts.append(ordered[owner, pl.ds(row, slots, stride=per_slot), :])
                top, rest = two_parts(jnp.concatenate(parts, axis=0))
                both = jnp.concatenate([top, rest], axis=0)
                out_ref[c, mode, pl.ds(tile * LANES, LANES)] = dot(
                    both, order_ref[...], ((0,), (0,))
                )


def restore(blocks, order, components, band_modes, rows, ht_count):
    columns = order.shape[1]
    return pl.pallas_call(
        functools.partial(restore_kernel, owners=len(blocks), ht_count=ht_count),
        out_shape=jax.ShapeDtypeStruct((components, band_modes, rows, columns), jnp.float32),
        in_specs=[VMEM] * (len(blocks) + 1),
        out_specs=VMEM,
        scratch_shapes=[pltpu.VMEM((len(blocks),) + blocks[0].shape, jnp.float32)],
        compiler_params=params(),
        cost_estimate=cost(8 * components * band_modes * rows * columns),
        name="restore",
    )(*blocks, order)


def exchange(blocks, axes):
    count, realizations = (len(blocks), lax.axis_size("real"))
    result = list(blocks)
    for position in range(1, count):
        steps = [order[position] for order in steps_of(count)]
        pairs = [
            (index * realizations + r, (index ^ steps[r % 2]) * realizations + r)
            for index in range(count)
            for r in range(realizations)
        ]
        result[position] = lax.ppermute(blocks[position], axes + ("real",), pairs)
    return result


def sum_kernel(first_ref, second_ref, _, out_ref):
    out_ref[...] = first_ref[...] + second_ref[...]


def ordered_sum(first, second, after):
    return pl.pallas_call(
        sum_kernel,
        out_shape=jax.ShapeDtypeStruct(first.shape, jnp.float32),
        in_specs=[VMEM, VMEM, pl.BlockSpec(memory_space=pl.ANY)],
        out_specs=VMEM,
        compiler_params=params(),
        cost_estimate=cost(12 * first.size),
        name="ordered_sum",
    )(first, second, after)


def swap(value, step):
    pairs = [(index, index ^ step) for index in range(lax.axis_size("real"))]
    return lax.ppermute(value, "real", pairs)


def local(velocity, low_index, neighbours, owner_map, mode_counts, helmholtz):
    components, reals_dev, band_modes, rows_ht, columns = velocity.shape
    kx_count, ht_count = (lax.axis_size("kx"), lax.axis_size("ht"))
    own_kx, own_ht = (lax.axis_index("kx"), lax.axis_index("ht"))
    owners, pieces, real_count = (kx_count * ht_count, PIECES, lax.axis_size("real"))
    rows = rows_ht // (kx_count * pieces)
    groups = LANES // rows if rows else 0
    slots = columns // 2 // owners
    if (
        columns != LANES or reals_dev != 1 or rows_ht % LANES or rows % 8 or LANES % rows or kx_count % groups or kx_count & (kx_count - 1)
        or (band_modes * 2 * components) % 8 or slots % 8 or owners & (owners - 1) or low_index.shape[0] >= kx_count * band_modes
        or low_index.shape[0] >= columns or low_index.shape[0] % 2 or real_count < 2 or real_count & (real_count - 1)
    ):
        return local_plain(velocity, low_index, neighbours, owner_map, mode_counts, helmholtz)
    realizations, members = (real_count, low_index.shape[0])
    chunks, modes = (components * band_modes, band_modes * kx_count)
    shape = (components, modes, rows, columns)
    extra_rows = -(-band_modes // 8) * 8
    split = velocity.reshape(chunks, pieces, kx_count, rows, columns)
    blocks = pack_first(split, neighbours, mode_counts, extra_rows)
    parts = [exchange(blocks, ("kx",))]
    for piece in range(1, pieces):
        block = pack(split, piece, parts[0][1])
        block = lax.all_to_all(block, "kx", split_axis=0, concat_axis=0, tiled=True)
        parts.append((block,))
    tables, order, slot_modes = slot_tables(owner_map, columns)
    small = 0.0
    for index, block in enumerate(parts[0]):
        lines = block[chunks * rows : chunks * rows + band_modes, : members + 1]
        here = (own_kx ^ step_at(kx_count, index)) == jnp.arange(kx_count)
        small = small + jnp.where(here[:, None, None], lines[None], 0.0)
    small = small.reshape(modes, members + 1).astype(jnp.int32)
    neighbours, mode_counts = (small[:, :-1], small[:, -1])
    after = slot_modes
    received = []
    for piece, part in enumerate(parts):
        slotted, physical, kept, sent = stress_terms(
            part, shape, low_index, neighbours, tables, after
        )
        forcing = high_terms(physical, low_index, neighbours, mode_counts, tables[2], slot_modes)
        kept = after = kept + swap(sent, 1)
        step = 2
        while step < realizations:
            kept = ordered_sum(kept, swap(kept, step), forcing)
            step *= 2
        blocks = outgoing(
            slotted, forcing, kept, swap(kept, 1), low_index, mode_counts, slot_modes, groups, band_modes,
            owners, realizations, piece > 0,
        )
        if piece:
            received += exchange([block.reshape(slots, -1, LANES) for block in blocks], ("kx", "ht"))
        else:
            block = blocks[0].reshape(owners, slots, -1, LANES)
            first = lax.all_to_all(block, ("kx", "ht"), split_axis=0, concat_axis=0, tiled=True)
    solved = solve(first, received, helmholtz, pieces, groups, kx_count, ht_count)
    returned = [block.reshape(-1, LANES) for block in exchange(solved, ("kx", "ht"))]
    result = restore(returned, order, components, band_modes, rows_ht, ht_count)
    return result.reshape(velocity.shape)


def solution(mesh):
    in_specs = (
        P(None, "real", "kx", "ht", None),
        P(),
        P("kx", None),
        P(),
        P("kx"),
        P(("kx", "ht"), None, None),
    )
    out_specs = P(None, "real", "kx", "ht", None)
    return jax.shard_map(local, mesh=mesh, in_specs=in_specs, out_specs=out_specs, check_vma=False)
```

```python
import functools

import jax
import jax.numpy as jnp
import numpy as np
from jax import lax
from jax.experimental import pallas as pl
from jax.experimental.pallas import tpu as pltpu
from jax.sharding import PartitionSpec as P

dt_step = 0.1


def spanwise_tables(mode_count, point_count):
    column_ids = jnp.arange(2 * mode_count)
    wavenumber = (column_ids // 2).astype(jnp.float32)
    imag_part = column_ids % 2
    positions = 2.0 * jnp.pi * jnp.arange(point_count).astype(jnp.float32) / point_count
    phases = wavenumber[:, None] * positions[None, :]
    forward = jnp.where(imag_part[:, None] == 0, jnp.cos(phases), -jnp.sin(phases)) / jnp.sqrt(
        jnp.float32(mode_count)
    )
    backward = forward.T * (2.0 * mode_count / point_count)
    return (forward, backward)


def nonlinear_rows(fields, low_index, neighbours, mode_counts, forward, backward):
    precision = lax.Precision.HIGH
    realizations, modes, columns = (fields.shape[1], fields.shape[2], fields.shape[4])
    low_select = (low_index[:, None] == jnp.arange(modes)[None, :]).astype(jnp.float32)
    high_mask = 1.0 - jnp.sum(low_select, axis=0)
    high_rows = high_mask[None, None, :, None, None]
    column_mask = ((jnp.arange(columns) // 2)[None, :] < mode_counts[:, None]).astype(jnp.float32)
    physical = jnp.dot(fields, forward, precision=precision)
    low_fields = jnp.take(physical, low_index, axis=2)
    high_low = jnp.zeros_like(physical)
    stresses = []
    for member in range(low_index.shape[0]):
        partner = jnp.take(physical, neighbours[:, member], axis=2)
        low_one = low_fields[:, :, member : member + 1]
        high_low = high_low + low_one * partner[1:2] + partner * low_one[1:2]
        stresses.append(jnp.sum(physical * (partner[1:2] * high_rows), axis=(1, 2)))
    stress = jnp.stack(stresses, axis=1) / realizations
    forcing = jnp.dot(high_low, backward, precision=precision) * high_rows
    low_forcing = jnp.dot(stress, backward, precision=precision)
    low_rows = jnp.einsum("jm,cjyk->cmyk", low_select, low_forcing, precision=lax.Precision.HIGHEST)
    forcing = (forcing + low_rows[:, None]) * column_mask[None, None, :, None, :]
    return fields + dt_step * forcing


def local_plain(velocity, low_index, neighbours, owner_map, mode_counts, helmholtz):
    components, reals_dev, band_modes, rows_ht, columns = velocity.shape
    kz_modes = columns // 2
    forward, backward = spanwise_tables(kz_modes, 4 * kz_modes)
    kx_count, ht_count = (lax.axis_size("kx"), lax.axis_size("ht"))
    real_count = lax.axis_size("real")
    modes, realizations = (band_modes * kx_count, reals_dev * real_count)
    slots_dev = kz_modes // (kx_count * ht_count)
    rows_dev = rows_ht // (kx_count * real_count)
    small = jnp.concatenate([neighbours, mode_counts[:, None]], axis=1)
    small = lax.all_gather(small, "kx", axis=0, tiled=True)
    neighbours, mode_counts = (small[:, :-1], small[:, -1])
    inverse_map = (
        jnp.zeros((kz_modes,), jnp.int32).at[owner_map].set(jnp.arange(kz_modes, dtype=jnp.int32))
    )
    split = velocity.reshape(
        components, reals_dev, band_modes, kx_count * real_count, rows_dev, columns
    )
    split = split.transpose(3, 0, 1, 2, 4, 5)
    split = lax.all_to_all(split, ("kx", "real"), split_axis=0, concat_axis=0, tiled=True)
    fields = split.reshape(
        kx_count, real_count, components, reals_dev, band_modes, rows_dev, columns
    )
    fields = fields.transpose(2, 1, 3, 0, 4, 5, 6).reshape(
        components, realizations, modes, rows_dev, columns
    )
    updated = nonlinear_rows(fields, low_index, neighbours, mode_counts, forward, backward)
    slotted = jnp.take(
        updated.reshape(components, realizations, modes, rows_dev, kz_modes, 2), owner_map, axis=4
    )
    slotted = slotted.reshape(
        components, real_count, reals_dev, modes, rows_dev, kx_count * ht_count, slots_dev, 2
    )
    outgoing = slotted.transpose(5, 1, 6, 2, 0, 3, 7, 4).reshape(
        kx_count * ht_count * real_count, slots_dev, reals_dev * components * modes * 2, rows_dev
    )
    incoming = lax.all_to_all(
        outgoing, ("kx", "ht", "real"), split_axis=0, concat_axis=0, tiled=True
    )
    incoming = incoming.reshape(
        kx_count, ht_count, real_count, slots_dev, reals_dev * components * modes * 2, rows_dev
    )
    incoming = incoming.transpose(3, 4, 1, 0, 2, 5).reshape(
        slots_dev, reals_dev * components * modes * 2, ht_count * rows_ht
    )
    solved = jnp.einsum("syx,snx->sny", helmholtz, incoming, precision=lax.Precision.HIGH)
    solved = solved.reshape(
        slots_dev, reals_dev, components, kx_count, band_modes, 2, ht_count, rows_ht
    )
    solved = solved.transpose(3, 6, 0, 5, 1, 2, 4, 7).reshape(
        kx_count * ht_count, slots_dev * 2, reals_dev * components * band_modes, rows_ht
    )
    returned = lax.all_to_all(solved, ("kx", "ht"), split_axis=0, concat_axis=0, tiled=True)
    restored = returned.reshape(
        kz_modes, 2, reals_dev, components, band_modes, rows_ht
    )
    restored = jnp.take(restored, inverse_map, axis=0)
    return restored.transpose(3, 2, 4, 5, 0, 1).reshape(velocity.shape)


LANES = 128
PIECES = 2
VMEM = pl.BlockSpec(memory_space=pltpu.VMEM)
SMEM = pl.BlockSpec(memory_space=pltpu.SMEM)


def params():
    return pltpu.CompilerParams(vmem_limit_bytes=48 * 1024 * 1024)


ORDERS = {4: (1, 3, 2), 8: (4, 1, 2, 6, 5, 3, 7)}


def steps_of(count):
    even = ORDERS.get(count, tuple(range(1, count)))
    odd = list(even)
    for first in range(0, count - 2, 2):
        odd[first], odd[first + 1] = (even[first + 1], even[first])
    return (0,) + tuple(even), (0,) + tuple(odd)


def step_at(count, position):
    even, odd = steps_of(count)
    return jnp.where((lax.axis_index("real") & 1) == 0, even[position], odd[position])


def cost(size):
    return pl.CostEstimate(flops=0, bytes_accessed=size, transcendentals=0)


def two_parts(value):
    top = value.astype(jnp.bfloat16)
    rest = (value - top.astype(jnp.float32)).astype(jnp.bfloat16)
    return top, rest


def dot(left, right, dims=((1,), (0,))):
    return lax.dot_general(left, right, (dims, ((), ())), preferred_element_type=jnp.float32)


def pack_first_kernel(near_ref, count_ref, velocity_ref, *out_refs):
    chunks, _, kx_count, rows, columns = velocity_ref.shape
    shape = (out_refs[0].shape[0] - chunks * rows, columns)
    row = lax.broadcasted_iota(jnp.int32, shape, 0)
    lane = lax.broadcasted_iota(jnp.int32, shape, 1)
    extra = jnp.zeros(shape, jnp.int32)
    modes, members = near_ref.shape
    for mode in range(modes):
        line = jnp.where(lane == members, count_ref[mode], 0)
        for member in range(members):
            line = jnp.where(lane == member, near_ref[mode, member], line)
        extra = jnp.where(row == mode, line, extra)
    extra = extra.astype(jnp.float32)
    own = lax.axis_index("kx")
    for index, out_ref in enumerate(out_refs):
        partner = own ^ step_at(kx_count, index)
        for chunk in range(chunks):
            out_ref[chunk * rows : (chunk + 1) * rows] = velocity_ref[chunk, 0, partner]
        out_ref[chunks * rows :] = extra


def pack_first(velocity, neighbours, mode_counts, extra_rows):
    chunks, _, kx_count, rows, columns = velocity.shape
    shape = jax.ShapeDtypeStruct((chunks * rows + extra_rows, columns), jnp.float32)
    return pl.pallas_call(
        pack_first_kernel,
        out_shape=(shape,) * kx_count,
        grid=(1,),
        in_specs=[
            SMEM,
            SMEM,
            pl.BlockSpec((chunks, 1, kx_count, rows, columns), lambda i: (0, 0, 0, 0, 0)),
        ],
        out_specs=(pl.BlockSpec(shape.shape, lambda i: (0, 0)),) * kx_count,
        cost_estimate=cost(4 * velocity.size),
        name="pack_first",
    )(neighbours, mode_counts, velocity)


def pack_kernel(velocity_ref, _, out_ref):
    chunks, _, kx_count, rows, columns = velocity_ref.shape
    for index in range(kx_count):
        for chunk in range(chunks):
            place = slice(chunk * rows, (chunk + 1) * rows)
            out_ref[index, place] = velocity_ref[chunk, 0, index]


def pack(velocity, piece, after):
    chunks, _, kx_count, rows, columns = velocity.shape
    shape = (kx_count, chunks * rows, columns)
    return pl.pallas_call(
        pack_kernel,
        out_shape=jax.ShapeDtypeStruct(shape, jnp.float32),
        grid=(1,),
        in_specs=[
            pl.BlockSpec((chunks, 1, kx_count, rows, columns), lambda i: (0, piece, 0, 0, 0)),
            pl.BlockSpec(memory_space=pl.ANY),
        ],
        out_specs=pl.BlockSpec(shape, lambda i: (0, 0, 0)),
        cost_estimate=cost(4 * velocity.size),
        name="pack",
    )(velocity, after)


def tables_kernel(owner_ref, top_ref, rest_ref, first_ref, back_ref, order_ref, slot_ref):
    columns = slot_ref.shape[1]
    modes = columns // 2
    lane = lax.broadcasted_iota(jnp.int32, (8, columns), 1)
    mode = jnp.zeros((8, columns), jnp.int32)
    for slot in range(modes):
        mode = jnp.where(lane % modes == slot, owner_ref[slot], mode)
    slot_ref[...] = mode
    wanted = 2 * mode + lane // modes
    row = lax.broadcasted_iota(jnp.int32, (columns, columns), 0)
    chosen = (row == wanted[:1]).astype(jnp.float32)
    select = chosen.astype(jnp.bfloat16)
    points = top_ref.shape[1]
    for half in range(2):
        rows = slice(half * columns, (half + 1) * columns)
        first_ref[rows, :points] = top_ref[...]
        first_ref[rows, points:] = select
        order_ref[rows] = chosen.T.astype(jnp.bfloat16)
    for index, table_ref in enumerate((top_ref, rest_ref)):
        back = dot(table_ref[...], select, ((0,), (0,))) * (2.0 * modes / points)
        back_ref[:, index * columns : (index + 1) * columns] = back.astype(jnp.bfloat16)


def spanwise_constants(columns, points):
    mode = np.arange(columns) // 2
    phase = 2.0 * np.pi * ((mode[:, None] * np.arange(points)[None, :]) % points) / points
    forward = np.where(np.arange(columns)[:, None] % 2 == 0, np.cos(phase), -np.sin(phase))
    forward = (forward / np.sqrt(columns // 2)).astype(np.float32)
    top = forward.astype(jnp.bfloat16)
    rest = (forward - top.astype(np.float32)).astype(jnp.bfloat16)
    return jnp.asarray(top), jnp.asarray(rest)


def slot_tables(owner_map, columns):
    points = 2 * columns
    top, rest = spanwise_constants(columns, points)
    first, back, order, slot_modes = pl.pallas_call(
        tables_kernel,
        out_shape=(
            jax.ShapeDtypeStruct((2 * columns, points + columns), jnp.bfloat16),
            jax.ShapeDtypeStruct((points, 2 * columns), jnp.bfloat16),
            jax.ShapeDtypeStruct((2 * columns, columns), jnp.bfloat16),
            jax.ShapeDtypeStruct((8, columns), jnp.int32),
        ),
        in_specs=[SMEM, VMEM, VMEM],
        out_specs=(VMEM,) * 4,
        compiler_params=params(),
        cost_estimate=cost(16 * points * columns),
        name="tables",
    )(owner_map, top, rest)
    return (first, rest, back), order, slot_modes


def list_high(low_ref, high_ref, modes):
    found = jnp.int32(0)
    for mode in range(modes):
        is_low = jnp.int32(0)
        for member in range(low_ref.shape[0]):
            is_low = is_low | (low_ref[member] == mode).astype(jnp.int32)
        high_ref[found] = mode
        found = found + 1 - is_low


def tile_at(step, points):
    halves = points // LANES
    return (
        pl.ds(pl.multiple_of((step // halves) * 8, 8), 8),
        pl.ds(pl.multiple_of((step % halves) * LANES, LANES), LANES),
    )


def inverse(fields, back_ref):
    columns = back_ref.shape[1] // 2
    top, rest = two_parts(fields)
    both = dot(top, back_ref[...])
    return both[:, :columns] + both[:, columns:] + dot(rest, back_ref[:, :columns])


def stress_kernel(low_ref, near_ref, *refs):
    block_refs, refs = (refs[:-10], refs[-10:])
    first_ref, second_ref, back_ref, _ = refs[:4]
    slotted_ref, physical, kept_ref, sent_ref, sums, high_ref = refs[4:]
    components, modes, rows, columns = slotted_ref.shape
    if len(block_refs) > 1:
        bands = len(block_refs)
        places = [lax.axis_index("kx") ^ step_at(bands, index) for index in range(bands)]
    else:
        bands = block_refs[0].shape[0]
        places = list(range(bands))
        block_refs = [block_refs[0].at[index] for index in range(bands)]
    points, band_modes = (physical.shape[3], modes // bands)
    members = sums.shape[1]
    odd = (lax.axis_index("real") & 1) == 1
    list_high(low_ref, high_ref, modes)
    size = band_modes * rows
    for c in range(components):
        joined = [block_ref[c * size : (c + 1) * size] for block_ref in block_refs]
        top, rest = two_parts(jnp.concatenate(joined, axis=0))
        both = dot(jnp.concatenate([top, rest], axis=1), first_ref[...])
        fields = both[:, :points] + dot(top, second_ref[...])
        for index in range(bands):
            place = pl.ds(places[index] * band_modes, band_modes)
            part = slice(index * size, (index + 1) * size)
            physical[c, place] = fields[part].reshape(band_modes, rows, points)
            slotted_ref[c, place] = both[part, points:].reshape(band_modes, rows, columns)

    def pairs(step, carry):
        place = tile_at(step, points)

        def one_high(index, totals):
            mode = high_ref[index]
            own = [physical[(c, mode) + place] for c in range(components)]
            totals = list(totals)
            for member in range(members):
                partner = physical[(1, near_ref[mode, member]) + place]
                for c in range(components):
                    slot = member * components + c
                    totals[slot] = totals[slot] + own[c] * partner
            return tuple(totals)

        empty = tuple(jnp.zeros((8, LANES), jnp.float32) for _ in range(members * components))
        totals = lax.fori_loop(0, modes - members, one_high, empty)
        for member in range(members):
            for c in range(components):
                sums[(c, member) + place] = totals[member * components + c]
        return carry

    lax.fori_loop(0, (rows // 8) * (points // LANES), pairs, 0)
    stress = inverse(sums[...].reshape(components * members * rows, points), back_ref)
    stress = stress.reshape(components, 2, members // 2, rows, columns)
    kept_ref[...] = jnp.where(odd, stress[:, 1], stress[:, 0])
    sent_ref[...] = jnp.where(odd, stress[:, 0], stress[:, 1])


def stress_terms(blocks, shape, low_index, neighbours, tables, after):
    components, modes, rows, columns = shape
    members, points = (low_index.shape[0], 2 * columns)
    half = jax.ShapeDtypeStruct((components, members // 2, rows, columns), jnp.float32)
    return pl.pallas_call(
        stress_kernel,
        out_shape=(
            jax.ShapeDtypeStruct(shape, jnp.float32),
            jax.ShapeDtypeStruct((components, modes, rows, points), jnp.float32),
            half,
            half,
        ),
        in_specs=[SMEM] * 2 + [VMEM] * (len(blocks) + 3) + [pl.BlockSpec(memory_space=pl.ANY)],
        out_specs=(VMEM,) * 4,
        scratch_shapes=[
            pltpu.VMEM((components, members, rows, points), jnp.float32),
            pltpu.SMEM((modes + 1,), jnp.int32),
        ],
        compiler_params=params(),
        cost_estimate=cost(4 * components * modes * rows * points * members),
        name="stress",
    )(low_index, neighbours, *blocks, *tables, after)


def products_kernel(
    low_ref, near_ref, count_ref, physical, back_ref, slot_ref, out_ref, products, high_ref
):
    components, modes, rows, points = physical.shape
    members, highs = (low_ref.shape[0], out_ref.shape[1])
    list_high(low_ref, high_ref, modes)

    def pairs(step, carry):
        place = tile_at(step, points)
        low = [
            [physical[(c, low_ref[member]) + place] for c in range(components)]
            for member in range(members)
        ]

        def one_high(index, inner):
            mode = high_ref[index]
            result = [jnp.zeros((8, LANES), jnp.float32) for _ in range(components)]
            for member in range(members):
                near = near_ref[mode, member]
                partner = [physical[(c, near) + place] for c in range(components)]
                for c in range(components):
                    if c == 1:
                        result[c] = result[c] + low[member][1] * partner[1]
                    else:
                        result[c] = result[c] + (
                            low[member][c] * partner[1] + partner[c] * low[member][1]
                        )
            for c in range(components):
                products[(c, index) + place] = result[c] * 2.0 if c == 1 else result[c]
            return inner

        lax.fori_loop(0, highs, one_high, 0)
        return carry

    lax.fori_loop(0, (rows // 8) * (points // LANES), pairs, 0)
    forcing = inverse(products[...].reshape(components * highs * rows, points), back_ref)
    forcing = forcing.reshape(out_ref.shape)
    for index in range(highs):
        active = slot_ref[:1] < count_ref[high_ref[index]]
        out_ref[:, index] = jnp.where(active, forcing[:, index] * dt_step, 0.0)


def high_terms(physical, low_index, neighbours, mode_counts, back, slot_modes):
    components, modes, rows, points = physical.shape
    highs = modes - low_index.shape[0]
    return pl.pallas_call(
        products_kernel,
        out_shape=jax.ShapeDtypeStruct((components, highs, rows, points // 2), jnp.float32),
        in_specs=[SMEM] * 3 + [VMEM] * 3,
        out_specs=VMEM,
        scratch_shapes=[
            pltpu.VMEM((components, highs, rows, points), jnp.float32),
            pltpu.SMEM((modes + 1,), jnp.int32),
        ],
        compiler_params=params(),
        cost_estimate=cost(4 * physical.size * low_index.shape[0]),
        name="products",
    )(low_index, neighbours, mode_counts, physical, back, slot_modes)


def outgoing_kernel(
    low_ref, count_ref, slotted_ref, forcing_ref, kept_ref, other_ref, slot_ref, *refs,
    groups, band_modes, owners, scale
):
    out_refs, (full, turned, high_ref) = (refs[:-3], refs[-3:])
    components, modes, rows, columns = slotted_ref.shape
    half, slots = (kept_ref.shape[1], columns // 2 // owners)
    per_slot = out_refs[0].shape[0] * len(out_refs) // (columns // 2)
    own = lax.axis_index("real") & 1
    list_high(low_ref, high_ref, modes)
    full[...] = slotted_ref[...]
    for index in range(forcing_ref.shape[1]):
        for c in range(components):
            full[c, high_ref[index]] += forcing_ref[c, index]
    for member in range(half):
        for part_ref, start in ((kept_ref, own * half), (other_ref, (1 - own) * half)):
            mode = low_ref[start + member]
            active = slot_ref[:1] < count_ref[mode]
            for c in range(components):
                full[c, mode] += jnp.where(active, part_ref[c, member] * scale, 0.0)
    inner = modes // groups
    if len(out_refs) > 1:
        me = lax.axis_index("kx") * lax.axis_size("ht") + lax.axis_index("ht")
        targets = [me ^ step_at(owners, position) for position in range(owners)]
    for c in range(components):
        for part in range(inner):
            tile = jnp.concatenate([full[c, part + inner * g] for g in range(groups)], axis=0)
            band_low, band_mode = (part // band_modes, part % band_modes)
            if len(out_refs) > 1:
                turned[...] = tile.T
            else:
                value = tile.T
            for p in range(2):
                row = ((band_low * 2 + p) * components + c) * band_modes + band_mode
                if len(out_refs) == 1:
                    out_refs[0][pl.ds(row, columns // 2, stride=per_slot), :] = value[
                        p * (columns // 2) : (p + 1) * (columns // 2)
                    ]
                    continue
                for out_ref, target in zip(out_refs, targets):
                    start = pl.multiple_of((p * owners + target) * slots, slots)
                    out_ref[pl.ds(row, slots, stride=per_slot), :] = turned[pl.ds(start, slots)]


def outgoing(
    slotted, forcing, kept, other, low_index, mode_counts, slot_modes, groups, band_modes, owners,
    realizations, separate,
):
    components, modes, rows, columns = slotted.shape
    total, lanes = ((columns // 2) * (modes // groups) * 2 * components, groups * rows)
    count = owners if separate else 1
    return pl.pallas_call(
        functools.partial(
            outgoing_kernel, groups=groups, band_modes=band_modes, owners=owners,
            scale=dt_step / realizations,
        ),
        out_shape=(jax.ShapeDtypeStruct((total // count, lanes), jnp.float32),) * count,
        in_specs=[SMEM, SMEM] + [VMEM] * 5,
        out_specs=(VMEM,) * count,
        scratch_shapes=[
            pltpu.VMEM(slotted.shape, jnp.float32), pltpu.VMEM((columns, lanes), jnp.float32),
            pltpu.SMEM((modes + 1,), jnp.int32),
        ],
        compiler_params=params(),
        cost_estimate=cost(8 * slotted.size),
        name="outgoing",
    )(low_index, mode_counts, slotted, forcing, kept, other, slot_modes)


def regroup(blocks, rows):
    count = len(blocks)
    lane = lax.broadcasted_iota(jnp.int32, blocks[0].shape, 1) // rows
    step = 1
    while step < count:
        take = (lane & step) == 0
        for i in range(count):
            if i & step == 0:
                here, there = (blocks[i], blocks[i + step])
                blocks[i] = jnp.where(take, here, pltpu.roll(there, step * rows, 1))
                blocks[i + step] = jnp.where(
                    take, pltpu.roll(here, LANES - step * rows, 1), there
                )
        step *= 2
    return blocks


def solve_kernel(*refs, groups, kx_count, ht_count, pieces):
    owners = kx_count * ht_count
    first_ref, refs = (refs[0], refs[1:])
    count = owners * (pieces - 1)
    block_refs, matrix_ref, refs = (refs[:count], refs[count], refs[count + 1 :])
    out_refs, (ordered, full) = (refs[:owners], refs[owners:])
    slots, heights = (matrix_ref.shape[0], matrix_ref.shape[1])
    own_kx, own_ht = (lax.axis_index("kx"), lax.axis_index("ht"))
    partners = []
    for position in range(owners):
        step = step_at(owners, position)
        partners.append((own_kx ^ (step // ht_count), own_ht ^ (step % ht_count)))
    for index, block_ref in enumerate(block_refs):
        kx, ht = partners[index % owners]
        ordered[index // owners, kx * ht_count + ht] = block_ref[...]
    rows, (lane_tiles, per_band) = (LANES // groups, out_refs[0].shape[1:3])
    for s in range(slots):
        tiles = []
        for h in range(ht_count):
            for piece in range(pieces):
                source = first_ref if piece == 0 else ordered.at[piece - 1]
                for first in range(0, kx_count, groups):
                    blocks = [source[(first + g) * ht_count + h, s] for g in range(groups)]
                    tiles.append(jnp.concatenate(regroup(blocks, rows), axis=0))
        fields = jnp.concatenate(tiles, axis=1)
        count = fields.shape[0]
        spare = -count % LANES
        if spare:
            fields = jnp.concatenate([fields, jnp.zeros((spare, heights), jnp.float32)], axis=0)
        top, rest = two_parts(fields)
        matrix_top, matrix_rest = two_parts(matrix_ref[s])
        last = ((1,), (1,))
        both = dot(matrix_top, jnp.concatenate([top, rest], axis=0), last)
        solved = both[:, : count + spare] + both[:, count + spare :] + dot(matrix_rest, top, last)
        for tile in range(heights // LANES):
            full[s % 2, tile] = solved[tile * LANES : (tile + 1) * LANES].T[:count]
        for out_ref, (kx, ht) in zip(out_refs, partners):
            band = pl.ds(pl.multiple_of(kx * per_band, 8), per_band)
            for tile in range(lane_tiles):
                out_ref[s, tile] = full[s % 2, ht * lane_tiles + tile, band]


def solve(first, blocks, helmholtz, pieces, groups, kx_count, ht_count):
    owners, slots, per_slot, lanes = first.shape
    heights, count = (helmholtz.shape[1], per_slot * groups)
    shape = (slots, heights // ht_count // LANES, count // kx_count, LANES)
    return pl.pallas_call(
        functools.partial(
            solve_kernel, groups=groups, kx_count=kx_count, ht_count=ht_count, pieces=pieces
        ),
        out_shape=(jax.ShapeDtypeStruct(shape, jnp.float32),) * owners,
        in_specs=[VMEM] * (2 + len(blocks)),
        out_specs=(VMEM,) * owners,
        scratch_shapes=[
            pltpu.VMEM((max(pieces - 1, 1),) + first.shape, jnp.float32),
            pltpu.VMEM((2, heights // LANES, count, LANES), jnp.float32),
        ],
        compiler_params=params(),
        cost_estimate=cost(4 * helmholtz.size),
        name="solve",
    )(first, *blocks, helmholtz)


def restore_kernel(*refs, owners, ht_count):
    block_refs, (order_ref, out_ref, ordered) = (refs[:-3], refs[-3:])
    components, band_modes, rows, columns = out_ref.shape
    slots = columns // 2 // owners
    per_slot = block_refs[0].shape[0] // slots
    me = lax.axis_index("kx") * ht_count + lax.axis_index("ht")
    for position, block_ref in enumerate(block_refs):
        ordered[me ^ step_at(owners, position)] = block_ref[...]
    for c in range(components):
        for mode in range(band_modes):
            for tile in range(rows // LANES):
                parts = []
                for p in range(2):
                    row = ((tile * 2 + p) * components + c) * band_modes + mode
                    for owner in range(owners):
                        parts.append(ordered[owner, pl.ds(row, slots, stride=per_slot), :])
                top, rest = two_parts(jnp.concatenate(parts, axis=0))
                both = jnp.concatenate([top, rest], axis=0)
                out_ref[c, mode, pl.ds(tile * LANES, LANES)] = dot(
                    both, order_ref[...], ((0,), (0,))
                )


def restore(blocks, order, components, band_modes, rows, ht_count):
    columns = order.shape[1]
    return pl.pallas_call(
        functools.partial(restore_kernel, owners=len(blocks), ht_count=ht_count),
        out_shape=jax.ShapeDtypeStruct((components, band_modes, rows, columns), jnp.float32),
        in_specs=[VMEM] * (len(blocks) + 1),
        out_specs=VMEM,
        scratch_shapes=[pltpu.VMEM((len(blocks),) + blocks[0].shape, jnp.float32)],
        compiler_params=params(),
        cost_estimate=cost(8 * components * band_modes * rows * columns),
        name="restore",
    )(*blocks, order)


def exchange(blocks, axes):
    count, realizations = (len(blocks), lax.axis_size("real"))
    result = list(blocks)
    for position in range(1, count):
        steps = [order[position] for order in steps_of(count)]
        pairs = [
            (index * realizations + r, (index ^ steps[r % 2]) * realizations + r)
            for index in range(count)
            for r in range(realizations)
        ]
        result[position] = lax.ppermute(blocks[position], axes + ("real",), pairs)
    return result


def sum_kernel(first_ref, second_ref, _, out_ref):
    out_ref[...] = first_ref[...] + second_ref[...]


def ordered_sum(first, second, after):
    return pl.pallas_call(
        sum_kernel,
        out_shape=jax.ShapeDtypeStruct(first.shape, jnp.float32),
        in_specs=[VMEM, VMEM, pl.BlockSpec(memory_space=pl.ANY)],
        out_specs=VMEM,
        compiler_params=params(),
        cost_estimate=cost(12 * first.size),
        name="ordered_sum",
    )(first, second, after)


def swap(value, step):
    pairs = [(index, index ^ step) for index in range(lax.axis_size("real"))]
    return lax.ppermute(value, "real", pairs)


def local(velocity, low_index, neighbours, owner_map, mode_counts, helmholtz):
    components, reals_dev, band_modes, rows_ht, columns = velocity.shape
    kx_count, ht_count = (lax.axis_size("kx"), lax.axis_size("ht"))
    own_kx, own_ht = (lax.axis_index("kx"), lax.axis_index("ht"))
    owners, pieces, real_count = (kx_count * ht_count, PIECES, lax.axis_size("real"))
    rows = rows_ht // (kx_count * pieces)
    groups = LANES // rows if rows else 0
    slots = columns // 2 // owners
    if (
        columns != LANES or reals_dev != 1 or rows_ht % LANES or rows % 8 or LANES % rows or kx_count % groups or kx_count & (kx_count - 1)
        or (band_modes * 2 * components) % 8 or slots % 8 or owners & (owners - 1) or low_index.shape[0] >= kx_count * band_modes
        or low_index.shape[0] >= columns or low_index.shape[0] % 2 or real_count < 2 or real_count & (real_count - 1)
    ):
        return local_plain(velocity, low_index, neighbours, owner_map, mode_counts, helmholtz)
    realizations, members = (real_count, low_index.shape[0])
    chunks, modes = (components * band_modes, band_modes * kx_count)
    shape = (components, modes, rows, columns)
    extra_rows = -(-band_modes // 8) * 8
    split = velocity.reshape(chunks, pieces, kx_count, rows, columns)
    blocks = pack_first(split, neighbours, mode_counts, extra_rows)
    parts = [exchange(blocks, ("kx",))]
    for piece in range(1, pieces):
        block = pack(split, piece, parts[0][1])
        block = lax.all_to_all(block, "kx", split_axis=0, concat_axis=0, tiled=True)
        parts.append((block,))
    tables, order, slot_modes = slot_tables(owner_map, columns)
    small = 0.0
    for index, block in enumerate(parts[0]):
        lines = block[chunks * rows : chunks * rows + band_modes, : members + 1]
        here = (own_kx ^ step_at(kx_count, index)) == jnp.arange(kx_count)
        small = small + jnp.where(here[:, None, None], lines[None], 0.0)
    small = small.reshape(modes, members + 1).astype(jnp.int32)
    neighbours, mode_counts = (small[:, :-1], small[:, -1])
    after = slot_modes
    received = []
    for piece, part in enumerate(parts):
        slotted, physical, kept, sent = stress_terms(
            part, shape, low_index, neighbours, tables, after
        )
        forcing = high_terms(physical, low_index, neighbours, mode_counts, tables[2], slot_modes)
        kept = after = kept + swap(sent, 1)
        step = 2
        while step < realizations:
            kept = ordered_sum(kept, swap(kept, step), forcing)
            step *= 2
        blocks = outgoing(
            slotted, forcing, kept, swap(kept, 1), low_index, mode_counts, slot_modes, groups, band_modes,
            owners, realizations, piece > 0,
        )
        if piece:
            received += exchange([block.reshape(slots, -1, LANES) for block in blocks], ("kx", "ht"))
        else:
            block = blocks[0].reshape(owners, slots, -1, LANES)
            first = lax.all_to_all(block, ("kx", "ht"), split_axis=0, concat_axis=0, tiled=True)
    solved = solve(first, received, helmholtz, pieces, groups, kx_count, ht_count)
    returned = [block.reshape(-1, LANES) for block in exchange(solved, ("kx", "ht"))]
    result = restore(returned, order, components, band_modes, rows_ht, ht_count)
    return result.reshape(velocity.shape)


def solution(mesh):
    in_specs = (
        P(None, "real", "kx", "ht", None),
        P(),
        P("kx", None),
        P(),
        P("kx"),
        P(("kx", "ht"), None, None),
    )
    out_specs = P(None, "real", "kx", "ht", None)
    return jax.shard_map(local, mesh=mesh, in_specs=in_specs, out_specs=out_specs, check_vma=False)
```

```python
import functools

import jax
import jax.numpy as jnp
import numpy as np
from jax import lax
from jax.experimental import pallas as pl
from jax.experimental.pallas import tpu as pltpu
from jax.sharding import PartitionSpec as P

dt_step = 0.1


def spanwise_tables(mode_count, point_count):
    column_ids = jnp.arange(2 * mode_count)
    wavenumber = (column_ids // 2).astype(jnp.float32)
    imag_part = column_ids % 2
    positions = 2.0 * jnp.pi * jnp.arange(point_count).astype(jnp.float32) / point_count
    phases = wavenumber[:, None] * positions[None, :]
    forward = jnp.where(imag_part[:, None] == 0, jnp.cos(phases), -jnp.sin(phases)) / jnp.sqrt(
        jnp.float32(mode_count)
    )
    backward = forward.T * (2.0 * mode_count / point_count)
    return (forward, backward)


def nonlinear_rows(fields, low_index, neighbours, mode_counts, forward, backward):
    precision = lax.Precision.HIGH
    realizations, modes, columns = (fields.shape[1], fields.shape[2], fields.shape[4])
    low_select = (low_index[:, None] == jnp.arange(modes)[None, :]).astype(jnp.float32)
    high_mask = 1.0 - jnp.sum(low_select, axis=0)
    high_rows = high_mask[None, None, :, None, None]
    column_mask = ((jnp.arange(columns) // 2)[None, :] < mode_counts[:, None]).astype(jnp.float32)
    physical = jnp.dot(fields, forward, precision=precision)
    low_fields = jnp.take(physical, low_index, axis=2)
    high_low = jnp.zeros_like(physical)
    stresses = []
    for member in range(low_index.shape[0]):
        partner = jnp.take(physical, neighbours[:, member], axis=2)
        low_one = low_fields[:, :, member : member + 1]
        high_low = high_low + low_one * partner[1:2] + partner * low_one[1:2]
        stresses.append(jnp.sum(physical * (partner[1:2] * high_rows), axis=(1, 2)))
    stress = jnp.stack(stresses, axis=1) / realizations
    forcing = jnp.dot(high_low, backward, precision=precision) * high_rows
    low_forcing = jnp.dot(stress, backward, precision=precision)
    low_rows = jnp.einsum("jm,cjyk->cmyk", low_select, low_forcing, precision=lax.Precision.HIGHEST)
    forcing = (forcing + low_rows[:, None]) * column_mask[None, None, :, None, :]
    return fields + dt_step * forcing


def local_plain(velocity, low_index, neighbours, owner_map, mode_counts, helmholtz):
    components, reals_dev, band_modes, rows_ht, columns = velocity.shape
    kz_modes = columns // 2
    forward, backward = spanwise_tables(kz_modes, 4 * kz_modes)
    kx_count, ht_count = (lax.axis_size("kx"), lax.axis_size("ht"))
    real_count = lax.axis_size("real")
    modes, realizations = (band_modes * kx_count, reals_dev * real_count)
    slots_dev = kz_modes // (kx_count * ht_count)
    rows_dev = rows_ht // (kx_count * real_count)
    small = jnp.concatenate([neighbours, mode_counts[:, None]], axis=1)
    small = lax.all_gather(small, "kx", axis=0, tiled=True)
    neighbours, mode_counts = (small[:, :-1], small[:, -1])
    inverse_map = (
        jnp.zeros((kz_modes,), jnp.int32).at[owner_map].set(jnp.arange(kz_modes, dtype=jnp.int32))
    )
    split = velocity.reshape(
        components, reals_dev, band_modes, kx_count * real_count, rows_dev, columns
    )
    split = split.transpose(3, 0, 1, 2, 4, 5)
    split = lax.all_to_all(split, ("kx", "real"), split_axis=0, concat_axis=0, tiled=True)
    fields = split.reshape(
        kx_count, real_count, components, reals_dev, band_modes, rows_dev, columns
    )
    fields = fields.transpose(2, 1, 3, 0, 4, 5, 6).reshape(
        components, realizations, modes, rows_dev, columns
    )
    updated = nonlinear_rows(fields, low_index, neighbours, mode_counts, forward, backward)
    slotted = jnp.take(
        updated.reshape(components, realizations, modes, rows_dev, kz_modes, 2), owner_map, axis=4
    )
    slotted = slotted.reshape(
        components, real_count, reals_dev, modes, rows_dev, kx_count * ht_count, slots_dev, 2
    )
    outgoing = slotted.transpose(5, 1, 6, 2, 0, 3, 7, 4).reshape(
        kx_count * ht_count * real_count, slots_dev, reals_dev * components * modes * 2, rows_dev
    )
    incoming = lax.all_to_all(
        outgoing, ("kx", "ht", "real"), split_axis=0, concat_axis=0, tiled=True
    )
    incoming = incoming.reshape(
        kx_count, ht_count, real_count, slots_dev, reals_dev * components * modes * 2, rows_dev
    )
    incoming = incoming.transpose(3, 4, 1, 0, 2, 5).reshape(
        slots_dev, reals_dev * components * modes * 2, ht_count * rows_ht
    )
    solved = jnp.einsum("syx,snx->sny", helmholtz, incoming, precision=lax.Precision.HIGH)
    solved = solved.reshape(
        slots_dev, reals_dev, components, kx_count, band_modes, 2, ht_count, rows_ht
    )
    solved = solved.transpose(3, 6, 0, 5, 1, 2, 4, 7).reshape(
        kx_count * ht_count, slots_dev * 2, reals_dev * components * band_modes, rows_ht
    )
    returned = lax.all_to_all(solved, ("kx", "ht"), split_axis=0, concat_axis=0, tiled=True)
    restored = returned.reshape(
        kz_modes, 2, reals_dev, components, band_modes, rows_ht
    )
    restored = jnp.take(restored, inverse_map, axis=0)
    return restored.transpose(3, 2, 4, 5, 0, 1).reshape(velocity.shape)


LANES = 128
PIECES = 2
VMEM = pl.BlockSpec(memory_space=pltpu.VMEM)
SMEM = pl.BlockSpec(memory_space=pltpu.SMEM)


def params():
    return pltpu.CompilerParams(vmem_limit_bytes=48 * 1024 * 1024)


ORDERS = {4: (1, 3, 2), 8: (4, 1, 2, 6, 5, 3, 7)}


def steps_of(count):
    even = ORDERS.get(count, tuple(range(1, count)))
    odd = list(even)
    for first in range(0, count - 2, 2):
        odd[first], odd[first + 1] = (even[first + 1], even[first])
    return (0,) + tuple(even), (0,) + tuple(odd)


def step_at(count, position):
    even, odd = steps_of(count)
    return jnp.where((lax.axis_index("real") & 1) == 0, even[position], odd[position])


def cost(size):
    return pl.CostEstimate(flops=0, bytes_accessed=size, transcendentals=0)


def two_parts(value):
    top = value.astype(jnp.bfloat16)
    rest = (value - top.astype(jnp.float32)).astype(jnp.bfloat16)
    return top, rest


def dot(left, right, dims=((1,), (0,))):
    return lax.dot_general(left, right, (dims, ((), ())), preferred_element_type=jnp.float32)


def pack_first_kernel(near_ref, count_ref, velocity_ref, *out_refs):
    chunks, _, kx_count, rows, columns = velocity_ref.shape
    shape = (out_refs[0].shape[0] - chunks * rows, columns)
    row = lax.broadcasted_iota(jnp.int32, shape, 0)
    lane = lax.broadcasted_iota(jnp.int32, shape, 1)
    extra = jnp.zeros(shape, jnp.int32)
    modes, members = near_ref.shape
    for mode in range(modes):
        line = jnp.where(lane == members, count_ref[mode], 0)
        for member in range(members):
            line = jnp.where(lane == member, near_ref[mode, member], line)
        extra = jnp.where(row == mode, line, extra)
    extra = extra.astype(jnp.float32)
    own = lax.axis_index("kx")
    for index, out_ref in enumerate(out_refs):
        partner = own ^ step_at(kx_count, index)
        for chunk in range(chunks):
            out_ref[chunk * rows : (chunk + 1) * rows] = velocity_ref[chunk, 0, partner]
        out_ref[chunks * rows :] = extra


def pack_first(velocity, neighbours, mode_counts, extra_rows):
    chunks, _, kx_count, rows, columns = velocity.shape
    shape = jax.ShapeDtypeStruct((chunks * rows + extra_rows, columns), jnp.float32)
    return pl.pallas_call(
        pack_first_kernel,
        out_shape=(shape,) * kx_count,
        grid=(1,),
        in_specs=[
            SMEM,
            SMEM,
            pl.BlockSpec((chunks, 1, kx_count, rows, columns), lambda i: (0, 0, 0, 0, 0)),
        ],
        out_specs=(pl.BlockSpec(shape.shape, lambda i: (0, 0)),) * kx_count,
        cost_estimate=cost(4 * velocity.size),
        name="pack_first",
    )(neighbours, mode_counts, velocity)


def pack_kernel(velocity_ref, _, out_ref):
    chunks, _, kx_count, rows, columns = velocity_ref.shape
    for index in range(kx_count):
        for chunk in range(chunks):
            place = slice(chunk * rows, (chunk + 1) * rows)
            out_ref[index, place] = velocity_ref[chunk, 0, index]


def pack(velocity, piece, after):
    chunks, _, kx_count, rows, columns = velocity.shape
    shape = (kx_count, chunks * rows, columns)
    return pl.pallas_call(
        pack_kernel,
        out_shape=jax.ShapeDtypeStruct(shape, jnp.float32),
        grid=(1,),
        in_specs=[
            pl.BlockSpec((chunks, 1, kx_count, rows, columns), lambda i: (0, piece, 0, 0, 0)),
            pl.BlockSpec(memory_space=pl.ANY),
        ],
        out_specs=pl.BlockSpec(shape, lambda i: (0, 0, 0)),
        cost_estimate=cost(4 * velocity.size),
        name="pack",
    )(velocity, after)


def tables_kernel(owner_ref, top_ref, rest_ref, first_ref, back_ref, order_ref, slot_ref):
    columns = slot_ref.shape[1]
    modes = columns // 2
    lane = lax.broadcasted_iota(jnp.int32, (8, columns), 1)
    mode = jnp.zeros((8, columns), jnp.int32)
    for slot in range(modes):
        mode = jnp.where(lane % modes == slot, owner_ref[slot], mode)
    slot_ref[...] = mode
    wanted = 2 * mode + lane // modes
    row = lax.broadcasted_iota(jnp.int32, (columns, columns), 0)
    chosen = (row == wanted[:1]).astype(jnp.float32)
    select = chosen.astype(jnp.bfloat16)
    points = top_ref.shape[1]
    for half in range(2):
        rows = slice(half * columns, (half + 1) * columns)
        first_ref[rows, :points] = top_ref[...]
        first_ref[rows, points:] = select
        order_ref[rows] = chosen.T.astype(jnp.bfloat16)
    for index, table_ref in enumerate((top_ref, rest_ref)):
        back = dot(table_ref[...], select, ((0,), (0,))) * (2.0 * modes / points)
        back_ref[:, index * columns : (index + 1) * columns] = back.astype(jnp.bfloat16)


def spanwise_constants(columns, points):
    mode = np.arange(columns) // 2
    phase = 2.0 * np.pi * ((mode[:, None] * np.arange(points)[None, :]) % points) / points
    forward = np.where(np.arange(columns)[:, None] % 2 == 0, np.cos(phase), -np.sin(phase))
    forward = (forward / np.sqrt(columns // 2)).astype(np.float32)
    top = forward.astype(jnp.bfloat16)
    rest = (forward - top.astype(np.float32)).astype(jnp.bfloat16)
    return jnp.asarray(top), jnp.asarray(rest)


def slot_tables(owner_map, columns):
    points = 2 * columns
    top, rest = spanwise_constants(columns, points)
    first, back, order, slot_modes = pl.pallas_call(
        tables_kernel,
        out_shape=(
            jax.ShapeDtypeStruct((2 * columns, points + columns), jnp.bfloat16),
            jax.ShapeDtypeStruct((points, 2 * columns), jnp.bfloat16),
            jax.ShapeDtypeStruct((2 * columns, columns), jnp.bfloat16),
            jax.ShapeDtypeStruct((8, columns), jnp.int32),
        ),
        in_specs=[SMEM, VMEM, VMEM],
        out_specs=(VMEM,) * 4,
        compiler_params=params(),
        cost_estimate=cost(16 * points * columns),
        name="tables",
    )(owner_map, top, rest)
    return (first, rest, back), order, slot_modes


def list_high(low_ref, high_ref, modes):
    found = jnp.int32(0)
    for mode in range(modes):
        is_low = jnp.int32(0)
        for member in range(low_ref.shape[0]):
            is_low = is_low | (low_ref[member] == mode).astype(jnp.int32)
        high_ref[found] = mode
        found = found + 1 - is_low


def tile_at(step, points):
    halves = points // LANES
    return (
        pl.ds(pl.multiple_of((step // halves) * 8, 8), 8),
        pl.ds(pl.multiple_of((step % halves) * LANES, LANES), LANES),
    )


def inverse(fields, back_ref):
    columns = back_ref.shape[1] // 2
    top, rest = two_parts(fields)
    both = dot(top, back_ref[...])
    return both[:, :columns] + both[:, columns:] + dot(rest, back_ref[:, :columns])


def stress_kernel(low_ref, near_ref, *refs):
    block_refs, refs = (refs[:-10], refs[-10:])
    first_ref, second_ref, back_ref, _ = refs[:4]
    slotted_ref, physical, kept_ref, sent_ref, sums, high_ref = refs[4:]
    components, modes, rows, columns = slotted_ref.shape
    if len(block_refs) > 1:
        bands = len(block_refs)
        places = [lax.axis_index("kx") ^ step_at(bands, index) for index in range(bands)]
    else:
        bands = block_refs[0].shape[0]
        places = list(range(bands))
        block_refs = [block_refs[0].at[index] for index in range(bands)]
    points, band_modes = (physical.shape[3], modes // bands)
    members = sums.shape[1]
    odd = (lax.axis_index("real") & 1) == 1
    list_high(low_ref, high_ref, modes)
    size = band_modes * rows
    for c in range(components):
        joined = [block_ref[c * size : (c + 1) * size] for block_ref in block_refs]
        top, rest = two_parts(jnp.concatenate(joined, axis=0))
        both = dot(jnp.concatenate([top, rest], axis=1), first_ref[...])
        fields = both[:, :points] + dot(top, second_ref[...])
        for index in range(bands):
            place = pl.ds(places[index] * band_modes, band_modes)
            part = slice(index * size, (index + 1) * size)
            physical[c, place] = fields[part].reshape(band_modes, rows, points)
            slotted_ref[c, place] = both[part, points:].reshape(band_modes, rows, columns)

    def pairs(step, carry):
        place = tile_at(step, points)

        def one_high(index, totals):
            mode = high_ref[index]
            own = [physical[(c, mode) + place] for c in range(components)]
            totals = list(totals)
            for member in range(members):
                partner = physical[(1, near_ref[mode, member]) + place]
                for c in range(components):
                    slot = member * components + c
                    totals[slot] = totals[slot] + own[c] * partner
            return tuple(totals)

        empty = tuple(jnp.zeros((8, LANES), jnp.float32) for _ in range(members * components))
        totals = lax.fori_loop(0, modes - members, one_high, empty)
        for member in range(members):
            for c in range(components):
                sums[(c, member) + place] = totals[member * components + c]
        return carry

    lax.fori_loop(0, (rows // 8) * (points // LANES), pairs, 0)
    stress = inverse(sums[...].reshape(components * members * rows, points), back_ref)
    stress = stress.reshape(components, 2, members // 2, rows, columns)
    kept_ref[...] = jnp.where(odd, stress[:, 1], stress[:, 0])
    sent_ref[...] = jnp.where(odd, stress[:, 0], stress[:, 1])


def stress_terms(blocks, shape, low_index, neighbours, tables, after):
    components, modes, rows, columns = shape
    members, points = (low_index.shape[0], 2 * columns)
    half = jax.ShapeDtypeStruct((components, members // 2, rows, columns), jnp.float32)
    return pl.pallas_call(
        stress_kernel,
        out_shape=(
            jax.ShapeDtypeStruct(shape, jnp.float32),
            jax.ShapeDtypeStruct((components, modes, rows, points), jnp.float32),
            half,
            half,
        ),
        in_specs=[SMEM] * 2 + [VMEM] * (len(blocks) + 3) + [pl.BlockSpec(memory_space=pl.ANY)],
        out_specs=(VMEM,) * 4,
        scratch_shapes=[
            pltpu.VMEM((components, members, rows, points), jnp.float32),
            pltpu.SMEM((modes + 1,), jnp.int32),
        ],
        compiler_params=params(),
        cost_estimate=cost(4 * components * modes * rows * points * members),
        name="stress",
    )(low_index, neighbours, *blocks, *tables, after)


def products_kernel(
    low_ref, near_ref, count_ref, physical, back_ref, slot_ref, out_ref, products, high_ref
):
    components, modes, rows, points = physical.shape
    members, highs = (low_ref.shape[0], out_ref.shape[1])
    list_high(low_ref, high_ref, modes)

    def pairs(step, carry):
        place = tile_at(step, points)
        low = [
            [physical[(c, low_ref[member]) + place] for c in range(components)]
            for member in range(members)
        ]

        def one_high(index, inner):
            mode = high_ref[index]
            result = [jnp.zeros((8, LANES), jnp.float32) for _ in range(components)]
            for member in range(members):
                near = near_ref[mode, member]
                partner = [physical[(c, near) + place] for c in range(components)]
                for c in range(components):
                    if c == 1:
                        result[c] = result[c] + low[member][1] * partner[1]
                    else:
                        result[c] = result[c] + (
                            low[member][c] * partner[1] + partner[c] * low[member][1]
                        )
            for c in range(components):
                products[(c, index) + place] = result[c] * 2.0 if c == 1 else result[c]
            return inner

        lax.fori_loop(0, highs, one_high, 0)
        return carry

    lax.fori_loop(0, (rows // 8) * (points // LANES), pairs, 0)
    forcing = inverse(products[...].reshape(components * highs * rows, points), back_ref)
    forcing = forcing.reshape(out_ref.shape)
    for index in range(highs):
        active = slot_ref[:1] < count_ref[high_ref[index]]
        out_ref[:, index] = jnp.where(active, forcing[:, index] * dt_step, 0.0)


def high_terms(physical, low_index, neighbours, mode_counts, back, slot_modes):
    components, modes, rows, points = physical.shape
    highs = modes - low_index.shape[0]
    return pl.pallas_call(
        products_kernel,
        out_shape=jax.ShapeDtypeStruct((components, highs, rows, points // 2), jnp.float32),
        in_specs=[SMEM] * 3 + [VMEM] * 3,
        out_specs=VMEM,
        scratch_shapes=[
            pltpu.VMEM((components, highs, rows, points), jnp.float32),
            pltpu.SMEM((modes + 1,), jnp.int32),
        ],
        compiler_params=params(),
        cost_estimate=cost(4 * physical.size * low_index.shape[0]),
        name="products",
    )(low_index, neighbours, mode_counts, physical, back, slot_modes)


def outgoing_kernel(
    low_ref, count_ref, slotted_ref, forcing_ref, kept_ref, other_ref, slot_ref, *refs,
    groups, band_modes, owners, scale
):
    out_refs, (full, turned, high_ref) = (refs[:-3], refs[-3:])
    components, modes, rows, columns = slotted_ref.shape
    half, slots = (kept_ref.shape[1], columns // 2 // owners)
    per_slot = out_refs[0].shape[0] * len(out_refs) // (columns // 2)
    own = lax.axis_index("real") & 1
    list_high(low_ref, high_ref, modes)
    full[...] = slotted_ref[...]
    for index in range(forcing_ref.shape[1]):
        for c in range(components):
            full[c, high_ref[index]] += forcing_ref[c, index]
    for member in range(half):
        for part_ref, start in ((kept_ref, own * half), (other_ref, (1 - own) * half)):
            mode = low_ref[start + member]
            active = slot_ref[:1] < count_ref[mode]
            for c in range(components):
                full[c, mode] += jnp.where(active, part_ref[c, member] * scale, 0.0)
    inner = modes // groups
    if len(out_refs) > 1:
        me = lax.axis_index("kx") * lax.axis_size("ht") + lax.axis_index("ht")
        targets = [me ^ step_at(owners, position) for position in range(owners)]
    for c in range(components):
        for part in range(inner):
            tile = jnp.concatenate([full[c, part + inner * g] for g in range(groups)], axis=0)
            band_low, band_mode = (part // band_modes, part % band_modes)
            if len(out_refs) > 1:
                turned[...] = tile.T
            else:
                value = tile.T
            for p in range(2):
                row = ((band_low * 2 + p) * components + c) * band_modes + band_mode
                if len(out_refs) == 1:
                    out_refs[0][pl.ds(row, columns // 2, stride=per_slot), :] = value[
                        p * (columns // 2) : (p + 1) * (columns // 2)
                    ]
                    continue
                for out_ref, target in zip(out_refs, targets):
                    start = pl.multiple_of((p * owners + target) * slots, slots)
                    out_ref[pl.ds(row, slots, stride=per_slot), :] = turned[pl.ds(start, slots)]


def outgoing(
    slotted, forcing, kept, other, low_index, mode_counts, slot_modes, groups, band_modes, owners,
    realizations, separate,
):
    components, modes, rows, columns = slotted.shape
    total, lanes = ((columns // 2) * (modes // groups) * 2 * components, groups * rows)
    count = owners if separate else 1
    return pl.pallas_call(
        functools.partial(
            outgoing_kernel, groups=groups, band_modes=band_modes, owners=owners,
            scale=dt_step / realizations,
        ),
        out_shape=(jax.ShapeDtypeStruct((total // count, lanes), jnp.float32),) * count,
        in_specs=[SMEM, SMEM] + [VMEM] * 5,
        out_specs=(VMEM,) * count,
        scratch_shapes=[
            pltpu.VMEM(slotted.shape, jnp.float32), pltpu.VMEM((columns, lanes), jnp.float32),
            pltpu.SMEM((modes + 1,), jnp.int32),
        ],
        compiler_params=params(),
        cost_estimate=cost(8 * slotted.size),
        name="outgoing",
    )(low_index, mode_counts, slotted, forcing, kept, other, slot_modes)


def regroup(blocks, rows):
    count = len(blocks)
    lane = lax.broadcasted_iota(jnp.int32, blocks[0].shape, 1) // rows
    step = 1
    while step < count:
        take = (lane & step) == 0
        for i in range(count):
            if i & step == 0:
                here, there = (blocks[i], blocks[i + step])
                blocks[i] = jnp.where(take, here, pltpu.roll(there, step * rows, 1))
                blocks[i + step] = jnp.where(
                    take, pltpu.roll(here, LANES - step * rows, 1), there
                )
        step *= 2
    return blocks


def split_kernel(matrix_ref, top_ref, rest_ref):
    top_ref[...], rest_ref[...] = two_parts(matrix_ref[...])


def split_matrix(helmholtz):
    slots, heights, _ = helmholtz.shape
    spec = pl.BlockSpec((1, heights, heights), lambda s: (s, 0, 0))
    shape = jax.ShapeDtypeStruct(helmholtz.shape, jnp.bfloat16)
    return pl.pallas_call(
        split_kernel,
        out_shape=(shape, shape),
        grid=(slots,),
        in_specs=[spec],
        out_specs=(spec, spec),
        compiler_params=params(),
        cost_estimate=cost(8 * helmholtz.size),
        name="split_matrix",
    )(helmholtz)


def solve_kernel(*refs, groups, kx_count, ht_count, pieces):
    owners = kx_count * ht_count
    first_ref, refs = (refs[0], refs[1:])
    count = owners * (pieces - 1)
    block_refs, part_refs, refs = (refs[:count], refs[count : count + 2], refs[count + 2 :])
    out_refs, (matrices, arrived, ordered, full) = (refs[:owners], refs[owners:])
    slots, heights = part_refs[0].shape[:2]
    copies = [
        [
            pltpu.make_async_copy(part_ref.at[s], matrices.at[i, s], arrived.at[i, s])
            for i, part_ref in enumerate(part_refs)
        ]
        for s in range(slots)
    ]
    for pair in copies:
        for copy in pair:
            copy.start()
    own_kx, own_ht = (lax.axis_index("kx"), lax.axis_index("ht"))
    partners = []
    for position in range(owners):
        step = step_at(owners, position)
        partners.append((own_kx ^ (step // ht_count), own_ht ^ (step % ht_count)))
    for index, block_ref in enumerate(block_refs):
        kx, ht = partners[index % owners]
        ordered[index // owners, kx * ht_count + ht] = block_ref[...]
    rows, (lane_tiles, per_band) = (LANES // groups, out_refs[0].shape[1:3])
    for s in range(slots):
        tiles = []
        for h in range(ht_count):
            for piece in range(pieces):
                source = first_ref if piece == 0 else ordered.at[piece - 1]
                for first in range(0, kx_count, groups):
                    blocks = [source[(first + g) * ht_count + h, s] for g in range(groups)]
                    tiles.append(jnp.concatenate(regroup(blocks, rows), axis=0))
        fields = jnp.concatenate(tiles, axis=1)
        count = fields.shape[0]
        spare = -count % LANES
        if spare:
            fields = jnp.concatenate([fields, jnp.zeros((spare, heights), jnp.float32)], axis=0)
        top, rest = two_parts(fields)
        for copy in copies[s]:
            copy.wait()
        matrix_top, matrix_rest = (matrices[0, s], matrices[1, s])
        last = ((1,), (1,))
        both = dot(matrix_top, jnp.concatenate([top, rest], axis=0), last)
        solved = both[:, : count + spare] + both[:, count + spare :] + dot(matrix_rest, top, last)
        for tile in range(heights // LANES):
            full[s % 2, tile] = solved[tile * LANES : (tile + 1) * LANES].T[:count]
        for out_ref, (kx, ht) in zip(out_refs, partners):
            band = pl.ds(pl.multiple_of(kx * per_band, 8), per_band)
            for tile in range(lane_tiles):
                out_ref[s, tile] = full[s % 2, ht * lane_tiles + tile, band]


def solve(first, blocks, parts, pieces, groups, kx_count, ht_count):
    owners, slots, per_slot, lanes = first.shape
    heights, count = (parts[0].shape[1], per_slot * groups)
    shape = (slots, heights // ht_count // LANES, count // kx_count, LANES)
    return pl.pallas_call(
        functools.partial(
            solve_kernel, groups=groups, kx_count=kx_count, ht_count=ht_count, pieces=pieces
        ),
        out_shape=(jax.ShapeDtypeStruct(shape, jnp.float32),) * owners,
        in_specs=[VMEM] * (1 + len(blocks)) + [pl.BlockSpec(memory_space=pl.ANY)] * 2,
        out_specs=(VMEM,) * owners,
        scratch_shapes=[
            pltpu.VMEM((2,) + parts[0].shape, jnp.bfloat16),
            pltpu.SemaphoreType.DMA((2, slots)),
            pltpu.VMEM((max(pieces - 1, 1),) + first.shape, jnp.float32),
            pltpu.VMEM((2, heights // LANES, count, LANES), jnp.float32),
        ],
        compiler_params=params(),
        cost_estimate=cost(4 * parts[0].size),
        name="solve",
    )(first, *blocks, *parts)


def restore_kernel(*refs, owners, ht_count):
    block_refs, (order_ref, out_ref, ordered) = (refs[:-3], refs[-3:])
    components, band_modes, rows, columns = out_ref.shape
    slots = columns // 2 // owners
    per_slot = block_refs[0].shape[0] // slots
    me = lax.axis_index("kx") * ht_count + lax.axis_index("ht")
    for position, block_ref in enumerate(block_refs):
        ordered[me ^ step_at(owners, position)] = block_ref[...]
    for c in range(components):
        for mode in range(band_modes):
            for tile in range(rows // LANES):
                parts = []
                for p in range(2):
                    row = ((tile * 2 + p) * components + c) * band_modes + mode
                    for owner in range(owners):
                        parts.append(ordered[owner, pl.ds(row, slots, stride=per_slot), :])
                top, rest = two_parts(jnp.concatenate(parts, axis=0))
                both = jnp.concatenate([top, rest], axis=0)
                out_ref[c, mode, pl.ds(tile * LANES, LANES)] = dot(
                    both, order_ref[...], ((0,), (0,))
                )


def restore(blocks, order, components, band_modes, rows, ht_count):
    columns = order.shape[1]
    return pl.pallas_call(
        functools.partial(restore_kernel, owners=len(blocks), ht_count=ht_count),
        out_shape=jax.ShapeDtypeStruct((components, band_modes, rows, columns), jnp.float32),
        in_specs=[VMEM] * (len(blocks) + 1),
        out_specs=VMEM,
        scratch_shapes=[pltpu.VMEM((len(blocks),) + blocks[0].shape, jnp.float32)],
        compiler_params=params(),
        cost_estimate=cost(8 * components * band_modes * rows * columns),
        name="restore",
    )(*blocks, order)


def exchange(blocks, axes):
    count, realizations = (len(blocks), lax.axis_size("real"))
    result = list(blocks)
    for position in range(1, count):
        steps = [order[position] for order in steps_of(count)]
        pairs = [
            (index * realizations + r, (index ^ steps[r % 2]) * realizations + r)
            for index in range(count)
            for r in range(realizations)
        ]
        result[position] = lax.ppermute(blocks[position], axes + ("real",), pairs)
    return result


def sum_kernel(first_ref, second_ref, _, out_ref):
    out_ref[...] = first_ref[...] + second_ref[...]


def ordered_sum(first, second, after):
    return pl.pallas_call(
        sum_kernel,
        out_shape=jax.ShapeDtypeStruct(first.shape, jnp.float32),
        in_specs=[VMEM, VMEM, pl.BlockSpec(memory_space=pl.ANY)],
        out_specs=VMEM,
        compiler_params=params(),
        cost_estimate=cost(12 * first.size),
        name="ordered_sum",
    )(first, second, after)


def swap(value, step):
    pairs = [(index, index ^ step) for index in range(lax.axis_size("real"))]
    return lax.ppermute(value, "real", pairs)


def local(velocity, low_index, neighbours, owner_map, mode_counts, helmholtz):
    components, reals_dev, band_modes, rows_ht, columns = velocity.shape
    kx_count, ht_count = (lax.axis_size("kx"), lax.axis_size("ht"))
    own_kx, own_ht = (lax.axis_index("kx"), lax.axis_index("ht"))
    owners, pieces, real_count = (kx_count * ht_count, PIECES, lax.axis_size("real"))
    rows = rows_ht // (kx_count * pieces)
    groups = LANES // rows if rows else 0
    slots = columns // 2 // owners
    if (
        columns != LANES or reals_dev != 1 or rows_ht % LANES or rows % 8 or LANES % rows or kx_count % groups or kx_count & (kx_count - 1)
        or (band_modes * 2 * components) % 8 or slots % 8 or owners & (owners - 1) or low_index.shape[0] >= kx_count * band_modes
        or low_index.shape[0] >= columns or low_index.shape[0] % 2 or real_count < 2 or real_count & (real_count - 1)
    ):
        return local_plain(velocity, low_index, neighbours, owner_map, mode_counts, helmholtz)
    realizations, members = (real_count, low_index.shape[0])
    chunks, modes = (components * band_modes, band_modes * kx_count)
    shape = (components, modes, rows, columns)
    extra_rows = -(-band_modes // 8) * 8
    split = velocity.reshape(chunks, pieces, kx_count, rows, columns)
    blocks = pack_first(split, neighbours, mode_counts, extra_rows)
    parts = [exchange(blocks, ("kx",))]
    for piece in range(1, pieces):
        block = pack(split, piece, parts[0][1])
        block = lax.all_to_all(block, "kx", split_axis=0, concat_axis=0, tiled=True)
        parts.append((block,))
    tables, order, slot_modes = slot_tables(owner_map, columns)
    small = 0.0
    for index, block in enumerate(parts[0]):
        lines = block[chunks * rows : chunks * rows + band_modes, : members + 1]
        here = (own_kx ^ step_at(kx_count, index)) == jnp.arange(kx_count)
        small = small + jnp.where(here[:, None, None], lines[None], 0.0)
    small = small.reshape(modes, members + 1).astype(jnp.int32)
    neighbours, mode_counts = (small[:, :-1], small[:, -1])
    after = slot_modes
    received = []
    for piece, part in enumerate(parts):
        slotted, physical, kept, sent = stress_terms(
            part, shape, low_index, neighbours, tables, after
        )
        forcing = high_terms(physical, low_index, neighbours, mode_counts, tables[2], slot_modes)
        kept = after = kept + swap(sent, 1)
        step = 2
        while step < realizations:
            kept = ordered_sum(kept, swap(kept, step), forcing)
            step *= 2
        blocks = outgoing(
            slotted, forcing, kept, swap(kept, 1), low_index, mode_counts, slot_modes, groups, band_modes,
            owners, realizations, piece > 0,
        )
        if piece:
            received += exchange([block.reshape(slots, -1, LANES) for block in blocks], ("kx", "ht"))
        else:
            block = blocks[0].reshape(owners, slots, -1, LANES)
            first = lax.all_to_all(block, ("kx", "ht"), split_axis=0, concat_axis=0, tiled=True)
    solved = solve(first, received, split_matrix(helmholtz), pieces, groups, kx_count, ht_count)
    returned = [block.reshape(-1, LANES) for block in exchange(solved, ("kx", "ht"))]
    result = restore(returned, order, components, band_modes, rows_ht, ht_count)
    return result.reshape(velocity.shape)


def solution(mesh):
    in_specs = (
        P(None, "real", "kx", "ht", None),
        P(),
        P("kx", None),
        P(),
        P("kx"),
        P(("kx", "ht"), None, None),
    )
    out_specs = P(None, "real", "kx", "ht", None)
    return jax.shard_map(local, mesh=mesh, in_specs=in_specs, out_specs=out_specs, check_vma=False)
```

```python
import functools

import jax
import jax.numpy as jnp
import numpy as np
from jax import lax
from jax.experimental import pallas as pl
from jax.experimental.pallas import tpu as pltpu
from jax.sharding import PartitionSpec as P

dt_step = 0.1


def spanwise_tables(mode_count, point_count):
    column_ids = jnp.arange(2 * mode_count)
    wavenumber = (column_ids // 2).astype(jnp.float32)
    imag_part = column_ids % 2
    positions = 2.0 * jnp.pi * jnp.arange(point_count).astype(jnp.float32) / point_count
    phases = wavenumber[:, None] * positions[None, :]
    forward = jnp.where(imag_part[:, None] == 0, jnp.cos(phases), -jnp.sin(phases)) / jnp.sqrt(
        jnp.float32(mode_count)
    )
    backward = forward.T * (2.0 * mode_count / point_count)
    return (forward, backward)


def nonlinear_rows(fields, low_index, neighbours, mode_counts, forward, backward):
    precision = lax.Precision.HIGH
    realizations, modes, columns = (fields.shape[1], fields.shape[2], fields.shape[4])
    low_select = (low_index[:, None] == jnp.arange(modes)[None, :]).astype(jnp.float32)
    high_mask = 1.0 - jnp.sum(low_select, axis=0)
    high_rows = high_mask[None, None, :, None, None]
    column_mask = ((jnp.arange(columns) // 2)[None, :] < mode_counts[:, None]).astype(jnp.float32)
    physical = jnp.dot(fields, forward, precision=precision)
    low_fields = jnp.take(physical, low_index, axis=2)
    high_low = jnp.zeros_like(physical)
    stresses = []
    for member in range(low_index.shape[0]):
        partner = jnp.take(physical, neighbours[:, member], axis=2)
        low_one = low_fields[:, :, member : member + 1]
        high_low = high_low + low_one * partner[1:2] + partner * low_one[1:2]
        stresses.append(jnp.sum(physical * (partner[1:2] * high_rows), axis=(1, 2)))
    stress = jnp.stack(stresses, axis=1) / realizations
    forcing = jnp.dot(high_low, backward, precision=precision) * high_rows
    low_forcing = jnp.dot(stress, backward, precision=precision)
    low_rows = jnp.einsum("jm,cjyk->cmyk", low_select, low_forcing, precision=lax.Precision.HIGHEST)
    forcing = (forcing + low_rows[:, None]) * column_mask[None, None, :, None, :]
    return fields + dt_step * forcing


def local_plain(velocity, low_index, neighbours, owner_map, mode_counts, helmholtz):
    components, reals_dev, band_modes, rows_ht, columns = velocity.shape
    kz_modes = columns // 2
    forward, backward = spanwise_tables(kz_modes, 4 * kz_modes)
    kx_count, ht_count = (lax.axis_size("kx"), lax.axis_size("ht"))
    real_count = lax.axis_size("real")
    modes, realizations = (band_modes * kx_count, reals_dev * real_count)
    slots_dev = kz_modes // (kx_count * ht_count)
    rows_dev = rows_ht // (kx_count * real_count)
    small = jnp.concatenate([neighbours, mode_counts[:, None]], axis=1)
    small = lax.all_gather(small, "kx", axis=0, tiled=True)
    neighbours, mode_counts = (small[:, :-1], small[:, -1])
    inverse_map = (
        jnp.zeros((kz_modes,), jnp.int32).at[owner_map].set(jnp.arange(kz_modes, dtype=jnp.int32))
    )
    split = velocity.reshape(
        components, reals_dev, band_modes, kx_count * real_count, rows_dev, columns
    )
    split = split.transpose(3, 0, 1, 2, 4, 5)
    split = lax.all_to_all(split, ("kx", "real"), split_axis=0, concat_axis=0, tiled=True)
    fields = split.reshape(
        kx_count, real_count, components, reals_dev, band_modes, rows_dev, columns
    )
    fields = fields.transpose(2, 1, 3, 0, 4, 5, 6).reshape(
        components, realizations, modes, rows_dev, columns
    )
    updated = nonlinear_rows(fields, low_index, neighbours, mode_counts, forward, backward)
    slotted = jnp.take(
        updated.reshape(components, realizations, modes, rows_dev, kz_modes, 2), owner_map, axis=4
    )
    slotted = slotted.reshape(
        components, real_count, reals_dev, modes, rows_dev, kx_count * ht_count, slots_dev, 2
    )
    outgoing = slotted.transpose(5, 1, 6, 2, 0, 3, 7, 4).reshape(
        kx_count * ht_count * real_count, slots_dev, reals_dev * components * modes * 2, rows_dev
    )
    incoming = lax.all_to_all(
        outgoing, ("kx", "ht", "real"), split_axis=0, concat_axis=0, tiled=True
    )
    incoming = incoming.reshape(
        kx_count, ht_count, real_count, slots_dev, reals_dev * components * modes * 2, rows_dev
    )
    incoming = incoming.transpose(3, 4, 1, 0, 2, 5).reshape(
        slots_dev, reals_dev * components * modes * 2, ht_count * rows_ht
    )
    solved = jnp.einsum("syx,snx->sny", helmholtz, incoming, precision=lax.Precision.HIGH)
    solved = solved.reshape(
        slots_dev, reals_dev, components, kx_count, band_modes, 2, ht_count, rows_ht
    )
    solved = solved.transpose(3, 6, 0, 5, 1, 2, 4, 7).reshape(
        kx_count * ht_count, slots_dev * 2, reals_dev * components * band_modes, rows_ht
    )
    returned = lax.all_to_all(solved, ("kx", "ht"), split_axis=0, concat_axis=0, tiled=True)
    restored = returned.reshape(
        kz_modes, 2, reals_dev, components, band_modes, rows_ht
    )
    restored = jnp.take(restored, inverse_map, axis=0)
    return restored.transpose(3, 2, 4, 5, 0, 1).reshape(velocity.shape)


LANES = 128
PIECES = 2
VMEM = pl.BlockSpec(memory_space=pltpu.VMEM)
SMEM = pl.BlockSpec(memory_space=pltpu.SMEM)


def params():
    return pltpu.CompilerParams(vmem_limit_bytes=48 * 1024 * 1024)


ORDERS = {4: (1, 3, 2), 8: (4, 1, 2, 6, 5, 3, 7)}


def steps_of(count):
    even = ORDERS.get(count, tuple(range(1, count)))
    odd = list(even)
    for first in range(0, count - 2, 2):
        odd[first], odd[first + 1] = (even[first + 1], even[first])
    return (0,) + tuple(even), (0,) + tuple(odd)


def step_at(count, position):
    even, odd = steps_of(count)
    return jnp.where((lax.axis_index("real") & 1) == 0, even[position], odd[position])


def cost(size):
    return pl.CostEstimate(flops=0, bytes_accessed=size, transcendentals=0)


def two_parts(value):
    top = value.astype(jnp.bfloat16)
    rest = (value - top.astype(jnp.float32)).astype(jnp.bfloat16)
    return top, rest


def dot(left, right, dims=((1,), (0,))):
    return lax.dot_general(left, right, (dims, ((), ())), preferred_element_type=jnp.float32)


def pack_first_kernel(near_ref, count_ref, velocity_ref, *out_refs):
    chunks, _, kx_count, rows, columns = velocity_ref.shape
    shape = (out_refs[0].shape[0] - chunks * rows, columns)
    row = lax.broadcasted_iota(jnp.int32, shape, 0)
    lane = lax.broadcasted_iota(jnp.int32, shape, 1)
    extra = jnp.zeros(shape, jnp.int32)
    modes, members = near_ref.shape
    for mode in range(modes):
        line = jnp.where(lane == members, count_ref[mode], 0)
        for member in range(members):
            line = jnp.where(lane == member, near_ref[mode, member], line)
        extra = jnp.where(row == mode, line, extra)
    extra = extra.astype(jnp.float32)
    own = lax.axis_index("kx")
    for index, out_ref in enumerate(out_refs):
        partner = own ^ step_at(kx_count, index)
        for chunk in range(chunks):
            out_ref[chunk * rows : (chunk + 1) * rows] = velocity_ref[chunk, 0, partner]
        out_ref[chunks * rows :] = extra


def pack_first(velocity, neighbours, mode_counts, extra_rows):
    chunks, _, kx_count, rows, columns = velocity.shape
    shape = jax.ShapeDtypeStruct((chunks * rows + extra_rows, columns), jnp.float32)
    return pl.pallas_call(
        pack_first_kernel,
        out_shape=(shape,) * kx_count,
        grid=(1,),
        in_specs=[
            SMEM,
            SMEM,
            pl.BlockSpec((chunks, 1, kx_count, rows, columns), lambda i: (0, 0, 0, 0, 0)),
        ],
        out_specs=(pl.BlockSpec(shape.shape, lambda i: (0, 0)),) * kx_count,
        cost_estimate=cost(4 * velocity.size),
        name="pack_first",
    )(neighbours, mode_counts, velocity)


def pack_kernel(velocity_ref, _, out_ref):
    chunks, _, kx_count, rows, columns = velocity_ref.shape
    for index in range(kx_count):
        for chunk in range(chunks):
            place = slice(chunk * rows, (chunk + 1) * rows)
            out_ref[index, place] = velocity_ref[chunk, 0, index]


def pack(velocity, piece, after):
    chunks, _, kx_count, rows, columns = velocity.shape
    shape = (kx_count, chunks * rows, columns)
    return pl.pallas_call(
        pack_kernel,
        out_shape=jax.ShapeDtypeStruct(shape, jnp.float32),
        grid=(1,),
        in_specs=[
            pl.BlockSpec((chunks, 1, kx_count, rows, columns), lambda i: (0, piece, 0, 0, 0)),
            pl.BlockSpec(memory_space=pl.ANY),
        ],
        out_specs=pl.BlockSpec(shape, lambda i: (0, 0, 0)),
        cost_estimate=cost(4 * velocity.size),
        name="pack",
    )(velocity, after)


def tables_kernel(owner_ref, top_ref, rest_ref, first_ref, back_ref, order_ref, slot_ref):
    columns = slot_ref.shape[1]
    modes = columns // 2
    lane = lax.broadcasted_iota(jnp.int32, (8, columns), 1)
    mode = jnp.zeros((8, columns), jnp.int32)
    for slot in range(modes):
        mode = jnp.where(lane % modes == slot, owner_ref[slot], mode)
    slot_ref[...] = mode
    wanted = 2 * mode + lane // modes
    row = lax.broadcasted_iota(jnp.int32, (columns, columns), 0)
    chosen = (row == wanted[:1]).astype(jnp.float32)
    select = chosen.astype(jnp.bfloat16)
    points = top_ref.shape[1]
    for half in range(2):
        rows = slice(half * columns, (half + 1) * columns)
        first_ref[rows, :points] = top_ref[...]
        first_ref[rows, points:] = select
        order_ref[rows] = chosen.T.astype(jnp.bfloat16)
    for index, table_ref in enumerate((top_ref, rest_ref)):
        back = dot(table_ref[...], select, ((0,), (0,))) * (2.0 * modes / points)
        back_ref[:, index * columns : (index + 1) * columns] = back.astype(jnp.bfloat16)


def spanwise_constants(columns, points):
    mode = np.arange(columns) // 2
    phase = 2.0 * np.pi * ((mode[:, None] * np.arange(points)[None, :]) % points) / points
    forward = np.where(np.arange(columns)[:, None] % 2 == 0, np.cos(phase), -np.sin(phase))
    forward = (forward / np.sqrt(columns // 2)).astype(np.float32)
    top = forward.astype(jnp.bfloat16)
    rest = (forward - top.astype(np.float32)).astype(jnp.bfloat16)
    return jnp.asarray(top), jnp.asarray(rest)


def slot_tables(owner_map, columns):
    points = 2 * columns
    top, rest = spanwise_constants(columns, points)
    first, back, order, slot_modes = pl.pallas_call(
        tables_kernel,
        out_shape=(
            jax.ShapeDtypeStruct((2 * columns, points + columns), jnp.bfloat16),
            jax.ShapeDtypeStruct((points, 2 * columns), jnp.bfloat16),
            jax.ShapeDtypeStruct((2 * columns, columns), jnp.bfloat16),
            jax.ShapeDtypeStruct((8, columns), jnp.int32),
        ),
        in_specs=[SMEM, VMEM, VMEM],
        out_specs=(VMEM,) * 4,
        compiler_params=params(),
        cost_estimate=cost(16 * points * columns),
        name="tables",
    )(owner_map, top, rest)
    return (first, rest, back), order, slot_modes


def list_high(low_ref, high_ref, modes):
    found = jnp.int32(0)
    for mode in range(modes):
        is_low = jnp.int32(0)
        for member in range(low_ref.shape[0]):
            is_low = is_low | (low_ref[member] == mode).astype(jnp.int32)
        high_ref[found] = mode
        found = found + 1 - is_low


def tile_at(step, points):
    halves = points // LANES
    return (
        pl.ds(pl.multiple_of((step // halves) * 8, 8), 8),
        pl.ds(pl.multiple_of((step % halves) * LANES, LANES), LANES),
    )


def inverse(fields, back_ref):
    columns = back_ref.shape[1] // 2
    top, rest = two_parts(fields)
    both = dot(top, back_ref[...])
    return both[:, :columns] + both[:, columns:] + dot(rest, back_ref[:, :columns])


def stress_kernel(low_ref, near_ref, *refs):
    block_refs, refs = (refs[:-10], refs[-10:])
    first_ref, second_ref, back_ref, _ = refs[:4]
    slotted_ref, physical, kept_ref, sent_ref, sums, high_ref = refs[4:]
    components, modes, rows, columns = slotted_ref.shape
    if len(block_refs) > 1:
        bands = len(block_refs)
        places = [lax.axis_index("kx") ^ step_at(bands, index) for index in range(bands)]
    else:
        bands = block_refs[0].shape[0]
        places = list(range(bands))
        block_refs = [block_refs[0].at[index] for index in range(bands)]
    points, band_modes = (physical.shape[3], modes // bands)
    members = sums.shape[1]
    odd = (lax.axis_index("real") & 1) == 1
    list_high(low_ref, high_ref, modes)
    size = band_modes * rows
    for c in range(components):
        joined = [block_ref[c * size : (c + 1) * size] for block_ref in block_refs]
        top, rest = two_parts(jnp.concatenate(joined, axis=0))
        both = dot(jnp.concatenate([top, rest], axis=1), first_ref[...])
        fields = both[:, :points] + dot(top, second_ref[...])
        for index in range(bands):
            place = pl.ds(places[index] * band_modes, band_modes)
            part = slice(index * size, (index + 1) * size)
            physical[c, place] = fields[part].reshape(band_modes, rows, points)
            slotted_ref[c, place] = both[part, points:].reshape(band_modes, rows, columns)

    def pairs(step, carry):
        place = tile_at(step, points)

        def one_high(index, totals):
            mode = high_ref[index]
            own = [physical[(c, mode) + place] for c in range(components)]
            totals = list(totals)
            for member in range(members):
                partner = physical[(1, near_ref[mode, member]) + place]
                for c in range(components):
                    slot = member * components + c
                    totals[slot] = totals[slot] + own[c] * partner
            return tuple(totals)

        empty = tuple(jnp.zeros((8, LANES), jnp.float32) for _ in range(members * components))
        totals = lax.fori_loop(0, modes - members, one_high, empty)
        for member in range(members):
            for c in range(components):
                sums[(c, member) + place] = totals[member * components + c]
        return carry

    lax.fori_loop(0, (rows // 8) * (points // LANES), pairs, 0)
    stress = inverse(sums[...].reshape(components * members * rows, points), back_ref)
    stress = stress.reshape(components, 2, members // 2, rows, columns)
    kept_ref[...] = jnp.where(odd, stress[:, 1], stress[:, 0])
    sent_ref[...] = jnp.where(odd, stress[:, 0], stress[:, 1])


def stress_terms(blocks, shape, low_index, neighbours, tables, after):
    components, modes, rows, columns = shape
    members, points = (low_index.shape[0], 2 * columns)
    half = jax.ShapeDtypeStruct((components, members // 2, rows, columns), jnp.float32)
    return pl.pallas_call(
        stress_kernel,
        out_shape=(
            jax.ShapeDtypeStruct(shape, jnp.float32),
            jax.ShapeDtypeStruct((components, modes, rows, points), jnp.float32),
            half,
            half,
        ),
        in_specs=[SMEM] * 2 + [VMEM] * (len(blocks) + 3) + [pl.BlockSpec(memory_space=pl.ANY)],
        out_specs=(VMEM,) * 4,
        scratch_shapes=[
            pltpu.VMEM((components, members, rows, points), jnp.float32),
            pltpu.SMEM((modes + 1,), jnp.int32),
        ],
        compiler_params=params(),
        cost_estimate=cost(4 * components * modes * rows * points * members),
        name="stress",
    )(low_index, neighbours, *blocks, *tables, after)


def products_kernel(
    low_ref, near_ref, count_ref, physical, back_ref, slot_ref, out_ref, products, high_ref
):
    components, modes, rows, points = physical.shape
    members, highs = (low_ref.shape[0], out_ref.shape[1])
    list_high(low_ref, high_ref, modes)

    def pairs(step, carry):
        place = tile_at(step, points)
        low = [
            [physical[(c, low_ref[member]) + place] for c in range(components)]
            for member in range(members)
        ]

        def one_high(index, inner):
            mode = high_ref[index]
            result = [jnp.zeros((8, LANES), jnp.float32) for _ in range(components)]
            for member in range(members):
                near = near_ref[mode, member]
                partner = [physical[(c, near) + place] for c in range(components)]
                for c in range(components):
                    if c == 1:
                        result[c] = result[c] + low[member][1] * partner[1]
                    else:
                        result[c] = result[c] + (
                            low[member][c] * partner[1] + partner[c] * low[member][1]
                        )
            for c in range(components):
                products[(c, index) + place] = result[c] * 2.0 if c == 1 else result[c]
            return inner

        lax.fori_loop(0, highs, one_high, 0)
        return carry

    lax.fori_loop(0, (rows // 8) * (points // LANES), pairs, 0)
    forcing = inverse(products[...].reshape(components * highs * rows, points), back_ref)
    forcing = forcing.reshape(out_ref.shape)
    for index in range(highs):
        active = slot_ref[:1] < count_ref[high_ref[index]]
        out_ref[:, index] = jnp.where(active, forcing[:, index] * dt_step, 0.0)


def high_terms(physical, low_index, neighbours, mode_counts, back, slot_modes):
    components, modes, rows, points = physical.shape
    highs = modes - low_index.shape[0]
    return pl.pallas_call(
        products_kernel,
        out_shape=jax.ShapeDtypeStruct((components, highs, rows, points // 2), jnp.float32),
        in_specs=[SMEM] * 3 + [VMEM] * 3,
        out_specs=VMEM,
        scratch_shapes=[
            pltpu.VMEM((components, highs, rows, points), jnp.float32),
            pltpu.SMEM((modes + 1,), jnp.int32),
        ],
        compiler_params=params(),
        cost_estimate=cost(4 * physical.size * low_index.shape[0]),
        name="products",
    )(low_index, neighbours, mode_counts, physical, back, slot_modes)


def outgoing_kernel(
    low_ref, count_ref, slotted_ref, forcing_ref, kept_ref, other_ref, slot_ref, *refs,
    groups, band_modes, owners, scale
):
    out_refs, (full, turned, high_ref) = (refs[:-3], refs[-3:])
    components, modes, rows, columns = slotted_ref.shape
    half, slots = (kept_ref.shape[1], columns // 2 // owners)
    per_slot = out_refs[0].shape[0] * len(out_refs) // (columns // 2)
    own = lax.axis_index("real") & 1
    list_high(low_ref, high_ref, modes)
    full[...] = slotted_ref[...]
    for index in range(forcing_ref.shape[1]):
        for c in range(components):
            full[c, high_ref[index]] += forcing_ref[c, index]
    for member in range(half):
        for part_ref, start in ((kept_ref, own * half), (other_ref, (1 - own) * half)):
            mode = low_ref[start + member]
            active = slot_ref[:1] < count_ref[mode]
            for c in range(components):
                full[c, mode] += jnp.where(active, part_ref[c, member] * scale, 0.0)
    inner = modes // groups
    if len(out_refs) > 1:
        me = lax.axis_index("kx") * lax.axis_size("ht") + lax.axis_index("ht")
        targets = [me ^ step_at(owners, position) for position in range(owners)]
    for c in range(components):
        for part in range(inner):
            tile = jnp.concatenate([full[c, part + inner * g] for g in range(groups)], axis=0)
            band_low, band_mode = (part // band_modes, part % band_modes)
            if len(out_refs) > 1:
                turned[...] = tile.T
            else:
                value = tile.T
            for p in range(2):
                row = ((band_low * 2 + p) * components + c) * band_modes + band_mode
                if len(out_refs) == 1:
                    out_refs[0][pl.ds(row, columns // 2, stride=per_slot), :] = value[
                        p * (columns // 2) : (p + 1) * (columns // 2)
                    ]
                    continue
                for out_ref, target in zip(out_refs, targets):
                    start = pl.multiple_of((p * owners + target) * slots, slots)
                    out_ref[pl.ds(row, slots, stride=per_slot), :] = turned[pl.ds(start, slots)]


def outgoing(
    slotted, forcing, kept, other, low_index, mode_counts, slot_modes, groups, band_modes, owners,
    realizations, separate,
):
    components, modes, rows, columns = slotted.shape
    total, lanes = ((columns // 2) * (modes // groups) * 2 * components, groups * rows)
    count = owners if separate else 1
    return pl.pallas_call(
        functools.partial(
            outgoing_kernel, groups=groups, band_modes=band_modes, owners=owners,
            scale=dt_step / realizations,
        ),
        out_shape=(jax.ShapeDtypeStruct((total // count, lanes), jnp.float32),) * count,
        in_specs=[SMEM, SMEM] + [VMEM] * 5,
        out_specs=(VMEM,) * count,
        scratch_shapes=[
            pltpu.VMEM(slotted.shape, jnp.float32), pltpu.VMEM((columns, lanes), jnp.float32),
            pltpu.SMEM((modes + 1,), jnp.int32),
        ],
        compiler_params=params(),
        cost_estimate=cost(8 * slotted.size),
        name="outgoing",
    )(low_index, mode_counts, slotted, forcing, kept, other, slot_modes)


def regroup(blocks, rows):
    count = len(blocks)
    lane = lax.broadcasted_iota(jnp.int32, blocks[0].shape, 1) // rows
    step = 1
    while step < count:
        take = (lane & step) == 0
        for i in range(count):
            if i & step == 0:
                here, there = (blocks[i], blocks[i + step])
                blocks[i] = jnp.where(take, here, pltpu.roll(there, step * rows, 1))
                blocks[i + step] = jnp.where(
                    take, pltpu.roll(here, LANES - step * rows, 1), there
                )
        step *= 2
    return blocks


def solve_kernel(*refs, groups, kx_count, ht_count, pieces):
    owners = kx_count * ht_count
    first_ref, refs = (refs[0], refs[1:])
    count = owners * (pieces - 1)
    block_refs, matrix_ref, refs = (refs[:count], refs[count], refs[count + 1 :])
    out_refs, (matrices, arrived, ordered, full) = (refs[:owners], refs[owners:])
    slots, heights = (matrix_ref.shape[0], matrix_ref.shape[1])
    copies = [
        pltpu.make_async_copy(matrix_ref.at[s], matrices.at[s], arrived.at[s])
        for s in range(slots)
    ]
    ahead = 2
    for copy in copies[:ahead]:
        copy.start()
    own_kx, own_ht = (lax.axis_index("kx"), lax.axis_index("ht"))
    partners = []
    for position in range(owners):
        step = step_at(owners, position)
        partners.append((own_kx ^ (step // ht_count), own_ht ^ (step % ht_count)))
    for index, block_ref in enumerate(block_refs):
        kx, ht = partners[index % owners]
        ordered[index // owners, kx * ht_count + ht] = block_ref[...]
    rows, (lane_tiles, per_band) = (LANES // groups, out_refs[0].shape[1:3])
    for s in range(slots):
        tiles = []
        for h in range(ht_count):
            for piece in range(pieces):
                source = first_ref if piece == 0 else ordered.at[piece - 1]
                for first in range(0, kx_count, groups):
                    blocks = [source[(first + g) * ht_count + h, s] for g in range(groups)]
                    tiles.append(jnp.concatenate(regroup(blocks, rows), axis=0))
        fields = jnp.concatenate(tiles, axis=1)
        count = fields.shape[0]
        spare = -count % LANES
        if spare:
            fields = jnp.concatenate([fields, jnp.zeros((spare, heights), jnp.float32)], axis=0)
        top, rest = two_parts(fields)
        copies[s].wait()
        if s + ahead < slots:
            copies[s + ahead].start()
        matrix_top, matrix_rest = two_parts(matrices[s])
        last = ((1,), (1,))
        both = dot(matrix_top, jnp.concatenate([top, rest], axis=0), last)
        solved = both[:, : count + spare] + both[:, count + spare :] + dot(matrix_rest, top, last)
        for tile in range(heights // LANES):
            full[s % 2, tile] = solved[tile * LANES : (tile + 1) * LANES].T[:count]
        for out_ref, (kx, ht) in zip(out_refs, partners):
            band = pl.ds(pl.multiple_of(kx * per_band, 8), per_band)
            for tile in range(lane_tiles):
                out_ref[s, tile] = full[s % 2, ht * lane_tiles + tile, band]


def solve(first, blocks, helmholtz, pieces, groups, kx_count, ht_count):
    owners, slots, per_slot, lanes = first.shape
    heights, count = (helmholtz.shape[1], per_slot * groups)
    shape = (slots, heights // ht_count // LANES, count // kx_count, LANES)
    return pl.pallas_call(
        functools.partial(
            solve_kernel, groups=groups, kx_count=kx_count, ht_count=ht_count, pieces=pieces
        ),
        out_shape=(jax.ShapeDtypeStruct(shape, jnp.float32),) * owners,
        in_specs=[VMEM] * (1 + len(blocks)) + [pl.BlockSpec(memory_space=pl.ANY)],
        out_specs=(VMEM,) * owners,
        scratch_shapes=[
            pltpu.VMEM(helmholtz.shape, jnp.float32),
            pltpu.SemaphoreType.DMA((slots,)),
            pltpu.VMEM((max(pieces - 1, 1),) + first.shape, jnp.float32),
            pltpu.VMEM((2, heights // LANES, count, LANES), jnp.float32),
        ],
        compiler_params=params(),
        cost_estimate=cost(4 * helmholtz.size),
        name="solve",
    )(first, *blocks, helmholtz)


def restore_kernel(*refs, owners, ht_count):
    block_refs, (order_ref, out_ref, ordered) = (refs[:-3], refs[-3:])
    components, band_modes, rows, columns = out_ref.shape
    slots = columns // 2 // owners
    per_slot = block_refs[0].shape[0] // slots
    me = lax.axis_index("kx") * ht_count + lax.axis_index("ht")
    for position, block_ref in enumerate(block_refs):
        ordered[me ^ step_at(owners, position)] = block_ref[...]
    for c in range(components):
        for mode in range(band_modes):
            for tile in range(rows // LANES):
                parts = []
                for p in range(2):
                    row = ((tile * 2 + p) * components + c) * band_modes + mode
                    for owner in range(owners):
                        parts.append(ordered[owner, pl.ds(row, slots, stride=per_slot), :])
                top, rest = two_parts(jnp.concatenate(parts, axis=0))
                both = jnp.concatenate([top, rest], axis=0)
                out_ref[c, mode, pl.ds(tile * LANES, LANES)] = dot(
                    both, order_ref[...], ((0,), (0,))
                )


def restore(blocks, order, components, band_modes, rows, ht_count):
    columns = order.shape[1]
    return pl.pallas_call(
        functools.partial(restore_kernel, owners=len(blocks), ht_count=ht_count),
        out_shape=jax.ShapeDtypeStruct((components, band_modes, rows, columns), jnp.float32),
        in_specs=[VMEM] * (len(blocks) + 1),
        out_specs=VMEM,
        scratch_shapes=[pltpu.VMEM((len(blocks),) + blocks[0].shape, jnp.float32)],
        compiler_params=params(),
        cost_estimate=cost(8 * components * band_modes * rows * columns),
        name="restore",
    )(*blocks, order)


def exchange(blocks, axes):
    count, realizations = (len(blocks), lax.axis_size("real"))
    result = list(blocks)
    for position in range(1, count):
        steps = [order[position] for order in steps_of(count)]
        pairs = [
            (index * realizations + r, (index ^ steps[r % 2]) * realizations + r)
            for index in range(count)
            for r in range(realizations)
        ]
        result[position] = lax.ppermute(blocks[position], axes + ("real",), pairs)
    return result


def sum_kernel(first_ref, second_ref, _, out_ref):
    out_ref[...] = first_ref[...] + second_ref[...]


def ordered_sum(first, second, after):
    return pl.pallas_call(
        sum_kernel,
        out_shape=jax.ShapeDtypeStruct(first.shape, jnp.float32),
        in_specs=[VMEM, VMEM, pl.BlockSpec(memory_space=pl.ANY)],
        out_specs=VMEM,
        compiler_params=params(),
        cost_estimate=cost(12 * first.size),
        name="ordered_sum",
    )(first, second, after)


def swap(value, step):
    pairs = [(index, index ^ step) for index in range(lax.axis_size("real"))]
    return lax.ppermute(value, "real", pairs)


def local(velocity, low_index, neighbours, owner_map, mode_counts, helmholtz):
    components, reals_dev, band_modes, rows_ht, columns = velocity.shape
    kx_count, ht_count = (lax.axis_size("kx"), lax.axis_size("ht"))
    own_kx, own_ht = (lax.axis_index("kx"), lax.axis_index("ht"))
    owners, pieces, real_count = (kx_count * ht_count, PIECES, lax.axis_size("real"))
    rows = rows_ht // (kx_count * pieces)
    groups = LANES // rows if rows else 0
    slots = columns // 2 // owners
    if (
        columns != LANES or reals_dev != 1 or rows_ht % LANES or rows % 8 or LANES % rows or kx_count % groups or kx_count & (kx_count - 1)
        or (band_modes * 2 * components) % 8 or slots % 8 or owners & (owners - 1) or low_index.shape[0] >= kx_count * band_modes
        or low_index.shape[0] >= columns or low_index.shape[0] % 2 or real_count < 2 or real_count & (real_count - 1)
    ):
        return local_plain(velocity, low_index, neighbours, owner_map, mode_counts, helmholtz)
    realizations, members = (real_count, low_index.shape[0])
    chunks, modes = (components * band_modes, band_modes * kx_count)
    shape = (components, modes, rows, columns)
    extra_rows = -(-band_modes // 8) * 8
    split = velocity.reshape(chunks, pieces, kx_count, rows, columns)
    blocks = pack_first(split, neighbours, mode_counts, extra_rows)
    parts = [exchange(blocks, ("kx",))]
    for piece in range(1, pieces):
        block = pack(split, piece, parts[0][1])
        block = lax.all_to_all(block, "kx", split_axis=0, concat_axis=0, tiled=True)
        parts.append((block,))
    tables, order, slot_modes = slot_tables(owner_map, columns)
    small = 0.0
    for index, block in enumerate(parts[0]):
        lines = block[chunks * rows : chunks * rows + band_modes, : members + 1]
        here = (own_kx ^ step_at(kx_count, index)) == jnp.arange(kx_count)
        small = small + jnp.where(here[:, None, None], lines[None], 0.0)
    small = small.reshape(modes, members + 1).astype(jnp.int32)
    neighbours, mode_counts = (small[:, :-1], small[:, -1])
    after = slot_modes
    received = []
    for piece, part in enumerate(parts):
        slotted, physical, kept, sent = stress_terms(
            part, shape, low_index, neighbours, tables, after
        )
        forcing = high_terms(physical, low_index, neighbours, mode_counts, tables[2], slot_modes)
        kept = after = kept + swap(sent, 1)
        step = 2
        while step < realizations:
            kept = ordered_sum(kept, swap(kept, step), forcing)
            step *= 2
        blocks = outgoing(
            slotted, forcing, kept, swap(kept, 1), low_index, mode_counts, slot_modes, groups, band_modes,
            owners, realizations, piece > 0,
        )
        if piece:
            received += exchange([block.reshape(slots, -1, LANES) for block in blocks], ("kx", "ht"))
        else:
            block = blocks[0].reshape(owners, slots, -1, LANES)
            first = lax.all_to_all(block, ("kx", "ht"), split_axis=0, concat_axis=0, tiled=True)
    solved = solve(first, received, helmholtz, pieces, groups, kx_count, ht_count)
    returned = [block.reshape(-1, LANES) for block in exchange(solved, ("kx", "ht"))]
    result = restore(returned, order, components, band_modes, rows_ht, ht_count)
    return result.reshape(velocity.shape)


def solution(mesh):
    in_specs = (
        P(None, "real", "kx", "ht", None),
        P(),
        P("kx", None),
        P(),
        P("kx"),
        P(("kx", "ht"), None, None),
    )
    out_specs = P(None, "real", "kx", "ht", None)
    return jax.shard_map(local, mesh=mesh, in_specs=in_specs, out_specs=out_specs, check_vma=False)
```

```python
import functools

import jax
import jax.numpy as jnp
import numpy as np
from jax import lax
from jax.experimental import pallas as pl
from jax.experimental.pallas import tpu as pltpu
from jax.sharding import PartitionSpec as P

dt_step = 0.1


def spanwise_tables(mode_count, point_count):
    column_ids = jnp.arange(2 * mode_count)
    wavenumber = (column_ids // 2).astype(jnp.float32)
    imag_part = column_ids % 2
    positions = 2.0 * jnp.pi * jnp.arange(point_count).astype(jnp.float32) / point_count
    phases = wavenumber[:, None] * positions[None, :]
    forward = jnp.where(imag_part[:, None] == 0, jnp.cos(phases), -jnp.sin(phases)) / jnp.sqrt(
        jnp.float32(mode_count)
    )
    backward = forward.T * (2.0 * mode_count / point_count)
    return (forward, backward)


def nonlinear_rows(fields, low_index, neighbours, mode_counts, forward, backward):
    precision = lax.Precision.HIGH
    realizations, modes, columns = (fields.shape[1], fields.shape[2], fields.shape[4])
    low_select = (low_index[:, None] == jnp.arange(modes)[None, :]).astype(jnp.float32)
    high_mask = 1.0 - jnp.sum(low_select, axis=0)
    high_rows = high_mask[None, None, :, None, None]
    column_mask = ((jnp.arange(columns) // 2)[None, :] < mode_counts[:, None]).astype(jnp.float32)
    physical = jnp.dot(fields, forward, precision=precision)
    low_fields = jnp.take(physical, low_index, axis=2)
    high_low = jnp.zeros_like(physical)
    stresses = []
    for member in range(low_index.shape[0]):
        partner = jnp.take(physical, neighbours[:, member], axis=2)
        low_one = low_fields[:, :, member : member + 1]
        high_low = high_low + low_one * partner[1:2] + partner * low_one[1:2]
        stresses.append(jnp.sum(physical * (partner[1:2] * high_rows), axis=(1, 2)))
    stress = jnp.stack(stresses, axis=1) / realizations
    forcing = jnp.dot(high_low, backward, precision=precision) * high_rows
    low_forcing = jnp.dot(stress, backward, precision=precision)
    low_rows = jnp.einsum("jm,cjyk->cmyk", low_select, low_forcing, precision=lax.Precision.HIGHEST)
    forcing = (forcing + low_rows[:, None]) * column_mask[None, None, :, None, :]
    return fields + dt_step * forcing


def local_plain(velocity, low_index, neighbours, owner_map, mode_counts, helmholtz):
    components, reals_dev, band_modes, rows_ht, columns = velocity.shape
    kz_modes = columns // 2
    forward, backward = spanwise_tables(kz_modes, 4 * kz_modes)
    kx_count, ht_count = (lax.axis_size("kx"), lax.axis_size("ht"))
    real_count = lax.axis_size("real")
    modes, realizations = (band_modes * kx_count, reals_dev * real_count)
    slots_dev = kz_modes // (kx_count * ht_count)
    rows_dev = rows_ht // (kx_count * real_count)
    small = jnp.concatenate([neighbours, mode_counts[:, None]], axis=1)
    small = lax.all_gather(small, "kx", axis=0, tiled=True)
    neighbours, mode_counts = (small[:, :-1], small[:, -1])
    inverse_map = (
        jnp.zeros((kz_modes,), jnp.int32).at[owner_map].set(jnp.arange(kz_modes, dtype=jnp.int32))
    )
    split = velocity.reshape(
        components, reals_dev, band_modes, kx_count * real_count, rows_dev, columns
    )
    split = split.transpose(3, 0, 1, 2, 4, 5)
    split = lax.all_to_all(split, ("kx", "real"), split_axis=0, concat_axis=0, tiled=True)
    fields = split.reshape(
        kx_count, real_count, components, reals_dev, band_modes, rows_dev, columns
    )
    fields = fields.transpose(2, 1, 3, 0, 4, 5, 6).reshape(
        components, realizations, modes, rows_dev, columns
    )
    updated = nonlinear_rows(fields, low_index, neighbours, mode_counts, forward, backward)
    slotted = jnp.take(
        updated.reshape(components, realizations, modes, rows_dev, kz_modes, 2), owner_map, axis=4
    )
    slotted = slotted.reshape(
        components, real_count, reals_dev, modes, rows_dev, kx_count * ht_count, slots_dev, 2
    )
    outgoing = slotted.transpose(5, 1, 6, 2, 0, 3, 7, 4).reshape(
        kx_count * ht_count * real_count, slots_dev, reals_dev * components * modes * 2, rows_dev
    )
    incoming = lax.all_to_all(
        outgoing, ("kx", "ht", "real"), split_axis=0, concat_axis=0, tiled=True
    )
    incoming = incoming.reshape(
        kx_count, ht_count, real_count, slots_dev, reals_dev * components * modes * 2, rows_dev
    )
    incoming = incoming.transpose(3, 4, 1, 0, 2, 5).reshape(
        slots_dev, reals_dev * components * modes * 2, ht_count * rows_ht
    )
    solved = jnp.einsum("syx,snx->sny", helmholtz, incoming, precision=lax.Precision.HIGH)
    solved = solved.reshape(
        slots_dev, reals_dev, components, kx_count, band_modes, 2, ht_count, rows_ht
    )
    solved = solved.transpose(3, 6, 0, 5, 1, 2, 4, 7).reshape(
        kx_count * ht_count, slots_dev * 2, reals_dev * components * band_modes, rows_ht
    )
    returned = lax.all_to_all(solved, ("kx", "ht"), split_axis=0, concat_axis=0, tiled=True)
    restored = returned.reshape(
        kz_modes, 2, reals_dev, components, band_modes, rows_ht
    )
    restored = jnp.take(restored, inverse_map, axis=0)
    return restored.transpose(3, 2, 4, 5, 0, 1).reshape(velocity.shape)


LANES = 128
PIECES = 2
VMEM = pl.BlockSpec(memory_space=pltpu.VMEM)
SMEM = pl.BlockSpec(memory_space=pltpu.SMEM)


def params():
    return pltpu.CompilerParams(vmem_limit_bytes=48 * 1024 * 1024)


ORDERS = {4: (1, 3, 2), 8: (4, 1, 2, 6, 5, 3, 7)}


def steps_of(count):
    even = ORDERS.get(count, tuple(range(1, count)))
    odd = list(even)
    for first in range(0, count - 2, 2):
        odd[first], odd[first + 1] = (even[first + 1], even[first])
    return (0,) + tuple(even), (0,) + tuple(odd)


def step_at(count, position):
    even, odd = steps_of(count)
    return jnp.where((lax.axis_index("real") & 1) == 0, even[position], odd[position])


def cost(size):
    return pl.CostEstimate(flops=0, bytes_accessed=size, transcendentals=0)


def two_parts(value):
    top = value.astype(jnp.bfloat16)
    rest = (value - top.astype(jnp.float32)).astype(jnp.bfloat16)
    return top, rest


def dot(left, right, dims=((1,), (0,))):
    return lax.dot_general(left, right, (dims, ((), ())), preferred_element_type=jnp.float32)


def pack_first_kernel(near_ref, count_ref, velocity_ref, *out_refs):
    chunks, _, kx_count, rows, columns = velocity_ref.shape
    shape = (out_refs[0].shape[0] - chunks * rows, columns)
    row = lax.broadcasted_iota(jnp.int32, shape, 0)
    lane = lax.broadcasted_iota(jnp.int32, shape, 1)
    extra = jnp.zeros(shape, jnp.int32)
    modes, members = near_ref.shape
    for mode in range(modes):
        line = jnp.where(lane == members, count_ref[mode], 0)
        for member in range(members):
            line = jnp.where(lane == member, near_ref[mode, member], line)
        extra = jnp.where(row == mode, line, extra)
    extra = extra.astype(jnp.float32)
    own = lax.axis_index("kx")
    for index, out_ref in enumerate(out_refs):
        partner = own ^ step_at(kx_count, index)
        for chunk in range(chunks):
            out_ref[chunk * rows : (chunk + 1) * rows] = velocity_ref[chunk, 0, partner]
        out_ref[chunks * rows :] = extra


def pack_first(velocity, neighbours, mode_counts, extra_rows):
    chunks, _, kx_count, rows, columns = velocity.shape
    shape = jax.ShapeDtypeStruct((chunks * rows + extra_rows, columns), jnp.float32)
    return pl.pallas_call(
        pack_first_kernel,
        out_shape=(shape,) * kx_count,
        grid=(1,),
        in_specs=[
            SMEM,
            SMEM,
            pl.BlockSpec((chunks, 1, kx_count, rows, columns), lambda i: (0, 0, 0, 0, 0)),
        ],
        out_specs=(pl.BlockSpec(shape.shape, lambda i: (0, 0)),) * kx_count,
        cost_estimate=cost(4 * velocity.size),
        name="pack_first",
    )(neighbours, mode_counts, velocity)


def pack_kernel(velocity_ref, _, out_ref):
    chunks, _, kx_count, rows, columns = velocity_ref.shape
    for index in range(kx_count):
        for chunk in range(chunks):
            place = slice(chunk * rows, (chunk + 1) * rows)
            out_ref[index, place] = velocity_ref[chunk, 0, index]


def pack(velocity, piece, after):
    chunks, _, kx_count, rows, columns = velocity.shape
    shape = (kx_count, chunks * rows, columns)
    return pl.pallas_call(
        pack_kernel,
        out_shape=jax.ShapeDtypeStruct(shape, jnp.float32),
        grid=(1,),
        in_specs=[
            pl.BlockSpec((chunks, 1, kx_count, rows, columns), lambda i: (0, piece, 0, 0, 0)),
            pl.BlockSpec(memory_space=pl.ANY),
        ],
        out_specs=pl.BlockSpec(shape, lambda i: (0, 0, 0)),
        cost_estimate=cost(4 * velocity.size),
        name="pack",
    )(velocity, after)


def tables_kernel(owner_ref, top_ref, rest_ref, first_ref, back_ref, order_ref, slot_ref):
    columns = slot_ref.shape[1]
    modes = columns // 2
    lane = lax.broadcasted_iota(jnp.int32, (8, columns), 1)
    mode = jnp.zeros((8, columns), jnp.int32)
    for slot in range(modes):
        mode = jnp.where(lane % modes == slot, owner_ref[slot], mode)
    slot_ref[...] = mode
    wanted = 2 * mode + lane // modes
    row = lax.broadcasted_iota(jnp.int32, (columns, columns), 0)
    chosen = (row == wanted[:1]).astype(jnp.float32)
    select = chosen.astype(jnp.bfloat16)
    points = top_ref.shape[1]
    for half in range(2):
        rows = slice(half * columns, (half + 1) * columns)
        first_ref[rows, :points] = top_ref[...]
        first_ref[rows, points:] = select
        order_ref[rows] = chosen.T.astype(jnp.bfloat16)
    for index, table_ref in enumerate((top_ref, rest_ref)):
        back = dot(table_ref[...], select, ((0,), (0,))) * (2.0 * modes / points)
        back_ref[:, index * columns : (index + 1) * columns] = back.astype(jnp.bfloat16)


def spanwise_constants(columns, points):
    mode = np.arange(columns) // 2
    phase = 2.0 * np.pi * ((mode[:, None] * np.arange(points)[None, :]) % points) / points
    forward = np.where(np.arange(columns)[:, None] % 2 == 0, np.cos(phase), -np.sin(phase))
    forward = (forward / np.sqrt(columns // 2)).astype(np.float32)
    top = forward.astype(jnp.bfloat16)
    rest = (forward - top.astype(np.float32)).astype(jnp.bfloat16)
    return jnp.asarray(top), jnp.asarray(rest)


def slot_tables(owner_map, columns):
    points = 2 * columns
    top, rest = spanwise_constants(columns, points)
    first, back, order, slot_modes = pl.pallas_call(
        tables_kernel,
        out_shape=(
            jax.ShapeDtypeStruct((2 * columns, points + columns), jnp.bfloat16),
            jax.ShapeDtypeStruct((points, 2 * columns), jnp.bfloat16),
            jax.ShapeDtypeStruct((2 * columns, columns), jnp.bfloat16),
            jax.ShapeDtypeStruct((8, columns), jnp.int32),
        ),
        in_specs=[SMEM, VMEM, VMEM],
        out_specs=(VMEM,) * 4,
        compiler_params=params(),
        cost_estimate=cost(16 * points * columns),
        name="tables",
    )(owner_map, top, rest)
    return (first, rest, back), order, slot_modes


def list_high(low_ref, high_ref, modes):
    found = jnp.int32(0)
    for mode in range(modes):
        is_low = jnp.int32(0)
        for member in range(low_ref.shape[0]):
            is_low = is_low | (low_ref[member] == mode).astype(jnp.int32)
        high_ref[found] = mode
        found = found + 1 - is_low


def tile_at(step, points):
    halves = points // LANES
    return (
        pl.ds(pl.multiple_of((step // halves) * 8, 8), 8),
        pl.ds(pl.multiple_of((step % halves) * LANES, LANES), LANES),
    )


def inverse(fields, back_ref):
    columns = back_ref.shape[1] // 2
    top, rest = two_parts(fields)
    both = dot(top, back_ref[...])
    return both[:, :columns] + both[:, columns:] + dot(rest, back_ref[:, :columns])


def stress_kernel(low_ref, near_ref, *refs):
    block_refs, refs = (refs[:-10], refs[-10:])
    first_ref, second_ref, back_ref, _ = refs[:4]
    slotted_ref, physical, kept_ref, sent_ref, sums, high_ref = refs[4:]
    components, modes, rows, columns = slotted_ref.shape
    if len(block_refs) > 1:
        bands = len(block_refs)
        places = [lax.axis_index("kx") ^ step_at(bands, index) for index in range(bands)]
    else:
        bands = block_refs[0].shape[0]
        places = list(range(bands))
        block_refs = [block_refs[0].at[index] for index in range(bands)]
    points, band_modes = (physical.shape[3], modes // bands)
    members = sums.shape[1]
    odd = (lax.axis_index("real") & 1) == 1
    list_high(low_ref, high_ref, modes)
    size = band_modes * rows
    for c in range(components):
        joined = [block_ref[c * size : (c + 1) * size] for block_ref in block_refs]
        top, rest = two_parts(jnp.concatenate(joined, axis=0))
        both = dot(jnp.concatenate([top, rest], axis=1), first_ref[...])
        fields = both[:, :points] + dot(top, second_ref[...])
        for index in range(bands):
            place = pl.ds(places[index] * band_modes, band_modes)
            part = slice(index * size, (index + 1) * size)
            physical[c, place] = fields[part].reshape(band_modes, rows, points)
            slotted_ref[c, place] = both[part, points:].reshape(band_modes, rows, columns)

    def pairs(step, carry):
        place = tile_at(step, points)

        def one_high(index, totals):
            mode = high_ref[index]
            own = [physical[(c, mode) + place] for c in range(components)]
            totals = list(totals)
            for member in range(members):
                partner = physical[(1, near_ref[mode, member]) + place]
                for c in range(components):
                    slot = member * components + c
                    totals[slot] = totals[slot] + own[c] * partner
            return tuple(totals)

        empty = tuple(jnp.zeros((8, LANES), jnp.float32) for _ in range(members * components))
        totals = lax.fori_loop(0, modes - members, one_high, empty)
        for member in range(members):
            for c in range(components):
                sums[(c, member) + place] = totals[member * components + c]
        return carry

    lax.fori_loop(0, (rows // 8) * (points // LANES), pairs, 0)
    stress = inverse(sums[...].reshape(components * members * rows, points), back_ref)
    stress = stress.reshape(components, 2, members // 2, rows, columns)
    kept_ref[...] = jnp.where(odd, stress[:, 1], stress[:, 0])
    sent_ref[...] = jnp.where(odd, stress[:, 0], stress[:, 1])


def stress_terms(blocks, shape, low_index, neighbours, tables, after):
    components, modes, rows, columns = shape
    members, points = (low_index.shape[0], 2 * columns)
    half = jax.ShapeDtypeStruct((components, members // 2, rows, columns), jnp.float32)
    return pl.pallas_call(
        stress_kernel,
        out_shape=(
            jax.ShapeDtypeStruct(shape, jnp.float32),
            jax.ShapeDtypeStruct((components, modes, rows, points), jnp.float32),
            half,
            half,
        ),
        in_specs=[SMEM] * 2 + [VMEM] * (len(blocks) + 3) + [pl.BlockSpec(memory_space=pl.ANY)],
        out_specs=(VMEM,) * 4,
        scratch_shapes=[
            pltpu.VMEM((components, members, rows, points), jnp.float32),
            pltpu.SMEM((modes + 1,), jnp.int32),
        ],
        compiler_params=params(),
        cost_estimate=cost(4 * components * modes * rows * points * members),
        name="stress",
    )(low_index, neighbours, *blocks, *tables, after)


def products_kernel(
    low_ref, near_ref, count_ref, physical, back_ref, slot_ref, out_ref, products, high_ref
):
    components, modes, rows, points = physical.shape
    members, highs = (low_ref.shape[0], out_ref.shape[1])
    list_high(low_ref, high_ref, modes)

    def pairs(step, carry):
        place = tile_at(step, points)
        low = [
            [physical[(c, low_ref[member]) + place] for c in range(components)]
            for member in range(members)
        ]

        def one_high(index, inner):
            mode = high_ref[index]
            result = [jnp.zeros((8, LANES), jnp.float32) for _ in range(components)]
            for member in range(members):
                near = near_ref[mode, member]
                partner = [physical[(c, near) + place] for c in range(components)]
                for c in range(components):
                    if c == 1:
                        result[c] = result[c] + low[member][1] * partner[1]
                    else:
                        result[c] = result[c] + (
                            low[member][c] * partner[1] + partner[c] * low[member][1]
                        )
            for c in range(components):
                products[(c, index) + place] = result[c] * 2.0 if c == 1 else result[c]
            return inner

        lax.fori_loop(0, highs, one_high, 0)
        return carry

    lax.fori_loop(0, (rows // 8) * (points // LANES), pairs, 0)
    forcing = inverse(products[...].reshape(components * highs * rows, points), back_ref)
    forcing = forcing.reshape(out_ref.shape)
    for index in range(highs):
        active = slot_ref[:1] < count_ref[high_ref[index]]
        out_ref[:, index] = jnp.where(active, forcing[:, index] * dt_step, 0.0)


def high_terms(physical, low_index, neighbours, mode_counts, back, slot_modes):
    components, modes, rows, points = physical.shape
    highs = modes - low_index.shape[0]
    return pl.pallas_call(
        products_kernel,
        out_shape=jax.ShapeDtypeStruct((components, highs, rows, points // 2), jnp.float32),
        in_specs=[SMEM] * 3 + [VMEM] * 3,
        out_specs=VMEM,
        scratch_shapes=[
            pltpu.VMEM((components, highs, rows, points), jnp.float32),
            pltpu.SMEM((modes + 1,), jnp.int32),
        ],
        compiler_params=params(),
        cost_estimate=cost(4 * physical.size * low_index.shape[0]),
        name="products",
    )(low_index, neighbours, mode_counts, physical, back, slot_modes)


def outgoing_kernel(
    low_ref, count_ref, slotted_ref, forcing_ref, kept_ref, other_ref, slot_ref, *refs,
    groups, band_modes, owners, scale
):
    out_refs, (full, turned, high_ref) = (refs[:-3], refs[-3:])
    components, modes, rows, columns = slotted_ref.shape
    half, slots = (kept_ref.shape[1], columns // 2 // owners)
    per_slot = out_refs[0].shape[0] * len(out_refs) // (columns // 2)
    own = lax.axis_index("real") & 1
    list_high(low_ref, high_ref, modes)
    full[...] = slotted_ref[...]
    for index in range(forcing_ref.shape[1]):
        for c in range(components):
            full[c, high_ref[index]] += forcing_ref[c, index]
    for member in range(half):
        for part_ref, start in ((kept_ref, own * half), (other_ref, (1 - own) * half)):
            mode = low_ref[start + member]
            active = slot_ref[:1] < count_ref[mode]
            for c in range(components):
                full[c, mode] += jnp.where(active, part_ref[c, member] * scale, 0.0)
    inner = modes // groups
    if len(out_refs) > 1:
        me = lax.axis_index("kx") * lax.axis_size("ht") + lax.axis_index("ht")
        targets = [me ^ step_at(owners, position) for position in range(owners)]
    for c in range(components):
        for part in range(inner):
            tile = jnp.concatenate([full[c, part + inner * g] for g in range(groups)], axis=0)
            band_low, band_mode = (part // band_modes, part % band_modes)
            if len(out_refs) > 1:
                turned[...] = tile.T
            else:
                value = tile.T
            for p in range(2):
                row = ((band_low * 2 + p) * components + c) * band_modes + band_mode
                if len(out_refs) == 1:
                    out_refs[0][pl.ds(row, columns // 2, stride=per_slot), :] = value[
                        p * (columns // 2) : (p + 1) * (columns // 2)
                    ]
                    continue
                for out_ref, target in zip(out_refs, targets):
                    start = pl.multiple_of((p * owners + target) * slots, slots)
                    out_ref[pl.ds(row, slots, stride=per_slot), :] = turned[pl.ds(start, slots)]


def outgoing(
    slotted, forcing, kept, other, low_index, mode_counts, slot_modes, groups, band_modes, owners,
    realizations, separate,
):
    components, modes, rows, columns = slotted.shape
    total, lanes = ((columns // 2) * (modes // groups) * 2 * components, groups * rows)
    count = owners if separate else 1
    return pl.pallas_call(
        functools.partial(
            outgoing_kernel, groups=groups, band_modes=band_modes, owners=owners,
            scale=dt_step / realizations,
        ),
        out_shape=(jax.ShapeDtypeStruct((total // count, lanes), jnp.float32),) * count,
        in_specs=[SMEM, SMEM] + [VMEM] * 5,
        out_specs=(VMEM,) * count,
        scratch_shapes=[
            pltpu.VMEM(slotted.shape, jnp.float32), pltpu.VMEM((columns, lanes), jnp.float32),
            pltpu.SMEM((modes + 1,), jnp.int32),
        ],
        compiler_params=params(),
        cost_estimate=cost(8 * slotted.size),
        name="outgoing",
    )(low_index, mode_counts, slotted, forcing, kept, other, slot_modes)


def regroup(blocks, rows):
    count = len(blocks)
    lane = lax.broadcasted_iota(jnp.int32, blocks[0].shape, 1) // rows
    step = 1
    while step < count:
        take = (lane & step) == 0
        for i in range(count):
            if i & step == 0:
                here, there = (blocks[i], blocks[i + step])
                blocks[i] = jnp.where(take, here, pltpu.roll(there, step * rows, 1))
                blocks[i + step] = jnp.where(
                    take, pltpu.roll(here, LANES - step * rows, 1), there
                )
        step *= 2
    return blocks


def solve_kernel(*refs, groups, kx_count, ht_count, pieces, piece):
    owners, last = (kx_count * ht_count, piece == pieces - 1)
    own_kx, own_ht = (lax.axis_index("kx"), lax.axis_index("ht"))
    partners = []
    for position in range(owners):
        step = step_at(owners, position)
        partners.append((own_kx ^ (step // ht_count), own_ht ^ (step % ht_count)))
    refs = list(refs)
    matrices = refs.pop()
    arrived = refs.pop()
    source = refs.pop(0)
    if piece:
        ordered = refs.pop()
        blocks = [source] + [refs.pop(0) for _ in range(owners - 1)]
        for block_ref, (kx, ht) in zip(blocks, partners):
            ordered[kx * ht_count + ht] = block_ref[...]
        source = ordered
    matrix_ref = refs.pop(0)
    slots, heights = (matrix_ref.shape[0], matrix_ref.shape[1])
    width = heights // ht_count // pieces
    copies = [
        [
            pltpu.make_async_copy(
                matrix_ref.at[s, :, pl.ds((h * pieces + piece) * width, width)],
                matrices.at[s, h],
                arrived.at[s, h],
            )
            for h in range(ht_count)
        ]
        for s in range(slots)
    ]
    ahead = min(3, slots)
    for s in range(ahead):
        for copy in copies[s]:
            copy.start()
    partial_ref = refs.pop(0) if piece else None
    if last:
        out_refs, full = (refs[:owners], refs[owners])
        lane_tiles, per_band = out_refs[0].shape[1:3]
    rows = LANES // groups
    for s in range(slots):
        tiles = []
        for h in range(ht_count):
            for first in range(0, kx_count, groups):
                blocks = [source[(first + g) * ht_count + h, s] for g in range(groups)]
                tiles.append(jnp.concatenate(regroup(blocks, rows), axis=0))
        fields = jnp.concatenate(tiles, axis=1)
        count = fields.shape[0]
        spare = -count % LANES
        if spare:
            empty = jnp.zeros((spare, fields.shape[1]), jnp.float32)
            fields = jnp.concatenate([fields, empty], axis=0)
        top, rest = two_parts(fields)
        for copy in copies[s]:
            copy.wait()
        if s + ahead < slots:
            for copy in copies[s + ahead]:
                copy.start()
        matrix = jnp.concatenate([matrices[s, h] for h in range(ht_count)], axis=1)
        matrix_top, matrix_rest = two_parts(matrix)
        contract = ((1,), (1,))
        both = dot(matrix_top, jnp.concatenate([top, rest], axis=0), contract)
        solved = both[:, : count + spare] + both[:, count + spare :]
        solved = solved + dot(matrix_rest, top, contract)
        if piece:
            solved = solved + partial_ref[s]
        if not last:
            refs[0][s] = solved
            continue
        for tile in range(heights // LANES):
            full[s % 2, tile] = solved[tile * LANES : (tile + 1) * LANES].T[:count]
        for out_ref, (kx, ht) in zip(out_refs, partners):
            band = pl.ds(pl.multiple_of(kx * per_band, 8), per_band)
            for tile in range(lane_tiles):
                out_ref[s, tile] = full[s % 2, ht * lane_tiles + tile, band]


def solve(blocks, helmholtz, piece, pieces, partial, groups, kx_count, ht_count):
    slots, per_slot, _ = blocks[0].shape[-3:]
    heights, owners, last = (helmholtz.shape[1], kx_count * ht_count, piece == pieces - 1)
    count = per_slot * groups
    scratch = []
    if last:
        shape = (slots, heights // ht_count // LANES, count // kx_count, LANES)
        out_shape = (jax.ShapeDtypeStruct(shape, jnp.float32),) * owners
        scratch.append(pltpu.VMEM((2, heights // LANES, count, LANES), jnp.float32))
    else:
        padded = -(-count // LANES) * LANES
        out_shape = jax.ShapeDtypeStruct((slots, heights, padded), jnp.float32)
    if piece:
        scratch.append(pltpu.VMEM((owners,) + blocks[0].shape, jnp.float32))
    width = heights // ht_count // pieces
    scratch += [
        pltpu.SemaphoreType.DMA((slots, ht_count)),
        pltpu.VMEM((slots, ht_count, heights, width), jnp.float32),
    ]
    started = [] if partial is None else [partial]
    return pl.pallas_call(
        functools.partial(
            solve_kernel, groups=groups, kx_count=kx_count, ht_count=ht_count, pieces=pieces,
            piece=piece,
        ),
        out_shape=out_shape,
        in_specs=[VMEM] * len(blocks) + [pl.BlockSpec(memory_space=pl.ANY)] + [VMEM] * len(started),
        out_specs=(VMEM,) * owners if last else VMEM,
        scratch_shapes=scratch,
        compiler_params=params(),
        cost_estimate=cost(8 * helmholtz.size // pieces),
        name="solve",
    )(*blocks, helmholtz, *started)


def restore_kernel(*refs, owners, ht_count):
    block_refs, (order_ref, out_ref, ordered) = (refs[:-3], refs[-3:])
    components, band_modes, rows, columns = out_ref.shape
    slots = columns // 2 // owners
    per_slot = block_refs[0].shape[0] // slots
    me = lax.axis_index("kx") * ht_count + lax.axis_index("ht")
    for position, block_ref in enumerate(block_refs):
        ordered[me ^ step_at(owners, position)] = block_ref[...]
    for c in range(components):
        for mode in range(band_modes):
            for tile in range(rows // LANES):
                parts = []
                for p in range(2):
                    row = ((tile * 2 + p) * components + c) * band_modes + mode
                    for owner in range(owners):
                        parts.append(ordered[owner, pl.ds(row, slots, stride=per_slot), :])
                top, rest = two_parts(jnp.concatenate(parts, axis=0))
                both = jnp.concatenate([top, rest], axis=0)
                out_ref[c, mode, pl.ds(tile * LANES, LANES)] = dot(
                    both, order_ref[...], ((0,), (0,))
                )


def restore(blocks, order, components, band_modes, rows, ht_count):
    columns = order.shape[1]
    return pl.pallas_call(
        functools.partial(restore_kernel, owners=len(blocks), ht_count=ht_count),
        out_shape=jax.ShapeDtypeStruct((components, band_modes, rows, columns), jnp.float32),
        in_specs=[VMEM] * (len(blocks) + 1),
        out_specs=VMEM,
        scratch_shapes=[pltpu.VMEM((len(blocks),) + blocks[0].shape, jnp.float32)],
        compiler_params=params(),
        cost_estimate=cost(8 * components * band_modes * rows * columns),
        name="restore",
    )(*blocks, order)


def exchange(blocks, axes):
    count, realizations = (len(blocks), lax.axis_size("real"))
    result = list(blocks)
    for position in range(1, count):
        steps = [order[position] for order in steps_of(count)]
        pairs = [
            (index * realizations + r, (index ^ steps[r % 2]) * realizations + r)
            for index in range(count)
            for r in range(realizations)
        ]
        result[position] = lax.ppermute(blocks[position], axes + ("real",), pairs)
    return result


def sum_kernel(first_ref, second_ref, _, out_ref):
    out_ref[...] = first_ref[...] + second_ref[...]


def ordered_sum(first, second, after):
    return pl.pallas_call(
        sum_kernel,
        out_shape=jax.ShapeDtypeStruct(first.shape, jnp.float32),
        in_specs=[VMEM, VMEM, pl.BlockSpec(memory_space=pl.ANY)],
        out_specs=VMEM,
        compiler_params=params(),
        cost_estimate=cost(12 * first.size),
        name="ordered_sum",
    )(first, second, after)


def swap(value, step):
    pairs = [(index, index ^ step) for index in range(lax.axis_size("real"))]
    return lax.ppermute(value, "real", pairs)


def local(velocity, low_index, neighbours, owner_map, mode_counts, helmholtz):
    components, reals_dev, band_modes, rows_ht, columns = velocity.shape
    kx_count, ht_count = (lax.axis_size("kx"), lax.axis_size("ht"))
    own_kx, own_ht = (lax.axis_index("kx"), lax.axis_index("ht"))
    owners, pieces, real_count = (kx_count * ht_count, PIECES, lax.axis_size("real"))
    rows = rows_ht // (kx_count * pieces)
    groups = LANES // rows if rows else 0
    slots = columns // 2 // owners
    if (
        columns != LANES or reals_dev != 1 or rows_ht % LANES or rows % 8 or LANES % rows or kx_count % groups or kx_count & (kx_count - 1)
        or (band_modes * 2 * components) % 8 or slots % 8 or owners & (owners - 1) or low_index.shape[0] >= kx_count * band_modes
        or low_index.shape[0] >= columns or low_index.shape[0] % 2 or real_count < 2 or real_count & (real_count - 1)
    ):
        return local_plain(velocity, low_index, neighbours, owner_map, mode_counts, helmholtz)
    realizations, members = (real_count, low_index.shape[0])
    chunks, modes = (components * band_modes, band_modes * kx_count)
    shape = (components, modes, rows, columns)
    extra_rows = -(-band_modes // 8) * 8
    split = velocity.reshape(chunks, pieces, kx_count, rows, columns)
    blocks = pack_first(split, neighbours, mode_counts, extra_rows)
    parts = [exchange(blocks, ("kx",))]
    for piece in range(1, pieces):
        block = pack(split, piece, parts[0][1])
        block = lax.all_to_all(block, "kx", split_axis=0, concat_axis=0, tiled=True)
        parts.append((block,))
    tables, order, slot_modes = slot_tables(owner_map, columns)
    small = 0.0
    for index, block in enumerate(parts[0]):
        lines = block[chunks * rows : chunks * rows + band_modes, : members + 1]
        here = (own_kx ^ step_at(kx_count, index)) == jnp.arange(kx_count)
        small = small + jnp.where(here[:, None, None], lines[None], 0.0)
    small = small.reshape(modes, members + 1).astype(jnp.int32)
    neighbours, mode_counts = (small[:, :-1], small[:, -1])
    after = slot_modes
    received = []
    for piece, part in enumerate(parts):
        slotted, physical, kept, sent = stress_terms(
            part, shape, low_index, neighbours, tables, after
        )
        forcing = high_terms(physical, low_index, neighbours, mode_counts, tables[2], slot_modes)
        kept = after = kept + swap(sent, 1)
        step = 2
        while step < realizations:
            kept = ordered_sum(kept, swap(kept, step), forcing)
            step *= 2
        blocks = outgoing(
            slotted, forcing, kept, swap(kept, 1), low_index, mode_counts, slot_modes, groups, band_modes,
            owners, realizations, piece > 0,
        )
        if piece:
            blocks = [block.reshape(slots, -1, LANES) for block in blocks]
            received.append(exchange(blocks, ("kx", "ht")))
        else:
            block = blocks[0].reshape(owners, slots, -1, LANES)
            block = lax.all_to_all(block, ("kx", "ht"), split_axis=0, concat_axis=0, tiled=True)
            received.append([block])
    solved = None
    for piece, blocks in enumerate(received):
        solved = solve(blocks, helmholtz, piece, pieces, solved, groups, kx_count, ht_count)
    returned = [block.reshape(-1, LANES) for block in exchange(solved, ("kx", "ht"))]
    result = restore(returned, order, components, band_modes, rows_ht, ht_count)
    return result.reshape(velocity.shape)


def solution(mesh):
    in_specs = (
        P(None, "real", "kx", "ht", None),
        P(),
        P("kx", None),
        P(),
        P("kx"),
        P(("kx", "ht"), None, None),
    )
    out_specs = P(None, "real", "kx", "ht", None)
    return jax.shard_map(local, mesh=mesh, in_specs=in_specs, out_specs=out_specs, check_vma=False)
```

```python
import functools

import jax
import jax.numpy as jnp
import numpy as np
from jax import lax
from jax.experimental import pallas as pl
from jax.experimental.pallas import tpu as pltpu
from jax.sharding import PartitionSpec as P

dt_step = 0.1


def spanwise_tables(mode_count, point_count):
    column_ids = jnp.arange(2 * mode_count)
    wavenumber = (column_ids // 2).astype(jnp.float32)
    imag_part = column_ids % 2
    positions = 2.0 * jnp.pi * jnp.arange(point_count).astype(jnp.float32) / point_count
    phases = wavenumber[:, None] * positions[None, :]
    forward = jnp.where(imag_part[:, None] == 0, jnp.cos(phases), -jnp.sin(phases)) / jnp.sqrt(
        jnp.float32(mode_count)
    )
    backward = forward.T * (2.0 * mode_count / point_count)
    return (forward, backward)


def nonlinear_rows(fields, low_index, neighbours, mode_counts, forward, backward):
    precision = lax.Precision.HIGH
    realizations, modes, columns = (fields.shape[1], fields.shape[2], fields.shape[4])
    low_select = (low_index[:, None] == jnp.arange(modes)[None, :]).astype(jnp.float32)
    high_mask = 1.0 - jnp.sum(low_select, axis=0)
    high_rows = high_mask[None, None, :, None, None]
    column_mask = ((jnp.arange(columns) // 2)[None, :] < mode_counts[:, None]).astype(jnp.float32)
    physical = jnp.dot(fields, forward, precision=precision)
    low_fields = jnp.take(physical, low_index, axis=2)
    high_low = jnp.zeros_like(physical)
    stresses = []
    for member in range(low_index.shape[0]):
        partner = jnp.take(physical, neighbours[:, member], axis=2)
        low_one = low_fields[:, :, member : member + 1]
        high_low = high_low + low_one * partner[1:2] + partner * low_one[1:2]
        stresses.append(jnp.sum(physical * (partner[1:2] * high_rows), axis=(1, 2)))
    stress = jnp.stack(stresses, axis=1) / realizations
    forcing = jnp.dot(high_low, backward, precision=precision) * high_rows
    low_forcing = jnp.dot(stress, backward, precision=precision)
    low_rows = jnp.einsum("jm,cjyk->cmyk", low_select, low_forcing, precision=lax.Precision.HIGHEST)
    forcing = (forcing + low_rows[:, None]) * column_mask[None, None, :, None, :]
    return fields + dt_step * forcing


def local_plain(velocity, low_index, neighbours, owner_map, mode_counts, helmholtz):
    components, reals_dev, band_modes, rows_ht, columns = velocity.shape
    kz_modes = columns // 2
    forward, backward = spanwise_tables(kz_modes, 4 * kz_modes)
    kx_count, ht_count = (lax.axis_size("kx"), lax.axis_size("ht"))
    real_count = lax.axis_size("real")
    modes, realizations = (band_modes * kx_count, reals_dev * real_count)
    slots_dev = kz_modes // (kx_count * ht_count)
    rows_dev = rows_ht // (kx_count * real_count)
    small = jnp.concatenate([neighbours, mode_counts[:, None]], axis=1)
    small = lax.all_gather(small, "kx", axis=0, tiled=True)
    neighbours, mode_counts = (small[:, :-1], small[:, -1])
    inverse_map = (
        jnp.zeros((kz_modes,), jnp.int32).at[owner_map].set(jnp.arange(kz_modes, dtype=jnp.int32))
    )
    split = velocity.reshape(
        components, reals_dev, band_modes, kx_count * real_count, rows_dev, columns
    )
    split = split.transpose(3, 0, 1, 2, 4, 5)
    split = lax.all_to_all(split, ("kx", "real"), split_axis=0, concat_axis=0, tiled=True)
    fields = split.reshape(
        kx_count, real_count, components, reals_dev, band_modes, rows_dev, columns
    )
    fields = fields.transpose(2, 1, 3, 0, 4, 5, 6).reshape(
        components, realizations, modes, rows_dev, columns
    )
    updated = nonlinear_rows(fields, low_index, neighbours, mode_counts, forward, backward)
    slotted = jnp.take(
        updated.reshape(components, realizations, modes, rows_dev, kz_modes, 2), owner_map, axis=4
    )
    slotted = slotted.reshape(
        components, real_count, reals_dev, modes, rows_dev, kx_count * ht_count, slots_dev, 2
    )
    outgoing = slotted.transpose(5, 1, 6, 2, 0, 3, 7, 4).reshape(
        kx_count * ht_count * real_count, slots_dev, reals_dev * components * modes * 2, rows_dev
    )
    incoming = lax.all_to_all(
        outgoing, ("kx", "ht", "real"), split_axis=0, concat_axis=0, tiled=True
    )
    incoming = incoming.reshape(
        kx_count, ht_count, real_count, slots_dev, reals_dev * components * modes * 2, rows_dev
    )
    incoming = incoming.transpose(3, 4, 1, 0, 2, 5).reshape(
        slots_dev, reals_dev * components * modes * 2, ht_count * rows_ht
    )
    solved = jnp.einsum("syx,snx->sny", helmholtz, incoming, precision=lax.Precision.HIGH)
    solved = solved.reshape(
        slots_dev, reals_dev, components, kx_count, band_modes, 2, ht_count, rows_ht
    )
    solved = solved.transpose(3, 6, 0, 5, 1, 2, 4, 7).reshape(
        kx_count * ht_count, slots_dev * 2, reals_dev * components * band_modes, rows_ht
    )
    returned = lax.all_to_all(solved, ("kx", "ht"), split_axis=0, concat_axis=0, tiled=True)
    restored = returned.reshape(
        kz_modes, 2, reals_dev, components, band_modes, rows_ht
    )
    restored = jnp.take(restored, inverse_map, axis=0)
    return restored.transpose(3, 2, 4, 5, 0, 1).reshape(velocity.shape)


LANES = 128
PIECES = 2
VMEM = pl.BlockSpec(memory_space=pltpu.VMEM)
SMEM = pl.BlockSpec(memory_space=pltpu.SMEM)


def params():
    return pltpu.CompilerParams(vmem_limit_bytes=48 * 1024 * 1024)


ORDERS = {4: (1, 3, 2), 8: (4, 1, 2, 6, 5, 3, 7)}


def steps_of(count):
    even = ORDERS.get(count, tuple(range(1, count)))
    odd = list(even)
    for first in range(0, count - 2, 2):
        odd[first], odd[first + 1] = (even[first + 1], even[first])
    return (0,) + tuple(even), (0,) + tuple(odd)


def step_at(count, position):
    even, odd = steps_of(count)
    return jnp.where((lax.axis_index("real") & 1) == 0, even[position], odd[position])


def cost(size):
    return pl.CostEstimate(flops=0, bytes_accessed=size, transcendentals=0)


def two_parts(value):
    top = value.astype(jnp.bfloat16)
    rest = (value - top.astype(jnp.float32)).astype(jnp.bfloat16)
    return top, rest


def dot(left, right, dims=((1,), (0,))):
    return lax.dot_general(left, right, (dims, ((), ())), preferred_element_type=jnp.float32)


def pack_first_kernel(near_ref, count_ref, velocity_ref, *out_refs):
    chunks, _, kx_count, rows, columns = velocity_ref.shape
    shape = (out_refs[0].shape[0] - chunks * rows, columns)
    row = lax.broadcasted_iota(jnp.int32, shape, 0)
    lane = lax.broadcasted_iota(jnp.int32, shape, 1)
    extra = jnp.zeros(shape, jnp.int32)
    modes, members = near_ref.shape
    for mode in range(modes):
        line = jnp.where(lane == members, count_ref[mode], 0)
        for member in range(members):
            line = jnp.where(lane == member, near_ref[mode, member], line)
        extra = jnp.where(row == mode, line, extra)
    extra = extra.astype(jnp.float32)
    own = lax.axis_index("kx")
    for index, out_ref in enumerate(out_refs):
        partner = own ^ step_at(kx_count, index)
        for chunk in range(chunks):
            out_ref[chunk * rows : (chunk + 1) * rows] = velocity_ref[chunk, 0, partner]
        out_ref[chunks * rows :] = extra


def pack_first(velocity, neighbours, mode_counts, extra_rows):
    chunks, _, kx_count, rows, columns = velocity.shape
    shape = jax.ShapeDtypeStruct((chunks * rows + extra_rows, columns), jnp.float32)
    return pl.pallas_call(
        pack_first_kernel,
        out_shape=(shape,) * kx_count,
        grid=(1,),
        in_specs=[
            SMEM,
            SMEM,
            pl.BlockSpec((chunks, 1, kx_count, rows, columns), lambda i: (0, 0, 0, 0, 0)),
        ],
        out_specs=(pl.BlockSpec(shape.shape, lambda i: (0, 0)),) * kx_count,
        cost_estimate=cost(4 * velocity.size),
        name="pack_first",
    )(neighbours, mode_counts, velocity)


def pack_kernel(velocity_ref, out_ref):
    chunks, _, kx_count, rows, columns = velocity_ref.shape
    for index in range(kx_count):
        for chunk in range(chunks):
            place = slice(chunk * rows, (chunk + 1) * rows)
            out_ref[index, place] = velocity_ref[chunk, 0, index]


def pack(velocity, piece):
    chunks, _, kx_count, rows, columns = velocity.shape
    shape = (kx_count, chunks * rows, columns)
    return pl.pallas_call(
        pack_kernel,
        out_shape=jax.ShapeDtypeStruct(shape, jnp.float32),
        grid=(1,),
        in_specs=[
            pl.BlockSpec((chunks, 1, kx_count, rows, columns), lambda i: (0, piece, 0, 0, 0)),
        ],
        out_specs=pl.BlockSpec(shape, lambda i: (0, 0, 0)),
        cost_estimate=cost(4 * velocity.size),
        name="pack",
    )(velocity)


def hand_on_kernel(value_ref, after_ref, out_ref):
    pass


def hand_on(value, after):
    return pl.pallas_call(
        hand_on_kernel,
        out_shape=jax.ShapeDtypeStruct(value.shape, value.dtype),
        in_specs=[pl.BlockSpec(memory_space=pl.ANY)] * 2,
        out_specs=pl.BlockSpec(memory_space=pl.ANY),
        input_output_aliases={0: 0},
        cost_estimate=cost(0),
        name="hand_on",
    )(value, after)


def tables_kernel(owner_ref, top_ref, rest_ref, first_ref, back_ref, order_ref, slot_ref):
    columns = slot_ref.shape[1]
    modes = columns // 2
    lane = lax.broadcasted_iota(jnp.int32, (8, columns), 1)
    mode = jnp.zeros((8, columns), jnp.int32)
    for slot in range(modes):
        mode = jnp.where(lane % modes == slot, owner_ref[slot], mode)
    slot_ref[...] = mode
    wanted = 2 * mode + lane // modes
    row = lax.broadcasted_iota(jnp.int32, (columns, columns), 0)
    chosen = (row == wanted[:1]).astype(jnp.float32)
    select = chosen.astype(jnp.bfloat16)
    points = top_ref.shape[1]
    for half in range(2):
        rows = slice(half * columns, (half + 1) * columns)
        first_ref[rows, :points] = top_ref[...]
        first_ref[rows, points:] = select
        order_ref[rows] = chosen.T.astype(jnp.bfloat16)
    for index, table_ref in enumerate((top_ref, rest_ref)):
        back = dot(table_ref[...], select, ((0,), (0,))) * (2.0 * modes / points)
        back_ref[:, index * columns : (index + 1) * columns] = back.astype(jnp.bfloat16)


def spanwise_constants(columns, points):
    mode = np.arange(columns) // 2
    phase = 2.0 * np.pi * ((mode[:, None] * np.arange(points)[None, :]) % points) / points
    forward = np.where(np.arange(columns)[:, None] % 2 == 0, np.cos(phase), -np.sin(phase))
    forward = (forward / np.sqrt(columns // 2)).astype(np.float32)
    top = forward.astype(jnp.bfloat16)
    rest = (forward - top.astype(np.float32)).astype(jnp.bfloat16)
    return jnp.asarray(top), jnp.asarray(rest)


def slot_tables(owner_map, columns):
    points = 2 * columns
    top, rest = spanwise_constants(columns, points)
    first, back, order, slot_modes = pl.pallas_call(
        tables_kernel,
        out_shape=(
            jax.ShapeDtypeStruct((2 * columns, points + columns), jnp.bfloat16),
            jax.ShapeDtypeStruct((points, 2 * columns), jnp.bfloat16),
            jax.ShapeDtypeStruct((2 * columns, columns), jnp.bfloat16),
            jax.ShapeDtypeStruct((8, columns), jnp.int32),
        ),
        in_specs=[SMEM, VMEM, VMEM],
        out_specs=(VMEM,) * 4,
        compiler_params=params(),
        cost_estimate=cost(16 * points * columns),
        name="tables",
    )(owner_map, top, rest)
    return (first, rest, back), order, slot_modes


def list_high(low_ref, high_ref, modes):
    found = jnp.int32(0)
    for mode in range(modes):
        is_low = jnp.int32(0)
        for member in range(low_ref.shape[0]):
            is_low = is_low | (low_ref[member] == mode).astype(jnp.int32)
        high_ref[found] = mode
        found = found + 1 - is_low


def tile_at(step, points):
    halves = points // LANES
    return (
        pl.ds(pl.multiple_of((step // halves) * 8, 8), 8),
        pl.ds(pl.multiple_of((step % halves) * LANES, LANES), LANES),
    )


def inverse(fields, back_ref):
    columns = back_ref.shape[1] // 2
    top, rest = two_parts(fields)
    both = dot(top, back_ref[...])
    return both[:, :columns] + both[:, columns:] + dot(rest, back_ref[:, :columns])


def stress_kernel(low_ref, near_ref, *refs):
    block_refs, refs = (refs[:-10], refs[-10:])
    first_ref, second_ref, back_ref, _ = refs[:4]
    slotted_ref, physical, kept_ref, sent_ref, sums, high_ref = refs[4:]
    components, modes, rows, columns = slotted_ref.shape
    if len(block_refs) > 1:
        bands = len(block_refs)
        places = [lax.axis_index("kx") ^ step_at(bands, index) for index in range(bands)]
    else:
        bands = block_refs[0].shape[0]
        places = list(range(bands))
        block_refs = [block_refs[0].at[index] for index in range(bands)]
    points, band_modes = (physical.shape[3], modes // bands)
    members = sums.shape[1]
    odd = (lax.axis_index("real") & 1) == 1
    list_high(low_ref, high_ref, modes)
    size = band_modes * rows
    for c in range(components):
        joined = [block_ref[c * size : (c + 1) * size] for block_ref in block_refs]
        top, rest = two_parts(jnp.concatenate(joined, axis=0))
        both = dot(jnp.concatenate([top, rest], axis=1), first_ref[...])
        fields = both[:, :points] + dot(top, second_ref[...])
        for index in range(bands):
            place = pl.ds(places[index] * band_modes, band_modes)
            part = slice(index * size, (index + 1) * size)
            physical[c, place] = fields[part].reshape(band_modes, rows, points)
            slotted_ref[c, place] = both[part, points:].reshape(band_modes, rows, columns)

    def pairs(step, carry):
        place = tile_at(step, points)

        def one_high(index, totals):
            mode = high_ref[index]
            own = [physical[(c, mode) + place] for c in range(components)]
            totals = list(totals)
            for member in range(members):
                partner = physical[(1, near_ref[mode, member]) + place]
                for c in range(components):
                    slot = member * components + c
                    totals[slot] = totals[slot] + own[c] * partner
            return tuple(totals)

        empty = tuple(jnp.zeros((8, LANES), jnp.float32) for _ in range(members * components))
        totals = lax.fori_loop(0, modes - members, one_high, empty)
        for member in range(members):
            for c in range(components):
                sums[(c, member) + place] = totals[member * components + c]
        return carry

    lax.fori_loop(0, (rows // 8) * (points // LANES), pairs, 0)
    stress = inverse(sums[...].reshape(components * members * rows, points), back_ref)
    stress = stress.reshape(components, 2, members // 2, rows, columns)
    kept_ref[...] = jnp.where(odd, stress[:, 1], stress[:, 0])
    sent_ref[...] = jnp.where(odd, stress[:, 0], stress[:, 1])


def stress_terms(blocks, shape, low_index, neighbours, tables, after):
    components, modes, rows, columns = shape
    members, points = (low_index.shape[0], 2 * columns)
    half = jax.ShapeDtypeStruct((components, members // 2, rows, columns), jnp.float32)
    return pl.pallas_call(
        stress_kernel,
        out_shape=(
            jax.ShapeDtypeStruct(shape, jnp.float32),
            jax.ShapeDtypeStruct((components, modes, rows, points), jnp.float32),
            half,
            half,
        ),
        in_specs=[SMEM] * 2 + [VMEM] * (len(blocks) + 3) + [pl.BlockSpec(memory_space=pl.ANY)],
        out_specs=(VMEM,) * 4,
        scratch_shapes=[
            pltpu.VMEM((components, members, rows, points), jnp.float32),
            pltpu.SMEM((modes + 1,), jnp.int32),
        ],
        compiler_params=params(),
        cost_estimate=cost(4 * components * modes * rows * points * members),
        name="stress",
    )(low_index, neighbours, *blocks, *tables, after)


def products_kernel(
    low_ref, near_ref, count_ref, physical, back_ref, slot_ref, out_ref, products, high_ref
):
    components, modes, rows, points = physical.shape
    members, highs = (low_ref.shape[0], out_ref.shape[1])
    list_high(low_ref, high_ref, modes)

    def pairs(step, carry):
        place = tile_at(step, points)
        low = [
            [physical[(c, low_ref[member]) + place] for c in range(components)]
            for member in range(members)
        ]

        def one_high(index, inner):
            mode = high_ref[index]
            result = [jnp.zeros((8, LANES), jnp.float32) for _ in range(components)]
            for member in range(members):
                near = near_ref[mode, member]
                partner = [physical[(c, near) + place] for c in range(components)]
                for c in range(components):
                    if c == 1:
                        result[c] = result[c] + low[member][1] * partner[1]
                    else:
                        result[c] = result[c] + (
                            low[member][c] * partner[1] + partner[c] * low[member][1]
                        )
            for c in range(components):
                products[(c, index) + place] = result[c] * 2.0 if c == 1 else result[c]
            return inner

        lax.fori_loop(0, highs, one_high, 0)
        return carry

    lax.fori_loop(0, (rows // 8) * (points // LANES), pairs, 0)
    forcing = inverse(products[...].reshape(components * highs * rows, points), back_ref)
    forcing = forcing.reshape(out_ref.shape)
    for index in range(highs):
        active = slot_ref[:1] < count_ref[high_ref[index]]
        out_ref[:, index] = jnp.where(active, forcing[:, index] * dt_step, 0.0)


def high_terms(physical, low_index, neighbours, mode_counts, back, slot_modes):
    components, modes, rows, points = physical.shape
    highs = modes - low_index.shape[0]
    return pl.pallas_call(
        products_kernel,
        out_shape=jax.ShapeDtypeStruct((components, highs, rows, points // 2), jnp.float32),
        in_specs=[SMEM] * 3 + [VMEM] * 3,
        out_specs=VMEM,
        scratch_shapes=[
            pltpu.VMEM((components, highs, rows, points), jnp.float32),
            pltpu.SMEM((modes + 1,), jnp.int32),
        ],
        compiler_params=params(),
        cost_estimate=cost(4 * physical.size * low_index.shape[0]),
        name="products",
    )(low_index, neighbours, mode_counts, physical, back, slot_modes)


def outgoing_kernel(
    low_ref, count_ref, slotted_ref, forcing_ref, kept_ref, other_ref, slot_ref, *refs,
    groups, band_modes, owners, scale
):
    out_refs, (full, turned, high_ref) = (refs[:-3], refs[-3:])
    components, modes, rows, columns = slotted_ref.shape
    half, slots = (kept_ref.shape[1], columns // 2 // owners)
    per_slot = out_refs[0].shape[0] * len(out_refs) // (columns // 2)
    own = lax.axis_index("real") & 1
    list_high(low_ref, high_ref, modes)
    full[...] = slotted_ref[...]
    for index in range(forcing_ref.shape[1]):
        for c in range(components):
            full[c, high_ref[index]] += forcing_ref[c, index]
    for member in range(half):
        for part_ref, start in ((kept_ref, own * half), (other_ref, (1 - own) * half)):
            mode = low_ref[start + member]
            active = slot_ref[:1] < count_ref[mode]
            for c in range(components):
                full[c, mode] += jnp.where(active, part_ref[c, member] * scale, 0.0)
    inner = modes // groups
    if len(out_refs) > 1:
        me = lax.axis_index("kx") * lax.axis_size("ht") + lax.axis_index("ht")
        targets = [me ^ step_at(owners, position) for position in range(owners)]
    for c in range(components):
        for part in range(inner):
            tile = jnp.concatenate([full[c, part + inner * g] for g in range(groups)], axis=0)
            band_low, band_mode = (part // band_modes, part % band_modes)
            if len(out_refs) > 1:
                turned[...] = tile.T
            else:
                value = tile.T
            for p in range(2):
                row = ((band_low * 2 + p) * components + c) * band_modes + band_mode
                if len(out_refs) == 1:
                    out_refs[0][pl.ds(row, columns // 2, stride=per_slot), :] = value[
                        p * (columns // 2) : (p + 1) * (columns // 2)
                    ]
                    continue
                for out_ref, target in zip(out_refs, targets):
                    start = pl.multiple_of((p * owners + target) * slots, slots)
                    out_ref[pl.ds(row, slots, stride=per_slot), :] = turned[pl.ds(start, slots)]


def outgoing(
    slotted, forcing, kept, other, low_index, mode_counts, slot_modes, groups, band_modes, owners,
    realizations, separate,
):
    components, modes, rows, columns = slotted.shape
    total, lanes = ((columns // 2) * (modes // groups) * 2 * components, groups * rows)
    count = owners if separate else 1
    return pl.pallas_call(
        functools.partial(
            outgoing_kernel, groups=groups, band_modes=band_modes, owners=owners,
            scale=dt_step / realizations,
        ),
        out_shape=(jax.ShapeDtypeStruct((total // count, lanes), jnp.float32),) * count,
        in_specs=[SMEM, SMEM] + [VMEM] * 5,
        out_specs=(VMEM,) * count,
        scratch_shapes=[
            pltpu.VMEM(slotted.shape, jnp.float32), pltpu.VMEM((columns, lanes), jnp.float32),
            pltpu.SMEM((modes + 1,), jnp.int32),
        ],
        compiler_params=params(),
        cost_estimate=cost(8 * slotted.size),
        name="outgoing",
    )(low_index, mode_counts, slotted, forcing, kept, other, slot_modes)


def regroup(blocks, rows):
    count = len(blocks)
    lane = lax.broadcasted_iota(jnp.int32, blocks[0].shape, 1) // rows
    step = 1
    while step < count:
        take = (lane & step) == 0
        for i in range(count):
            if i & step == 0:
                here, there = (blocks[i], blocks[i + step])
                blocks[i] = jnp.where(take, here, pltpu.roll(there, step * rows, 1))
                blocks[i + step] = jnp.where(
                    take, pltpu.roll(here, LANES - step * rows, 1), there
                )
        step *= 2
    return blocks


def solve_kernel(*refs, groups, kx_count, ht_count, pieces, piece):
    owners, last = (kx_count * ht_count, piece == pieces - 1)
    own_kx, own_ht = (lax.axis_index("kx"), lax.axis_index("ht"))
    partners = []
    for position in range(owners):
        step = step_at(owners, position)
        partners.append((own_kx ^ (step // ht_count), own_ht ^ (step % ht_count)))
    refs = list(refs)
    matrices = refs.pop()
    arrived = refs.pop()
    source = refs.pop(0)
    if piece:
        ordered = refs.pop()
        blocks = [source] + [refs.pop(0) for _ in range(owners - 1)]
        for block_ref, (kx, ht) in zip(blocks, partners):
            ordered[kx * ht_count + ht] = block_ref[...]
        source = ordered
    matrix_ref = refs.pop(0)
    slots, heights = (matrix_ref.shape[0], matrix_ref.shape[1])
    width = heights // ht_count // pieces
    copies = [
        [
            pltpu.make_async_copy(
                matrix_ref.at[s, :, pl.ds((h * pieces + piece) * width, width)],
                matrices.at[s, h],
                arrived.at[s, h],
            )
            for h in range(ht_count)
        ]
        for s in range(slots)
    ]
    ahead = min(3, slots)
    for s in range(ahead):
        for copy in copies[s]:
            copy.start()
    partial_ref = refs.pop(0) if piece else None
    if last:
        out_refs, full = (refs[:owners], refs[owners])
        lane_tiles, per_band = out_refs[0].shape[1:3]
    rows = LANES // groups
    for s in range(slots):
        tiles = []
        for h in range(ht_count):
            for first in range(0, kx_count, groups):
                blocks = [source[(first + g) * ht_count + h, s] for g in range(groups)]
                tiles.append(jnp.concatenate(regroup(blocks, rows), axis=0))
        fields = jnp.concatenate(tiles, axis=1)
        count = fields.shape[0]
        spare = -count % LANES
        if spare:
            empty = jnp.zeros((spare, fields.shape[1]), jnp.float32)
            fields = jnp.concatenate([fields, empty], axis=0)
        top, rest = two_parts(fields)
        for copy in copies[s]:
            copy.wait()
        if s + ahead < slots:
            for copy in copies[s + ahead]:
                copy.start()
        matrix = jnp.concatenate([matrices[s, h] for h in range(ht_count)], axis=1)
        matrix_top, matrix_rest = two_parts(matrix)
        contract = ((1,), (1,))
        both = dot(matrix_top, jnp.concatenate([top, rest], axis=0), contract)
        solved = both[:, : count + spare] + both[:, count + spare :]
        solved = solved + dot(matrix_rest, top, contract)
        if piece:
            solved = solved + partial_ref[s]
        if not last:
            refs[0][s] = solved
            continue
        for tile in range(heights // LANES):
            full[s % 2, tile] = solved[tile * LANES : (tile + 1) * LANES].T[:count]
        for out_ref, (kx, ht) in zip(out_refs, partners):
            band = pl.ds(pl.multiple_of(kx * per_band, 8), per_band)
            for tile in range(lane_tiles):
                out_ref[s, tile] = full[s % 2, ht * lane_tiles + tile, band]


def solve(blocks, helmholtz, piece, pieces, partial, groups, kx_count, ht_count):
    slots, per_slot, _ = blocks[0].shape[-3:]
    heights, owners, last = (helmholtz.shape[1], kx_count * ht_count, piece == pieces - 1)
    count = per_slot * groups
    scratch = []
    if last:
        shape = (slots, heights // ht_count // LANES, count // kx_count, LANES)
        out_shape = (jax.ShapeDtypeStruct(shape, jnp.float32),) * owners
        scratch.append(pltpu.VMEM((2, heights // LANES, count, LANES), jnp.float32))
    else:
        padded = -(-count // LANES) * LANES
        out_shape = jax.ShapeDtypeStruct((slots, heights, padded), jnp.float32)
    if piece:
        scratch.append(pltpu.VMEM((owners,) + blocks[0].shape, jnp.float32))
    width = heights // ht_count // pieces
    scratch += [
        pltpu.SemaphoreType.DMA((slots, ht_count)),
        pltpu.VMEM((slots, ht_count, heights, width), jnp.float32),
    ]
    started = [] if partial is None else [partial]
    return pl.pallas_call(
        functools.partial(
            solve_kernel, groups=groups, kx_count=kx_count, ht_count=ht_count, pieces=pieces,
            piece=piece,
        ),
        out_shape=out_shape,
        in_specs=[VMEM] * len(blocks) + [pl.BlockSpec(memory_space=pl.ANY)] + [VMEM] * len(started),
        out_specs=(VMEM,) * owners if last else VMEM,
        scratch_shapes=scratch,
        compiler_params=params(),
        cost_estimate=cost(8 * helmholtz.size // pieces),
        name="solve",
    )(*blocks, helmholtz, *started)


def restore_kernel(*refs, owners, ht_count):
    block_refs, (order_ref, out_ref, ordered) = (refs[:-3], refs[-3:])
    components, band_modes, rows, columns = out_ref.shape
    slots = columns // 2 // owners
    per_slot = block_refs[0].shape[0] // slots
    me = lax.axis_index("kx") * ht_count + lax.axis_index("ht")
    for position, block_ref in enumerate(block_refs):
        ordered[me ^ step_at(owners, position)] = block_ref[...]
    for c in range(components):
        for mode in range(band_modes):
            for tile in range(rows // LANES):
                parts = []
                for p in range(2):
                    row = ((tile * 2 + p) * components + c) * band_modes + mode
                    for owner in range(owners):
                        parts.append(ordered[owner, pl.ds(row, slots, stride=per_slot), :])
                top, rest = two_parts(jnp.concatenate(parts, axis=0))
                both = jnp.concatenate([top, rest], axis=0)
                out_ref[c, mode, pl.ds(tile * LANES, LANES)] = dot(
                    both, order_ref[...], ((0,), (0,))
                )


def restore(blocks, order, components, band_modes, rows, ht_count):
    columns = order.shape[1]
    return pl.pallas_call(
        functools.partial(restore_kernel, owners=len(blocks), ht_count=ht_count),
        out_shape=jax.ShapeDtypeStruct((components, band_modes, rows, columns), jnp.float32),
        in_specs=[VMEM] * (len(blocks) + 1),
        out_specs=VMEM,
        scratch_shapes=[pltpu.VMEM((len(blocks),) + blocks[0].shape, jnp.float32)],
        compiler_params=params(),
        cost_estimate=cost(8 * components * band_modes * rows * columns),
        name="restore",
    )(*blocks, order)


def exchange(blocks, axes):
    count, realizations = (len(blocks), lax.axis_size("real"))
    result = list(blocks)
    for position in range(1, count):
        steps = [order[position] for order in steps_of(count)]
        pairs = [
            (index * realizations + r, (index ^ steps[r % 2]) * realizations + r)
            for index in range(count)
            for r in range(realizations)
        ]
        result[position] = lax.ppermute(blocks[position], axes + ("real",), pairs)
    return result


def sum_kernel(first_ref, second_ref, _, out_ref):
    out_ref[...] = first_ref[...] + second_ref[...]


def ordered_sum(first, second, after):
    return pl.pallas_call(
        sum_kernel,
        out_shape=jax.ShapeDtypeStruct(first.shape, jnp.float32),
        in_specs=[VMEM, VMEM, pl.BlockSpec(memory_space=pl.ANY)],
        out_specs=VMEM,
        compiler_params=params(),
        cost_estimate=cost(12 * first.size),
        name="ordered_sum",
    )(first, second, after)


def swap(value, step):
    pairs = [(index, index ^ step) for index in range(lax.axis_size("real"))]
    return lax.ppermute(value, "real", pairs)


def local(velocity, low_index, neighbours, owner_map, mode_counts, helmholtz):
    components, reals_dev, band_modes, rows_ht, columns = velocity.shape
    kx_count, ht_count = (lax.axis_size("kx"), lax.axis_size("ht"))
    own_kx, own_ht = (lax.axis_index("kx"), lax.axis_index("ht"))
    owners, pieces, real_count = (kx_count * ht_count, PIECES, lax.axis_size("real"))
    rows = rows_ht // (kx_count * pieces)
    groups = LANES // rows if rows else 0
    slots = columns // 2 // owners
    if (
        columns != LANES or reals_dev != 1 or rows_ht % LANES or rows % 8 or LANES % rows or kx_count % groups or kx_count & (kx_count - 1)
        or (band_modes * 2 * components) % 8 or slots % 8 or owners & (owners - 1) or low_index.shape[0] >= kx_count * band_modes
        or low_index.shape[0] >= columns or low_index.shape[0] % 2 or real_count < 2 or real_count & (real_count - 1)
    ):
        return local_plain(velocity, low_index, neighbours, owner_map, mode_counts, helmholtz)
    realizations, members = (real_count, low_index.shape[0])
    chunks, modes = (components * band_modes, band_modes * kx_count)
    shape = (components, modes, rows, columns)
    extra_rows = -(-band_modes // 8) * 8
    split = velocity.reshape(chunks, pieces, kx_count, rows, columns)
    blocks = pack_first(split, neighbours, mode_counts, extra_rows)
    parts = [exchange(blocks, ("kx",))]
    for piece in range(1, pieces):
        block = hand_on(pack(split, piece), parts[0][min(2, kx_count - 1)])
        block = lax.all_to_all(block, "kx", split_axis=0, concat_axis=0, tiled=True)
        parts.append((block,))
    tables, order, slot_modes = slot_tables(owner_map, columns)
    small = 0.0
    for index, block in enumerate(parts[0]):
        lines = block[chunks * rows : chunks * rows + band_modes, : members + 1]
        here = (own_kx ^ step_at(kx_count, index)) == jnp.arange(kx_count)
        small = small + jnp.where(here[:, None, None], lines[None], 0.0)
    small = small.reshape(modes, members + 1).astype(jnp.int32)
    neighbours, mode_counts = (small[:, :-1], small[:, -1])
    after = slot_modes
    received = []
    for piece, part in enumerate(parts):
        slotted, physical, kept, sent = stress_terms(
            part, shape, low_index, neighbours, tables, after
        )
        forcing = high_terms(physical, low_index, neighbours, mode_counts, tables[2], slot_modes)
        kept = after = kept + swap(sent, 1)
        step = 2
        while step < realizations:
            kept = ordered_sum(kept, swap(kept, step), forcing)
            step *= 2
        blocks = outgoing(
            slotted, forcing, kept, swap(kept, 1), low_index, mode_counts, slot_modes, groups, band_modes,
            owners, realizations, piece > 0,
        )
        if piece:
            blocks = [block.reshape(slots, -1, LANES) for block in blocks]
            received.append(exchange(blocks, ("kx", "ht")))
        else:
            block = blocks[0].reshape(owners, slots, -1, LANES)
            block = lax.all_to_all(block, ("kx", "ht"), split_axis=0, concat_axis=0, tiled=True)
            received.append([block])
    solved = None
    for piece, blocks in enumerate(received):
        solved = solve(blocks, helmholtz, piece, pieces, solved, groups, kx_count, ht_count)
    returned = [block.reshape(-1, LANES) for block in exchange(solved, ("kx", "ht"))]
    result = restore(returned, order, components, band_modes, rows_ht, ht_count)
    return result.reshape(velocity.shape)


def solution(mesh):
    in_specs = (
        P(None, "real", "kx", "ht", None),
        P(),
        P("kx", None),
        P(),
        P("kx"),
        P(("kx", "ht"), None, None),
    )
    out_specs = P(None, "real", "kx", "ht", None)
    return jax.shard_map(local, mesh=mesh, in_specs=in_specs, out_specs=out_specs, check_vma=False)
```

```python
import functools

import jax
import jax.numpy as jnp
import numpy as np
from jax import lax
from jax.experimental import pallas as pl
from jax.experimental.pallas import tpu as pltpu
from jax.sharding import PartitionSpec as P

dt_step = 0.1


def spanwise_tables(mode_count, point_count):
    column_ids = jnp.arange(2 * mode_count)
    wavenumber = (column_ids // 2).astype(jnp.float32)
    imag_part = column_ids % 2
    positions = 2.0 * jnp.pi * jnp.arange(point_count).astype(jnp.float32) / point_count
    phases = wavenumber[:, None] * positions[None, :]
    forward = jnp.where(imag_part[:, None] == 0, jnp.cos(phases), -jnp.sin(phases)) / jnp.sqrt(
        jnp.float32(mode_count)
    )
    backward = forward.T * (2.0 * mode_count / point_count)
    return (forward, backward)


def nonlinear_rows(fields, low_index, neighbours, mode_counts, forward, backward):
    precision = lax.Precision.HIGH
    realizations, modes, columns = (fields.shape[1], fields.shape[2], fields.shape[4])
    low_select = (low_index[:, None] == jnp.arange(modes)[None, :]).astype(jnp.float32)
    high_mask = 1.0 - jnp.sum(low_select, axis=0)
    high_rows = high_mask[None, None, :, None, None]
    column_mask = ((jnp.arange(columns) // 2)[None, :] < mode_counts[:, None]).astype(jnp.float32)
    physical = jnp.dot(fields, forward, precision=precision)
    low_fields = jnp.take(physical, low_index, axis=2)
    high_low = jnp.zeros_like(physical)
    stresses = []
    for member in range(low_index.shape[0]):
        partner = jnp.take(physical, neighbours[:, member], axis=2)
        low_one = low_fields[:, :, member : member + 1]
        high_low = high_low + low_one * partner[1:2] + partner * low_one[1:2]
        stresses.append(jnp.sum(physical * (partner[1:2] * high_rows), axis=(1, 2)))
    stress = jnp.stack(stresses, axis=1) / realizations
    forcing = jnp.dot(high_low, backward, precision=precision) * high_rows
    low_forcing = jnp.dot(stress, backward, precision=precision)
    low_rows = jnp.einsum("jm,cjyk->cmyk", low_select, low_forcing, precision=lax.Precision.HIGHEST)
    forcing = (forcing + low_rows[:, None]) * column_mask[None, None, :, None, :]
    return fields + dt_step * forcing


def local_plain(velocity, low_index, neighbours, owner_map, mode_counts, helmholtz):
    components, reals_dev, band_modes, rows_ht, columns = velocity.shape
    kz_modes = columns // 2
    forward, backward = spanwise_tables(kz_modes, 4 * kz_modes)
    kx_count, ht_count = (lax.axis_size("kx"), lax.axis_size("ht"))
    real_count = lax.axis_size("real")
    modes, realizations = (band_modes * kx_count, reals_dev * real_count)
    slots_dev = kz_modes // (kx_count * ht_count)
    rows_dev = rows_ht // (kx_count * real_count)
    small = jnp.concatenate([neighbours, mode_counts[:, None]], axis=1)
    small = lax.all_gather(small, "kx", axis=0, tiled=True)
    neighbours, mode_counts = (small[:, :-1], small[:, -1])
    inverse_map = (
        jnp.zeros((kz_modes,), jnp.int32).at[owner_map].set(jnp.arange(kz_modes, dtype=jnp.int32))
    )
    split = velocity.reshape(
        components, reals_dev, band_modes, kx_count * real_count, rows_dev, columns
    )
    split = split.transpose(3, 0, 1, 2, 4, 5)
    split = lax.all_to_all(split, ("kx", "real"), split_axis=0, concat_axis=0, tiled=True)
    fields = split.reshape(
        kx_count, real_count, components, reals_dev, band_modes, rows_dev, columns
    )
    fields = fields.transpose(2, 1, 3, 0, 4, 5, 6).reshape(
        components, realizations, modes, rows_dev, columns
    )
    updated = nonlinear_rows(fields, low_index, neighbours, mode_counts, forward, backward)
    slotted = jnp.take(
        updated.reshape(components, realizations, modes, rows_dev, kz_modes, 2), owner_map, axis=4
    )
    slotted = slotted.reshape(
        components, real_count, reals_dev, modes, rows_dev, kx_count * ht_count, slots_dev, 2
    )
    outgoing = slotted.transpose(5, 1, 6, 2, 0, 3, 7, 4).reshape(
        kx_count * ht_count * real_count, slots_dev, reals_dev * components * modes * 2, rows_dev
    )
    incoming = lax.all_to_all(
        outgoing, ("kx", "ht", "real"), split_axis=0, concat_axis=0, tiled=True
    )
    incoming = incoming.reshape(
        kx_count, ht_count, real_count, slots_dev, reals_dev * components * modes * 2, rows_dev
    )
    incoming = incoming.transpose(3, 4, 1, 0, 2, 5).reshape(
        slots_dev, reals_dev * components * modes * 2, ht_count * rows_ht
    )
    solved = jnp.einsum("syx,snx->sny", helmholtz, incoming, precision=lax.Precision.HIGH)
    solved = solved.reshape(
        slots_dev, reals_dev, components, kx_count, band_modes, 2, ht_count, rows_ht
    )
    solved = solved.transpose(3, 6, 0, 5, 1, 2, 4, 7).reshape(
        kx_count * ht_count, slots_dev * 2, reals_dev * components * band_modes, rows_ht
    )
    returned = lax.all_to_all(solved, ("kx", "ht"), split_axis=0, concat_axis=0, tiled=True)
    restored = returned.reshape(
        kz_modes, 2, reals_dev, components, band_modes, rows_ht
    )
    restored = jnp.take(restored, inverse_map, axis=0)
    return restored.transpose(3, 2, 4, 5, 0, 1).reshape(velocity.shape)


LANES = 128
PIECES = 2
VMEM = pl.BlockSpec(memory_space=pltpu.VMEM)
SMEM = pl.BlockSpec(memory_space=pltpu.SMEM)


def params():
    return pltpu.CompilerParams(vmem_limit_bytes=48 * 1024 * 1024)


ORDERS = {4: (1, 3, 2), 8: (4, 1, 2, 6, 5, 3, 7)}


def steps_of(count):
    even = ORDERS.get(count, tuple(range(1, count)))
    odd = list(even)
    for first in range(0, count - 2, 2):
        odd[first], odd[first + 1] = (even[first + 1], even[first])
    return (0,) + tuple(even), (0,) + tuple(odd)


def step_at(count, position):
    even, odd = steps_of(count)
    return jnp.where((lax.axis_index("real") & 1) == 0, even[position], odd[position])


def cost(size):
    return pl.CostEstimate(flops=0, bytes_accessed=size, transcendentals=0)


def two_parts(value):
    top = value.astype(jnp.bfloat16)
    rest = (value - top.astype(jnp.float32)).astype(jnp.bfloat16)
    return top, rest


def dot(left, right, dims=((1,), (0,))):
    return lax.dot_general(left, right, (dims, ((), ())), preferred_element_type=jnp.float32)


def pack_first_kernel(near_ref, count_ref, velocity_ref, *refs):
    out_refs, arrived = (refs[:-1], refs[-1])
    chunks, _, kx_count, rows, columns = velocity_ref.shape
    own = lax.axis_index("kx")
    copies = []
    for index, out_ref in enumerate(out_refs):
        partner = own ^ step_at(kx_count, index)
        for chunk in range(chunks):
            copies.append(
                pltpu.make_async_copy(
                    velocity_ref.at[chunk, 0, partner],
                    out_ref.at[pl.ds(chunk * rows, rows)],
                    arrived.at[index, chunk],
                )
            )
            copies[-1].start()
    shape = (out_refs[0].shape[0] - chunks * rows, columns)
    row = lax.broadcasted_iota(jnp.int32, shape, 0)
    lane = lax.broadcasted_iota(jnp.int32, shape, 1)
    extra = jnp.zeros(shape, jnp.int32)
    modes, members = near_ref.shape
    for mode in range(modes):
        line = jnp.where(lane == members, count_ref[mode], 0)
        for member in range(members):
            line = jnp.where(lane == member, near_ref[mode, member], line)
        extra = jnp.where(row == mode, line, extra)
    extra = extra.astype(jnp.float32)
    for out_ref in out_refs:
        out_ref[chunks * rows :] = extra
    for copy in copies:
        copy.wait()


def pack_first(velocity, neighbours, mode_counts, extra_rows):
    chunks, _, kx_count, rows, columns = velocity.shape
    shape = jax.ShapeDtypeStruct((chunks * rows + extra_rows, columns), jnp.float32)
    return pl.pallas_call(
        pack_first_kernel,
        out_shape=(shape,) * kx_count,
        in_specs=[SMEM, SMEM, pl.BlockSpec(memory_space=pl.ANY)],
        out_specs=(VMEM,) * kx_count,
        scratch_shapes=[pltpu.SemaphoreType.DMA((kx_count, chunks))],
        cost_estimate=cost(4 * velocity.size),
        name="pack_first",
    )(neighbours, mode_counts, velocity)


def pack_kernel(velocity_ref, out_ref):
    chunks, _, kx_count, rows, columns = velocity_ref.shape
    for index in range(kx_count):
        for chunk in range(chunks):
            place = slice(chunk * rows, (chunk + 1) * rows)
            out_ref[index, place] = velocity_ref[chunk, 0, index]


def pack(velocity, piece):
    chunks, _, kx_count, rows, columns = velocity.shape
    shape = (kx_count, chunks * rows, columns)
    return pl.pallas_call(
        pack_kernel,
        out_shape=jax.ShapeDtypeStruct(shape, jnp.float32),
        grid=(1,),
        in_specs=[
            pl.BlockSpec((chunks, 1, kx_count, rows, columns), lambda i: (0, piece, 0, 0, 0)),
        ],
        out_specs=pl.BlockSpec(shape, lambda i: (0, 0, 0)),
        cost_estimate=cost(4 * velocity.size),
        name="pack",
    )(velocity)


def hand_on_kernel(value_ref, after_ref, out_ref):
    pass


def hand_on(value, after):
    return pl.pallas_call(
        hand_on_kernel,
        out_shape=jax.ShapeDtypeStruct(value.shape, value.dtype),
        in_specs=[pl.BlockSpec(memory_space=pl.ANY)] * 2,
        out_specs=pl.BlockSpec(memory_space=pl.ANY),
        input_output_aliases={0: 0},
        cost_estimate=cost(0),
        name="hand_on",
    )(value, after)


def tables_kernel(owner_ref, top_ref, rest_ref, first_ref, back_ref, order_ref, slot_ref):
    columns = slot_ref.shape[1]
    modes = columns // 2
    lane = lax.broadcasted_iota(jnp.int32, (8, columns), 1)
    mode = jnp.zeros((8, columns), jnp.int32)
    for slot in range(modes):
        mode = jnp.where(lane % modes == slot, owner_ref[slot], mode)
    slot_ref[...] = mode
    wanted = 2 * mode + lane // modes
    row = lax.broadcasted_iota(jnp.int32, (columns, columns), 0)
    chosen = (row == wanted[:1]).astype(jnp.float32)
    select = chosen.astype(jnp.bfloat16)
    points = top_ref.shape[1]
    for half in range(2):
        rows = slice(half * columns, (half + 1) * columns)
        first_ref[rows, :points] = top_ref[...]
        first_ref[rows, points:] = select
        order_ref[rows] = chosen.T.astype(jnp.bfloat16)
    for index, table_ref in enumerate((top_ref, rest_ref)):
        back = dot(table_ref[...], select, ((0,), (0,))) * (2.0 * modes / points)
        back_ref[:, index * columns : (index + 1) * columns] = back.astype(jnp.bfloat16)


def spanwise_constants(columns, points):
    mode = np.arange(columns) // 2
    phase = 2.0 * np.pi * ((mode[:, None] * np.arange(points)[None, :]) % points) / points
    forward = np.where(np.arange(columns)[:, None] % 2 == 0, np.cos(phase), -np.sin(phase))
    forward = (forward / np.sqrt(columns // 2)).astype(np.float32)
    top = forward.astype(jnp.bfloat16)
    rest = (forward - top.astype(np.float32)).astype(jnp.bfloat16)
    return jnp.asarray(top), jnp.asarray(rest)


def slot_tables(owner_map, columns):
    points = 2 * columns
    top, rest = spanwise_constants(columns, points)
    first, back, order, slot_modes = pl.pallas_call(
        tables_kernel,
        out_shape=(
            jax.ShapeDtypeStruct((2 * columns, points + columns), jnp.bfloat16),
            jax.ShapeDtypeStruct((points, 2 * columns), jnp.bfloat16),
            jax.ShapeDtypeStruct((2 * columns, columns), jnp.bfloat16),
            jax.ShapeDtypeStruct((8, columns), jnp.int32),
        ),
        in_specs=[SMEM, VMEM, VMEM],
        out_specs=(VMEM,) * 4,
        compiler_params=params(),
        cost_estimate=cost(16 * points * columns),
        name="tables",
    )(owner_map, top, rest)
    return (first, rest, back), order, slot_modes


def list_high(low_ref, high_ref, modes):
    found = jnp.int32(0)
    for mode in range(modes):
        is_low = jnp.int32(0)
        for member in range(low_ref.shape[0]):
            is_low = is_low | (low_ref[member] == mode).astype(jnp.int32)
        high_ref[found] = mode
        found = found + 1 - is_low


def tile_at(step, points):
    halves = points // LANES
    return (
        pl.ds(pl.multiple_of((step // halves) * 8, 8), 8),
        pl.ds(pl.multiple_of((step % halves) * LANES, LANES), LANES),
    )


def inverse(fields, back_ref):
    columns = back_ref.shape[1] // 2
    top, rest = two_parts(fields)
    both = dot(top, back_ref[...])
    return both[:, :columns] + both[:, columns:] + dot(rest, back_ref[:, :columns])


def stress_kernel(low_ref, near_ref, *refs):
    block_refs, refs = (refs[:-10], refs[-10:])
    first_ref, second_ref, back_ref, _ = refs[:4]
    slotted_ref, physical, kept_ref, sent_ref, sums, high_ref = refs[4:]
    components, modes, rows, columns = slotted_ref.shape
    if len(block_refs) > 1:
        bands = len(block_refs)
        places = [lax.axis_index("kx") ^ step_at(bands, index) for index in range(bands)]
    else:
        bands = block_refs[0].shape[0]
        places = list(range(bands))
        block_refs = [block_refs[0].at[index] for index in range(bands)]
    points, band_modes = (physical.shape[3], modes // bands)
    members = sums.shape[1]
    odd = (lax.axis_index("real") & 1) == 1
    list_high(low_ref, high_ref, modes)
    size = band_modes * rows
    for c in range(components):
        joined = [block_ref[c * size : (c + 1) * size] for block_ref in block_refs]
        top, rest = two_parts(jnp.concatenate(joined, axis=0))
        both = dot(jnp.concatenate([top, rest], axis=1), first_ref[...])
        fields = both[:, :points] + dot(top, second_ref[...])
        for index in range(bands):
            place = pl.ds(places[index] * band_modes, band_modes)
            part = slice(index * size, (index + 1) * size)
            physical[c, place] = fields[part].reshape(band_modes, rows, points)
            slotted_ref[c, place] = both[part, points:].reshape(band_modes, rows, columns)

    def pairs(step, carry):
        place = tile_at(step, points)

        def one_high(index, totals):
            mode = high_ref[index]
            own = [physical[(c, mode) + place] for c in range(components)]
            totals = list(totals)
            for member in range(members):
                partner = physical[(1, near_ref[mode, member]) + place]
                for c in range(components):
                    slot = member * components + c
                    totals[slot] = totals[slot] + own[c] * partner
            return tuple(totals)

        empty = tuple(jnp.zeros((8, LANES), jnp.float32) for _ in range(members * components))
        totals = lax.fori_loop(0, modes - members, one_high, empty)
        for member in range(members):
            for c in range(components):
                sums[(c, member) + place] = totals[member * components + c]
        return carry

    lax.fori_loop(0, (rows // 8) * (points // LANES), pairs, 0)
    stress = inverse(sums[...].reshape(components * members * rows, points), back_ref)
    stress = stress.reshape(components, 2, members // 2, rows, columns)
    kept_ref[...] = jnp.where(odd, stress[:, 1], stress[:, 0])
    sent_ref[...] = jnp.where(odd, stress[:, 0], stress[:, 1])


def stress_terms(blocks, shape, low_index, neighbours, tables, after):
    components, modes, rows, columns = shape
    members, points = (low_index.shape[0], 2 * columns)
    half = jax.ShapeDtypeStruct((components, members // 2, rows, columns), jnp.float32)
    return pl.pallas_call(
        stress_kernel,
        out_shape=(
            jax.ShapeDtypeStruct(shape, jnp.float32),
            jax.ShapeDtypeStruct((components, modes, rows, points), jnp.float32),
            half,
            half,
        ),
        in_specs=[SMEM] * 2 + [VMEM] * (len(blocks) + 3) + [pl.BlockSpec(memory_space=pl.ANY)],
        out_specs=(VMEM,) * 4,
        scratch_shapes=[
            pltpu.VMEM((components, members, rows, points), jnp.float32),
            pltpu.SMEM((modes + 1,), jnp.int32),
        ],
        compiler_params=params(),
        cost_estimate=cost(4 * components * modes * rows * points * members),
        name="stress",
    )(low_index, neighbours, *blocks, *tables, after)


def products_kernel(
    low_ref, near_ref, count_ref, physical, back_ref, slot_ref, out_ref, products, high_ref
):
    components, modes, rows, points = physical.shape
    members, highs = (low_ref.shape[0], out_ref.shape[1])
    list_high(low_ref, high_ref, modes)

    def pairs(step, carry):
        place = tile_at(step, points)
        low = [
            [physical[(c, low_ref[member]) + place] for c in range(components)]
            for member in range(members)
        ]

        def one_high(index, inner):
            mode = high_ref[index]
            result = [jnp.zeros((8, LANES), jnp.float32) for _ in range(components)]
            for member in range(members):
                near = near_ref[mode, member]
                partner = [physical[(c, near) + place] for c in range(components)]
                for c in range(components):
                    if c == 1:
                        result[c] = result[c] + low[member][1] * partner[1]
                    else:
                        result[c] = result[c] + (
                            low[member][c] * partner[1] + partner[c] * low[member][1]
                        )
            for c in range(components):
                products[(c, index) + place] = result[c] * 2.0 if c == 1 else result[c]
            return inner

        lax.fori_loop(0, highs, one_high, 0)
        return carry

    lax.fori_loop(0, (rows // 8) * (points // LANES), pairs, 0)
    forcing = inverse(products[...].reshape(components * highs * rows, points), back_ref)
    forcing = forcing.reshape(out_ref.shape)
    for index in range(highs):
        active = slot_ref[:1] < count_ref[high_ref[index]]
        out_ref[:, index] = jnp.where(active, forcing[:, index] * dt_step, 0.0)


def high_terms(physical, low_index, neighbours, mode_counts, back, slot_modes):
    components, modes, rows, points = physical.shape
    highs = modes - low_index.shape[0]
    return pl.pallas_call(
        products_kernel,
        out_shape=jax.ShapeDtypeStruct((components, highs, rows, points // 2), jnp.float32),
        in_specs=[SMEM] * 3 + [VMEM] * 3,
        out_specs=VMEM,
        scratch_shapes=[
            pltpu.VMEM((components, highs, rows, points), jnp.float32),
            pltpu.SMEM((modes + 1,), jnp.int32),
        ],
        compiler_params=params(),
        cost_estimate=cost(4 * physical.size * low_index.shape[0]),
        name="products",
    )(low_index, neighbours, mode_counts, physical, back, slot_modes)


def outgoing_kernel(
    low_ref, count_ref, slotted_ref, forcing_ref, kept_ref, other_ref, slot_ref, *refs,
    groups, band_modes, owners, scale
):
    out_refs, (full, turned, high_ref) = (refs[:-3], refs[-3:])
    components, modes, rows, columns = slotted_ref.shape
    half, slots = (kept_ref.shape[1], columns // 2 // owners)
    per_slot = out_refs[0].shape[0] * len(out_refs) // (columns // 2)
    own = lax.axis_index("real") & 1
    list_high(low_ref, high_ref, modes)
    full[...] = slotted_ref[...]
    for index in range(forcing_ref.shape[1]):
        for c in range(components):
            full[c, high_ref[index]] += forcing_ref[c, index]
    for member in range(half):
        for part_ref, start in ((kept_ref, own * half), (other_ref, (1 - own) * half)):
            mode = low_ref[start + member]
            active = slot_ref[:1] < count_ref[mode]
            for c in range(components):
                full[c, mode] += jnp.where(active, part_ref[c, member] * scale, 0.0)
    inner = modes // groups
    if len(out_refs) > 1:
        me = lax.axis_index("kx") * lax.axis_size("ht") + lax.axis_index("ht")
        targets = [me ^ step_at(owners, position) for position in range(owners)]
    for c in range(components):
        for part in range(inner):
            tile = jnp.concatenate([full[c, part + inner * g] for g in range(groups)], axis=0)
            band_low, band_mode = (part // band_modes, part % band_modes)
            if len(out_refs) > 1:
                turned[...] = tile.T
            else:
                value = tile.T
            for p in range(2):
                row = ((band_low * 2 + p) * components + c) * band_modes + band_mode
                if len(out_refs) == 1:
                    out_refs[0][pl.ds(row, columns // 2, stride=per_slot), :] = value[
                        p * (columns // 2) : (p + 1) * (columns // 2)
                    ]
                    continue
                for out_ref, target in zip(out_refs, targets):
                    start = pl.multiple_of((p * owners + target) * slots, slots)
                    out_ref[pl.ds(row, slots, stride=per_slot), :] = turned[pl.ds(start, slots)]


def outgoing(
    slotted, forcing, kept, other, low_index, mode_counts, slot_modes, groups, band_modes, owners,
    realizations, separate,
):
    components, modes, rows, columns = slotted.shape
    total, lanes = ((columns // 2) * (modes // groups) * 2 * components, groups * rows)
    count = owners if separate else 1
    return pl.pallas_call(
        functools.partial(
            outgoing_kernel, groups=groups, band_modes=band_modes, owners=owners,
            scale=dt_step / realizations,
        ),
        out_shape=(jax.ShapeDtypeStruct((total // count, lanes), jnp.float32),) * count,
        in_specs=[SMEM, SMEM] + [VMEM] * 5,
        out_specs=(VMEM,) * count,
        scratch_shapes=[
            pltpu.VMEM(slotted.shape, jnp.float32), pltpu.VMEM((columns, lanes), jnp.float32),
            pltpu.SMEM((modes + 1,), jnp.int32),
        ],
        compiler_params=params(),
        cost_estimate=cost(8 * slotted.size),
        name="outgoing",
    )(low_index, mode_counts, slotted, forcing, kept, other, slot_modes)


def regroup(blocks, rows):
    count = len(blocks)
    lane = lax.broadcasted_iota(jnp.int32, blocks[0].shape, 1) // rows
    step = 1
    while step < count:
        take = (lane & step) == 0
        for i in range(count):
            if i & step == 0:
                here, there = (blocks[i], blocks[i + step])
                blocks[i] = jnp.where(take, here, pltpu.roll(there, step * rows, 1))
                blocks[i + step] = jnp.where(
                    take, pltpu.roll(here, LANES - step * rows, 1), there
                )
        step *= 2
    return blocks


def solve_kernel(*refs, groups, kx_count, ht_count, pieces, piece):
    owners, last = (kx_count * ht_count, piece == pieces - 1)
    own_kx, own_ht = (lax.axis_index("kx"), lax.axis_index("ht"))
    partners = []
    for position in range(owners):
        step = step_at(owners, position)
        partners.append((own_kx ^ (step // ht_count), own_ht ^ (step % ht_count)))
    refs = list(refs)
    operands = refs.pop()
    matrices = refs.pop()
    arrived = refs.pop()
    source = refs.pop(0)
    if piece:
        ordered = refs.pop()
        blocks = [source] + [refs.pop(0) for _ in range(owners - 1)]
        for block_ref, (kx, ht) in zip(blocks, partners):
            ordered[kx * ht_count + ht] = block_ref[...]
        source = ordered
    matrix_ref = refs.pop(0)
    slots, heights = (matrix_ref.shape[0], matrix_ref.shape[1])
    width = heights // ht_count // pieces
    copies = [
        [
            pltpu.make_async_copy(
                matrix_ref.at[s, :, pl.ds((h * pieces + piece) * width, width)],
                matrices.at[s, h],
                arrived.at[s, h],
            )
            for h in range(ht_count)
        ]
        for s in range(slots)
    ]
    batch = max(slots // 2, 1)
    for s in range(batch):
        for copy in copies[s]:
            copy.start()
    partial_ref = refs.pop(0) if piece else None
    rows = LANES // groups
    for s in range(slots):
        tiles = []
        for h in range(ht_count):
            for first in range(0, kx_count, groups):
                blocks = [source[(first + g) * ht_count + h, s] for g in range(groups)]
                tiles.append(jnp.concatenate(regroup(blocks, rows), axis=0))
        fields = jnp.concatenate(tiles, axis=1)
        count = fields.shape[0]
        spare = -count % LANES
        if spare:
            empty = jnp.zeros((spare, fields.shape[1]), jnp.float32)
            fields = jnp.concatenate([fields, empty], axis=0)
        operands[s] = jnp.concatenate(two_parts(fields), axis=0)
    padded = count + spare
    for s in range(slots):
        if s % batch == 0:
            for t in range(s, min(s + batch, slots)):
                for copy in copies[t]:
                    copy.wait()
            for t in range(s + batch, min(s + 2 * batch, slots)):
                for copy in copies[t]:
                    copy.start()
        matrix = jnp.concatenate([matrices[s, h] for h in range(ht_count)], axis=1)
        matrix_top, matrix_rest = two_parts(matrix)
        contract = ((1,), (1,))
        both = dot(matrix_top, operands[s], contract)
        solved = both[:, :padded] + both[:, padded:]
        solved = solved + dot(matrix_rest, operands[s, :padded], contract)
        if piece:
            solved = solved + partial_ref[s]
        if not last:
            refs[0][s] = solved
            continue
        full = refs[owners]
        for tile in range(heights // LANES):
            full[s, tile] = solved[tile * LANES : (tile + 1) * LANES].T[:count]
    if not last:
        return
    out_refs = refs[:owners]
    lane_tiles, per_band = out_refs[0].shape[1:3]
    for out_ref, (kx, ht) in zip(out_refs, partners):
        band = pl.ds(pl.multiple_of(kx * per_band, 8), per_band)
        for s in range(slots):
            for tile in range(lane_tiles):
                out_ref[s, tile] = full[s, ht * lane_tiles + tile, band]


def solve(blocks, helmholtz, piece, pieces, partial, groups, kx_count, ht_count):
    slots, per_slot, _ = blocks[0].shape[-3:]
    heights, owners, last = (helmholtz.shape[1], kx_count * ht_count, piece == pieces - 1)
    count = per_slot * groups
    padded = -(-count // LANES) * LANES
    scratch = []
    if last:
        shape = (slots, heights // ht_count // LANES, count // kx_count, LANES)
        out_shape = (jax.ShapeDtypeStruct(shape, jnp.float32),) * owners
        scratch.append(pltpu.VMEM((slots, heights // LANES, count, LANES), jnp.float32))
    else:
        out_shape = jax.ShapeDtypeStruct((slots, heights, padded), jnp.float32)
    if piece:
        scratch.append(pltpu.VMEM((owners,) + blocks[0].shape, jnp.float32))
    width = heights // ht_count // pieces
    scratch += [
        pltpu.SemaphoreType.DMA((slots, ht_count)),
        pltpu.VMEM((slots, ht_count, heights, width), jnp.float32),
        pltpu.VMEM((slots, 2 * padded, ht_count * width), jnp.bfloat16),
    ]
    started = [] if partial is None else [partial]
    return pl.pallas_call(
        functools.partial(
            solve_kernel, groups=groups, kx_count=kx_count, ht_count=ht_count, pieces=pieces,
            piece=piece,
        ),
        out_shape=out_shape,
        in_specs=[VMEM] * len(blocks) + [pl.BlockSpec(memory_space=pl.ANY)] + [VMEM] * len(started),
        out_specs=(VMEM,) * owners if last else VMEM,
        scratch_shapes=scratch,
        compiler_params=params(),
        cost_estimate=cost(8 * helmholtz.size // pieces),
        name="solve",
    )(*blocks, helmholtz, *started)


def restore_kernel(*refs, owners, ht_count):
    block_refs, (order_ref, out_ref, ordered) = (refs[:-3], refs[-3:])
    components, band_modes, rows, columns = out_ref.shape
    slots = columns // 2 // owners
    per_slot = block_refs[0].shape[0] // slots
    me = lax.axis_index("kx") * ht_count + lax.axis_index("ht")
    for position, block_ref in enumerate(block_refs):
        ordered[me ^ step_at(owners, position)] = block_ref[...]
    for c in range(components):
        for mode in range(band_modes):
            for tile in range(rows // LANES):
                parts = []
                for p in range(2):
                    row = ((tile * 2 + p) * components + c) * band_modes + mode
                    for owner in range(owners):
                        parts.append(ordered[owner, pl.ds(row, slots, stride=per_slot), :])
                top, rest = two_parts(jnp.concatenate(parts, axis=0))
                both = jnp.concatenate([top, rest], axis=0)
                out_ref[c, mode, pl.ds(tile * LANES, LANES)] = dot(
                    both, order_ref[...], ((0,), (0,))
                )


def restore(blocks, order, components, band_modes, rows, ht_count):
    columns = order.shape[1]
    return pl.pallas_call(
        functools.partial(restore_kernel, owners=len(blocks), ht_count=ht_count),
        out_shape=jax.ShapeDtypeStruct((components, band_modes, rows, columns), jnp.float32),
        in_specs=[VMEM] * (len(blocks) + 1),
        out_specs=VMEM,
        scratch_shapes=[pltpu.VMEM((len(blocks),) + blocks[0].shape, jnp.float32)],
        compiler_params=params(),
        cost_estimate=cost(8 * components * band_modes * rows * columns),
        name="restore",
    )(*blocks, order)


def exchange(blocks, axes):
    count, realizations = (len(blocks), lax.axis_size("real"))
    result = list(blocks)
    for position in range(1, count):
        steps = [order[position] for order in steps_of(count)]
        pairs = [
            (index * realizations + r, (index ^ steps[r % 2]) * realizations + r)
            for index in range(count)
            for r in range(realizations)
        ]
        result[position] = lax.ppermute(blocks[position], axes + ("real",), pairs)
    return result


def sum_kernel(first_ref, second_ref, _, out_ref):
    out_ref[...] = first_ref[...] + second_ref[...]


def ordered_sum(first, second, after):
    return pl.pallas_call(
        sum_kernel,
        out_shape=jax.ShapeDtypeStruct(first.shape, jnp.float32),
        in_specs=[VMEM, VMEM, pl.BlockSpec(memory_space=pl.ANY)],
        out_specs=VMEM,
        compiler_params=params(),
        cost_estimate=cost(12 * first.size),
        name="ordered_sum",
    )(first, second, after)


def swap(value, step):
    pairs = [(index, index ^ step) for index in range(lax.axis_size("real"))]
    return lax.ppermute(value, "real", pairs)


def local(velocity, low_index, neighbours, owner_map, mode_counts, helmholtz):
    components, reals_dev, band_modes, rows_ht, columns = velocity.shape
    kx_count, ht_count = (lax.axis_size("kx"), lax.axis_size("ht"))
    own_kx, own_ht = (lax.axis_index("kx"), lax.axis_index("ht"))
    owners, pieces, real_count = (kx_count * ht_count, PIECES, lax.axis_size("real"))
    rows = rows_ht // (kx_count * pieces)
    groups = LANES // rows if rows else 0
    slots = columns // 2 // owners
    if (
        columns != LANES or reals_dev != 1 or rows_ht % LANES or rows % 8 or LANES % rows or kx_count % groups or kx_count & (kx_count - 1)
        or (band_modes * 2 * components) % 8 or slots % 8 or owners & (owners - 1) or low_index.shape[0] >= kx_count * band_modes
        or low_index.shape[0] >= columns or low_index.shape[0] % 2 or real_count < 2 or real_count & (real_count - 1)
    ):
        return local_plain(velocity, low_index, neighbours, owner_map, mode_counts, helmholtz)
    realizations, members = (real_count, low_index.shape[0])
    chunks, modes = (components * band_modes, band_modes * kx_count)
    shape = (components, modes, rows, columns)
    extra_rows = -(-band_modes // 8) * 8
    split = velocity.reshape(chunks, pieces, kx_count, rows, columns)
    blocks = pack_first(split, neighbours, mode_counts, extra_rows)
    parts = [exchange(blocks, ("kx",))]
    for piece in range(1, pieces):
        block = hand_on(pack(split, piece), parts[0][min(2, kx_count - 1)])
        block = lax.all_to_all(block, "kx", split_axis=0, concat_axis=0, tiled=True)
        parts.append((block,))
    tables, order, slot_modes = slot_tables(owner_map, columns)
    small = 0.0
    for index, block in enumerate(parts[0]):
        lines = block[chunks * rows : chunks * rows + band_modes, : members + 1]
        here = (own_kx ^ step_at(kx_count, index)) == jnp.arange(kx_count)
        small = small + jnp.where(here[:, None, None], lines[None], 0.0)
    small = small.reshape(modes, members + 1).astype(jnp.int32)
    neighbours, mode_counts = (small[:, :-1], small[:, -1])
    after = slot_modes
    received = []
    for piece, part in enumerate(parts):
        slotted, physical, kept, sent = stress_terms(
            part, shape, low_index, neighbours, tables, after
        )
        forcing = high_terms(physical, low_index, neighbours, mode_counts, tables[2], slot_modes)
        kept = after = kept + swap(sent, 1)
        step = 2
        while step < realizations:
            kept = ordered_sum(kept, swap(kept, step), forcing)
            step *= 2
        blocks = outgoing(
            slotted, forcing, kept, swap(kept, 1), low_index, mode_counts, slot_modes, groups, band_modes,
            owners, realizations, piece > 0,
        )
        if piece:
            blocks = [block.reshape(slots, -1, LANES) for block in blocks]
            received.append(exchange(blocks, ("kx", "ht")))
        else:
            block = blocks[0].reshape(owners, slots, -1, LANES)
            block = lax.all_to_all(block, ("kx", "ht"), split_axis=0, concat_axis=0, tiled=True)
            received.append([block])
    solved = None
    for piece, blocks in enumerate(received):
        solved = solve(blocks, helmholtz, piece, pieces, solved, groups, kx_count, ht_count)
    returned = [block.reshape(-1, LANES) for block in exchange(solved, ("kx", "ht"))]
    result = restore(returned, order, components, band_modes, rows_ht, ht_count)
    return result.reshape(velocity.shape)


def solution(mesh):
    in_specs = (
        P(None, "real", "kx", "ht", None),
        P(),
        P("kx", None),
        P(),
        P("kx"),
        P(("kx", "ht"), None, None),
    )
    out_specs = P(None, "real", "kx", "ht", None)
    return jax.shard_map(local, mesh=mesh, in_specs=in_specs, out_specs=out_specs, check_vma=False)
```

```python
import functools

import jax
import jax.numpy as jnp
import numpy as np
from jax import lax
from jax.experimental import pallas as pl
from jax.experimental.pallas import tpu as pltpu
from jax.sharding import PartitionSpec as P

dt_step = 0.1


def spanwise_tables(mode_count, point_count):
    column_ids = jnp.arange(2 * mode_count)
    wavenumber = (column_ids // 2).astype(jnp.float32)
    imag_part = column_ids % 2
    positions = 2.0 * jnp.pi * jnp.arange(point_count).astype(jnp.float32) / point_count
    phases = wavenumber[:, None] * positions[None, :]
    forward = jnp.where(imag_part[:, None] == 0, jnp.cos(phases), -jnp.sin(phases)) / jnp.sqrt(
        jnp.float32(mode_count)
    )
    backward = forward.T * (2.0 * mode_count / point_count)
    return (forward, backward)


def nonlinear_rows(fields, low_index, neighbours, mode_counts, forward, backward):
    precision = lax.Precision.HIGH
    realizations, modes, columns = (fields.shape[1], fields.shape[2], fields.shape[4])
    low_select = (low_index[:, None] == jnp.arange(modes)[None, :]).astype(jnp.float32)
    high_mask = 1.0 - jnp.sum(low_select, axis=0)
    high_rows = high_mask[None, None, :, None, None]
    column_mask = ((jnp.arange(columns) // 2)[None, :] < mode_counts[:, None]).astype(jnp.float32)
    physical = jnp.dot(fields, forward, precision=precision)
    low_fields = jnp.take(physical, low_index, axis=2)
    high_low = jnp.zeros_like(physical)
    stresses = []
    for member in range(low_index.shape[0]):
        partner = jnp.take(physical, neighbours[:, member], axis=2)
        low_one = low_fields[:, :, member : member + 1]
        high_low = high_low + low_one * partner[1:2] + partner * low_one[1:2]
        stresses.append(jnp.sum(physical * (partner[1:2] * high_rows), axis=(1, 2)))
    stress = jnp.stack(stresses, axis=1) / realizations
    forcing = jnp.dot(high_low, backward, precision=precision) * high_rows
    low_forcing = jnp.dot(stress, backward, precision=precision)
    low_rows = jnp.einsum("jm,cjyk->cmyk", low_select, low_forcing, precision=lax.Precision.HIGHEST)
    forcing = (forcing + low_rows[:, None]) * column_mask[None, None, :, None, :]
    return fields + dt_step * forcing


def local_plain(velocity, low_index, neighbours, owner_map, mode_counts, helmholtz):
    components, reals_dev, band_modes, rows_ht, columns = velocity.shape
    kz_modes = columns // 2
    forward, backward = spanwise_tables(kz_modes, 4 * kz_modes)
    kx_count, ht_count = (lax.axis_size("kx"), lax.axis_size("ht"))
    real_count = lax.axis_size("real")
    modes, realizations = (band_modes * kx_count, reals_dev * real_count)
    slots_dev = kz_modes // (kx_count * ht_count)
    rows_dev = rows_ht // (kx_count * real_count)
    small = jnp.concatenate([neighbours, mode_counts[:, None]], axis=1)
    small = lax.all_gather(small, "kx", axis=0, tiled=True)
    neighbours, mode_counts = (small[:, :-1], small[:, -1])
    inverse_map = (
        jnp.zeros((kz_modes,), jnp.int32).at[owner_map].set(jnp.arange(kz_modes, dtype=jnp.int32))
    )
    split = velocity.reshape(
        components, reals_dev, band_modes, kx_count * real_count, rows_dev, columns
    )
    split = split.transpose(3, 0, 1, 2, 4, 5)
    split = lax.all_to_all(split, ("kx", "real"), split_axis=0, concat_axis=0, tiled=True)
    fields = split.reshape(
        kx_count, real_count, components, reals_dev, band_modes, rows_dev, columns
    )
    fields = fields.transpose(2, 1, 3, 0, 4, 5, 6).reshape(
        components, realizations, modes, rows_dev, columns
    )
    updated = nonlinear_rows(fields, low_index, neighbours, mode_counts, forward, backward)
    slotted = jnp.take(
        updated.reshape(components, realizations, modes, rows_dev, kz_modes, 2), owner_map, axis=4
    )
    slotted = slotted.reshape(
        components, real_count, reals_dev, modes, rows_dev, kx_count * ht_count, slots_dev, 2
    )
    outgoing = slotted.transpose(5, 1, 6, 2, 0, 3, 7, 4).reshape(
        kx_count * ht_count * real_count, slots_dev, reals_dev * components * modes * 2, rows_dev
    )
    incoming = lax.all_to_all(
        outgoing, ("kx", "ht", "real"), split_axis=0, concat_axis=0, tiled=True
    )
    incoming = incoming.reshape(
        kx_count, ht_count, real_count, slots_dev, reals_dev * components * modes * 2, rows_dev
    )
    incoming = incoming.transpose(3, 4, 1, 0, 2, 5).reshape(
        slots_dev, reals_dev * components * modes * 2, ht_count * rows_ht
    )
    solved = jnp.einsum("syx,snx->sny", helmholtz, incoming, precision=lax.Precision.HIGH)
    solved = solved.reshape(
        slots_dev, reals_dev, components, kx_count, band_modes, 2, ht_count, rows_ht
    )
    solved = solved.transpose(3, 6, 0, 5, 1, 2, 4, 7).reshape(
        kx_count * ht_count, slots_dev * 2, reals_dev * components * band_modes, rows_ht
    )
    returned = lax.all_to_all(solved, ("kx", "ht"), split_axis=0, concat_axis=0, tiled=True)
    restored = returned.reshape(
        kz_modes, 2, reals_dev, components, band_modes, rows_ht
    )
    restored = jnp.take(restored, inverse_map, axis=0)
    return restored.transpose(3, 2, 4, 5, 0, 1).reshape(velocity.shape)


LANES = 128
PIECES = 2
VMEM = pl.BlockSpec(memory_space=pltpu.VMEM)
SMEM = pl.BlockSpec(memory_space=pltpu.SMEM)


def params():
    return pltpu.CompilerParams(vmem_limit_bytes=48 * 1024 * 1024)


ORDERS = {
    4: ((1, 3, 2), (3, 1, 2)),
    8: ((4, 1, 6, 2, 5, 3, 7), (5, 4, 1, 6, 2, 7, 3)),
}


def steps_of(count):
    even, odd = ORDERS.get(count, (tuple(range(1, count)),) * 2)
    return (0,) + even, (0,) + odd


def step_at(count, position):
    even, odd = steps_of(count)
    return jnp.where((lax.axis_index("real") & 1) == 0, even[position], odd[position])


def cost(size):
    return pl.CostEstimate(flops=0, bytes_accessed=size, transcendentals=0)


def two_parts(value):
    top = value.astype(jnp.bfloat16)
    rest = (value - top.astype(jnp.float32)).astype(jnp.bfloat16)
    return top, rest


def dot(left, right, dims=((1,), (0,))):
    return lax.dot_general(left, right, (dims, ((), ())), preferred_element_type=jnp.float32)


def pack_first_kernel(near_ref, count_ref, velocity_ref, *out_refs):
    chunks, _, kx_count, rows, columns = velocity_ref.shape
    shape = (out_refs[0].shape[0] - chunks * rows, columns)
    row = lax.broadcasted_iota(jnp.int32, shape, 0)
    lane = lax.broadcasted_iota(jnp.int32, shape, 1)
    extra = jnp.zeros(shape, jnp.int32)
    modes, members = near_ref.shape
    for mode in range(modes):
        line = jnp.where(lane == members, count_ref[mode], 0)
        for member in range(members):
            line = jnp.where(lane == member, near_ref[mode, member], line)
        extra = jnp.where(row == mode, line, extra)
    extra = extra.astype(jnp.float32)
    own = lax.axis_index("kx")
    for index, out_ref in enumerate(out_refs):
        partner = own ^ step_at(kx_count, index)
        for chunk in range(chunks):
            out_ref[chunk * rows : (chunk + 1) * rows] = velocity_ref[chunk, 0, partner]
        out_ref[chunks * rows :] = extra


def pack_first(velocity, neighbours, mode_counts, extra_rows):
    chunks, _, kx_count, rows, columns = velocity.shape
    shape = jax.ShapeDtypeStruct((chunks * rows + extra_rows, columns), jnp.float32)
    return pl.pallas_call(
        pack_first_kernel,
        out_shape=(shape,) * kx_count,
        grid=(1,),
        in_specs=[
            SMEM,
            SMEM,
            pl.BlockSpec((chunks, 1, kx_count, rows, columns), lambda i: (0, 0, 0, 0, 0)),
        ],
        out_specs=(pl.BlockSpec(shape.shape, lambda i: (0, 0)),) * kx_count,
        cost_estimate=cost(4 * velocity.size),
        name="pack_first",
    )(neighbours, mode_counts, velocity)


def pack_kernel(velocity_ref, out_ref):
    chunks, _, kx_count, rows, columns = velocity_ref.shape
    for index in range(kx_count):
        for chunk in range(chunks):
            place = slice(chunk * rows, (chunk + 1) * rows)
            out_ref[index, place] = velocity_ref[chunk, 0, index]


def pack(velocity, piece):
    chunks, _, kx_count, rows, columns = velocity.shape
    shape = (kx_count, chunks * rows, columns)
    return pl.pallas_call(
        pack_kernel,
        out_shape=jax.ShapeDtypeStruct(shape, jnp.float32),
        grid=(1,),
        in_specs=[
            pl.BlockSpec((chunks, 1, kx_count, rows, columns), lambda i: (0, piece, 0, 0, 0)),
        ],
        out_specs=pl.BlockSpec(shape, lambda i: (0, 0, 0)),
        cost_estimate=cost(4 * velocity.size),
        name="pack",
    )(velocity)


def hand_on_kernel(value_ref, after_ref, out_ref):
    pass


def hand_on(value, after):
    return pl.pallas_call(
        hand_on_kernel,
        out_shape=jax.ShapeDtypeStruct(value.shape, value.dtype),
        in_specs=[pl.BlockSpec(memory_space=pl.ANY)] * 2,
        out_specs=pl.BlockSpec(memory_space=pl.ANY),
        input_output_aliases={0: 0},
        cost_estimate=cost(0),
        name="hand_on",
    )(value, after)


def tables_kernel(owner_ref, top_ref, rest_ref, first_ref, back_ref, order_ref, slot_ref):
    columns = slot_ref.shape[1]
    modes = columns // 2
    lane = lax.broadcasted_iota(jnp.int32, (8, columns), 1)
    mode = jnp.zeros((8, columns), jnp.int32)
    for slot in range(modes):
        mode = jnp.where(lane % modes == slot, owner_ref[slot], mode)
    slot_ref[...] = mode
    wanted = 2 * mode + lane // modes
    row = lax.broadcasted_iota(jnp.int32, (columns, columns), 0)
    chosen = (row == wanted[:1]).astype(jnp.float32)
    select = chosen.astype(jnp.bfloat16)
    points = top_ref.shape[1]
    for half in range(2):
        rows = slice(half * columns, (half + 1) * columns)
        first_ref[rows, :points] = top_ref[...]
        first_ref[rows, points:] = select
        order_ref[rows] = chosen.T.astype(jnp.bfloat16)
    for index, table_ref in enumerate((top_ref, rest_ref)):
        back = dot(table_ref[...], select, ((0,), (0,))) * (2.0 * modes / points)
        back_ref[:, index * columns : (index + 1) * columns] = back.astype(jnp.bfloat16)


def spanwise_constants(columns, points):
    mode = np.arange(columns) // 2
    phase = 2.0 * np.pi * ((mode[:, None] * np.arange(points)[None, :]) % points) / points
    forward = np.where(np.arange(columns)[:, None] % 2 == 0, np.cos(phase), -np.sin(phase))
    forward = (forward / np.sqrt(columns // 2)).astype(np.float32)
    top = forward.astype(jnp.bfloat16)
    rest = (forward - top.astype(np.float32)).astype(jnp.bfloat16)
    return jnp.asarray(top), jnp.asarray(rest)


def slot_tables(owner_map, columns):
    points = 2 * columns
    top, rest = spanwise_constants(columns, points)
    first, back, order, slot_modes = pl.pallas_call(
        tables_kernel,
        out_shape=(
            jax.ShapeDtypeStruct((2 * columns, points + columns), jnp.bfloat16),
            jax.ShapeDtypeStruct((points, 2 * columns), jnp.bfloat16),
            jax.ShapeDtypeStruct((2 * columns, columns), jnp.bfloat16),
            jax.ShapeDtypeStruct((8, columns), jnp.int32),
        ),
        in_specs=[SMEM, VMEM, VMEM],
        out_specs=(VMEM,) * 4,
        compiler_params=params(),
        cost_estimate=cost(16 * points * columns),
        name="tables",
    )(owner_map, top, rest)
    return (first, rest, back), order, slot_modes


def list_high(low_ref, high_ref, modes):
    found = jnp.int32(0)
    for mode in range(modes):
        is_low = jnp.int32(0)
        for member in range(low_ref.shape[0]):
            is_low = is_low | (low_ref[member] == mode).astype(jnp.int32)
        high_ref[found] = mode
        found = found + 1 - is_low


def tile_at(step, points):
    halves = points // LANES
    return (
        pl.ds(pl.multiple_of((step // halves) * 8, 8), 8),
        pl.ds(pl.multiple_of((step % halves) * LANES, LANES), LANES),
    )


def inverse(fields, back_ref):
    columns = back_ref.shape[1] // 2
    top, rest = two_parts(fields)
    both = dot(top, back_ref[...])
    return both[:, :columns] + both[:, columns:] + dot(rest, back_ref[:, :columns])


def stress_kernel(low_ref, near_ref, *refs):
    block_refs, refs = (refs[:-10], refs[-10:])
    first_ref, second_ref, back_ref, _ = refs[:4]
    slotted_ref, physical, kept_ref, sent_ref, sums, high_ref = refs[4:]
    components, modes, rows, columns = slotted_ref.shape
    if len(block_refs) > 1:
        bands = len(block_refs)
        places = [lax.axis_index("kx") ^ step_at(bands, index) for index in range(bands)]
    else:
        bands = block_refs[0].shape[0]
        places = list(range(bands))
        block_refs = [block_refs[0].at[index] for index in range(bands)]
    points, band_modes = (physical.shape[3], modes // bands)
    members = sums.shape[1]
    odd = (lax.axis_index("real") & 1) == 1
    list_high(low_ref, high_ref, modes)
    size = band_modes * rows
    for c in range(components):
        joined = [block_ref[c * size : (c + 1) * size] for block_ref in block_refs]
        top, rest = two_parts(jnp.concatenate(joined, axis=0))
        both = dot(jnp.concatenate([top, rest], axis=1), first_ref[...])
        fields = both[:, :points] + dot(top, second_ref[...])
        for index in range(bands):
            place = pl.ds(places[index] * band_modes, band_modes)
            part = slice(index * size, (index + 1) * size)
            physical[c, place] = fields[part].reshape(band_modes, rows, points)
            slotted_ref[c, place] = both[part, points:].reshape(band_modes, rows, columns)

    def pairs(step, carry):
        place = tile_at(step, points)

        def one_high(index, totals):
            mode = high_ref[index]
            own = [physical[(c, mode) + place] for c in range(components)]
            totals = list(totals)
            for member in range(members):
                partner = physical[(1, near_ref[mode, member]) + place]
                for c in range(components):
                    slot = member * components + c
                    totals[slot] = totals[slot] + own[c] * partner
            return tuple(totals)

        empty = tuple(jnp.zeros((8, LANES), jnp.float32) for _ in range(members * components))
        totals = lax.fori_loop(0, modes - members, one_high, empty)
        for member in range(members):
            for c in range(components):
                sums[(c, member) + place] = totals[member * components + c]
        return carry

    lax.fori_loop(0, (rows // 8) * (points // LANES), pairs, 0)
    stress = inverse(sums[...].reshape(components * members * rows, points), back_ref)
    stress = stress.reshape(components, 2, members // 2, rows, columns)
    kept_ref[...] = jnp.where(odd, stress[:, 1], stress[:, 0])
    sent_ref[...] = jnp.where(odd, stress[:, 0], stress[:, 1])


def stress_terms(blocks, shape, low_index, neighbours, tables, after):
    components, modes, rows, columns = shape
    members, points = (low_index.shape[0], 2 * columns)
    half = jax.ShapeDtypeStruct((components, members // 2, rows, columns), jnp.float32)
    return pl.pallas_call(
        stress_kernel,
        out_shape=(
            jax.ShapeDtypeStruct(shape, jnp.float32),
            jax.ShapeDtypeStruct((components, modes, rows, points), jnp.float32),
            half,
            half,
        ),
        in_specs=[SMEM] * 2 + [VMEM] * (len(blocks) + 3) + [pl.BlockSpec(memory_space=pl.ANY)],
        out_specs=(VMEM,) * 4,
        scratch_shapes=[
            pltpu.VMEM((components, members, rows, points), jnp.float32),
            pltpu.SMEM((modes + 1,), jnp.int32),
        ],
        compiler_params=params(),
        cost_estimate=cost(4 * components * modes * rows * points * members),
        name="stress",
    )(low_index, neighbours, *blocks, *tables, after)


def products_kernel(
    low_ref, near_ref, count_ref, physical, back_ref, slot_ref, out_ref, products, high_ref
):
    components, modes, rows, points = physical.shape
    members, highs = (low_ref.shape[0], out_ref.shape[1])
    list_high(low_ref, high_ref, modes)

    def pairs(step, carry):
        place = tile_at(step, points)
        low = [
            [physical[(c, low_ref[member]) + place] for c in range(components)]
            for member in range(members)
        ]

        def one_high(index, inner):
            mode = high_ref[index]
            result = [jnp.zeros((8, LANES), jnp.float32) for _ in range(components)]
            for member in range(members):
                near = near_ref[mode, member]
                partner = [physical[(c, near) + place] for c in range(components)]
                for c in range(components):
                    if c == 1:
                        result[c] = result[c] + low[member][1] * partner[1]
                    else:
                        result[c] = result[c] + (
                            low[member][c] * partner[1] + partner[c] * low[member][1]
                        )
            for c in range(components):
                products[(c, index) + place] = result[c] * 2.0 if c == 1 else result[c]
            return inner

        lax.fori_loop(0, highs, one_high, 0)
        return carry

    lax.fori_loop(0, (rows // 8) * (points // LANES), pairs, 0)
    forcing = inverse(products[...].reshape(components * highs * rows, points), back_ref)
    forcing = forcing.reshape(out_ref.shape)
    for index in range(highs):
        active = slot_ref[:1] < count_ref[high_ref[index]]
        out_ref[:, index] = jnp.where(active, forcing[:, index] * dt_step, 0.0)


def high_terms(physical, low_index, neighbours, mode_counts, back, slot_modes):
    components, modes, rows, points = physical.shape
    highs = modes - low_index.shape[0]
    return pl.pallas_call(
        products_kernel,
        out_shape=jax.ShapeDtypeStruct((components, highs, rows, points // 2), jnp.float32),
        in_specs=[SMEM] * 3 + [VMEM] * 3,
        out_specs=VMEM,
        scratch_shapes=[
            pltpu.VMEM((components, highs, rows, points), jnp.float32),
            pltpu.SMEM((modes + 1,), jnp.int32),
        ],
        compiler_params=params(),
        cost_estimate=cost(4 * physical.size * low_index.shape[0]),
        name="products",
    )(low_index, neighbours, mode_counts, physical, back, slot_modes)


def outgoing_kernel(
    low_ref, count_ref, slotted_ref, forcing_ref, kept_ref, other_ref, slot_ref, *refs,
    groups, band_modes, owners, scale
):
    out_refs, (full, turned, high_ref) = (refs[:-3], refs[-3:])
    components, modes, rows, columns = slotted_ref.shape
    half, slots = (kept_ref.shape[1], columns // 2 // owners)
    per_slot = out_refs[0].shape[0] * len(out_refs) // (columns // 2)
    own = lax.axis_index("real") & 1
    list_high(low_ref, high_ref, modes)
    full[...] = slotted_ref[...]
    for index in range(forcing_ref.shape[1]):
        for c in range(components):
            full[c, high_ref[index]] += forcing_ref[c, index]
    for member in range(half):
        for part_ref, start in ((kept_ref, own * half), (other_ref, (1 - own) * half)):
            mode = low_ref[start + member]
            active = slot_ref[:1] < count_ref[mode]
            for c in range(components):
                full[c, mode] += jnp.where(active, part_ref[c, member] * scale, 0.0)
    inner = modes // groups
    if len(out_refs) > 1:
        me = lax.axis_index("kx") * lax.axis_size("ht") + lax.axis_index("ht")
        targets = [me ^ step_at(owners, position) for position in range(owners)]
    for c in range(components):
        for part in range(inner):
            tile = jnp.concatenate([full[c, part + inner * g] for g in range(groups)], axis=0)
            band_low, band_mode = (part // band_modes, part % band_modes)
            if len(out_refs) > 1:
                turned[...] = tile.T
            else:
                value = tile.T
            for p in range(2):
                row = ((band_low * 2 + p) * components + c) * band_modes + band_mode
                if len(out_refs) == 1:
                    out_refs[0][pl.ds(row, columns // 2, stride=per_slot), :] = value[
                        p * (columns // 2) : (p + 1) * (columns // 2)
                    ]
                    continue
                for out_ref, target in zip(out_refs, targets):
                    start = pl.multiple_of((p * owners + target) * slots, slots)
                    out_ref[pl.ds(row, slots, stride=per_slot), :] = turned[pl.ds(start, slots)]


def outgoing(
    slotted, forcing, kept, other, low_index, mode_counts, slot_modes, groups, band_modes, owners,
    realizations, separate,
):
    components, modes, rows, columns = slotted.shape
    total, lanes = ((columns // 2) * (modes // groups) * 2 * components, groups * rows)
    count = owners if separate else 1
    return pl.pallas_call(
        functools.partial(
            outgoing_kernel, groups=groups, band_modes=band_modes, owners=owners,
            scale=dt_step / realizations,
        ),
        out_shape=(jax.ShapeDtypeStruct((total // count, lanes), jnp.float32),) * count,
        in_specs=[SMEM, SMEM] + [VMEM] * 5,
        out_specs=(VMEM,) * count,
        scratch_shapes=[
            pltpu.VMEM(slotted.shape, jnp.float32), pltpu.VMEM((columns, lanes), jnp.float32),
            pltpu.SMEM((modes + 1,), jnp.int32),
        ],
        compiler_params=params(),
        cost_estimate=cost(8 * slotted.size),
        name="outgoing",
    )(low_index, mode_counts, slotted, forcing, kept, other, slot_modes)


def regroup(blocks, rows):
    count = len(blocks)
    lane = lax.broadcasted_iota(jnp.int32, blocks[0].shape, 1) // rows
    step = 1
    while step < count:
        take = (lane & step) == 0
        for i in range(count):
            if i & step == 0:
                here, there = (blocks[i], blocks[i + step])
                blocks[i] = jnp.where(take, here, pltpu.roll(there, step * rows, 1))
                blocks[i + step] = jnp.where(
                    take, pltpu.roll(here, LANES - step * rows, 1), there
                )
        step *= 2
    return blocks


def solve_kernel(*refs, groups, kx_count, ht_count, pieces, piece):
    owners, last = (kx_count * ht_count, piece == pieces - 1)
    own_kx, own_ht = (lax.axis_index("kx"), lax.axis_index("ht"))
    partners = []
    for position in range(owners):
        step = step_at(owners, position)
        partners.append((own_kx ^ (step // ht_count), own_ht ^ (step % ht_count)))
    refs = list(refs)
    matrices = refs.pop()
    arrived = refs.pop()
    source = refs.pop(0)
    if piece:
        ordered = refs.pop()
        blocks = [source] + [refs.pop(0) for _ in range(owners - 1)]
        for block_ref, (kx, ht) in zip(blocks, partners):
            ordered[kx * ht_count + ht] = block_ref[...]
        source = ordered
    matrix_ref = refs.pop(0)
    slots, heights = (matrix_ref.shape[0], matrix_ref.shape[1])
    width = heights // ht_count // pieces
    copies = [
        [
            pltpu.make_async_copy(
                matrix_ref.at[s, :, pl.ds((h * pieces + piece) * width, width)],
                matrices.at[s, h],
                arrived.at[s, h],
            )
            for h in range(ht_count)
        ]
        for s in range(slots)
    ]
    ahead = min(3, slots)
    for s in range(ahead):
        for copy in copies[s]:
            copy.start()
    partial_ref = refs.pop(0) if piece else None
    if last:
        out_refs, full = (refs[:owners], refs[owners])
        lane_tiles, per_band = out_refs[0].shape[1:3]
    rows = LANES // groups
    for s in range(slots):
        tiles = []
        for h in range(ht_count):
            for first in range(0, kx_count, groups):
                blocks = [source[(first + g) * ht_count + h, s] for g in range(groups)]
                tiles.append(jnp.concatenate(regroup(blocks, rows), axis=0))
        fields = jnp.concatenate(tiles, axis=1)
        count = fields.shape[0]
        spare = -count % LANES
        if spare:
            empty = jnp.zeros((spare, fields.shape[1]), jnp.float32)
            fields = jnp.concatenate([fields, empty], axis=0)
        top, rest = two_parts(fields)
        for copy in copies[s]:
            copy.wait()
        if s + ahead < slots:
            for copy in copies[s + ahead]:
                copy.start()
        matrix = jnp.concatenate([matrices[s, h] for h in range(ht_count)], axis=1)
        matrix_top, matrix_rest = two_parts(matrix)
        contract = ((1,), (1,))
        both = dot(matrix_top, jnp.concatenate([top, rest], axis=0), contract)
        solved = both[:, : count + spare] + both[:, count + spare :]
        solved = solved + dot(matrix_rest, top, contract)
        if piece:
            solved = solved + partial_ref[s]
        if not last:
            refs[0][s] = solved
            continue
        for tile in range(heights // LANES):
            full[s % 2, tile] = solved[tile * LANES : (tile + 1) * LANES].T[:count]
        for out_ref, (kx, ht) in zip(out_refs, partners):
            band = pl.ds(pl.multiple_of(kx * per_band, 8), per_band)
            for tile in range(lane_tiles):
                out_ref[s, tile] = full[s % 2, ht * lane_tiles + tile, band]


def solve(blocks, helmholtz, piece, pieces, partial, groups, kx_count, ht_count):
    slots, per_slot, _ = blocks[0].shape[-3:]
    heights, owners, last = (helmholtz.shape[1], kx_count * ht_count, piece == pieces - 1)
    count = per_slot * groups
    scratch = []
    if last:
        shape = (slots, heights // ht_count // LANES, count // kx_count, LANES)
        out_shape = (jax.ShapeDtypeStruct(shape, jnp.float32),) * owners
        scratch.append(pltpu.VMEM((2, heights // LANES, count, LANES), jnp.float32))
    else:
        padded = -(-count // LANES) * LANES
        out_shape = jax.ShapeDtypeStruct((slots, heights, padded), jnp.float32)
    if piece:
        scratch.append(pltpu.VMEM((owners,) + blocks[0].shape, jnp.float32))
    width = heights // ht_count // pieces
    scratch += [
        pltpu.SemaphoreType.DMA((slots, ht_count)),
        pltpu.VMEM((slots, ht_count, heights, width), jnp.float32),
    ]
    started = [] if partial is None else [partial]
    return pl.pallas_call(
        functools.partial(
            solve_kernel, groups=groups, kx_count=kx_count, ht_count=ht_count, pieces=pieces,
            piece=piece,
        ),
        out_shape=out_shape,
        in_specs=[VMEM] * len(blocks) + [pl.BlockSpec(memory_space=pl.ANY)] + [VMEM] * len(started),
        out_specs=(VMEM,) * owners if last else VMEM,
        scratch_shapes=scratch,
        compiler_params=params(),
        cost_estimate=cost(8 * helmholtz.size // pieces),
        name="solve",
    )(*blocks, helmholtz, *started)


def restore_kernel(*refs, owners, ht_count):
    block_refs, (order_ref, out_ref, ordered) = (refs[:-3], refs[-3:])
    components, band_modes, rows, columns = out_ref.shape
    slots = columns // 2 // owners
    per_slot = block_refs[0].shape[0] // slots
    me = lax.axis_index("kx") * ht_count + lax.axis_index("ht")
    for position, block_ref in enumerate(block_refs):
        ordered[me ^ step_at(owners, position)] = block_ref[...]
    for c in range(components):
        for mode in range(band_modes):
            for tile in range(rows // LANES):
                parts = []
                for p in range(2):
                    row = ((tile * 2 + p) * components + c) * band_modes + mode
                    for owner in range(owners):
                        parts.append(ordered[owner, pl.ds(row, slots, stride=per_slot), :])
                top, rest = two_parts(jnp.concatenate(parts, axis=0))
                both = jnp.concatenate([top, rest], axis=0)
                out_ref[c, mode, pl.ds(tile * LANES, LANES)] = dot(
                    both, order_ref[...], ((0,), (0,))
                )


def restore(blocks, order, components, band_modes, rows, ht_count):
    columns = order.shape[1]
    return pl.pallas_call(
        functools.partial(restore_kernel, owners=len(blocks), ht_count=ht_count),
        out_shape=jax.ShapeDtypeStruct((components, band_modes, rows, columns), jnp.float32),
        in_specs=[VMEM] * (len(blocks) + 1),
        out_specs=VMEM,
        scratch_shapes=[pltpu.VMEM((len(blocks),) + blocks[0].shape, jnp.float32)],
        compiler_params=params(),
        cost_estimate=cost(8 * components * band_modes * rows * columns),
        name="restore",
    )(*blocks, order)


def exchange(blocks, axes):
    count, realizations = (len(blocks), lax.axis_size("real"))
    result = list(blocks)
    for position in range(1, count):
        steps = [order[position] for order in steps_of(count)]
        pairs = [
            (index * realizations + r, (index ^ steps[r % 2]) * realizations + r)
            for index in range(count)
            for r in range(realizations)
        ]
        result[position] = lax.ppermute(blocks[position], axes + ("real",), pairs)
    return result


def sum_kernel(first_ref, second_ref, _, out_ref):
    out_ref[...] = first_ref[...] + second_ref[...]


def ordered_sum(first, second, after):
    return pl.pallas_call(
        sum_kernel,
        out_shape=jax.ShapeDtypeStruct(first.shape, jnp.float32),
        in_specs=[VMEM, VMEM, pl.BlockSpec(memory_space=pl.ANY)],
        out_specs=VMEM,
        compiler_params=params(),
        cost_estimate=cost(12 * first.size),
        name="ordered_sum",
    )(first, second, after)


def swap(value, step):
    pairs = [(index, index ^ step) for index in range(lax.axis_size("real"))]
    return lax.ppermute(value, "real", pairs)


def local(velocity, low_index, neighbours, owner_map, mode_counts, helmholtz):
    components, reals_dev, band_modes, rows_ht, columns = velocity.shape
    kx_count, ht_count = (lax.axis_size("kx"), lax.axis_size("ht"))
    own_kx, own_ht = (lax.axis_index("kx"), lax.axis_index("ht"))
    owners, pieces, real_count = (kx_count * ht_count, PIECES, lax.axis_size("real"))
    rows = rows_ht // (kx_count * pieces)
    groups = LANES // rows if rows else 0
    slots = columns // 2 // owners
    if (
        columns != LANES or reals_dev != 1 or rows_ht % LANES or rows % 8 or LANES % rows or kx_count % groups or kx_count & (kx_count - 1)
        or (band_modes * 2 * components) % 8 or slots % 8 or owners & (owners - 1) or low_index.shape[0] >= kx_count * band_modes
        or low_index.shape[0] >= columns or low_index.shape[0] % 2 or real_count < 2 or real_count & (real_count - 1)
    ):
        return local_plain(velocity, low_index, neighbours, owner_map, mode_counts, helmholtz)
    realizations, members = (real_count, low_index.shape[0])
    chunks, modes = (components * band_modes, band_modes * kx_count)
    shape = (components, modes, rows, columns)
    extra_rows = -(-band_modes // 8) * 8
    split = velocity.reshape(chunks, pieces, kx_count, rows, columns)
    blocks = pack_first(split, neighbours, mode_counts, extra_rows)
    parts = [exchange(blocks, ("kx",))]
    for piece in range(1, pieces):
        block = hand_on(pack(split, piece), parts[0][min(2, kx_count - 1)])
        block = lax.all_to_all(block, "kx", split_axis=0, concat_axis=0, tiled=True)
        parts.append((block,))
    tables, order, slot_modes = slot_tables(owner_map, columns)
    small = 0.0
    for index, block in enumerate(parts[0]):
        lines = block[chunks * rows : chunks * rows + band_modes, : members + 1]
        here = (own_kx ^ step_at(kx_count, index)) == jnp.arange(kx_count)
        small = small + jnp.where(here[:, None, None], lines[None], 0.0)
    small = small.reshape(modes, members + 1).astype(jnp.int32)
    neighbours, mode_counts = (small[:, :-1], small[:, -1])
    after = slot_modes
    received = []
    for piece, part in enumerate(parts):
        slotted, physical, kept, sent = stress_terms(
            part, shape, low_index, neighbours, tables, after
        )
        forcing = high_terms(physical, low_index, neighbours, mode_counts, tables[2], slot_modes)
        kept = after = kept + swap(sent, 1)
        step = 2
        while step < realizations:
            kept = ordered_sum(kept, swap(kept, step), forcing)
            step *= 2
        blocks = outgoing(
            slotted, forcing, kept, swap(kept, 1), low_index, mode_counts, slot_modes, groups, band_modes,
            owners, realizations, piece > 0,
        )
        if piece:
            blocks = [block.reshape(slots, -1, LANES) for block in blocks]
            received.append(exchange(blocks, ("kx", "ht")))
        else:
            block = blocks[0].reshape(owners, slots, -1, LANES)
            block = lax.all_to_all(block, ("kx", "ht"), split_axis=0, concat_axis=0, tiled=True)
            received.append([block])
    solved = None
    for piece, blocks in enumerate(received):
        solved = solve(blocks, helmholtz, piece, pieces, solved, groups, kx_count, ht_count)
    returned = [block.reshape(-1, LANES) for block in exchange(solved, ("kx", "ht"))]
    result = restore(returned, order, components, band_modes, rows_ht, ht_count)
    return result.reshape(velocity.shape)


def solution(mesh):
    in_specs = (
        P(None, "real", "kx", "ht", None),
        P(),
        P("kx", None),
        P(),
        P("kx"),
        P(("kx", "ht"), None, None),
    )
    out_specs = P(None, "real", "kx", "ht", None)
    return jax.shard_map(local, mesh=mesh, in_specs=in_specs, out_specs=out_specs, check_vma=False)
```

```python
import functools

import jax
import jax.numpy as jnp
import numpy as np
from jax import lax
from jax.experimental import pallas as pl
from jax.experimental.pallas import tpu as pltpu
from jax.sharding import PartitionSpec as P

dt_step = 0.1


def spanwise_tables(mode_count, point_count):
    column_ids = jnp.arange(2 * mode_count)
    wavenumber = (column_ids // 2).astype(jnp.float32)
    imag_part = column_ids % 2
    positions = 2.0 * jnp.pi * jnp.arange(point_count).astype(jnp.float32) / point_count
    phases = wavenumber[:, None] * positions[None, :]
    forward = jnp.where(imag_part[:, None] == 0, jnp.cos(phases), -jnp.sin(phases)) / jnp.sqrt(
        jnp.float32(mode_count)
    )
    backward = forward.T * (2.0 * mode_count / point_count)
    return (forward, backward)


def nonlinear_rows(fields, low_index, neighbours, mode_counts, forward, backward):
    precision = lax.Precision.HIGH
    realizations, modes, columns = (fields.shape[1], fields.shape[2], fields.shape[4])
    low_select = (low_index[:, None] == jnp.arange(modes)[None, :]).astype(jnp.float32)
    high_mask = 1.0 - jnp.sum(low_select, axis=0)
    high_rows = high_mask[None, None, :, None, None]
    column_mask = ((jnp.arange(columns) // 2)[None, :] < mode_counts[:, None]).astype(jnp.float32)
    physical = jnp.dot(fields, forward, precision=precision)
    low_fields = jnp.take(physical, low_index, axis=2)
    high_low = jnp.zeros_like(physical)
    stresses = []
    for member in range(low_index.shape[0]):
        partner = jnp.take(physical, neighbours[:, member], axis=2)
        low_one = low_fields[:, :, member : member + 1]
        high_low = high_low + low_one * partner[1:2] + partner * low_one[1:2]
        stresses.append(jnp.sum(physical * (partner[1:2] * high_rows), axis=(1, 2)))
    stress = jnp.stack(stresses, axis=1) / realizations
    forcing = jnp.dot(high_low, backward, precision=precision) * high_rows
    low_forcing = jnp.dot(stress, backward, precision=precision)
    low_rows = jnp.einsum("jm,cjyk->cmyk", low_select, low_forcing, precision=lax.Precision.HIGHEST)
    forcing = (forcing + low_rows[:, None]) * column_mask[None, None, :, None, :]
    return fields + dt_step * forcing


def local_plain(velocity, low_index, neighbours, owner_map, mode_counts, helmholtz):
    components, reals_dev, band_modes, rows_ht, columns = velocity.shape
    kz_modes = columns // 2
    forward, backward = spanwise_tables(kz_modes, 4 * kz_modes)
    kx_count, ht_count = (lax.axis_size("kx"), lax.axis_size("ht"))
    real_count = lax.axis_size("real")
    modes, realizations = (band_modes * kx_count, reals_dev * real_count)
    slots_dev = kz_modes // (kx_count * ht_count)
    rows_dev = rows_ht // (kx_count * real_count)
    small = jnp.concatenate([neighbours, mode_counts[:, None]], axis=1)
    small = lax.all_gather(small, "kx", axis=0, tiled=True)
    neighbours, mode_counts = (small[:, :-1], small[:, -1])
    inverse_map = (
        jnp.zeros((kz_modes,), jnp.int32).at[owner_map].set(jnp.arange(kz_modes, dtype=jnp.int32))
    )
    split = velocity.reshape(
        components, reals_dev, band_modes, kx_count * real_count, rows_dev, columns
    )
    split = split.transpose(3, 0, 1, 2, 4, 5)
    split = lax.all_to_all(split, ("kx", "real"), split_axis=0, concat_axis=0, tiled=True)
    fields = split.reshape(
        kx_count, real_count, components, reals_dev, band_modes, rows_dev, columns
    )
    fields = fields.transpose(2, 1, 3, 0, 4, 5, 6).reshape(
        components, realizations, modes, rows_dev, columns
    )
    updated = nonlinear_rows(fields, low_index, neighbours, mode_counts, forward, backward)
    slotted = jnp.take(
        updated.reshape(components, realizations, modes, rows_dev, kz_modes, 2), owner_map, axis=4
    )
    slotted = slotted.reshape(
        components, real_count, reals_dev, modes, rows_dev, kx_count * ht_count, slots_dev, 2
    )
    outgoing = slotted.transpose(5, 1, 6, 2, 0, 3, 7, 4).reshape(
        kx_count * ht_count * real_count, slots_dev, reals_dev * components * modes * 2, rows_dev
    )
    incoming = lax.all_to_all(
        outgoing, ("kx", "ht", "real"), split_axis=0, concat_axis=0, tiled=True
    )
    incoming = incoming.reshape(
        kx_count, ht_count, real_count, slots_dev, reals_dev * components * modes * 2, rows_dev
    )
    incoming = incoming.transpose(3, 4, 1, 0, 2, 5).reshape(
        slots_dev, reals_dev * components * modes * 2, ht_count * rows_ht
    )
    solved = jnp.einsum("syx,snx->sny", helmholtz, incoming, precision=lax.Precision.HIGH)
    solved = solved.reshape(
        slots_dev, reals_dev, components, kx_count, band_modes, 2, ht_count, rows_ht
    )
    solved = solved.transpose(3, 6, 0, 5, 1, 2, 4, 7).reshape(
        kx_count * ht_count, slots_dev * 2, reals_dev * components * band_modes, rows_ht
    )
    returned = lax.all_to_all(solved, ("kx", "ht"), split_axis=0, concat_axis=0, tiled=True)
    restored = returned.reshape(
        kz_modes, 2, reals_dev, components, band_modes, rows_ht
    )
    restored = jnp.take(restored, inverse_map, axis=0)
    return restored.transpose(3, 2, 4, 5, 0, 1).reshape(velocity.shape)


LANES = 128
PIECES = 2
VMEM = pl.BlockSpec(memory_space=pltpu.VMEM)
SMEM = pl.BlockSpec(memory_space=pltpu.SMEM)


def params():
    return pltpu.CompilerParams(vmem_limit_bytes=24 * 1024 * 1024)


ORDERS = {4: (1, 3, 2), 8: (4, 1, 2, 6, 5, 3, 7)}


def steps_of(count):
    even = ORDERS.get(count, tuple(range(1, count)))
    odd = list(even)
    for first in range(0, count - 2, 2):
        odd[first], odd[first + 1] = (even[first + 1], even[first])
    return (0,) + tuple(even), (0,) + tuple(odd)


def step_at(count, position):
    even, odd = steps_of(count)
    return jnp.where((lax.axis_index("real") & 1) == 0, even[position], odd[position])


def cost(size):
    return pl.CostEstimate(flops=0, bytes_accessed=size, transcendentals=0)


def two_parts(value):
    top = value.astype(jnp.bfloat16)
    rest = (value - top.astype(jnp.float32)).astype(jnp.bfloat16)
    return top, rest


def dot(left, right, dims=((1,), (0,))):
    return lax.dot_general(left, right, (dims, ((), ())), preferred_element_type=jnp.float32)


def pack_first_kernel(near_ref, count_ref, velocity_ref, *out_refs):
    chunks, _, kx_count, rows, columns = velocity_ref.shape
    shape = (out_refs[0].shape[0] - chunks * rows, columns)
    row = lax.broadcasted_iota(jnp.int32, shape, 0)
    lane = lax.broadcasted_iota(jnp.int32, shape, 1)
    extra = jnp.zeros(shape, jnp.int32)
    modes, members = near_ref.shape
    for mode in range(modes):
        line = jnp.where(lane == members, count_ref[mode], 0)
        for member in range(members):
            line = jnp.where(lane == member, near_ref[mode, member], line)
        extra = jnp.where(row == mode, line, extra)
    extra = extra.astype(jnp.float32)
    own = lax.axis_index("kx")
    for index, out_ref in enumerate(out_refs):
        partner = own ^ step_at(kx_count, index)
        for chunk in range(chunks):
            out_ref[chunk * rows : (chunk + 1) * rows] = velocity_ref[chunk, 0, partner]
        out_ref[chunks * rows :] = extra


def pack_first(velocity, neighbours, mode_counts, extra_rows):
    chunks, _, kx_count, rows, columns = velocity.shape
    shape = jax.ShapeDtypeStruct((chunks * rows + extra_rows, columns), jnp.float32)
    return pl.pallas_call(
        pack_first_kernel,
        out_shape=(shape,) * kx_count,
        grid=(1,),
        in_specs=[
            SMEM,
            SMEM,
            pl.BlockSpec((chunks, 1, kx_count, rows, columns), lambda i: (0, 0, 0, 0, 0)),
        ],
        out_specs=(pl.BlockSpec(shape.shape, lambda i: (0, 0)),) * kx_count,
        cost_estimate=cost(4 * velocity.size),
        name="pack_first",
    )(neighbours, mode_counts, velocity)


def pack_kernel(velocity_ref, out_ref):
    chunks, _, kx_count, rows, columns = velocity_ref.shape
    for index in range(kx_count):
        for chunk in range(chunks):
            place = slice(chunk * rows, (chunk + 1) * rows)
            out_ref[index, place] = velocity_ref[chunk, 0, index]


def pack(velocity, piece):
    chunks, _, kx_count, rows, columns = velocity.shape
    shape = (kx_count, chunks * rows, columns)
    return pl.pallas_call(
        pack_kernel,
        out_shape=jax.ShapeDtypeStruct(shape, jnp.float32),
        grid=(1,),
        in_specs=[
            pl.BlockSpec((chunks, 1, kx_count, rows, columns), lambda i: (0, piece, 0, 0, 0)),
        ],
        out_specs=pl.BlockSpec(shape, lambda i: (0, 0, 0)),
        cost_estimate=cost(4 * velocity.size),
        name="pack",
    )(velocity)


def hand_on_kernel(value_ref, after_ref, out_ref):
    pass


def hand_on(value, after):
    return pl.pallas_call(
        hand_on_kernel,
        out_shape=jax.ShapeDtypeStruct(value.shape, value.dtype),
        in_specs=[pl.BlockSpec(memory_space=pl.ANY)] * 2,
        out_specs=pl.BlockSpec(memory_space=pl.ANY),
        input_output_aliases={0: 0},
        cost_estimate=cost(0),
        name="hand_on",
    )(value, after)


def tables_kernel(owner_ref, top_ref, rest_ref, first_ref, back_ref, order_ref, slot_ref):
    columns = slot_ref.shape[1]
    modes = columns // 2
    lane = lax.broadcasted_iota(jnp.int32, (8, columns), 1)
    mode = jnp.zeros((8, columns), jnp.int32)
    for slot in range(modes):
        mode = jnp.where(lane % modes == slot, owner_ref[slot], mode)
    slot_ref[...] = mode
    wanted = 2 * mode + lane // modes
    row = lax.broadcasted_iota(jnp.int32, (columns, columns), 0)
    chosen = (row == wanted[:1]).astype(jnp.float32)
    select = chosen.astype(jnp.bfloat16)
    points = top_ref.shape[1]
    for half in range(2):
        rows = slice(half * columns, (half + 1) * columns)
        first_ref[rows, :points] = top_ref[...]
        first_ref[rows, points:] = select
        order_ref[rows] = chosen.T.astype(jnp.bfloat16)
    for index, table_ref in enumerate((top_ref, rest_ref)):
        back = dot(table_ref[...], select, ((0,), (0,))) * (2.0 * modes / points)
        back_ref[:, index * columns : (index + 1) * columns] = back.astype(jnp.bfloat16)


def spanwise_constants(columns, points):
    mode = np.arange(columns) // 2
    phase = 2.0 * np.pi * ((mode[:, None] * np.arange(points)[None, :]) % points) / points
    forward = np.where(np.arange(columns)[:, None] % 2 == 0, np.cos(phase), -np.sin(phase))
    forward = (forward / np.sqrt(columns // 2)).astype(np.float32)
    top = forward.astype(jnp.bfloat16)
    rest = (forward - top.astype(np.float32)).astype(jnp.bfloat16)
    return jnp.asarray(top), jnp.asarray(rest)


def slot_tables(owner_map, columns):
    points = 2 * columns
    top, rest = spanwise_constants(columns, points)
    first, back, order, slot_modes = pl.pallas_call(
        tables_kernel,
        out_shape=(
            jax.ShapeDtypeStruct((2 * columns, points + columns), jnp.bfloat16),
            jax.ShapeDtypeStruct((points, 2 * columns), jnp.bfloat16),
            jax.ShapeDtypeStruct((2 * columns, columns), jnp.bfloat16),
            jax.ShapeDtypeStruct((8, columns), jnp.int32),
        ),
        in_specs=[SMEM, VMEM, VMEM],
        out_specs=(VMEM,) * 4,
        compiler_params=params(),
        cost_estimate=cost(16 * points * columns),
        name="tables",
    )(owner_map, top, rest)
    return (first, rest, back), order, slot_modes


def list_high(low_ref, high_ref, modes):
    found = jnp.int32(0)
    for mode in range(modes):
        is_low = jnp.int32(0)
        for member in range(low_ref.shape[0]):
            is_low = is_low | (low_ref[member] == mode).astype(jnp.int32)
        high_ref[found] = mode
        found = found + 1 - is_low


def tile_at(step, points):
    halves = points // LANES
    return (
        pl.ds(pl.multiple_of((step // halves) * 8, 8), 8),
        pl.ds(pl.multiple_of((step % halves) * LANES, LANES), LANES),
    )


def inverse(fields, back_ref):
    columns = back_ref.shape[1] // 2
    top, rest = two_parts(fields)
    both = dot(top, back_ref[...])
    return both[:, :columns] + both[:, columns:] + dot(rest, back_ref[:, :columns])


def stress_kernel(low_ref, near_ref, *refs):
    block_refs, refs = (refs[:-10], refs[-10:])
    first_ref, second_ref, back_ref, _ = refs[:4]
    slotted_ref, physical, kept_ref, sent_ref, sums, high_ref = refs[4:]
    components, modes, rows, columns = slotted_ref.shape
    if len(block_refs) > 1:
        bands = len(block_refs)
        places = [lax.axis_index("kx") ^ step_at(bands, index) for index in range(bands)]
    else:
        bands = block_refs[0].shape[0]
        places = list(range(bands))
        block_refs = [block_refs[0].at[index] for index in range(bands)]
    points, band_modes = (physical.shape[3], modes // bands)
    members = sums.shape[1]
    odd = (lax.axis_index("real") & 1) == 1
    list_high(low_ref, high_ref, modes)
    size = band_modes * rows
    for c in range(components):
        joined = [block_ref[c * size : (c + 1) * size] for block_ref in block_refs]
        top, rest = two_parts(jnp.concatenate(joined, axis=0))
        both = dot(jnp.concatenate([top, rest], axis=1), first_ref[...])
        fields = both[:, :points] + dot(top, second_ref[...])
        for index in range(bands):
            place = pl.ds(places[index] * band_modes, band_modes)
            part = slice(index * size, (index + 1) * size)
            physical[c, place] = fields[part].reshape(band_modes, rows, points)
            slotted_ref[c, place] = both[part, points:].reshape(band_modes, rows, columns)

    def pairs(step, carry):
        place = tile_at(step, points)

        def one_high(index, totals):
            mode = high_ref[index]
            own = [physical[(c, mode) + place] for c in range(components)]
            totals = list(totals)
            for member in range(members):
                partner = physical[(1, near_ref[mode, member]) + place]
                for c in range(components):
                    slot = member * components + c
                    totals[slot] = totals[slot] + own[c] * partner
            return tuple(totals)

        empty = tuple(jnp.zeros((8, LANES), jnp.float32) for _ in range(members * components))
        totals = lax.fori_loop(0, modes - members, one_high, empty)
        for member in range(members):
            for c in range(components):
                sums[(c, member) + place] = totals[member * components + c]
        return carry

    lax.fori_loop(0, (rows // 8) * (points // LANES), pairs, 0)
    stress = inverse(sums[...].reshape(components * members * rows, points), back_ref)
    stress = stress.reshape(components, 2, members // 2, rows, columns)
    kept_ref[...] = jnp.where(odd, stress[:, 1], stress[:, 0])
    sent_ref[...] = jnp.where(odd, stress[:, 0], stress[:, 1])


def stress_terms(blocks, shape, low_index, neighbours, tables, after):
    components, modes, rows, columns = shape
    members, points = (low_index.shape[0], 2 * columns)
    half = jax.ShapeDtypeStruct((components, members // 2, rows, columns), jnp.float32)
    return pl.pallas_call(
        stress_kernel,
        out_shape=(
            jax.ShapeDtypeStruct(shape, jnp.float32),
            jax.ShapeDtypeStruct((components, modes, rows, points), jnp.float32),
            half,
            half,
        ),
        in_specs=[SMEM] * 2 + [VMEM] * (len(blocks) + 3) + [pl.BlockSpec(memory_space=pl.ANY)],
        out_specs=(VMEM,) * 4,
        scratch_shapes=[
            pltpu.VMEM((components, members, rows, points), jnp.float32),
            pltpu.SMEM((modes + 1,), jnp.int32),
        ],
        compiler_params=params(),
        cost_estimate=cost(4 * components * modes * rows * points * members),
        name="stress",
    )(low_index, neighbours, *blocks, *tables, after)


def products_kernel(
    low_ref, near_ref, count_ref, physical, back_ref, slot_ref, out_ref, products, high_ref
):
    components, modes, rows, points = physical.shape
    members, highs = (low_ref.shape[0], out_ref.shape[1])
    list_high(low_ref, high_ref, modes)

    def pairs(step, carry):
        place = tile_at(step, points)
        low = [
            [physical[(c, low_ref[member]) + place] for c in range(components)]
            for member in range(members)
        ]

        def one_high(index, inner):
            mode = high_ref[index]
            result = [jnp.zeros((8, LANES), jnp.float32) for _ in range(components)]
            for member in range(members):
                near = near_ref[mode, member]
                partner = [physical[(c, near) + place] for c in range(components)]
                for c in range(components):
                    if c == 1:
                        result[c] = result[c] + low[member][1] * partner[1]
                    else:
                        result[c] = result[c] + (
                            low[member][c] * partner[1] + partner[c] * low[member][1]
                        )
            for c in range(components):
                products[(c, index) + place] = result[c] * 2.0 if c == 1 else result[c]
            return inner

        lax.fori_loop(0, highs, one_high, 0)
        return carry

    lax.fori_loop(0, (rows // 8) * (points // LANES), pairs, 0)
    forcing = inverse(products[...].reshape(components * highs * rows, points), back_ref)
    forcing = forcing.reshape(out_ref.shape)
    for index in range(highs):
        active = slot_ref[:1] < count_ref[high_ref[index]]
        out_ref[:, index] = jnp.where(active, forcing[:, index] * dt_step, 0.0)


def high_terms(physical, low_index, neighbours, mode_counts, back, slot_modes):
    components, modes, rows, points = physical.shape
    highs = modes - low_index.shape[0]
    return pl.pallas_call(
        products_kernel,
        out_shape=jax.ShapeDtypeStruct((components, highs, rows, points // 2), jnp.float32),
        in_specs=[SMEM] * 3 + [VMEM] * 3,
        out_specs=VMEM,
        scratch_shapes=[
            pltpu.VMEM((components, highs, rows, points), jnp.float32),
            pltpu.SMEM((modes + 1,), jnp.int32),
        ],
        compiler_params=params(),
        cost_estimate=cost(4 * physical.size * low_index.shape[0]),
        name="products",
    )(low_index, neighbours, mode_counts, physical, back, slot_modes)


def outgoing_kernel(
    low_ref, count_ref, slotted_ref, forcing_ref, kept_ref, other_ref, slot_ref, *refs,
    groups, band_modes, owners, scale
):
    out_refs, (full, turned, high_ref) = (refs[:-3], refs[-3:])
    components, modes, rows, columns = slotted_ref.shape
    half, slots = (kept_ref.shape[1], columns // 2 // owners)
    per_slot = out_refs[0].shape[0] * len(out_refs) // (columns // 2)
    own = lax.axis_index("real") & 1
    list_high(low_ref, high_ref, modes)
    full[...] = slotted_ref[...]
    for index in range(forcing_ref.shape[1]):
        for c in range(components):
            full[c, high_ref[index]] += forcing_ref[c, index]
    for member in range(half):
        for part_ref, start in ((kept_ref, own * half), (other_ref, (1 - own) * half)):
            mode = low_ref[start + member]
            active = slot_ref[:1] < count_ref[mode]
            for c in range(components):
                full[c, mode] += jnp.where(active, part_ref[c, member] * scale, 0.0)
    inner = modes // groups
    if len(out_refs) > 1:
        me = lax.axis_index("kx") * lax.axis_size("ht") + lax.axis_index("ht")
        targets = [me ^ step_at(owners, position) for position in range(owners)]
    for c in range(components):
        for part in range(inner):
            tile = jnp.concatenate([full[c, part + inner * g] for g in range(groups)], axis=0)
            band_low, band_mode = (part // band_modes, part % band_modes)
            if len(out_refs) > 1:
                turned[...] = tile.T
            else:
                value = tile.T
            for p in range(2):
                row = ((band_low * 2 + p) * components + c) * band_modes + band_mode
                if len(out_refs) == 1:
                    out_refs[0][pl.ds(row, columns // 2, stride=per_slot), :] = value[
                        p * (columns // 2) : (p + 1) * (columns // 2)
                    ]
                    continue
                for out_ref, target in zip(out_refs, targets):
                    start = pl.multiple_of((p * owners + target) * slots, slots)
                    out_ref[pl.ds(row, slots, stride=per_slot), :] = turned[pl.ds(start, slots)]


def outgoing(
    slotted, forcing, kept, other, low_index, mode_counts, slot_modes, groups, band_modes, owners,
    realizations, separate,
):
    components, modes, rows, columns = slotted.shape
    total, lanes = ((columns // 2) * (modes // groups) * 2 * components, groups * rows)
    count = owners if separate else 1
    return pl.pallas_call(
        functools.partial(
            outgoing_kernel, groups=groups, band_modes=band_modes, owners=owners,
            scale=dt_step / realizations,
        ),
        out_shape=(jax.ShapeDtypeStruct((total // count, lanes), jnp.float32),) * count,
        in_specs=[SMEM, SMEM] + [VMEM] * 5,
        out_specs=(VMEM,) * count,
        scratch_shapes=[
            pltpu.VMEM(slotted.shape, jnp.float32), pltpu.VMEM((columns, lanes), jnp.float32),
            pltpu.SMEM((modes + 1,), jnp.int32),
        ],
        compiler_params=params(),
        cost_estimate=cost(8 * slotted.size),
        name="outgoing",
    )(low_index, mode_counts, slotted, forcing, kept, other, slot_modes)


def regroup(blocks, rows):
    count = len(blocks)
    lane = lax.broadcasted_iota(jnp.int32, blocks[0].shape, 1) // rows
    step = 1
    while step < count:
        take = (lane & step) == 0
        for i in range(count):
            if i & step == 0:
                here, there = (blocks[i], blocks[i + step])
                blocks[i] = jnp.where(take, here, pltpu.roll(there, step * rows, 1))
                blocks[i + step] = jnp.where(
                    take, pltpu.roll(here, LANES - step * rows, 1), there
                )
        step *= 2
    return blocks


def solve_kernel(*refs, groups, kx_count, ht_count, pieces, piece):
    owners, last = (kx_count * ht_count, piece == pieces - 1)
    own_kx, own_ht = (lax.axis_index("kx"), lax.axis_index("ht"))
    partners = []
    for position in range(owners):
        step = step_at(owners, position)
        partners.append((own_kx ^ (step // ht_count), own_ht ^ (step % ht_count)))
    refs = list(refs)
    matrices = refs.pop()
    arrived = refs.pop()
    source = refs.pop(0)
    if piece:
        ordered = refs.pop()
        blocks = [source] + [refs.pop(0) for _ in range(owners - 1)]
        for block_ref, (kx, ht) in zip(blocks, partners):
            ordered[kx * ht_count + ht] = block_ref[...]
        source = ordered
    matrix_ref = refs.pop(0)
    slots, heights = (matrix_ref.shape[0], matrix_ref.shape[1])
    width = heights // ht_count // pieces
    copies = [
        [
            pltpu.make_async_copy(
                matrix_ref.at[s, :, pl.ds((h * pieces + piece) * width, width)],
                matrices.at[s, h],
                arrived.at[s, h],
            )
            for h in range(ht_count)
        ]
        for s in range(slots)
    ]
    ahead = min(3, slots)
    for s in range(ahead):
        for copy in copies[s]:
            copy.start()
    partial_ref = refs.pop(0) if piece else None
    if last:
        out_refs, full = (refs[:owners], refs[owners])
        lane_tiles, per_band = out_refs[0].shape[1:3]
    rows = LANES // groups
    for s in range(slots):
        tiles = []
        for h in range(ht_count):
            for first in range(0, kx_count, groups):
                blocks = [source[(first + g) * ht_count + h, s] for g in range(groups)]
                tiles.append(jnp.concatenate(regroup(blocks, rows), axis=0))
        fields = jnp.concatenate(tiles, axis=1)
        count = fields.shape[0]
        spare = -count % LANES
        if spare:
            empty = jnp.zeros((spare, fields.shape[1]), jnp.float32)
            fields = jnp.concatenate([fields, empty], axis=0)
        top, rest = two_parts(fields)
        for copy in copies[s]:
            copy.wait()
        if s + ahead < slots:
            for copy in copies[s + ahead]:
                copy.start()
        matrix = jnp.concatenate([matrices[s, h] for h in range(ht_count)], axis=1)
        matrix_top, matrix_rest = two_parts(matrix)
        contract = ((1,), (1,))
        both = dot(matrix_top, jnp.concatenate([top, rest], axis=0), contract)
        solved = both[:, : count + spare] + both[:, count + spare :]
        solved = solved + dot(matrix_rest, top, contract)
        if piece:
            solved = solved + partial_ref[s]
        if not last:
            refs[0][s] = solved
            continue
        for tile in range(heights // LANES):
            full[s % 2, tile] = solved[tile * LANES : (tile + 1) * LANES].T[:count]
        for out_ref, (kx, ht) in zip(out_refs, partners):
            band = pl.ds(pl.multiple_of(kx * per_band, 8), per_band)
            for tile in range(lane_tiles):
                out_ref[s, tile] = full[s % 2, ht * lane_tiles + tile, band]


def solve(blocks, helmholtz, piece, pieces, partial, groups, kx_count, ht_count):
    slots, per_slot, _ = blocks[0].shape[-3:]
    heights, owners, last = (helmholtz.shape[1], kx_count * ht_count, piece == pieces - 1)
    count = per_slot * groups
    scratch = []
    if last:
        shape = (slots, heights // ht_count // LANES, count // kx_count, LANES)
        out_shape = (jax.ShapeDtypeStruct(shape, jnp.float32),) * owners
        scratch.append(pltpu.VMEM((2, heights // LANES, count, LANES), jnp.float32))
    else:
        padded = -(-count // LANES) * LANES
        out_shape = jax.ShapeDtypeStruct((slots, heights, padded), jnp.float32)
    if piece:
        scratch.append(pltpu.VMEM((owners,) + blocks[0].shape, jnp.float32))
    width = heights // ht_count // pieces
    scratch += [
        pltpu.SemaphoreType.DMA((slots, ht_count)),
        pltpu.VMEM((slots, ht_count, heights, width), jnp.float32),
    ]
    started = [] if partial is None else [partial]
    return pl.pallas_call(
        functools.partial(
            solve_kernel, groups=groups, kx_count=kx_count, ht_count=ht_count, pieces=pieces,
            piece=piece,
        ),
        out_shape=out_shape,
        in_specs=[VMEM] * len(blocks) + [pl.BlockSpec(memory_space=pl.ANY)] + [VMEM] * len(started),
        out_specs=(VMEM,) * owners if last else VMEM,
        scratch_shapes=scratch,
        compiler_params=params(),
        cost_estimate=cost(8 * helmholtz.size // pieces),
        name="solve",
    )(*blocks, helmholtz, *started)


def restore_kernel(*refs, owners, ht_count):
    block_refs, (order_ref, out_ref, ordered) = (refs[:-3], refs[-3:])
    components, band_modes, rows, columns = out_ref.shape
    slots = columns // 2 // owners
    per_slot = block_refs[0].shape[0] // slots
    me = lax.axis_index("kx") * ht_count + lax.axis_index("ht")
    for position, block_ref in enumerate(block_refs):
        ordered[me ^ step_at(owners, position)] = block_ref[...]
    for c in range(components):
        for mode in range(band_modes):
            for tile in range(rows // LANES):
                parts = []
                for p in range(2):
                    row = ((tile * 2 + p) * components + c) * band_modes + mode
                    for owner in range(owners):
                        parts.append(ordered[owner, pl.ds(row, slots, stride=per_slot), :])
                top, rest = two_parts(jnp.concatenate(parts, axis=0))
                both = jnp.concatenate([top, rest], axis=0)
                out_ref[c, mode, pl.ds(tile * LANES, LANES)] = dot(
                    both, order_ref[...], ((0,), (0,))
                )


def restore(blocks, order, components, band_modes, rows, ht_count):
    columns = order.shape[1]
    return pl.pallas_call(
        functools.partial(restore_kernel, owners=len(blocks), ht_count=ht_count),
        out_shape=jax.ShapeDtypeStruct((components, band_modes, rows, columns), jnp.float32),
        in_specs=[VMEM] * (len(blocks) + 1),
        out_specs=VMEM,
        scratch_shapes=[pltpu.VMEM((len(blocks),) + blocks[0].shape, jnp.float32)],
        compiler_params=params(),
        cost_estimate=cost(8 * components * band_modes * rows * columns),
        name="restore",
    )(*blocks, order)


def exchange(blocks, axes):
    count, realizations = (len(blocks), lax.axis_size("real"))
    result = list(blocks)
    for position in range(1, count):
        steps = [order[position] for order in steps_of(count)]
        pairs = [
            (index * realizations + r, (index ^ steps[r % 2]) * realizations + r)
            for index in range(count)
            for r in range(realizations)
        ]
        result[position] = lax.ppermute(blocks[position], axes + ("real",), pairs)
    return result


def sum_kernel(first_ref, second_ref, _, out_ref):
    out_ref[...] = first_ref[...] + second_ref[...]


def ordered_sum(first, second, after):
    return pl.pallas_call(
        sum_kernel,
        out_shape=jax.ShapeDtypeStruct(first.shape, jnp.float32),
        in_specs=[VMEM, VMEM, pl.BlockSpec(memory_space=pl.ANY)],
        out_specs=VMEM,
        compiler_params=params(),
        cost_estimate=cost(12 * first.size),
        name="ordered_sum",
    )(first, second, after)


def swap(value, step):
    pairs = [(index, index ^ step) for index in range(lax.axis_size("real"))]
    return lax.ppermute(value, "real", pairs)


def local(velocity, low_index, neighbours, owner_map, mode_counts, helmholtz):
    components, reals_dev, band_modes, rows_ht, columns = velocity.shape
    kx_count, ht_count = (lax.axis_size("kx"), lax.axis_size("ht"))
    own_kx, own_ht = (lax.axis_index("kx"), lax.axis_index("ht"))
    owners, pieces, real_count = (kx_count * ht_count, PIECES, lax.axis_size("real"))
    rows = rows_ht // (kx_count * pieces)
    groups = LANES // rows if rows else 0
    slots = columns // 2 // owners
    if (
        columns != LANES or reals_dev != 1 or rows_ht % LANES or rows % 8 or LANES % rows or kx_count % groups or kx_count & (kx_count - 1)
        or (band_modes * 2 * components) % 8 or slots % 8 or owners & (owners - 1) or low_index.shape[0] >= kx_count * band_modes
        or low_index.shape[0] >= columns or low_index.shape[0] % 2 or real_count < 2 or real_count & (real_count - 1)
    ):
        return local_plain(velocity, low_index, neighbours, owner_map, mode_counts, helmholtz)
    realizations, members = (real_count, low_index.shape[0])
    chunks, modes = (components * band_modes, band_modes * kx_count)
    shape = (components, modes, rows, columns)
    extra_rows = -(-band_modes // 8) * 8
    split = velocity.reshape(chunks, pieces, kx_count, rows, columns)
    blocks = pack_first(split, neighbours, mode_counts, extra_rows)
    parts = [exchange(blocks, ("kx",))]
    for piece in range(1, pieces):
        block = hand_on(pack(split, piece), parts[0][min(2, kx_count - 1)])
        block = lax.all_to_all(block, "kx", split_axis=0, concat_axis=0, tiled=True)
        parts.append((block,))
    tables, order, slot_modes = slot_tables(owner_map, columns)
    small = 0.0
    for index, block in enumerate(parts[0]):
        lines = block[chunks * rows : chunks * rows + band_modes, : members + 1]
        here = (own_kx ^ step_at(kx_count, index)) == jnp.arange(kx_count)
        small = small + jnp.where(here[:, None, None], lines[None], 0.0)
    small = small.reshape(modes, members + 1).astype(jnp.int32)
    neighbours, mode_counts = (small[:, :-1], small[:, -1])
    after = slot_modes
    received = []
    for piece, part in enumerate(parts):
        slotted, physical, kept, sent = stress_terms(
            part, shape, low_index, neighbours, tables, after
        )
        forcing = high_terms(physical, low_index, neighbours, mode_counts, tables[2], slot_modes)
        kept = after = kept + swap(sent, 1)
        step = 2
        while step < realizations:
            kept = ordered_sum(kept, swap(kept, step), forcing)
            step *= 2
        blocks = outgoing(
            slotted, forcing, kept, swap(kept, 1), low_index, mode_counts, slot_modes, groups, band_modes,
            owners, realizations, piece > 0,
        )
        if piece:
            blocks = [block.reshape(slots, -1, LANES) for block in blocks]
            received.append(exchange(blocks, ("kx", "ht")))
        else:
            block = blocks[0].reshape(owners, slots, -1, LANES)
            block = lax.all_to_all(block, ("kx", "ht"), split_axis=0, concat_axis=0, tiled=True)
            received.append([block])
    solved = None
    for piece, blocks in enumerate(received):
        solved = solve(blocks, helmholtz, piece, pieces, solved, groups, kx_count, ht_count)
    returned = [block.reshape(-1, LANES) for block in exchange(solved, ("kx", "ht"))]
    result = restore(returned, order, components, band_modes, rows_ht, ht_count)
    return result.reshape(velocity.shape)


def solution(mesh):
    in_specs = (
        P(None, "real", "kx", "ht", None),
        P(),
        P("kx", None),
        P(),
        P("kx"),
        P(("kx", "ht"), None, None),
    )
    out_specs = P(None, "real", "kx", "ht", None)
    return jax.shard_map(local, mesh=mesh, in_specs=in_specs, out_specs=out_specs, check_vma=False)
```

```python
import functools

import jax
import jax.numpy as jnp
import numpy as np
from jax import lax
from jax.experimental import pallas as pl
from jax.experimental.pallas import tpu as pltpu
from jax.sharding import PartitionSpec as P

dt_step = 0.1


def spanwise_tables(mode_count, point_count):
    column_ids = jnp.arange(2 * mode_count)
    wavenumber = (column_ids // 2).astype(jnp.float32)
    imag_part = column_ids % 2
    positions = 2.0 * jnp.pi * jnp.arange(point_count).astype(jnp.float32) / point_count
    phases = wavenumber[:, None] * positions[None, :]
    forward = jnp.where(imag_part[:, None] == 0, jnp.cos(phases), -jnp.sin(phases)) / jnp.sqrt(
        jnp.float32(mode_count)
    )
    backward = forward.T * (2.0 * mode_count / point_count)
    return (forward, backward)


def nonlinear_rows(fields, low_index, neighbours, mode_counts, forward, backward):
    precision = lax.Precision.HIGH
    realizations, modes, columns = (fields.shape[1], fields.shape[2], fields.shape[4])
    low_select = (low_index[:, None] == jnp.arange(modes)[None, :]).astype(jnp.float32)
    high_mask = 1.0 - jnp.sum(low_select, axis=0)
    high_rows = high_mask[None, None, :, None, None]
    column_mask = ((jnp.arange(columns) // 2)[None, :] < mode_counts[:, None]).astype(jnp.float32)
    physical = jnp.dot(fields, forward, precision=precision)
    low_fields = jnp.take(physical, low_index, axis=2)
    high_low = jnp.zeros_like(physical)
    stresses = []
    for member in range(low_index.shape[0]):
        partner = jnp.take(physical, neighbours[:, member], axis=2)
        low_one = low_fields[:, :, member : member + 1]
        high_low = high_low + low_one * partner[1:2] + partner * low_one[1:2]
        stresses.append(jnp.sum(physical * (partner[1:2] * high_rows), axis=(1, 2)))
    stress = jnp.stack(stresses, axis=1) / realizations
    forcing = jnp.dot(high_low, backward, precision=precision) * high_rows
    low_forcing = jnp.dot(stress, backward, precision=precision)
    low_rows = jnp.einsum("jm,cjyk->cmyk", low_select, low_forcing, precision=lax.Precision.HIGHEST)
    forcing = (forcing + low_rows[:, None]) * column_mask[None, None, :, None, :]
    return fields + dt_step * forcing


def local_plain(velocity, low_index, neighbours, owner_map, mode_counts, helmholtz):
    components, reals_dev, band_modes, rows_ht, columns = velocity.shape
    kz_modes = columns // 2
    forward, backward = spanwise_tables(kz_modes, 4 * kz_modes)
    kx_count, ht_count = (lax.axis_size("kx"), lax.axis_size("ht"))
    real_count = lax.axis_size("real")
    modes, realizations = (band_modes * kx_count, reals_dev * real_count)
    slots_dev = kz_modes // (kx_count * ht_count)
    rows_dev = rows_ht // (kx_count * real_count)
    small = jnp.concatenate([neighbours, mode_counts[:, None]], axis=1)
    small = lax.all_gather(small, "kx", axis=0, tiled=True)
    neighbours, mode_counts = (small[:, :-1], small[:, -1])
    inverse_map = (
        jnp.zeros((kz_modes,), jnp.int32).at[owner_map].set(jnp.arange(kz_modes, dtype=jnp.int32))
    )
    split = velocity.reshape(
        components, reals_dev, band_modes, kx_count * real_count, rows_dev, columns
    )
    split = split.transpose(3, 0, 1, 2, 4, 5)
    split = lax.all_to_all(split, ("kx", "real"), split_axis=0, concat_axis=0, tiled=True)
    fields = split.reshape(
        kx_count, real_count, components, reals_dev, band_modes, rows_dev, columns
    )
    fields = fields.transpose(2, 1, 3, 0, 4, 5, 6).reshape(
        components, realizations, modes, rows_dev, columns
    )
    updated = nonlinear_rows(fields, low_index, neighbours, mode_counts, forward, backward)
    slotted = jnp.take(
        updated.reshape(components, realizations, modes, rows_dev, kz_modes, 2), owner_map, axis=4
    )
    slotted = slotted.reshape(
        components, real_count, reals_dev, modes, rows_dev, kx_count * ht_count, slots_dev, 2
    )
    outgoing = slotted.transpose(5, 1, 6, 2, 0, 3, 7, 4).reshape(
        kx_count * ht_count * real_count, slots_dev, reals_dev * components * modes * 2, rows_dev
    )
    incoming = lax.all_to_all(
        outgoing, ("kx", "ht", "real"), split_axis=0, concat_axis=0, tiled=True
    )
    incoming = incoming.reshape(
        kx_count, ht_count, real_count, slots_dev, reals_dev * components * modes * 2, rows_dev
    )
    incoming = incoming.transpose(3, 4, 1, 0, 2, 5).reshape(
        slots_dev, reals_dev * components * modes * 2, ht_count * rows_ht
    )
    solved = jnp.einsum("syx,snx->sny", helmholtz, incoming, precision=lax.Precision.HIGH)
    solved = solved.reshape(
        slots_dev, reals_dev, components, kx_count, band_modes, 2, ht_count, rows_ht
    )
    solved = solved.transpose(3, 6, 0, 5, 1, 2, 4, 7).reshape(
        kx_count * ht_count, slots_dev * 2, reals_dev * components * band_modes, rows_ht
    )
    returned = lax.all_to_all(solved, ("kx", "ht"), split_axis=0, concat_axis=0, tiled=True)
    restored = returned.reshape(
        kz_modes, 2, reals_dev, components, band_modes, rows_ht
    )
    restored = jnp.take(restored, inverse_map, axis=0)
    return restored.transpose(3, 2, 4, 5, 0, 1).reshape(velocity.shape)


LANES = 128
PIECES = 2
VMEM = pl.BlockSpec(memory_space=pltpu.VMEM)
SMEM = pl.BlockSpec(memory_space=pltpu.SMEM)


def params():
    return pltpu.CompilerParams(vmem_limit_bytes=24 * 1024 * 1024)


ORDERS = {4: (1, 3, 2), 8: (4, 1, 2, 6, 5, 3, 7)}


def steps_of(count):
    even = ORDERS.get(count, tuple(range(1, count)))
    odd = list(even)
    for first in range(0, count - 2, 2):
        odd[first], odd[first + 1] = (even[first + 1], even[first])
    return (0,) + tuple(even), (0,) + tuple(odd)


def step_at(count, position):
    even, odd = steps_of(count)
    return jnp.where((lax.axis_index("real") & 1) == 0, even[position], odd[position])


def cost(size):
    return pl.CostEstimate(flops=0, bytes_accessed=size, transcendentals=0)


def two_parts(value):
    top = value.astype(jnp.bfloat16)
    rest = (value - top.astype(jnp.float32)).astype(jnp.bfloat16)
    return top, rest


def dot(left, right, dims=((1,), (0,))):
    return lax.dot_general(left, right, (dims, ((), ())), preferred_element_type=jnp.float32)


def pack_first_kernel(near_ref, count_ref, velocity_ref, *out_refs):
    chunks, _, kx_count, rows, columns = velocity_ref.shape
    shape = (out_refs[0].shape[0] - chunks * rows, columns)
    row = lax.broadcasted_iota(jnp.int32, shape, 0)
    lane = lax.broadcasted_iota(jnp.int32, shape, 1)
    extra = jnp.zeros(shape, jnp.int32)
    modes, members = near_ref.shape
    for mode in range(modes):
        line = jnp.where(lane == members, count_ref[mode], 0)
        for member in range(members):
            line = jnp.where(lane == member, near_ref[mode, member], line)
        extra = jnp.where(row == mode, line, extra)
    extra = extra.astype(jnp.float32)
    own = lax.axis_index("kx")
    for index, out_ref in enumerate(out_refs):
        partner = own ^ step_at(kx_count, index)
        for chunk in range(chunks):
            out_ref[chunk * rows : (chunk + 1) * rows] = velocity_ref[chunk, 0, partner]
        out_ref[chunks * rows :] = extra


def pack_first(velocity, neighbours, mode_counts, extra_rows):
    chunks, _, kx_count, rows, columns = velocity.shape
    shape = jax.ShapeDtypeStruct((chunks * rows + extra_rows, columns), jnp.float32)
    return pl.pallas_call(
        pack_first_kernel,
        out_shape=(shape,) * kx_count,
        grid=(1,),
        in_specs=[
            SMEM,
            SMEM,
            pl.BlockSpec((chunks, 1, kx_count, rows, columns), lambda i: (0, 0, 0, 0, 0)),
        ],
        out_specs=(pl.BlockSpec(shape.shape, lambda i: (0, 0)),) * kx_count,
        cost_estimate=cost(4 * velocity.size),
        name="pack_first",
    )(neighbours, mode_counts, velocity)


def pack_kernel(velocity_ref, out_ref):
    chunks, _, kx_count, rows, columns = velocity_ref.shape
    for index in range(kx_count):
        for chunk in range(chunks):
            place = slice(chunk * rows, (chunk + 1) * rows)
            out_ref[index, place] = velocity_ref[chunk, 0, index]


def pack(velocity, piece):
    chunks, _, kx_count, rows, columns = velocity.shape
    shape = (kx_count, chunks * rows, columns)
    return pl.pallas_call(
        pack_kernel,
        out_shape=jax.ShapeDtypeStruct(shape, jnp.float32),
        grid=(1,),
        in_specs=[
            pl.BlockSpec((chunks, 1, kx_count, rows, columns), lambda i: (0, piece, 0, 0, 0)),
        ],
        out_specs=pl.BlockSpec(shape, lambda i: (0, 0, 0)),
        cost_estimate=cost(4 * velocity.size),
        name="pack",
    )(velocity)


def hand_on_kernel(value_ref, after_ref, out_ref):
    pass


def hand_on(value, after):
    return pl.pallas_call(
        hand_on_kernel,
        out_shape=jax.ShapeDtypeStruct(value.shape, value.dtype),
        in_specs=[pl.BlockSpec(memory_space=pl.ANY)] * 2,
        out_specs=pl.BlockSpec(memory_space=pl.ANY),
        input_output_aliases={0: 0},
        cost_estimate=cost(0),
        name="hand_on",
    )(value, after)


def tables_kernel(owner_ref, top_ref, rest_ref, first_ref, back_ref, order_ref, slot_ref):
    columns = slot_ref.shape[1]
    modes = columns // 2
    lane = lax.broadcasted_iota(jnp.int32, (8, columns), 1)
    mode = jnp.zeros((8, columns), jnp.int32)
    for slot in range(modes):
        mode = jnp.where(lane % modes == slot, owner_ref[slot], mode)
    slot_ref[...] = mode
    wanted = 2 * mode + lane // modes
    row = lax.broadcasted_iota(jnp.int32, (columns, columns), 0)
    chosen = (row == wanted[:1]).astype(jnp.float32)
    select = chosen.astype(jnp.bfloat16)
    points = top_ref.shape[1]
    for half in range(2):
        rows = slice(half * columns, (half + 1) * columns)
        first_ref[rows, :points] = top_ref[...]
        first_ref[rows, points:] = select
        order_ref[rows] = chosen.T.astype(jnp.bfloat16)
    for index, table_ref in enumerate((top_ref, rest_ref)):
        back = dot(table_ref[...], select, ((0,), (0,))) * (2.0 * modes / points)
        back_ref[:, index * columns : (index + 1) * columns] = back.astype(jnp.bfloat16)


def spanwise_constants(columns, points):
    mode = np.arange(columns) // 2
    phase = 2.0 * np.pi * ((mode[:, None] * np.arange(points)[None, :]) % points) / points
    forward = np.where(np.arange(columns)[:, None] % 2 == 0, np.cos(phase), -np.sin(phase))
    forward = (forward / np.sqrt(columns // 2)).astype(np.float32)
    top = forward.astype(jnp.bfloat16)
    rest = (forward - top.astype(np.float32)).astype(jnp.bfloat16)
    return jnp.asarray(top), jnp.asarray(rest)


def slot_tables(owner_map, columns):
    points = 2 * columns
    top, rest = spanwise_constants(columns, points)
    first, back, order, slot_modes = pl.pallas_call(
        tables_kernel,
        out_shape=(
            jax.ShapeDtypeStruct((2 * columns, points + columns), jnp.bfloat16),
            jax.ShapeDtypeStruct((points, 2 * columns), jnp.bfloat16),
            jax.ShapeDtypeStruct((2 * columns, columns), jnp.bfloat16),
            jax.ShapeDtypeStruct((8, columns), jnp.int32),
        ),
        in_specs=[SMEM, VMEM, VMEM],
        out_specs=(VMEM,) * 4,
        compiler_params=params(),
        cost_estimate=cost(16 * points * columns),
        name="tables",
    )(owner_map, top, rest)
    return (first, rest, back), order, slot_modes


def list_high(low_ref, high_ref, modes):
    found = jnp.int32(0)
    for mode in range(modes):
        is_low = jnp.int32(0)
        for member in range(low_ref.shape[0]):
            is_low = is_low | (low_ref[member] == mode).astype(jnp.int32)
        high_ref[found] = mode
        found = found + 1 - is_low


def tile_at(step, points):
    halves = points // LANES
    return (
        pl.ds(pl.multiple_of((step // halves) * 8, 8), 8),
        pl.ds(pl.multiple_of((step % halves) * LANES, LANES), LANES),
    )


def inverse(fields, back_ref):
    columns = back_ref.shape[1] // 2
    top, rest = two_parts(fields)
    both = dot(top, back_ref[...])
    return both[:, :columns] + both[:, columns:] + dot(rest, back_ref[:, :columns])


def stress_kernel(low_ref, near_ref, *refs):
    block_refs, refs = (refs[:-10], refs[-10:])
    first_ref, second_ref, back_ref, _ = refs[:4]
    slotted_ref, physical, kept_ref, sent_ref, sums, high_ref = refs[4:]
    components, modes, rows, columns = slotted_ref.shape
    if len(block_refs) > 1:
        bands = len(block_refs)
        places = [lax.axis_index("kx") ^ step_at(bands, index) for index in range(bands)]
    else:
        bands = block_refs[0].shape[0]
        places = list(range(bands))
        block_refs = [block_refs[0].at[index] for index in range(bands)]
    points, band_modes = (physical.shape[3], modes // bands)
    members = sums.shape[1]
    odd = (lax.axis_index("real") & 1) == 1
    list_high(low_ref, high_ref, modes)
    size = band_modes * rows
    for c in range(components):
        joined = [block_ref[c * size : (c + 1) * size] for block_ref in block_refs]
        top, rest = two_parts(jnp.concatenate(joined, axis=0))
        both = dot(jnp.concatenate([top, rest], axis=1), first_ref[...])
        fields = both[:, :points] + dot(top, second_ref[...])
        for index in range(bands):
            place = pl.ds(places[index] * band_modes, band_modes)
            part = slice(index * size, (index + 1) * size)
            physical[c, place] = fields[part].reshape(band_modes, rows, points)
            slotted_ref[c, place] = both[part, points:].reshape(band_modes, rows, columns)

    def pairs(step, carry):
        place = tile_at(step, points)

        def one_high(index, totals):
            mode = high_ref[index]
            own = [physical[(c, mode) + place] for c in range(components)]
            totals = list(totals)
            for member in range(members):
                partner = physical[(1, near_ref[mode, member]) + place]
                for c in range(components):
                    slot = member * components + c
                    totals[slot] = totals[slot] + own[c] * partner
            return tuple(totals)

        empty = tuple(jnp.zeros((8, LANES), jnp.float32) for _ in range(members * components))
        totals = lax.fori_loop(0, modes - members, one_high, empty)
        for member in range(members):
            for c in range(components):
                sums[(c, member) + place] = totals[member * components + c]
        return carry

    lax.fori_loop(0, (rows // 8) * (points // LANES), pairs, 0)
    stress = inverse(sums[...].reshape(components * members * rows, points), back_ref)
    stress = stress.reshape(components, 2, members // 2, rows, columns)
    kept_ref[...] = jnp.where(odd, stress[:, 1], stress[:, 0])
    sent_ref[...] = jnp.where(odd, stress[:, 0], stress[:, 1])


def stress_terms(blocks, shape, low_index, neighbours, tables, after):
    components, modes, rows, columns = shape
    members, points = (low_index.shape[0], 2 * columns)
    half = jax.ShapeDtypeStruct((components, members // 2, rows, columns), jnp.float32)
    return pl.pallas_call(
        stress_kernel,
        out_shape=(
            jax.ShapeDtypeStruct(shape, jnp.float32),
            jax.ShapeDtypeStruct((components, modes, rows, points), jnp.float32),
            half,
            half,
        ),
        in_specs=[SMEM] * 2 + [VMEM] * (len(blocks) + 3) + [pl.BlockSpec(memory_space=pl.ANY)],
        out_specs=(VMEM,) * 4,
        scratch_shapes=[
            pltpu.VMEM((components, members, rows, points), jnp.float32),
            pltpu.SMEM((modes + 1,), jnp.int32),
        ],
        compiler_params=params(),
        cost_estimate=cost(4 * components * modes * rows * points * members),
        name="stress",
    )(low_index, neighbours, *blocks, *tables, after)


def products_kernel(
    low_ref, near_ref, count_ref, physical, back_ref, slot_ref, out_ref, products, high_ref
):
    components, modes, rows, points = physical.shape
    members, highs = (low_ref.shape[0], out_ref.shape[1])
    list_high(low_ref, high_ref, modes)

    def pairs(step, carry):
        place = tile_at(step, points)
        low = [
            [physical[(c, low_ref[member]) + place] for c in range(components)]
            for member in range(members)
        ]

        def one_high(index, inner):
            mode = high_ref[index]
            result = [jnp.zeros((8, LANES), jnp.float32) for _ in range(components)]
            for member in range(members):
                near = near_ref[mode, member]
                partner = [physical[(c, near) + place] for c in range(components)]
                for c in range(components):
                    if c == 1:
                        result[c] = result[c] + low[member][1] * partner[1]
                    else:
                        result[c] = result[c] + (
                            low[member][c] * partner[1] + partner[c] * low[member][1]
                        )
            for c in range(components):
                products[(c, index) + place] = result[c] * 2.0 if c == 1 else result[c]
            return inner

        lax.fori_loop(0, highs, one_high, 0)
        return carry

    lax.fori_loop(0, (rows // 8) * (points // LANES), pairs, 0)
    forcing = inverse(products[...].reshape(components * highs * rows, points), back_ref)
    forcing = forcing.reshape(out_ref.shape)
    for index in range(highs):
        active = slot_ref[:1] < count_ref[high_ref[index]]
        out_ref[:, index] = jnp.where(active, forcing[:, index] * dt_step, 0.0)


def high_terms(physical, low_index, neighbours, mode_counts, back, slot_modes):
    components, modes, rows, points = physical.shape
    highs = modes - low_index.shape[0]
    return pl.pallas_call(
        products_kernel,
        out_shape=jax.ShapeDtypeStruct((components, highs, rows, points // 2), jnp.float32),
        in_specs=[SMEM] * 3 + [VMEM] * 3,
        out_specs=VMEM,
        scratch_shapes=[
            pltpu.VMEM((components, highs, rows, points), jnp.float32),
            pltpu.SMEM((modes + 1,), jnp.int32),
        ],
        compiler_params=params(),
        cost_estimate=cost(4 * physical.size * low_index.shape[0]),
        name="products",
    )(low_index, neighbours, mode_counts, physical, back, slot_modes)


def outgoing_kernel(
    low_ref, count_ref, slotted_ref, forcing_ref, kept_ref, other_ref, slot_ref, *refs,
    groups, band_modes, owners, scale
):
    out_refs, (full, turned, high_ref) = (refs[:-3], refs[-3:])
    components, modes, rows, columns = slotted_ref.shape
    half, slots = (kept_ref.shape[1], columns // 2 // owners)
    per_slot = out_refs[0].shape[0] * len(out_refs) // (columns // 2)
    own = lax.axis_index("real") & 1
    list_high(low_ref, high_ref, modes)
    full[...] = slotted_ref[...]
    for index in range(forcing_ref.shape[1]):
        for c in range(components):
            full[c, high_ref[index]] += forcing_ref[c, index]
    for member in range(half):
        for part_ref, start in ((kept_ref, own * half), (other_ref, (1 - own) * half)):
            mode = low_ref[start + member]
            active = slot_ref[:1] < count_ref[mode]
            for c in range(components):
                full[c, mode] += jnp.where(active, part_ref[c, member] * scale, 0.0)
    inner = modes // groups
    if len(out_refs) > 1:
        me = lax.axis_index("kx") * lax.axis_size("ht") + lax.axis_index("ht")
        targets = [me ^ step_at(owners, position) for position in range(owners)]
    for c in range(components):
        for part in range(inner):
            tile = jnp.concatenate([full[c, part + inner * g] for g in range(groups)], axis=0)
            band_low, band_mode = (part // band_modes, part % band_modes)
            if len(out_refs) > 1:
                turned[...] = tile.T
            else:
                value = tile.T
            for p in range(2):
                row = ((band_low * 2 + p) * components + c) * band_modes + band_mode
                if len(out_refs) == 1:
                    out_refs[0][pl.ds(row, columns // 2, stride=per_slot), :] = value[
                        p * (columns // 2) : (p + 1) * (columns // 2)
                    ]
                    continue
                for out_ref, target in zip(out_refs, targets):
                    start = pl.multiple_of((p * owners + target) * slots, slots)
                    out_ref[pl.ds(row, slots, stride=per_slot), :] = turned[pl.ds(start, slots)]


def outgoing(
    slotted, forcing, kept, other, low_index, mode_counts, slot_modes, groups, band_modes, owners,
    realizations, separate,
):
    components, modes, rows, columns = slotted.shape
    total, lanes = ((columns // 2) * (modes // groups) * 2 * components, groups * rows)
    count = owners if separate else 1
    return pl.pallas_call(
        functools.partial(
            outgoing_kernel, groups=groups, band_modes=band_modes, owners=owners,
            scale=dt_step / realizations,
        ),
        out_shape=(jax.ShapeDtypeStruct((total // count, lanes), jnp.float32),) * count,
        in_specs=[SMEM, SMEM] + [VMEM] * 5,
        out_specs=(VMEM,) * count,
        scratch_shapes=[
            pltpu.VMEM(slotted.shape, jnp.float32), pltpu.VMEM((columns, lanes), jnp.float32),
            pltpu.SMEM((modes + 1,), jnp.int32),
        ],
        compiler_params=params(),
        cost_estimate=cost(8 * slotted.size),
        name="outgoing",
    )(low_index, mode_counts, slotted, forcing, kept, other, slot_modes)


def regroup(blocks, rows):
    count = len(blocks)
    lane = lax.broadcasted_iota(jnp.int32, blocks[0].shape, 1) // rows
    step = 1
    while step < count:
        take = (lane & step) == 0
        for i in range(count):
            if i & step == 0:
                here, there = (blocks[i], blocks[i + step])
                blocks[i] = jnp.where(take, here, pltpu.roll(there, step * rows, 1))
                blocks[i + step] = jnp.where(
                    take, pltpu.roll(here, LANES - step * rows, 1), there
                )
        step *= 2
    return blocks


def solve_kernel(*refs, groups, kx_count, ht_count, pieces, piece):
    owners, last = (kx_count * ht_count, piece == pieces - 1)
    own_kx, own_ht = (lax.axis_index("kx"), lax.axis_index("ht"))
    partners = []
    for position in range(owners):
        step = step_at(owners, position)
        partners.append((own_kx ^ (step // ht_count), own_ht ^ (step % ht_count)))
    refs = list(refs)
    matrices = refs.pop()
    arrived = refs.pop()
    source = refs.pop(0)
    if piece:
        ordered = refs.pop()
        blocks = [source] + [refs.pop(0) for _ in range(owners - 1)]
        for block_ref, (kx, ht) in zip(blocks, partners):
            ordered[kx * ht_count + ht] = block_ref[...]
        source = ordered
    matrix_ref = refs.pop(0)
    slots, heights = (matrix_ref.shape[0], matrix_ref.shape[1])
    width = heights // ht_count // pieces
    copies = [
        [
            pltpu.make_async_copy(
                matrix_ref.at[s, :, pl.ds((h * pieces + piece) * width, width)],
                matrices.at[s, h],
                arrived.at[s, h],
            )
            for h in range(ht_count)
        ]
        for s in range(slots)
    ]
    ahead = min(3, slots)
    for s in range(ahead):
        for copy in copies[s]:
            copy.start()
    partial_ref = refs.pop(0) if piece else None
    if last:
        out_refs, full = (refs[:owners], refs[owners])
        lane_tiles, per_band = out_refs[0].shape[1:3]
    rows = LANES // groups
    for s in range(slots):
        tiles = []
        for h in range(ht_count):
            for first in range(0, kx_count, groups):
                blocks = [source[(first + g) * ht_count + h, s] for g in range(groups)]
                tiles.append(jnp.concatenate(regroup(blocks, rows), axis=0))
        fields = jnp.concatenate(tiles, axis=1)
        count = fields.shape[0]
        spare = -count % LANES
        if spare:
            empty = jnp.zeros((spare, fields.shape[1]), jnp.float32)
            fields = jnp.concatenate([fields, empty], axis=0)
        top, rest = two_parts(fields)
        for copy in copies[s]:
            copy.wait()
        if s + ahead < slots:
            for copy in copies[s + ahead]:
                copy.start()
        matrix = jnp.concatenate([matrices[s, h] for h in range(ht_count)], axis=1)
        matrix_top, matrix_rest = two_parts(matrix)
        contract = ((1,), (1,))
        both = dot(matrix_top, jnp.concatenate([top, rest], axis=0), contract)
        solved = both[:, : count + spare] + both[:, count + spare :]
        solved = solved + dot(matrix_rest, top, contract)
        if piece:
            solved = solved + partial_ref[s]
        if not last:
            refs[0][s] = solved
            continue
        for tile in range(heights // LANES):
            full[s % 2, tile] = solved[tile * LANES : (tile + 1) * LANES].T[:count]
        for out_ref, (kx, ht) in zip(out_refs, partners):
            band = pl.ds(pl.multiple_of(kx * per_band, 8), per_band)
            for tile in range(lane_tiles):
                out_ref[s, tile] = full[s % 2, ht * lane_tiles + tile, band]


def solve(blocks, helmholtz, piece, pieces, partial, groups, kx_count, ht_count):
    slots, per_slot, _ = blocks[0].shape[-3:]
    heights, owners, last = (helmholtz.shape[1], kx_count * ht_count, piece == pieces - 1)
    count = per_slot * groups
    scratch = []
    if last:
        shape = (slots, heights // ht_count // LANES, count // kx_count, LANES)
        out_shape = (jax.ShapeDtypeStruct(shape, jnp.float32),) * owners
        scratch.append(pltpu.VMEM((2, heights // LANES, count, LANES), jnp.float32))
    else:
        padded = -(-count // LANES) * LANES
        out_shape = jax.ShapeDtypeStruct((slots, heights, padded), jnp.float32)
    if piece:
        scratch.append(pltpu.VMEM((owners,) + blocks[0].shape, jnp.float32))
    width = heights // ht_count // pieces
    scratch += [
        pltpu.SemaphoreType.DMA((slots, ht_count)),
        pltpu.VMEM((slots, ht_count, heights, width), jnp.float32),
    ]
    started = [] if partial is None else [partial]
    return pl.pallas_call(
        functools.partial(
            solve_kernel, groups=groups, kx_count=kx_count, ht_count=ht_count, pieces=pieces,
            piece=piece,
        ),
        out_shape=out_shape,
        in_specs=[VMEM] * len(blocks) + [pl.BlockSpec(memory_space=pl.ANY)] + [VMEM] * len(started),
        out_specs=(VMEM,) * owners if last else VMEM,
        scratch_shapes=scratch,
        compiler_params=params(),
        cost_estimate=cost(8 * helmholtz.size // pieces),
        name="solve",
    )(*blocks, helmholtz, *started)


def restore_kernel(*refs, owners, ht_count):
    block_refs, (order_ref, out_ref, ordered) = (refs[:-3], refs[-3:])
    components, band_modes, rows, columns = out_ref.shape
    slots = columns // 2 // owners
    per_slot = block_refs[0].shape[0] // slots
    me = lax.axis_index("kx") * ht_count + lax.axis_index("ht")
    for position, block_ref in enumerate(block_refs):
        ordered[me ^ step_at(owners, position)] = block_ref[...]
    for c in range(components):
        for mode in range(band_modes):
            tiles = []
            for tile in range(rows // LANES):
                parts = []
                for p in range(2):
                    row = ((tile * 2 + p) * components + c) * band_modes + mode
                    for owner in range(owners):
                        parts.append(ordered[owner, pl.ds(row, slots, stride=per_slot), :])
                tiles.append(jnp.concatenate(parts, axis=0))
            top, rest = two_parts(jnp.concatenate(tiles, axis=1))
            both = jnp.concatenate([top, rest], axis=0)
            out_ref[c, mode] = dot(both, order_ref[...], ((0,), (0,)))


def restore(blocks, order, components, band_modes, rows, ht_count):
    columns = order.shape[1]
    return pl.pallas_call(
        functools.partial(restore_kernel, owners=len(blocks), ht_count=ht_count),
        out_shape=jax.ShapeDtypeStruct((components, band_modes, rows, columns), jnp.float32),
        in_specs=[VMEM] * (len(blocks) + 1),
        out_specs=VMEM,
        scratch_shapes=[pltpu.VMEM((len(blocks),) + blocks[0].shape, jnp.float32)],
        compiler_params=params(),
        cost_estimate=cost(8 * components * band_modes * rows * columns),
        name="restore",
    )(*blocks, order)


def exchange(blocks, axes):
    count, realizations = (len(blocks), lax.axis_size("real"))
    result = list(blocks)
    for position in range(1, count):
        steps = [order[position] for order in steps_of(count)]
        pairs = [
            (index * realizations + r, (index ^ steps[r % 2]) * realizations + r)
            for index in range(count)
            for r in range(realizations)
        ]
        result[position] = lax.ppermute(blocks[position], axes + ("real",), pairs)
    return result


def sum_kernel(first_ref, second_ref, _, out_ref):
    out_ref[...] = first_ref[...] + second_ref[...]


def ordered_sum(first, second, after):
    return pl.pallas_call(
        sum_kernel,
        out_shape=jax.ShapeDtypeStruct(first.shape, jnp.float32),
        in_specs=[VMEM, VMEM, pl.BlockSpec(memory_space=pl.ANY)],
        out_specs=VMEM,
        compiler_params=params(),
        cost_estimate=cost(12 * first.size),
        name="ordered_sum",
    )(first, second, after)


def swap(value, step):
    pairs = [(index, index ^ step) for index in range(lax.axis_size("real"))]
    return lax.ppermute(value, "real", pairs)


def local(velocity, low_index, neighbours, owner_map, mode_counts, helmholtz):
    components, reals_dev, band_modes, rows_ht, columns = velocity.shape
    kx_count, ht_count = (lax.axis_size("kx"), lax.axis_size("ht"))
    own_kx, own_ht = (lax.axis_index("kx"), lax.axis_index("ht"))
    owners, pieces, real_count = (kx_count * ht_count, PIECES, lax.axis_size("real"))
    rows = rows_ht // (kx_count * pieces)
    groups = LANES // rows if rows else 0
    slots = columns // 2 // owners
    if (
        columns != LANES or reals_dev != 1 or rows_ht % LANES or rows % 8 or LANES % rows or kx_count % groups or kx_count & (kx_count - 1)
        or (band_modes * 2 * components) % 8 or slots % 8 or owners & (owners - 1) or low_index.shape[0] >= kx_count * band_modes
        or low_index.shape[0] >= columns or low_index.shape[0] % 2 or real_count < 2 or real_count & (real_count - 1)
    ):
        return local_plain(velocity, low_index, neighbours, owner_map, mode_counts, helmholtz)
    realizations, members = (real_count, low_index.shape[0])
    chunks, modes = (components * band_modes, band_modes * kx_count)
    shape = (components, modes, rows, columns)
    extra_rows = -(-band_modes // 8) * 8
    split = velocity.reshape(chunks, pieces, kx_count, rows, columns)
    blocks = pack_first(split, neighbours, mode_counts, extra_rows)
    parts = [exchange(blocks, ("kx",))]
    for piece in range(1, pieces):
        block = hand_on(pack(split, piece), parts[0][min(2, kx_count - 1)])
        block = lax.all_to_all(block, "kx", split_axis=0, concat_axis=0, tiled=True)
        parts.append((block,))
    tables, order, slot_modes = slot_tables(owner_map, columns)
    small = 0.0
    for index, block in enumerate(parts[0]):
        lines = block[chunks * rows : chunks * rows + band_modes, : members + 1]
        here = (own_kx ^ step_at(kx_count, index)) == jnp.arange(kx_count)
        small = small + jnp.where(here[:, None, None], lines[None], 0.0)
    small = small.reshape(modes, members + 1).astype(jnp.int32)
    neighbours, mode_counts = (small[:, :-1], small[:, -1])
    after = slot_modes
    received = []
    for piece, part in enumerate(parts):
        slotted, physical, kept, sent = stress_terms(
            part, shape, low_index, neighbours, tables, after
        )
        forcing = high_terms(physical, low_index, neighbours, mode_counts, tables[2], slot_modes)
        kept = after = kept + swap(sent, 1)
        step = 2
        while step < realizations:
            kept = ordered_sum(kept, swap(kept, step), forcing)
            step *= 2
        blocks = outgoing(
            slotted, forcing, kept, swap(kept, 1), low_index, mode_counts, slot_modes, groups, band_modes,
            owners, realizations, piece > 0,
        )
        if piece:
            blocks = [block.reshape(slots, -1, LANES) for block in blocks]
            received.append(exchange(blocks, ("kx", "ht")))
        else:
            block = blocks[0].reshape(owners, slots, -1, LANES)
            block = lax.all_to_all(block, ("kx", "ht"), split_axis=0, concat_axis=0, tiled=True)
            received.append([block])
    solved = None
    for piece, blocks in enumerate(received):
        solved = solve(blocks, helmholtz, piece, pieces, solved, groups, kx_count, ht_count)
    returned = [block.reshape(-1, LANES) for block in exchange(solved, ("kx", "ht"))]
    result = restore(returned, order, components, band_modes, rows_ht, ht_count)
    return result.reshape(velocity.shape)


def solution(mesh):
    in_specs = (
        P(None, "real", "kx", "ht", None),
        P(),
        P("kx", None),
        P(),
        P("kx"),
        P(("kx", "ht"), None, None),
    )
    out_specs = P(None, "real", "kx", "ht", None)
    return jax.shard_map(local, mesh=mesh, in_specs=in_specs, out_specs=out_specs, check_vma=False)
```
